128 devices in a mesh: dp: 4 (over z), expert: 8 (over y, core), tensor: 4 (over x).
Axes of the slice: x: 4, y: 4, z: 4, core: 2. Of those that a mesh axis runs over, the one named last changes fastest.
Arguments:
- tokens: bfloat16 [5120, 2048], P(('dp', 'expert')), may hold values from -6 to 6
- cotangent: bfloat16 [5120, 2048], P(('dp', 'expert')), may hold values from -6 to 6
- attn_gain: bfloat16 [2048], replicated, may hold values from 0.5 to 1.5
- mlp_gain: bfloat16 [2048], replicated, may hold values from 0.5 to 1.5
- attn_router: bfloat16 [2048, 8], P(('dp', 'expert')), may hold values from -0.09375 to 0.09375
- key_value_weight: bfloat16 [2048, 2, 2048], P(('dp', 'expert'), None, 'tensor'), may hold values from -0.125 to 0.125
- query_matrix: bfloat16 [2048, 8, 2048], P(('dp', 'expert'), None, 'tensor'), may hold values from -0.125 to 0.125
- output_matrix: bfloat16 [2048, 8, 2048], P(('dp', 'expert'), None, 'tensor'), may hold values from -0.75 to 0.75
- mlp_router: bfloat16 [2048, 8], P(('dp', 'expert')), may hold values from -0.09375 to 0.09375
- gate_up_weight: bfloat16 [8, 2048, 2, 5632], P('expert', 'dp', None, 'tensor'), may hold values from -0.125 to 0.125
- down_weight: bfloat16 [8, 5632, 2048], P('expert', 'tensor', 'dp'), may hold values from -0.15625 to 0.15625
- attn_routes: int32 [5120, 2], P(('dp', 'expert')), may hold values from 0 to 7, all different within a row
- mlp_routes: int32 [5120, 2], P(('dp', 'expert')), may hold values from 0 to 7, all different within a row
- priority: int32 [32, 160], P(('dp', 'expert')), may hold values from 0 to 159, each once within a row
- segments: int32 [5120], replicated, may hold values from 0 to 2, as said below
Outputs:
- output: bfloat16 [5120, 2048], P(('dp', 'expert'))
- input_grad: bfloat16 [5120, 2048], P(('dp', 'expert'))
- attn_gain_grad: float32 [2048], P(('dp', 'expert'))
- mlp_gain_grad: float32 [2048], P(('dp', 'expert'))
- attn_router_grad: float32 [2048, 8], P(('dp', 'expert'))
- kv_grad: float32 [2048, 2, 2048], P(('dp', 'expert'), None, 'tensor')
- query_grad: float32 [2048, 8, 2048], P(('dp', 'expert'), None, 'tensor')
- out_grad: float32 [2048, 8, 2048], P(('dp', 'expert'), None, 'tensor')
- mlp_router_grad: float32 [2048, 8], P(('dp', 'expert'))
- gate_up_grad: float32 [8, 2048, 2, 5632], P('expert', 'dp', None, 'tensor')
- down_grad: float32 [8, 5632, 2048], P('expert', 'tensor', 'dp')
The draws below stay inside these ranges and needn't reach their ends.
Inputs may be any that keep to these rules, and one draw needn't show every extreme that they name: `attn_routes`: each token names two different attention experts. `mlp_routes`: each token names two different feed-forward experts. `priority`: each row is an order of the 160 tokens of one group. `segments`: each sequence of 1280 tokens holds three documents numbered 0, 1, 2 in order; the first ends within the sequence's first 40 tokens and the last begins within its last 40 tokens.
All inputs are finite; a program needn't handle non-finite values.
Results may differ from the reference program's by a relative error of at most 0.025.
Values may be sent and summed in bfloat16 or wider, within the bound.
No kernel may reach another device: no remote copies, remote signals or barrier semaphores. Data moves between devices by JAX's collectives and lax.ppermute only.
A program may use at most 320 MiB of HBM per device.

```python
import jax
import jax.numpy as jnp
from jax import lax

MODEL_WIDTH = 2048
KEY_VALUE_HEADS = 16
HEAD_SIZE = 128
ATTENTION_EXPERTS = 8
FF = 5632
WINDOW = 1024
SEQUENCE_TOKENS = 1280
TOK_DEV = 160
SEQUENCE_COUNT = 4
TOKEN_TOTAL = 5120
GROUPS = 32
MLP_EXP = 8
CAP = 50


def draw_segments(key, part):
    key = jax.random.fold_in(key, 11)
    first_key, second_key = jax.random.split(key, 2)
    spots = jnp.arange(SEQUENCE_TOKENS, dtype=jnp.int32)[None, :]
    edge = TOK_DEV // 4
    begin = jax.random.randint(first_key, (SEQUENCE_COUNT, 1), 1, edge + 1)
    finish = jax.random.randint(second_key, (SEQUENCE_COUNT, 1), SEQUENCE_TOKENS - edge, SEQUENCE_TOKENS)
    numbers = (spots >= begin).astype(jnp.int32) + (spots >= finish).astype(jnp.int32)
    return numbers.astype(jnp.int32).reshape(SEQUENCE_COUNT * SEQUENCE_TOKENS)


def strengthened(array, key, source, target, shards_of, factor):
    owner, partner = [(jnp.arange(array.shape[dim]) // (array.shape[dim] // shards_of)).reshape([-1 if axis == dim else 1 for axis in range(array.ndim)]) for dim in (source, target)]
    chosen = jax.random.permutation(key, shards_of)[partner]
    strong = (owner == chosen) | (owner == (partner + shards_of // 2) % shards_of)
    return jnp.where(strong, factor * array, array)


def shard_levels(own_key, shape, cuts, smallest, largest):
    def one(dim, parts):
        heights = jax.random.uniform(jax.random.fold_in(jax.random.fold_in(own_key, 6), dim), (parts,), jnp.float32, smallest / len(cuts), largest / len(cuts))
        return jnp.repeat(jnp.exp(heights), shape[dim] // parts).reshape((-1,) + (1,) * (len(shape) - dim - 1))

    factor_of = one(*cuts[0])
    for cut in cuts[1:]:
        factor_of = factor_of * one(*cut)
    return factor_of


def different_ones(rng, rows, count, top, lift):
    order = jax.random.permutation(jax.random.fold_in(rng, 1), count)
    boost = order
    for power in range(3):
        boost = boost * boost // count
    boost = boost * lift // count
    chance = jax.random.randint(jax.random.fold_in(rng, 2), (rows, count), 0, 4096) + boost
    sure = jax.random.permutation(jax.random.fold_in(rng, 3), rows)[jnp.arange(count) % rows]
    chance = jnp.where(jnp.arange(rows)[:, None] == sure[None, :], 1 << 14, chance)
    score = chance * count + jnp.arange(count)
    return lax.top_k(score.astype(jnp.int32), top)[1].astype(jnp.int32)


def scatter_about(stream_key, dims, deviation, most, cuts=(), kind=jnp.bfloat16):
    level = shard_levels(stream_key, dims, cuts, -0.22, 0.18) if cuts else 1.0
    drawn = jax.random.normal(stream_key, dims, jnp.float32) * deviation * level
    return jnp.minimum(jnp.maximum(drawn, -most), most).astype(kind)


def noise_with(own_key, extent, spread, bound, cuts, heavy, kind=jnp.bfloat16):
    values = spread * jax.random.normal(own_key, extent, jnp.float32)
    if cuts:
        values = values * shard_levels(own_key, extent, cuts, -0.22, 0.18)
    return jnp.clip(strengthened(values, jax.random.fold_in(own_key, 3), *heavy), -bound, bound).astype(kind)


def setup_inputs(seed: int = 0) -> dict:
    streams_of = jax.random.split(jax.random.key(seed), 16)
    tokens = scatter_about(streams_of[0], (TOKEN_TOTAL, MODEL_WIDTH), 1.0, 6.0, ((0, 32),))
    cotangent = noise_with(streams_of[1], (TOKEN_TOTAL, MODEL_WIDTH), 1.0, 6.0, ((0, 32),), (0, 1, 32, 2.75))
    attn_gain = jnp.clip(1.0 + 0.1 * jax.random.normal(streams_of[2], (MODEL_WIDTH,), jnp.float32), 0.5, 1.5).astype(jnp.bfloat16)
    mlp_gain = jnp.clip(1.0 + 0.1 * jax.random.normal(streams_of[3], (MODEL_WIDTH,), jnp.float32), 0.5, 1.5).astype(jnp.bfloat16)
    attn_router = scatter_about(streams_of[4], (MODEL_WIDTH, ATTENTION_EXPERTS), (2 * MODEL_WIDTH) ** -0.5, 0.09375, ((0, 32),))
    key_value_weight = scatter_about(streams_of[5], (MODEL_WIDTH, 2, KEY_VALUE_HEADS * HEAD_SIZE), MODEL_WIDTH ** -0.5, 0.125, ((0, 32), (2, 4)))
    query_matrix = scatter_about(streams_of[6], (MODEL_WIDTH, ATTENTION_EXPERTS, KEY_VALUE_HEADS * HEAD_SIZE), MODEL_WIDTH ** -0.5, 0.125, ((0, 32), (2, 4)))
    output_matrix = scatter_about(streams_of[7], (MODEL_WIDTH, ATTENTION_EXPERTS, KEY_VALUE_HEADS * HEAD_SIZE), (KEY_VALUE_HEADS * HEAD_SIZE // 32) ** -0.5, 0.75, ((0, 32), (2, 4)))
    mlp_router = scatter_about(streams_of[8], (MODEL_WIDTH, MLP_EXP), (2 * MODEL_WIDTH) ** -0.5, 0.09375, ((0, 32),))
    gate_up_weight = scatter_about(streams_of[9], (MLP_EXP, MODEL_WIDTH, 2, FF), MODEL_WIDTH ** -0.5, 0.125, ((0, 8), (1, 4), (3, 4)))
    down_weight = scatter_about(streams_of[10], (MLP_EXP, FF, MODEL_WIDTH), (FF // 4) ** -0.5, 0.15625, ((0, 8), (1, 4), (2, 4)))
    attn_routes = different_ones(streams_of[11], TOKEN_TOTAL, ATTENTION_EXPERTS, 2, 2048)
    mlp_routes = different_ones(streams_of[12], TOKEN_TOTAL, MLP_EXP, 2, 4096)
    priority = jax.vmap(lambda own: jax.random.permutation(own, TOK_DEV))(jax.random.split(streams_of[13], GROUPS)).reshape((GROUPS, TOK_DEV)).astype(jnp.int32)
    segments = draw_segments(jax.random.fold_in(streams_of[15], 71), 0)
    return {"tokens": tokens, "cotangent": cotangent, "attn_gain": attn_gain, "mlp_gain": mlp_gain, "attn_router": attn_router, "key_value_weight": key_value_weight, "query_matrix": query_matrix, "output_matrix": output_matrix, "mlp_router": mlp_router, "gate_up_weight": gate_up_weight, "down_weight": down_weight, "attn_routes": attn_routes, "mlp_routes": mlp_routes, "priority": priority, "segments": segments}


NORM_EPS = 1e-06
PRECISE = lax.Precision.HIGHEST

@jax.custom_vjp
def reduced_precision(v):
    return lax.optimization_barrier(v.astype(jnp.bfloat16)).astype(jnp.float32)

@jax.custom_vjp
def reduced_precision_back(v):
    return v

def low_keep(v):
    return (reduced_precision(v), None)

def low_pass(kept, grad):
    return (grad,)

def back_keep(v):
    return (v, None)

def back_low(kept, grad):
    return (reduced_precision(grad),)
reduced_precision.defvjp(low_keep, low_pass)
reduced_precision_back.defvjp(back_keep, back_low)

def rms_scale(values):
    return lax.rsqrt(lax.optimization_barrier(jnp.mean(values * values, axis=-1, keepdims=True)) + NORM_EPS)

def apply_rotary(heads, cosine_table, sine_table):
    half_width = heads.shape[-1] // 2
    first_half = heads[..., :half_width]
    second_half = heads[..., half_width:]
    return jnp.concatenate([first_half * cosine_table - second_half * sine_table, second_half * cosine_table + first_half * sine_table], axis=-1)

def pair_gates(logits, choose):
    chosen = jnp.einsum('te,tje->tj', logits, choose, precision=PRECISE)
    row_max = lax.optimization_barrier(jnp.max(chosen, axis=1, keepdims=True))
    weights = jnp.exp(chosen - row_max)
    return weights / lax.optimization_barrier(jnp.sum(weights, axis=1, keepdims=True))

def slot_table(mlp_routes, priority):
    grouped = mlp_routes.reshape(GROUPS, TOK_DEV, 2)

    def one_group(packed_item):
        route_group, ranking = packed_item
        at_rank = jnp.zeros((TOK_DEV,), jnp.int32).at[ranking].set(jnp.arange(TOK_DEV, dtype=jnp.int32))
        ordered = route_group[at_rank].reshape(2 * TOK_DEV)
        onehot = (ordered[:, None] == jnp.arange(MLP_EXP, dtype=jnp.int32)[None, :]).astype(jnp.int32)
        earlier = jnp.cumsum(onehot, axis=0) - onehot
        slot_ordered = lax.optimization_barrier(jnp.sum(earlier * onehot, axis=1)).astype(jnp.int32).reshape(TOK_DEV, 2)
        return slot_ordered[ranking]
    return lax.map(one_group, (grouped, priority)).reshape(TOKEN_TOTAL, 2).astype(jnp.int32)

def reference(tokens, cotangent, attn_gain, mlp_gain, attn_router, key_value_weight, query_matrix, output_matrix, mlp_router, gate_up_weight, down_weight, attn_routes, mlp_routes, priority, segments):
    position = (jnp.arange(TOKEN_TOTAL) % SEQUENCE_TOKENS).astype(jnp.float32)
    inverse = 10000.0 ** (-(jnp.arange(HEAD_SIZE // 2).astype(jnp.float32) * 2.0 / HEAD_SIZE))
    angle = position[:, None] * inverse[None, :]
    cosine_table = jnp.cos(angle)[:, None, :]
    sine_table = jnp.sin(angle)[:, None, :]
    slots = slot_table(mlp_routes, priority)
    kept = slots < CAP
    group_of = (jnp.arange(TOKEN_TOTAL, dtype=jnp.int32) // TOK_DEV)[:, None]
    total_rows = MLP_EXP * GROUPS * CAP
    dest = jnp.where(kept, mlp_routes * (GROUPS * CAP) + group_of * CAP + slots, total_rows).astype(jnp.int32)
    fetch = jnp.minimum(dest, total_rows - 1).astype(jnp.int32)
    keep_float = kept.astype(jnp.float32)
    attn_pick = (attn_routes[:, :, None] == jnp.arange(ATTENTION_EXPERTS, dtype=jnp.int32)[None, None, :]).astype(jnp.float32)
    mlp_pick = (mlp_routes[:, :, None] == jnp.arange(MLP_EXP, dtype=jnp.int32)[None, None, :]).astype(jnp.float32)
    segment_rows = segments.reshape(SEQUENCE_COUNT, SEQUENCE_TOKENS)
    spots = jnp.arange(SEQUENCE_TOKENS, dtype=jnp.int32)
    allowed_base = (spots[None, :] <= spots[:, None]) & (spots[:, None] - spots[None, :] < WINDOW)
    scale = HEAD_SIZE ** (-0.5)

    def attend_heads(packed_item):
        query_sequence, key_seq, value_seq, seg_seq = packed_item
        query_four_axes = query_sequence.reshape(SEQUENCE_TOKENS, 2, KEY_VALUE_HEADS, HEAD_SIZE)
        score = reduced_precision_back(jnp.einsum('qjhd,khd->jhqk', query_four_axes, key_seq, precision=PRECISE) * scale)
        allowed = allowed_base & (seg_seq[:, None] == seg_seq[None, :])
        score = jnp.where(allowed[None, None], score, -1e+30)
        row_max = lax.optimization_barrier(jnp.max(score, axis=-1, keepdims=True))
        weights = jnp.exp(score - row_max)
        prob = weights / lax.optimization_barrier(jnp.sum(weights, axis=-1, keepdims=True))
        return jnp.einsum('jhqk,khd->qjhd', reduced_precision(prob), value_seq, precision=PRECISE)

    def expert(packed_item):
        inputs, w_pair, w_back = packed_item
        gate_up = reduced_precision_back(jnp.einsum('rd,dcf->rcf', inputs, w_pair, precision=PRECISE))
        gate_part = gate_up[:, 0]
        activated = reduced_precision(gate_part * jax.nn.sigmoid(gate_part) * gate_up[:, 1])
        return reduced_precision(reduced_precision_back(jnp.dot(activated, w_back, precision=PRECISE)))

    def forward(x_in, gain_a, gain_m, router_a, w_kv, w_query, w_out, router_m, w_gate_up, w_down):
        xn1 = reduced_precision(x_in * rms_scale(x_in) * gain_a)
        key_value_projected = reduced_precision_back(jnp.einsum('td,dch->tch', xn1, w_kv, precision=PRECISE))
        key_head_rows = reduced_precision(apply_rotary(key_value_projected[:, 0].reshape(TOKEN_TOTAL, KEY_VALUE_HEADS, HEAD_SIZE), cosine_table, sine_table))
        value_head_rows = reduced_precision(key_value_projected[:, 1].reshape(TOKEN_TOTAL, KEY_VALUE_HEADS, HEAD_SIZE))
        q_all = reduced_precision_back(jnp.einsum('td,deh->teh', xn1, w_query, precision=PRECISE))
        query_selected = jnp.einsum('tje,teh->tjh', attn_pick, q_all, precision=PRECISE)
        query_rows = reduced_precision(apply_rotary(query_selected.reshape(TOKEN_TOTAL, 2 * KEY_VALUE_HEADS, HEAD_SIZE), cosine_table, sine_table))
        attended_rows = lax.map(jax.checkpoint(attend_heads), (query_rows.reshape(SEQUENCE_COUNT, SEQUENCE_TOKENS, 2 * KEY_VALUE_HEADS, HEAD_SIZE), key_head_rows.reshape(SEQUENCE_COUNT, SEQUENCE_TOKENS, KEY_VALUE_HEADS, HEAD_SIZE), value_head_rows.reshape(SEQUENCE_COUNT, SEQUENCE_TOKENS, KEY_VALUE_HEADS, HEAD_SIZE), segment_rows))
        attended_rows = reduced_precision_back(attended_rows.reshape(TOKEN_TOTAL, 2, KEY_VALUE_HEADS * HEAD_SIZE))
        gate_a = pair_gates(jnp.dot(xn1, router_a, precision=PRECISE), attn_pick)
        mixed = reduced_precision(jnp.einsum('tje,tj,tjh->teh', attn_pick, gate_a, attended_rows, precision=PRECISE))
        branch = reduced_precision_back(jnp.einsum('teh,deh->td', mixed, w_out, precision=PRECISE))
        hidden = x_in + branch
        xn2 = reduced_precision(hidden * rms_scale(hidden) * gain_m)
        gate_m = pair_gates(jnp.dot(xn2, router_m, precision=PRECISE), mlp_pick)
        pair_rows = jnp.broadcast_to(xn2[:, None, :], (TOKEN_TOTAL, 2, MODEL_WIDTH)).reshape(2 * TOKEN_TOTAL, MODEL_WIDTH)
        buffer = jnp.zeros((total_rows + 1, MODEL_WIDTH), jnp.float32).at[dest.reshape(-1)].set(pair_rows)[:total_rows]
        buffer = reduced_precision_back(buffer.reshape(MLP_EXP, GROUPS * CAP, MODEL_WIDTH))
        results = lax.map(jax.checkpoint(expert), (buffer, w_gate_up, w_down))
        fetched = results.reshape(total_rows, MODEL_WIDTH)[fetch.reshape(-1)].reshape(TOKEN_TOTAL, 2, MODEL_WIDTH)
        moe_out = jnp.einsum('tj,tjd->td', gate_m * keep_float, fetched, precision=PRECISE)
        return hidden + moe_out
    primals = (tokens.astype(jnp.float32), attn_gain.astype(jnp.float32), mlp_gain.astype(jnp.float32), attn_router.astype(jnp.float32), key_value_weight.astype(jnp.float32), query_matrix.astype(jnp.float32), output_matrix.astype(jnp.float32), mlp_router.astype(jnp.float32), gate_up_weight.astype(jnp.float32), down_weight.astype(jnp.float32))
    result, pullback = jax.vjp(forward, *primals)
    grads = pullback(cotangent.astype(jnp.float32))
    return (result.astype(jnp.bfloat16), grads[0].astype(jnp.bfloat16), grads[1], grads[2], grads[3], grads[4], grads[5], grads[6], grads[7], grads[8], grads[9])
```

```python
import jax
import jax.numpy as jnp
from jax import lax
from jax.experimental import pallas as pl
from jax.experimental.pallas import tpu as pltpu
from jax.sharding import Mesh
from jax.sharding import PartitionSpec as P

MODEL_WIDTH = 2048
HEAD_SIZE = 128
EXPERTS = 8
WINDOW = 1024
NORM_EPS = 1e-06
BF = jnp.bfloat16
F32 = jnp.float32
ROWS = (((0,), (0,)), ((), ()))
LAST = (((1,), (1,)), ((), ()))
UP = [(0, 1), (1, 2), (2, 3), (3, 0)]
DOWN = [(0, 3), (1, 0), (2, 1), (3, 2)]
SWAP = [(0, 1), (1, 0)]


def exchange(blocks, axis):
    return lax.all_to_all(blocks, axis, split_axis=0, concat_axis=0, tiled=True)


def spread(block, axis, count):
    return exchange(jnp.broadcast_to(block, (count, *block.shape)), axis)


def from_ahead(block, axis, steps):
    return lax.ppermute(block, axis, [(i, (i - steps) % 4) for i in range(4)])


def in_order(pieces, first):
    both = jnp.stack(pieces + pieces[:3])
    return lax.dynamic_slice_in_dim(both, lax.rem(4 - first, 4), 4)


def gather_direct(block, axis):
    pieces = [block] + [from_ahead(block, axis, k) for k in (1, 2, 3)]
    return in_order(pieces, lax.axis_index(axis))


def pick_block(blocks, index):
    return lax.dynamic_index_in_dim(blocks, lax.rem(index, 4), 0, keepdims=False)


def send_direct(blocks, axis):
    me = lax.axis_index(axis)
    return [pick_block(blocks, me)] + [
        from_ahead(pick_block(blocks, me + 4 - k), axis, k) for k in (1, 2, 3)
    ]


def sum_direct(blocks, axis):
    return sum(p.astype(F32) for p in send_direct(blocks, axis))


def ring_pieces(block, axis):
    half = block.shape[0] // 2
    before = lax.ppermute(block, axis, UP)
    after = lax.ppermute(block, axis, DOWN)
    far_low = lax.ppermute(before[:half], axis, UP)
    far_high = lax.ppermute(after[half:], axis, DOWN)
    return [block, after, far_low, far_high, before]


def ring_sum(blocks, axis):
    me = lax.axis_index(axis)
    half = blocks.shape[1] // 2
    far = pick_block(blocks, me + 2)
    low = lax.ppermute(far[:half], axis, UP)
    high = lax.ppermute(far[half:], axis, DOWN)
    right, left = pick_block(blocks, me + 1), pick_block(blocks, me + 3)
    right = jnp.concatenate([(right[:half].astype(F32) + low.astype(F32)).astype(BF), right[half:]])
    left = jnp.concatenate([left[:half], (left[half:].astype(F32) + high.astype(F32)).astype(BF)])
    return (
        pick_block(blocks, me).astype(F32)
        + lax.ppermute(right, axis, UP).astype(F32)
        + lax.ppermute(left, axis, DOWN).astype(F32)
    )


def assemble(own, other, place, core, columns):
    def kernel(at_ref, *refs):
        out, sem = refs[10], refs[11]
        z, c = at_ref[0], at_ref[1]
        copies = []
        for half, pieces in ((c, refs[:5]), (1 - c, refs[5:10])):
            for piece, shift, low, count in zip(
                pieces, (0, 1, 2, 2, 3), (0, 0, 0, 2, 0), (4, 4, 2, 2, 4)
            ):
                copies.append(
                    pltpu.make_async_copy(
                        piece, out.at[lax.rem(z + shift, 4), pl.ds(low, count), half], sem.at[len(copies)]
                    )
                )
        for copy in copies:
            copy.start()
        for copy in copies:
            copy.wait()

    shaped = [p.reshape(-1, 64, columns) for p in (*own, *other)]
    return pl.pallas_call(
        kernel,
        out_shape=jax.ShapeDtypeStruct((4, 4, 2, 64, columns), BF),
        in_specs=[pl.BlockSpec(memory_space=pltpu.SMEM)] + [pl.BlockSpec(memory_space=pl.ANY)] * 10,
        out_specs=pl.BlockSpec(memory_space=pltpu.VMEM),
        scratch_shapes=[pltpu.SemaphoreType.DMA((10,))],
        compiler_params=pltpu.CompilerParams(vmem_limit_bytes=16 * 1024 * 1024),
        cost_estimate=pl.CostEstimate(
            flops=0, bytes_accessed=8 * MODEL_WIDTH * columns, transcendentals=0
        ),
    )(jnp.stack([place, core]), *shaped).reshape(MODEL_WIDTH, columns)


def heads_first(shard):
    columns = shard.shape[1] * HEAD_SIZE
    return shard.reshape(64, -1, 4, HEAD_SIZE).transpose(2, 0, 1, 3).reshape(4, 64, columns)


def gather_rows(by_head, place, core):
    columns = by_head.shape[2]
    own = ring_pieces(exchange(by_head, "y").reshape(256, columns), "dp")
    other = [lax.ppermute(p, "core", SWAP) for p in own]
    return assemble(own, other, place, core, columns), own


def scatter_rows(grad, core):
    columns = grad.shape[1]
    parts = grad.reshape(16, 2, 64, columns)
    keep = lax.dynamic_index_in_dim(parts, core, 1, keepdims=False)
    give = lax.dynamic_index_in_dim(parts, 1 - core, 1, keepdims=False)
    both = keep.astype(F32) + lax.ppermute(give, "core", SWAP).astype(F32)
    summed = ring_sum(both.astype(BF).reshape(4, 256, columns), "dp")
    return in_order(
        send_direct(summed.astype(BF).reshape(4, 64, columns), "y"), lax.axis_index("y")
    )


def heads_last(blocks):
    heads = blocks.shape[2] // HEAD_SIZE
    return (
        blocks.reshape(4, 64, heads, HEAD_SIZE)
        .transpose(1, 2, 0, 3)
        .reshape(64, heads, 4 * HEAD_SIZE)
        .astype(F32)
    )


def rms_scale(values):
    return lax.rsqrt(jnp.mean(values * values, axis=-1, keepdims=True) + NORM_EPS)


def turn(heads, cosine, sine):
    first, second = heads[..., :64], heads[..., 64:]
    return jnp.concatenate([first * cosine - second * sine, second * cosine + first * sine], axis=-1)


def pick_of(routes):
    return (routes[:, :, None] == jnp.arange(EXPERTS, dtype=jnp.int32)[None, None, :]).astype(F32)


def pair_gates(logits, pick):
    chosen = jnp.sum(logits[:, None, :] * pick, axis=-1)
    weights = jnp.exp(chosen - jnp.max(chosen, axis=1, keepdims=True))
    return weights / jnp.sum(weights, axis=1, keepdims=True)


def gate_back(gates, grad_gates, pick):
    inner = gates * (grad_gates - jnp.sum(gates * grad_gates, axis=1, keepdims=True))
    return jnp.sum(inner[:, :, None] * pick, axis=1)


def norm_back(grad_normed, values, factor, gain):
    gain_part = jnp.sum(grad_normed * values * factor, axis=0)
    inner = grad_normed * gain
    grad_values = factor * inner - values * factor * factor * factor * jnp.mean(
        inner * values, axis=-1, keepdims=True
    )
    return grad_values, gain_part


def in_two(values):
    high = values.astype(BF)
    low = (values - high.astype(F32)).astype(BF)
    return jnp.concatenate([high, low], axis=1)


def widen(columns):
    return jnp.pad(columns, ((0, 0), (0, HEAD_SIZE - columns.shape[1])))


def body(
    tokens,
    cotangent,
    attn_gain,
    mlp_gain,
    attn_router,
    key_value_weight,
    query_matrix,
    output_matrix,
    mlp_router,
    gate_up_weight,
    down_weight,
    attn_routes,
    mlp_routes,
    priority,
    segments,
):
    z, y = lax.axis_index("dp"), lax.axis_index("y")
    core, x = lax.axis_index("core"), lax.axis_index("tensor")
    count = tokens.shape[0]
    quarter = count // 4
    capacity = 50
    room = 56
    sequence = 8 * count
    plane = ("y", "tensor")

    gate_up_w = lax.all_gather(gate_up_weight[0].reshape(512, 2816), "dp", axis=0, tiled=True)

    routers_own = jnp.concatenate([attn_router, mlp_router], axis=1)
    in_own = jnp.concatenate([query_matrix, key_value_weight], axis=1)
    in_w, _ = gather_rows(
        jnp.concatenate(
            [heads_first(in_own), jnp.broadcast_to(widen(routers_own), (4, 64, HEAD_SIZE))], axis=2
        ),
        z,
        core,
    )
    out_w, out_pieces = gather_rows(heads_first(output_matrix), z, core)
    router_m = in_w[:, 1288:1296]

    down_own, _ = lax.optimization_barrier((down_weight[0], out_pieces[2]))
    down_pieces = ring_pieces(down_own, "dp")
    down_w = lax.dynamic_slice_in_dim(
        jnp.concatenate(
            [
                down_pieces[0],
                down_pieces[1],
                jnp.concatenate([down_pieces[2], down_pieces[3]], axis=0),
                down_pieces[4],
                down_pieces[0],
                down_pieces[1],
                jnp.concatenate([down_pieces[2], down_pieces[3]], axis=0),
            ],
            axis=1,
        ),
        lax.rem(4 - z, 4) * 512,
        MODEL_WIDTH,
        axis=1,
    )

    sent = jnp.concatenate([tokens, widen(attn_routes.astype(BF))], axis=1)
    arrived = gather_direct(sent, "y").reshape(4 * count, MODEL_WIDTH + HEAD_SIZE)
    values = arrived[:, :MODEL_WIDTH].astype(F32)
    routes = arrived[:, MODEL_WIDTH : MODEL_WIDTH + 2].astype(jnp.int32)
    gain_a, gain_m = attn_gain.astype(F32), mlp_gain.astype(F32)
    xn1 = (values * rms_scale(values) * gain_a).astype(BF)
    pick_a = pick_of(routes)

    ranking = priority[0]
    pick_m = pick_of(mlp_routes)
    before = (ranking[None, :] < ranking[:, None]).astype(BF)
    earlier = jnp.dot(before, jnp.sum(pick_m, axis=1).astype(BF), preferred_element_type=F32)
    slots = jnp.sum(pick_m * earlier[:, None, :], axis=-1).astype(jnp.int32)
    kept = slots < capacity
    dest = jnp.where(kept, mlp_routes * room + slots, -1)
    lanes = jnp.arange(EXPERTS * room, dtype=jnp.int32)
    to_row = (dest.T[:, :, None] == lanes[None, None, :]).astype(BF)
    any_row = to_row[0] + to_row[1]
    both_rows = to_row.reshape(2 * count, EXPERTS * room)

    def to_experts(rows):
        columns = rows.shape[1]
        return exchange(rows.reshape(EXPERTS, room, columns), ("y", "core")).reshape(
            EXPERTS * room, columns
        )

    def with_other(j):
        others = jnp.concatenate([pick_m[:, 1 - j], jnp.ones((count, 1), F32)], axis=1)
        return jnp.concatenate([cotangent, widen(others.astype(BF))], axis=1)

    grad_sent = lax.dot_general(
        both_rows,
        jnp.concatenate([with_other(0), with_other(1)], axis=0),
        ROWS,
        preferred_element_type=F32,
    ).astype(BF)
    grad_sent, _ = lax.optimization_barrier((grad_sent, out_pieces[0]))
    grad_landed = to_experts(grad_sent)

    def places(half):
        blocks = 2 * jnp.arange(4, dtype=jnp.int32)[:, None] + half
        return (blocks * count + jnp.arange(count, dtype=jnp.int32)[None, :]).reshape(-1)

    place = places(core)
    key_place = jnp.concatenate([place, places(1 - core)])
    of_sequence = lax.dynamic_slice_in_dim(segments, z * sequence, sequence)
    own_segment = jnp.take(of_sequence, place)
    key_segment = jnp.concatenate([own_segment, jnp.take(of_sequence, places(1 - core))])
    allowed = (
        (key_place[None, :] <= place[:, None])
        & (place[:, None] - key_place[None, :] < WINDOW)
        & (own_segment[:, None] == key_segment[None, :])
    )
    inverse = 10000.0 ** (-(jnp.arange(HEAD_SIZE // 2).astype(F32) * 2.0 / HEAD_SIZE))
    angle = place.astype(F32)[:, None] * inverse[None, :]
    cosine, sine = jnp.cos(angle), jnp.sin(angle)

    projected = jnp.dot(xn1, in_w, preferred_element_type=F32)
    gate_a = pair_gates(projected[:, 1280:1288], pick_a)
    key_own = turn(projected[:, 1024:1152], cosine, sine).astype(BF)
    value_own = projected[:, 1152:1280].astype(BF)
    kv_own = jnp.concatenate([key_own, value_own], axis=1)
    kv_other = lax.ppermute(kv_own, "core", SWAP)
    keys = jnp.concatenate([key_own, kv_other[:, :HEAD_SIZE]], axis=0)
    vals = jnp.concatenate([value_own, kv_other[:, HEAD_SIZE:]], axis=0)
    q_all = projected[:, :1024].reshape(-1, EXPERTS, HEAD_SIZE)
    q_pick = jnp.sum(pick_a[:, :, :, None] * q_all[:, None], axis=2)
    query = turn(q_pick, cosine[:, None], sine[:, None]).astype(BF)
    scale = HEAD_SIZE ** (-0.5)
    score = jnp.where(
        allowed[None], jnp.einsum("sjd,kd->jsk", query, keys, preferred_element_type=F32) * scale, -1e30
    )
    row_max = jnp.max(score, axis=-1, keepdims=True)
    weights = jnp.exp(score - row_max)
    totals = jnp.sum(weights, axis=-1, keepdims=True)
    prob = weights / totals
    attended = jnp.einsum("jsk,kd->sjd", prob.astype(BF), vals, preferred_element_type=F32)
    mixed = jnp.sum(
        (pick_a * gate_a[:, :, None])[:, :, :, None] * attended[:, :, None, :], axis=1
    ).astype(BF).reshape(-1, EXPERTS * HEAD_SIZE)
    branch_part = lax.dot_general(mixed, out_w, LAST, preferred_element_type=F32).astype(BF)
    branch = exchange(branch_part.reshape(16, quarter, MODEL_WIDTH), plane).astype(F32).sum(axis=0)

    first = x * quarter
    own_values = lax.dynamic_slice_in_dim(tokens, first, quarter).astype(F32)
    own_factor = rms_scale(own_values)
    hidden = own_values + branch
    factor_m = rms_scale(hidden)
    xn2_own = (hidden * factor_m * gain_m).astype(BF)
    xn2 = spread(xn2_own, "tensor", 4).reshape(count, MODEL_WIDTH)
    gate_m = pair_gates(jnp.dot(xn2, router_m, preferred_element_type=F32), pick_m)
    weight_m = gate_m * kept.astype(F32)

    received = to_experts(
        lax.dot_general(any_row, xn2, ROWS, preferred_element_type=F32).astype(BF)
    )
    grad_received = grad_landed[:, :MODEL_WIDTH]
    other_pick = grad_landed[:, MODEL_WIDTH : MODEL_WIDTH + EXPERTS].astype(F32)
    valid = grad_landed[:, MODEL_WIDTH + EXPERTS : MODEL_WIDTH + EXPERTS + 1].astype(F32)
    row_logits = jnp.dot(received, router_m, preferred_element_type=F32)
    here = (jnp.arange(EXPERTS, dtype=jnp.int32) == 2 * y + core).astype(F32)
    own_logit = jnp.sum(row_logits * here[None], axis=1, keepdims=True)
    other_logit = jnp.sum(row_logits * other_pick, axis=1, keepdims=True)
    top = jnp.maximum(own_logit, other_logit)
    own_weight = jnp.exp(own_logit - top)
    row_gate = valid * own_weight / (own_weight + jnp.exp(other_logit - top))

    width = down_weight.shape[1]
    grad_act_raw = lax.dot_general(grad_received, down_w, LAST, preferred_element_type=F32)
    grad_expert = (row_gate * grad_received.astype(F32)).astype(BF)
    gate_up = jnp.dot(received, gate_up_w, preferred_element_type=F32)
    gate_part, up_part = gate_up[:, :width], gate_up[:, width:]
    sigmoid_gate = jax.nn.sigmoid(gate_part)
    silu_gate = gate_part * sigmoid_gate
    activated = (silu_gate * up_part).astype(BF)
    grad_act = row_gate * grad_act_raw
    grad_gate_up = jnp.concatenate(
        [
            grad_act * up_part * sigmoid_gate * (1.0 + gate_part * (1.0 - sigmoid_gate)),
            grad_act * silu_gate,
        ],
        axis=1,
    ).astype(BF)
    row_gate_grad = jnp.sum(activated.astype(F32) * grad_act_raw, axis=1, keepdims=True)
    grad_rows = lax.dot_general(grad_gate_up, gate_up_w, LAST, preferred_element_type=F32).astype(BF)
    grad_returned = to_experts(jnp.concatenate([grad_rows, widen(in_two(row_gate_grad))], axis=1))
    grad_gate_up_w = lax.dot_general(
        received, grad_gate_up, ROWS, preferred_element_type=F32
    ).astype(BF)
    grad_down_w = lax.dot_general(activated, grad_expert, ROWS, preferred_element_type=F32).astype(BF)
    gate_up_grad = (
        lax.psum_scatter(grad_gate_up_w, "dp", scatter_dimension=0, tiled=True)
        .reshape(1, 512, 2, width)
        .astype(F32)
    )
    down_grad = ring_sum(grad_down_w.reshape(width, 4, 512).transpose(1, 0, 2), "dp")[None]

    grad_xn2_part = jnp.dot(
        any_row, grad_returned[:, :MODEL_WIDTH], preferred_element_type=F32
    ).astype(BF)
    row_gate_parts = grad_returned[:, MODEL_WIDTH : MODEL_WIDTH + 2]
    gate_m_part = jnp.sum(
        jnp.einsum("jtr,rd->tjd", to_row, row_gate_parts, preferred_element_type=F32), axis=2
    )
    shares = jnp.concatenate([grad_xn2_part, widen(in_two(gate_m_part))], axis=1)
    landed = (
        exchange(shares.reshape(4, quarter, MODEL_WIDTH + HEAD_SIZE), "tensor")
        .astype(F32)
        .sum(axis=0)
    )
    grad_gate_m = (
        landed[:, MODEL_WIDTH : MODEL_WIDTH + 2] + landed[:, MODEL_WIDTH + 2 : MODEL_WIDTH + 4]
    )

    def quarter_of(array, offset=0):
        return lax.dynamic_slice_in_dim(array, first + offset, quarter)

    grad_logit_m = gate_back(quarter_of(gate_m), grad_gate_m, quarter_of(pick_m))
    grad_xn2 = landed[:, :MODEL_WIDTH] + lax.dot_general(
        grad_logit_m, router_m.astype(F32), LAST, preferred_element_type=F32
    )
    grad_norm, gain_m_part = norm_back(grad_xn2, hidden, factor_m, gain_m)
    grad_hidden = quarter_of(cotangent).astype(F32) + grad_norm
    grad_branch = spread(grad_hidden.astype(BF), plane, 16).reshape(4 * count, MODEL_WIDTH)

    expert_part = jnp.dot(activated, down_w, preferred_element_type=F32).astype(BF)
    expert_part, _ = lax.optimization_barrier((expert_part, grad_branch))
    returned = to_experts(expert_part)
    fetched = jnp.einsum("jtr,rd->jtd", to_row, returned, preferred_element_type=F32)
    moe_part = jnp.sum(weight_m.T[:, :, None] * fetched, axis=0).astype(BF)
    moe = sum_direct(moe_part.reshape(4, quarter, MODEL_WIDTH), "tensor")
    output = gather_direct((hidden + moe).astype(BF), "tensor").reshape(count, MODEL_WIDTH)

    grad_mixed = jnp.dot(grad_branch, out_w, preferred_element_type=F32).reshape(
        -1, EXPERTS, HEAD_SIZE
    )
    grad_pick = jnp.sum(pick_a[:, :, :, None] * grad_mixed[:, None], axis=2)
    grad_gate_part = jnp.sum(grad_pick * attended, axis=-1)
    grad_attended = (gate_a[:, :, None] * grad_pick).astype(BF)
    grad_prob = jnp.einsum("sjd,kd->jsk", grad_attended, vals, preferred_element_type=F32)
    row_delta = jnp.sum(prob * grad_prob, axis=-1, keepdims=True)
    grad_score = (prob * (grad_prob - row_delta)).astype(BF)
    grad_query = jnp.einsum("jsk,kd->sjd", grad_score, keys, preferred_element_type=F32) * scale
    grad_keys = jnp.einsum("jsk,sjd->kd", grad_score, query, preferred_element_type=F32) * scale
    grad_vals = jnp.einsum("jsk,sjd->kd", prob.astype(BF), grad_attended, preferred_element_type=F32)
    half = 4 * count
    grad_kv_raw = jnp.concatenate([grad_keys, grad_vals], axis=1)
    from_other = lax.ppermute(grad_kv_raw[half:].astype(BF), "core", SWAP).astype(F32)
    own_grad_kv = grad_kv_raw[:half] + from_other
    grad_kv = jnp.concatenate(
        [turn(own_grad_kv[:, :HEAD_SIZE], cosine, -sine), own_grad_kv[:, HEAD_SIZE:]], axis=1
    ).astype(BF)
    grad_q_pick = turn(grad_query, cosine[:, None], -sine[:, None])
    grad_q_all = (
        jnp.sum(pick_a[:, :, :, None] * grad_q_pick[:, :, None, :], axis=1)
        .astype(BF)
        .reshape(-1, EXPERTS * HEAD_SIZE)
    )
    out_grad = heads_last(
        scatter_rows(
            lax.dot_general(grad_branch, mixed, ROWS, preferred_element_type=F32).astype(BF), core
        )
    )
    grad_logit_a = gate_back(gate_a, grad_gate_part, pick_a)
    grad_in = jnp.concatenate([grad_q_all, grad_kv, widen(grad_logit_a.astype(BF))], axis=1)
    grad_xn1_part = lax.dot_general(grad_in, in_w, LAST, preferred_element_type=F32).astype(BF)
    landed_a = (
        exchange(grad_xn1_part.reshape(16, quarter, MODEL_WIDTH), plane).astype(F32).sum(axis=0)
    )
    grad_x_norm, _ = norm_back(landed_a, own_values, own_factor, gain_a)
    input_grad = gather_direct((grad_hidden + grad_x_norm).astype(BF), "tensor").reshape(
        count, MODEL_WIDTH
    )

    small = jnp.concatenate(
        [
            jnp.zeros((MODEL_WIDTH, 1288), BF),
            lax.dot_general(
                xn2_own, grad_logit_m.astype(BF), ROWS, preferred_element_type=F32
            ).astype(BF),
            gain_m_part[:, None].astype(BF),
            jnp.zeros((MODEL_WIDTH, 111), BF),
        ],
        axis=1,
    )
    in_parts = scatter_rows(
        lax.dot_general(xn1, grad_in, ROWS, preferred_element_type=F32).astype(BF) + small, core
    )
    in_grad = heads_last(in_parts[:, :, :1280])
    query_grad, kv_grad = in_grad[:, :8], in_grad[:, 8:]
    small_part = jnp.sum(in_parts[:, :, 1280:].astype(F32), axis=0)
    gain_rows = lax.dynamic_slice_in_dim(gain_a, z * 512 + y * 128 + core * 64, 64)
    gain_a_part = (
        jnp.sum(in_grad * in_own.astype(F32), axis=(1, 2))
        + jnp.sum(small_part[:, :8] * attn_router.astype(F32), axis=1)
    ) / gain_rows
    small_sent = jnp.concatenate([small_part[:, :17], gain_a_part[:, None]], axis=1)
    small_bf = widen(small_sent.astype(BF))
    small_sum = sum(
        p.astype(F32) for p in [small_bf] + [from_ahead(small_bf, "tensor", k) for k in (1, 2, 3)]
    )
    return (
        output,
        input_grad,
        small_sum[:, 17],
        small_sum[:, 16],
        small_sum[:, :8],
        kv_grad,
        query_grad,
        out_grad,
        small_sum[:, 8:16],
        gate_up_grad,
        down_grad,
    )


def solution(mesh):
    split = Mesh(mesh.devices.reshape(4, 4, 2, 4), ("dp", "y", "core", "tensor"))
    rows = ("dp", "y", "core")
    expert = ("y", "core")
    placed = (
        P(rows, None),
        P(rows, None),
        P(),
        P(),
        P(rows, None),
        P(rows, None, "tensor"),
        P(rows, None, "tensor"),
        P(rows, None, "tensor"),
        P(rows, None),
        P(expert, "dp", None, "tensor"),
        P(expert, "tensor", "dp"),
        P(rows, None),
        P(rows, None),
        P(rows, None),
        P(),
    )
    return jax.shard_map(
        body,
        mesh=split,
        in_specs=placed,
        out_specs=(
            P(rows, None),
            P(rows, None),
            P(rows),
            P(rows),
            P(rows, None),
            P(rows, None, "tensor"),
            P(rows, None, "tensor"),
            P(rows, None, "tensor"),
            P(rows, None),
            P(expert, "dp", None, "tensor"),
            P(expert, "tensor", "dp"),
        ),
        check_vma=False,
    )
```

```python
import jax
import jax.numpy as jnp
from jax import lax
from jax.experimental import pallas as pl
from jax.experimental.pallas import tpu as pltpu
from jax.sharding import Mesh
from jax.sharding import PartitionSpec as P

MODEL_WIDTH = 2048
HEAD_SIZE = 128
EXPERTS = 8
WINDOW = 1024
NORM_EPS = 1e-06
BF = jnp.bfloat16
F32 = jnp.float32
ROWS = (((0,), (0,)), ((), ()))
LAST = (((1,), (1,)), ((), ()))
UP = [(0, 1), (1, 2), (2, 3), (3, 0)]
DOWN = [(0, 3), (1, 0), (2, 1), (3, 2)]
SWAP = [(0, 1), (1, 0)]


def exchange(blocks, axis):
    return lax.all_to_all(blocks, axis, split_axis=0, concat_axis=0, tiled=True)


def spread(block, axis, count):
    return exchange(jnp.broadcast_to(block, (count, *block.shape)), axis)


def from_ahead(block, axis, steps):
    return lax.ppermute(block, axis, [(i, (i - steps) % 4) for i in range(4)])


def in_order(pieces, first):
    both = jnp.stack(pieces + pieces[:3])
    return lax.dynamic_slice_in_dim(both, lax.rem(4 - first, 4), 4)


def gather_direct(block, axis):
    pieces = [block] + [from_ahead(block, axis, k) for k in (1, 2, 3)]
    return in_order(pieces, lax.axis_index(axis))


def pick_block(blocks, index):
    return lax.dynamic_index_in_dim(blocks, lax.rem(index, 4), 0, keepdims=False)


def send_direct(blocks, axis):
    me = lax.axis_index(axis)
    return [pick_block(blocks, me)] + [
        from_ahead(pick_block(blocks, me + 4 - k), axis, k) for k in (1, 2, 3)
    ]


def sum_direct(blocks, axis):
    return sum(p.astype(F32) for p in send_direct(blocks, axis))


def ring_pieces(block, axis):
    half = block.shape[0] // 2
    before = lax.ppermute(block, axis, UP)
    after = lax.ppermute(block, axis, DOWN)
    far_low = lax.ppermute(before[:half], axis, UP)
    far_high = lax.ppermute(after[half:], axis, DOWN)
    return [block, after, far_low, far_high, before]


def ring_sum(blocks, axis):
    me = lax.axis_index(axis)
    half = blocks.shape[1] // 2
    far = pick_block(blocks, me + 2)
    low = lax.ppermute(far[:half], axis, UP)
    high = lax.ppermute(far[half:], axis, DOWN)
    right, left = pick_block(blocks, me + 1), pick_block(blocks, me + 3)
    right = jnp.concatenate([(right[:half].astype(F32) + low.astype(F32)).astype(BF), right[half:]])
    left = jnp.concatenate([left[:half], (left[half:].astype(F32) + high.astype(F32)).astype(BF)])
    return (
        pick_block(blocks, me).astype(F32)
        + lax.ppermute(right, axis, UP).astype(F32)
        + lax.ppermute(left, axis, DOWN).astype(F32)
    )


def heads_first(shard):
    columns = shard.shape[1] * HEAD_SIZE
    return shard.reshape(64, -1, 4, HEAD_SIZE).transpose(2, 0, 1, 3).reshape(4, 64, columns)


def after(value, other):
    return lax.optimization_barrier((value, other))[0]


def core_first(rows):
    return rows.reshape(-1, 4, 4, 2, 64).transpose(0, 1, 3, 2, 4).reshape(-1, MODEL_WIDTH)


def core_last(rows):
    return rows.reshape(-1, 4, 2, 4, 64).transpose(0, 1, 3, 2, 4).reshape(-1, MODEL_WIDTH)


def scatter_rows(grad, core):
    columns = grad.shape[1]
    parts = grad.reshape(4, 2, 256, columns)
    keep = lax.dynamic_index_in_dim(parts, core, 1, keepdims=False)
    give = lax.dynamic_index_in_dim(parts, 1 - core, 1, keepdims=False)
    both = keep.astype(F32) + lax.ppermute(give, "core", SWAP).astype(F32)
    summed = ring_sum(both.astype(BF), "dp")
    return in_order(
        send_direct(summed.astype(BF).reshape(4, 64, columns), "y"), lax.axis_index("y")
    )


def heads_last(blocks):
    heads = blocks.shape[2] // HEAD_SIZE
    return (
        blocks.reshape(4, 64, heads, HEAD_SIZE)
        .transpose(1, 2, 0, 3)
        .reshape(64, heads, 4 * HEAD_SIZE)
        .astype(F32)
    )


def rms_scale(values):
    return lax.rsqrt(jnp.mean(values * values, axis=-1, keepdims=True) + NORM_EPS)


def turn(heads, cosine, sine):
    first, second = heads[..., :64], heads[..., 64:]
    return jnp.concatenate([first * cosine - second * sine, second * cosine + first * sine], axis=-1)


EXTENTS = (256, 384, 512, 640)
SCALE = HEAD_SIZE**-0.5


def masked_scores(query, key, row_meta, key_meta):
    raw = lax.dot_general(query, key, LAST, preferred_element_type=F32) * SCALE
    gap = row_meta[:, 0:1] - key_meta[0:1]
    allowed = (gap >= 0) & (gap < WINDOW) & (row_meta[:, 1:2] == key_meta[1:2])
    return jnp.where(jnp.concatenate([allowed, allowed], axis=0), raw, -1e30)


def forward_kernel(proj, own, other, routes, cosine, sine, row_meta, key_meta, *outs):
    query_out, attended_out, total_out, gates_out, mixed_out = outs
    count = proj.shape[0] // 4
    for i in range(4):
        rows = pl.ds(count * i, count)
        extent = EXTENTS[i]
        logits = proj[rows, 1280:1288]
        lane = lax.broadcasted_iota(jnp.int32, (count, EXPERTS), 1)
        named = [routes[rows, 0:1], routes[rows, 1:2]]
        chosen = [jnp.sum(jnp.where(lane == n, logits, 0.0), axis=1, keepdims=True) for n in named]
        top = jnp.maximum(chosen[0], chosen[1])
        power = [jnp.exp(c - top) for c in chosen]
        gates = [p / (power[0] + power[1]) for p in power]
        gates_out[rows, 0:1] = gates[0]
        gates_out[rows, 1:2] = gates[1]
        cos, sin = cosine[rows, :], sine[rows, :]
        picked = []
        for n in named:
            q = jnp.zeros((count, HEAD_SIZE), F32)
            for e in range(EXPERTS):
                q = q + jnp.where(n == e, proj[rows, HEAD_SIZE * e : HEAD_SIZE * (e + 1)], 0.0)
            picked.append(q * cos + pltpu.roll(q, 64, 1) * sin)
        query = jnp.concatenate(picked, axis=0).astype(BF)
        query_out[i] = query
        halves = (own, other)
        scores = [
            masked_scores(
                query, h[:extent, :HEAD_SIZE], row_meta[rows, :], key_meta[k, :, :extent]
            )
            for k, h in enumerate(halves)
        ]
        row_max = jnp.maximum(
            jnp.max(scores[0], axis=1, keepdims=True), jnp.max(scores[1], axis=1, keepdims=True)
        )
        weights = [jnp.exp(s - row_max) for s in scores]
        total = jnp.sum(weights[0], axis=1, keepdims=True) + jnp.sum(weights[1], axis=1, keepdims=True)
        inverse = 1.0 / total
        attended = sum(
            jnp.dot((w * inverse).astype(BF), h[:extent, HEAD_SIZE:], preferred_element_type=F32)
            for w, h in zip(weights, halves)
        )
        attended_out[i] = attended
        total_out[i] = row_max + jnp.log(total)
        for e in range(EXPERTS):
            mixed_out[rows, HEAD_SIZE * e : HEAD_SIZE * (e + 1)] = (
                jnp.where(named[0] == e, gates[0], 0.0) * attended[:count]
                + jnp.where(named[1] == e, gates[1], 0.0) * attended[count:]
            ).astype(BF)


def backward_kernel(
    grad_mixed, query_in, own, other, attended_in, total_in, gates_in, routes, cosine, sine, row_meta, key_meta, *outs
):
    grad_query_out, grad_logit_out, grad_own_out, grad_other_out, sums = outs
    count = grad_mixed.shape[0] // 4
    sums[...] = jnp.zeros_like(sums)
    for i in range(4):
        rows = pl.ds(count * i, count)
        extent = EXTENTS[i]
        named = [routes[rows, 0:1], routes[rows, 1:2]]
        gates = [gates_in[rows, 0:1], gates_in[rows, 1:2]]
        cos, sin = cosine[rows, :], sine[rows, :]
        attended = attended_in[i]
        picked = []
        for n in named:
            g = jnp.zeros((count, HEAD_SIZE), F32)
            for e in range(EXPERTS):
                g = g + jnp.where(n == e, grad_mixed[rows, HEAD_SIZE * e : HEAD_SIZE * (e + 1)], 0.0)
            picked.append(g)
        gate_grads = [
            jnp.sum(p * attended[count * j : count * (j + 1)], axis=1, keepdims=True)
            for j, p in enumerate(picked)
        ]
        level = gates[0] * gate_grads[0] + gates[1] * gate_grads[1]
        lane = lax.broadcasted_iota(jnp.int32, (count, HEAD_SIZE), 1)
        grad_logit_out[rows, :] = sum(
            jnp.where(lane == n, g * (d - level), 0.0) for n, g, d in zip(named, gates, gate_grads)
        ).astype(BF)
        grad_attended = jnp.concatenate(
            [gates[0] * picked[0], gates[1] * picked[1]], axis=0
        ).astype(BF)
        query = query_in[i]
        total = total_in[i]
        probs, grad_probs = [], []
        delta = jnp.zeros((2 * count, 1), F32)
        for k, h in enumerate((own, other)):
            score = masked_scores(
                query, h[:extent, :HEAD_SIZE], row_meta[rows, :], key_meta[k, :, :extent]
            )
            prob = jnp.exp(score - total)
            grad_prob = lax.dot_general(
                grad_attended, h[:extent, HEAD_SIZE:], LAST, preferred_element_type=F32
            )
            delta = delta + jnp.sum(prob * grad_prob, axis=1, keepdims=True)
            probs.append(prob)
            grad_probs.append(grad_prob)
        grad_query = jnp.zeros((2 * count, HEAD_SIZE), F32)
        for k, h in enumerate((own, other)):
            grad_score = (probs[k] * (grad_probs[k] - delta)).astype(BF)
            grad_query = grad_query + jnp.dot(
                grad_score, h[:extent, :HEAD_SIZE], preferred_element_type=F32
            )
            sums[k, :extent, :HEAD_SIZE] += (
                lax.dot_general(grad_score, query, ROWS, preferred_element_type=F32) * SCALE
            )
            sums[k, :extent, HEAD_SIZE:] += lax.dot_general(
                probs[k].astype(BF), grad_attended, ROWS, preferred_element_type=F32
            )
        grad_query = grad_query * SCALE
        turned = [
            g * cos - pltpu.roll(g, 64, 1) * sin for g in (grad_query[:count], grad_query[count:])
        ]
        for e in range(EXPERTS):
            grad_query_out[rows, HEAD_SIZE * e : HEAD_SIZE * (e + 1)] = (
                jnp.where(named[0] == e, turned[0], 0.0) + jnp.where(named[1] == e, turned[1], 0.0)
            ).astype(BF)
    grad_own_out[...] = sums[0]
    grad_other_out[...] = sums[1].astype(BF)


def in_vmem(kernel, outs, scratch, flops, *args):
    spec = pl.BlockSpec(memory_space=pltpu.VMEM)
    moved = sum(a.size * a.dtype.itemsize for a in args)
    return pl.pallas_call(
        kernel,
        out_shape=outs,
        in_specs=[spec] * len(args),
        out_specs=[spec] * len(outs),
        scratch_shapes=scratch,
        compiler_params=pltpu.CompilerParams(vmem_limit_bytes=40 * 1024 * 1024),
        cost_estimate=pl.CostEstimate(flops=flops, bytes_accessed=moved, transcendentals=1 << 20),
    )(*args)


def pick_of(routes):
    return (routes[:, :, None] == jnp.arange(EXPERTS, dtype=jnp.int32)[None, None, :]).astype(F32)


def pair_gates(logits, pick):
    chosen = jnp.sum(logits[:, None, :] * pick, axis=-1)
    weights = jnp.exp(chosen - jnp.max(chosen, axis=1, keepdims=True))
    return weights / jnp.sum(weights, axis=1, keepdims=True)


def gate_back(gates, grad_gates, pick):
    inner = gates * (grad_gates - jnp.sum(gates * grad_gates, axis=1, keepdims=True))
    return jnp.sum(inner[:, :, None] * pick, axis=1)


def norm_back(grad_normed, values, factor, gain):
    gain_part = jnp.sum(grad_normed * values * factor, axis=0)
    inner = grad_normed * gain
    grad_values = factor * inner - values * factor * factor * factor * jnp.mean(
        inner * values, axis=-1, keepdims=True
    )
    return grad_values, gain_part


def in_two(values):
    high = values.astype(BF)
    low = (values - high.astype(F32)).astype(BF)
    return jnp.concatenate([high, low], axis=1)


def widen(columns):
    return jnp.pad(columns, ((0, 0), (0, HEAD_SIZE - columns.shape[1])))


def body(
    tokens,
    cotangent,
    attn_gain,
    mlp_gain,
    attn_router,
    key_value_weight,
    query_matrix,
    output_matrix,
    mlp_router,
    gate_up_weight,
    down_weight,
    attn_routes,
    mlp_routes,
    priority,
    segments,
):
    z, y = lax.axis_index("dp"), lax.axis_index("y")
    core, x = lax.axis_index("core"), lax.axis_index("tensor")
    count = tokens.shape[0]
    quarter = count // 4
    capacity = 50
    room = 56
    sequence = 8 * count
    plane = ("y", "tensor")

    routers_own = jnp.concatenate([attn_router, mlp_router], axis=1)
    in_own = jnp.concatenate([query_matrix, key_value_weight], axis=1)
    mine = exchange(
        jnp.concatenate(
            [
                heads_first(in_own),
                jnp.broadcast_to(widen(routers_own), (4, 64, HEAD_SIZE)),
                heads_first(output_matrix),
            ],
            axis=2,
        ),
        "y",
    ).reshape(256, 2432)
    lines = ("dp", "core")
    in_w = lax.all_gather(mine[:, :1408], lines, axis=0, tiled=True)
    out_w = lax.all_gather(after(mine[:, 1408:], in_w), lines, axis=0, tiled=True)
    gate_up_w = lax.all_gather(
        after(gate_up_weight[0].reshape(512, 2816), out_w), "dp", axis=0, tiled=True
    )
    router_m = in_w[:, 1288:1296].reshape(4, 2, 4, 64, 8).transpose(0, 2, 1, 3, 4).reshape(-1, 8)

    down_pieces = ring_pieces(down_weight[0], "dp")
    down_w = jnp.concatenate(
        [
            down_pieces[0],
            down_pieces[1],
            jnp.concatenate([down_pieces[2], down_pieces[3]], axis=0),
            down_pieces[4],
        ],
        axis=1,
    )

    def turned(columns, blocks):
        twice = jnp.concatenate([columns, columns], axis=1)
        return lax.dynamic_slice_in_dim(twice, blocks * 512, MODEL_WIDTH, axis=1)

    sent = jnp.concatenate([core_first(tokens), widen(attn_routes.astype(BF))], axis=1)
    arrived = spread(after(sent, mine), "y", 4).reshape(4 * count, MODEL_WIDTH + HEAD_SIZE)
    values = arrived[:, :MODEL_WIDTH].astype(F32)
    routes = arrived[:, MODEL_WIDTH : MODEL_WIDTH + 2].astype(jnp.int32)
    gain_a = core_first(attn_gain.astype(F32))[0]
    gain_m = core_first(mlp_gain.astype(F32))[0]
    xn1 = (values * rms_scale(values) * gain_a).astype(BF)

    ranking = priority[0]
    pick_m = pick_of(mlp_routes)
    before = (ranking[None, :] < ranking[:, None]).astype(BF)
    earlier = jnp.dot(before, jnp.sum(pick_m, axis=1).astype(BF), preferred_element_type=F32)
    slots = jnp.sum(pick_m * earlier[:, None, :], axis=-1).astype(jnp.int32)
    kept = slots < capacity
    dest = jnp.where(kept, mlp_routes * room + slots, -1)
    lanes = jnp.arange(EXPERTS * room, dtype=jnp.int32)
    to_row = (dest.T[:, :, None] == lanes[None, None, :]).astype(BF)
    any_row = to_row[0] + to_row[1]
    both_rows = to_row.reshape(2 * count, EXPERTS * room)

    def to_experts(rows):
        columns = rows.shape[1]
        return exchange(rows.reshape(EXPERTS, room, columns), ("y", "core")).reshape(
            EXPERTS * room, columns
        )

    def with_other(j):
        others = jnp.concatenate([pick_m[:, 1 - j], jnp.ones((count, 1), F32)], axis=1)
        return jnp.concatenate([cotangent, widen(others.astype(BF))], axis=1)

    grad_sent = lax.dot_general(
        both_rows,
        jnp.concatenate([with_other(0), with_other(1)], axis=0),
        ROWS,
        preferred_element_type=F32,
    ).astype(BF)
    grad_landed = to_experts(after(grad_sent, arrived))

    def places(half):
        blocks = 2 * jnp.arange(4, dtype=jnp.int32)[:, None] + half
        return (blocks * count + jnp.arange(count, dtype=jnp.int32)[None, :]).reshape(-1)

    of_sequence = lax.dynamic_slice_in_dim(segments, z * sequence, sequence).reshape(4, 2, count)

    def meta(half):
        documents = lax.dynamic_index_in_dim(of_sequence, half, 1, keepdims=False).reshape(-1)
        return jnp.stack([places(half), documents])

    key_meta = jnp.stack([meta(core), meta(1 - core)])
    row_meta = key_meta[0].T
    inverse = 10000.0 ** (-(jnp.arange(HEAD_SIZE // 2).astype(F32) * 2.0 / HEAD_SIZE))
    angle = places(core).astype(F32)[:, None] * inverse[None, :]
    cosine = jnp.tile(jnp.cos(angle), (1, 2))
    sine = jnp.concatenate([-jnp.sin(angle), jnp.sin(angle)], axis=1)

    def swapped(rows):
        return jnp.concatenate([rows[:, 64:], rows[:, :64]], axis=1)

    half = 4 * count
    projected = jnp.dot(xn1, in_w, preferred_element_type=F32)
    key_raw = projected[:, 1024:1152]
    kv_own = jnp.concatenate(
        [key_raw * cosine + swapped(key_raw) * sine, projected[:, 1152:1280]], axis=1
    ).astype(BF)
    kv_other = lax.ppermute(kv_own, "core", SWAP)
    shared = (routes, cosine, sine, row_meta, key_meta)
    query, attended, totals, gate_a, mixed = in_vmem(
        forward_kernel,
        [
            jax.ShapeDtypeStruct((4, 2 * count, HEAD_SIZE), BF),
            jax.ShapeDtypeStruct((4, 2 * count, HEAD_SIZE), F32),
            jax.ShapeDtypeStruct((4, 2 * count, 1), F32),
            jax.ShapeDtypeStruct((half, 2), F32),
            jax.ShapeDtypeStruct((half, EXPERTS * HEAD_SIZE), BF),
        ],
        [],
        6 << 28,
        projected,
        kv_own,
        kv_other,
        *shared,
    )
    branch_part = lax.dot_general(mixed, out_w, LAST, preferred_element_type=F32).astype(BF)
    branch_part = after(branch_part, grad_landed)
    branch = exchange(branch_part.reshape(16, quarter, MODEL_WIDTH), plane).astype(F32).sum(axis=0)

    first = x * quarter
    own_values = core_first(lax.dynamic_slice_in_dim(tokens, first, quarter)).astype(F32)
    own_factor = rms_scale(own_values)
    hidden = own_values + branch
    factor_m = rms_scale(hidden)
    xn2_own = (hidden * factor_m * gain_m).astype(BF)
    xn2 = spread(core_last(xn2_own), "tensor", 4).reshape(count, MODEL_WIDTH)
    gate_m = pair_gates(jnp.dot(xn2, router_m, preferred_element_type=F32), pick_m)
    weight_m = gate_m * kept.astype(F32)

    received = to_experts(
        lax.dot_general(any_row, xn2, ROWS, preferred_element_type=F32).astype(BF)
    )
    grad_received = grad_landed[:, :MODEL_WIDTH]
    other_pick = grad_landed[:, MODEL_WIDTH : MODEL_WIDTH + EXPERTS].astype(F32)
    valid = grad_landed[:, MODEL_WIDTH + EXPERTS : MODEL_WIDTH + EXPERTS + 1].astype(F32)
    row_logits = jnp.dot(received, router_m, preferred_element_type=F32)
    here = (jnp.arange(EXPERTS, dtype=jnp.int32) == 2 * y + core).astype(F32)
    own_logit = jnp.sum(row_logits * here[None], axis=1, keepdims=True)
    other_logit = jnp.sum(row_logits * other_pick, axis=1, keepdims=True)
    top = jnp.maximum(own_logit, other_logit)
    own_weight = jnp.exp(own_logit - top)
    row_gate = valid * own_weight / (own_weight + jnp.exp(other_logit - top))

    width = down_weight.shape[1]
    grad_act_raw = lax.dot_general(
        turned(grad_received, z), down_w, LAST, preferred_element_type=F32
    )
    grad_expert = (row_gate * grad_received.astype(F32)).astype(BF)
    gate_up = jnp.dot(received, gate_up_w, preferred_element_type=F32)
    gate_part, up_part = gate_up[:, :width], gate_up[:, width:]
    sigmoid_gate = jax.nn.sigmoid(gate_part)
    silu_gate = gate_part * sigmoid_gate
    activated = (silu_gate * up_part).astype(BF)
    grad_act = row_gate * grad_act_raw
    grad_gate_up = jnp.concatenate(
        [
            grad_act * up_part * sigmoid_gate * (1.0 + gate_part * (1.0 - sigmoid_gate)),
            grad_act * silu_gate,
        ],
        axis=1,
    ).astype(BF)
    row_gate_grad = jnp.sum(activated.astype(F32) * grad_act_raw, axis=1, keepdims=True)
    grad_rows = lax.dot_general(grad_gate_up, gate_up_w, LAST, preferred_element_type=F32).astype(BF)
    grad_returned = to_experts(jnp.concatenate([grad_rows, widen(in_two(row_gate_grad))], axis=1))
    grad_gate_up_w = lax.dot_general(
        received, grad_gate_up, ROWS, preferred_element_type=F32
    ).astype(BF)
    grad_down_w = lax.dot_general(activated, grad_expert, ROWS, preferred_element_type=F32).astype(BF)
    gate_up_sum = lax.psum_scatter(grad_gate_up_w, "dp", scatter_dimension=0, tiled=True)
    gate_up_grad = gate_up_sum.reshape(1, 512, 2, width).astype(F32)
    down_grad = lax.psum_scatter(
        after(grad_down_w, gate_up_sum), "dp", scatter_dimension=1, tiled=True
    ).astype(F32)[None]

    grad_xn2_part = jnp.dot(
        any_row, grad_returned[:, :MODEL_WIDTH], preferred_element_type=F32
    ).astype(BF)
    row_gate_parts = grad_returned[:, MODEL_WIDTH : MODEL_WIDTH + 2]
    gate_m_part = jnp.sum(
        jnp.einsum("jtr,rd->tjd", to_row, row_gate_parts, preferred_element_type=F32), axis=2
    )
    shares = jnp.concatenate([grad_xn2_part, widen(in_two(gate_m_part))], axis=1)
    landed = (
        exchange(shares.reshape(4, quarter, MODEL_WIDTH + HEAD_SIZE), "tensor")
        .astype(F32)
        .sum(axis=0)
    )
    grad_gate_m = (
        landed[:, MODEL_WIDTH : MODEL_WIDTH + 2] + landed[:, MODEL_WIDTH + 2 : MODEL_WIDTH + 4]
    )

    def quarter_of(array, offset=0):
        return lax.dynamic_slice_in_dim(array, first + offset, quarter)

    grad_logit_m = gate_back(quarter_of(gate_m), grad_gate_m, quarter_of(pick_m))
    grad_xn2 = landed[:, :MODEL_WIDTH] + lax.dot_general(
        grad_logit_m, router_m.astype(F32), LAST, preferred_element_type=F32
    )
    grad_norm, gain_m_part = norm_back(core_first(grad_xn2), hidden, factor_m, gain_m)
    grad_hidden = core_first(quarter_of(cotangent)).astype(F32) + grad_norm
    grad_branch = spread(grad_hidden.astype(BF), plane, 16).reshape(4 * count, MODEL_WIDTH)

    expert_part = turned(
        jnp.dot(activated, down_w, preferred_element_type=F32).astype(BF), lax.rem(4 - z, 4)
    )
    returned = to_experts(after(expert_part, grad_branch))
    fetched = jnp.einsum("jtr,rd->jtd", to_row, returned, preferred_element_type=F32)
    moe_part = jnp.sum(weight_m.T[:, :, None] * fetched, axis=0).astype(BF)
    moe = sum_direct(moe_part.reshape(4, quarter, MODEL_WIDTH), "tensor")
    output_own = (core_last(hidden) + moe).astype(BF)

    grad_mixed = jnp.dot(grad_branch, out_w, preferred_element_type=F32)
    grad_q_all, grad_logit_a, grad_kv_own, grad_kv_give = in_vmem(
        backward_kernel,
        [
            jax.ShapeDtypeStruct((half, EXPERTS * HEAD_SIZE), BF),
            jax.ShapeDtypeStruct((half, HEAD_SIZE), BF),
            jax.ShapeDtypeStruct((half, 2 * HEAD_SIZE), F32),
            jax.ShapeDtypeStruct((half, 2 * HEAD_SIZE), BF),
        ],
        [pltpu.VMEM((2, half, 2 * HEAD_SIZE), F32)],
        12 << 28,
        grad_mixed,
        query,
        kv_own,
        kv_other,
        attended,
        totals,
        gate_a,
        *shared,
    )
    own_grad_kv = grad_kv_own + lax.ppermute(grad_kv_give, "core", SWAP).astype(F32)
    grad_key = own_grad_kv[:, :HEAD_SIZE]
    grad_kv = jnp.concatenate(
        [grad_key * cosine - swapped(grad_key) * sine, own_grad_kv[:, HEAD_SIZE:]], axis=1
    ).astype(BF)
    grad_in = jnp.concatenate([grad_q_all, grad_kv, grad_logit_a], axis=1)
    out_grad = heads_last(
        scatter_rows(
            lax.dot_general(grad_branch, mixed, ROWS, preferred_element_type=F32).astype(BF), core
        )
    )
    grad_xn1_part = lax.dot_general(grad_in, in_w, LAST, preferred_element_type=F32).astype(BF)
    landed_a = (
        exchange(grad_xn1_part.reshape(16, quarter, MODEL_WIDTH), plane).astype(F32).sum(axis=0)
    )
    grad_x_norm, _ = norm_back(landed_a, own_values, own_factor, gain_a)
    ends = jnp.concatenate(
        [output_own, core_last((grad_hidden + grad_x_norm).astype(BF))], axis=1
    )
    both_ends = spread(ends, "tensor", 4).reshape(count, 2 * MODEL_WIDTH)
    output, input_grad = both_ends[:, :MODEL_WIDTH], both_ends[:, MODEL_WIDTH:]

    gain_row = jnp.pad(gain_m_part[None].astype(BF), ((0, 7), (0, 0)))
    tall = jnp.concatenate([xn1, xn2_own, gain_row], axis=0)
    router_cols = jnp.pad(grad_logit_m.astype(BF), ((0, 0), (1288, 112)))
    gain_cols = (
        (jnp.arange(8)[:, None] == 0) & (jnp.arange(1408)[None, :] == 1296)
    ).astype(BF)
    grad_tall = jnp.concatenate([grad_in, router_cols, gain_cols], axis=0)
    in_parts = scatter_rows(
        lax.dot_general(tall, grad_tall, ROWS, preferred_element_type=F32).astype(BF), core
    )
    in_grad = heads_last(in_parts[:, :, :1280])
    query_grad, kv_grad = in_grad[:, :8], in_grad[:, 8:]
    small_part = jnp.sum(in_parts[:, :, 1280:].astype(F32), axis=0)
    gain_rows = lax.dynamic_slice_in_dim(attn_gain.astype(F32), z * 512 + y * 128 + core * 64, 64)
    gain_a_part = (
        jnp.sum(in_grad * in_own.astype(F32), axis=(1, 2))
        + jnp.sum(small_part[:, :8] * attn_router.astype(F32), axis=1)
    ) / gain_rows
    small_sent = jnp.concatenate([small_part[:, :17], gain_a_part[:, None]], axis=1)
    small_bf = widen(small_sent.astype(BF))
    small_sum = sum(
        p.astype(F32) for p in [small_bf] + [from_ahead(small_bf, "tensor", k) for k in (1, 2, 3)]
    )
    return (
        output,
        input_grad,
        small_sum[:, 17],
        small_sum[:, 16],
        small_sum[:, :8],
        kv_grad,
        query_grad,
        out_grad,
        small_sum[:, 8:16],
        gate_up_grad,
        down_grad,
    )


def solution(mesh):
    split = Mesh(mesh.devices.reshape(4, 4, 2, 4), ("dp", "y", "core", "tensor"))
    rows = ("dp", "y", "core")
    expert = ("y", "core")
    placed = (
        P(rows, None),
        P(rows, None),
        P(),
        P(),
        P(rows, None),
        P(rows, None, "tensor"),
        P(rows, None, "tensor"),
        P(rows, None, "tensor"),
        P(rows, None),
        P(expert, "dp", None, "tensor"),
        P(expert, "tensor", "dp"),
        P(rows, None),
        P(rows, None),
        P(rows, None),
        P(),
    )
    return jax.shard_map(
        body,
        mesh=split,
        in_specs=placed,
        out_specs=(
            P(rows, None),
            P(rows, None),
            P(rows),
            P(rows),
            P(rows, None),
            P(rows, None, "tensor"),
            P(rows, None, "tensor"),
            P(rows, None, "tensor"),
            P(rows, None),
            P(expert, "dp", None, "tensor"),
            P(expert, "tensor", "dp"),
        ),
        check_vma=False,
    )
```

```python
import jax
import jax.numpy as jnp
from jax import lax
from jax.experimental import pallas as pl
from jax.experimental.pallas import tpu as pltpu
from jax.sharding import Mesh
from jax.sharding import PartitionSpec as P

MODEL_WIDTH = 2048
HEAD_SIZE = 128
EXPERTS = 8
WINDOW = 1024
NORM_EPS = 1e-06
BF = jnp.bfloat16
F32 = jnp.float32
ROWS = (((0,), (0,)), ((), ()))
LAST = (((1,), (1,)), ((), ()))
UP = [(0, 1), (1, 2), (2, 3), (3, 0)]
DOWN = [(0, 3), (1, 0), (2, 1), (3, 2)]
SWAP = [(0, 1), (1, 0)]


def exchange(blocks, axis):
    return lax.all_to_all(blocks, axis, split_axis=0, concat_axis=0, tiled=True)


def spread(block, axis, count):
    return exchange(jnp.broadcast_to(block, (count, *block.shape)), axis)


def from_ahead(block, axis, steps):
    return lax.ppermute(block, axis, [(i, (i - steps) % 4) for i in range(4)])


def in_order(pieces, first):
    both = jnp.stack(pieces + pieces[:3])
    return lax.dynamic_slice_in_dim(both, lax.rem(4 - first, 4), 4)


def pick_block(blocks, index):
    return lax.dynamic_index_in_dim(blocks, lax.rem(index, 4), 0, keepdims=False)


def send_direct(blocks, axis):
    me = lax.axis_index(axis)
    return [pick_block(blocks, me)] + [
        from_ahead(pick_block(blocks, me + 4 - k), axis, k) for k in (1, 2, 3)
    ]


def sum_direct(blocks, axis):
    return sum(p.astype(F32) for p in send_direct(blocks, axis))


def ring_pieces(block, axis):
    half = block.shape[0] // 2
    before = lax.ppermute(block, axis, UP)
    after = lax.ppermute(block, axis, DOWN)
    far_low = lax.ppermute(before[:half], axis, UP)
    far_high = lax.ppermute(after[half:], axis, DOWN)
    return [block, after, far_low, far_high, before]


def heads_first(shard):
    columns = shard.shape[1] * HEAD_SIZE
    return shard.reshape(64, -1, 4, HEAD_SIZE).transpose(2, 0, 1, 3).reshape(4, 64, columns)


def after(value, other):
    return lax.optimization_barrier((value, other))[0]


def core_first(rows):
    return rows.reshape(-1, 4, 4, 2, 64).transpose(0, 1, 3, 2, 4).reshape(-1, MODEL_WIDTH)


def core_last(rows):
    return rows.reshape(-1, 4, 2, 4, 64).transpose(0, 1, 3, 2, 4).reshape(-1, MODEL_WIDTH)


def core_sum(grad, core):
    columns = grad.shape[1]
    parts = grad.reshape(4, 2, 256, columns)
    keep = lax.dynamic_index_in_dim(parts, core, 1, keepdims=False)
    give = lax.dynamic_index_in_dim(parts, 1 - core, 1, keepdims=False)
    return (keep.astype(F32) + lax.ppermute(give, "core", SWAP).astype(F32)).astype(BF)


def ring_first(blocks, axis):
    me = lax.axis_index(axis)
    half = blocks.shape[1] // 2
    far = pick_block(blocks, me + 2)
    low = lax.ppermute(far[:half], axis, UP)
    high = lax.ppermute(far[half:], axis, DOWN)
    right, left = pick_block(blocks, me + 1), pick_block(blocks, me + 3)
    right = jnp.concatenate([(right[:half].astype(F32) + low.astype(F32)).astype(BF), right[half:]])
    left = jnp.concatenate([left[:half], (left[half:].astype(F32) + high.astype(F32)).astype(BF)])
    return right, left


def ring_second(blocks, right, left, axis):
    return (
        pick_block(blocks, lax.axis_index(axis)).astype(F32)
        + lax.ppermute(right, axis, UP).astype(F32)
        + lax.ppermute(left, axis, DOWN).astype(F32)
    )


def heads_last(blocks):
    heads = blocks.shape[2] // HEAD_SIZE
    return (
        blocks.reshape(4, 64, heads, HEAD_SIZE)
        .transpose(1, 2, 0, 3)
        .reshape(64, heads, 4 * HEAD_SIZE)
        .astype(F32)
    )


def rms_scale(values):
    return lax.rsqrt(jnp.mean(values * values, axis=-1, keepdims=True) + NORM_EPS)


def turn(heads, cosine, sine):
    first, second = heads[..., :64], heads[..., 64:]
    return jnp.concatenate([first * cosine - second * sine, second * cosine + first * sine], axis=-1)


EXTENTS = (256, 384, 512, 640)
SCALE = HEAD_SIZE**-0.5


def masked_scores(query, key, row_meta, key_meta):
    raw = lax.dot_general(query, key, LAST, preferred_element_type=F32) * SCALE
    gap = row_meta[:, 0:1] - key_meta[0:1]
    allowed = (gap >= 0) & (gap < WINDOW) & (row_meta[:, 1:2] == key_meta[1:2])
    return jnp.where(jnp.concatenate([allowed, allowed], axis=0), raw, -1e30)


def forward_kernel(proj, own, other, routes, cosine, sine, row_meta, key_meta, *outs):
    query_out, attended_out, total_out, gates_out, mixed_out = outs
    count = proj.shape[0] // 4
    for i in range(4):
        rows = pl.ds(count * i, count)
        extent = EXTENTS[i]
        logits = proj[rows, 1280:1288]
        lane = lax.broadcasted_iota(jnp.int32, (count, EXPERTS), 1)
        named = [routes[rows, 0:1], routes[rows, 1:2]]
        chosen = [jnp.sum(jnp.where(lane == n, logits, 0.0), axis=1, keepdims=True) for n in named]
        top = jnp.maximum(chosen[0], chosen[1])
        power = [jnp.exp(c - top) for c in chosen]
        gates = [p / (power[0] + power[1]) for p in power]
        gates_out[rows, 0:1] = gates[0]
        gates_out[rows, 1:2] = gates[1]
        cos, sin = cosine[rows, :], sine[rows, :]
        picked = []
        for n in named:
            q = jnp.zeros((count, HEAD_SIZE), F32)
            for e in range(EXPERTS):
                q = q + jnp.where(n == e, proj[rows, HEAD_SIZE * e : HEAD_SIZE * (e + 1)], 0.0)
            picked.append(q * cos + pltpu.roll(q, 64, 1) * sin)
        query = jnp.concatenate(picked, axis=0).astype(BF)
        query_out[i] = query
        halves = (own, other)
        scores = [
            masked_scores(
                query, h[:extent, :HEAD_SIZE], row_meta[rows, :], key_meta[k, :, :extent]
            )
            for k, h in enumerate(halves)
        ]
        row_max = jnp.maximum(
            jnp.max(scores[0], axis=1, keepdims=True), jnp.max(scores[1], axis=1, keepdims=True)
        )
        weights = [jnp.exp(s - row_max) for s in scores]
        total = jnp.sum(weights[0], axis=1, keepdims=True) + jnp.sum(weights[1], axis=1, keepdims=True)
        inverse = 1.0 / total
        attended = sum(
            jnp.dot((w * inverse).astype(BF), h[:extent, HEAD_SIZE:], preferred_element_type=F32)
            for w, h in zip(weights, halves)
        )
        attended_out[i] = attended
        total_out[i] = row_max + jnp.log(total)
        for e in range(EXPERTS):
            mixed_out[rows, HEAD_SIZE * e : HEAD_SIZE * (e + 1)] = (
                jnp.where(named[0] == e, gates[0], 0.0) * attended[:count]
                + jnp.where(named[1] == e, gates[1], 0.0) * attended[count:]
            ).astype(BF)


def backward_kernel(
    grad_mixed, query_in, own, other, attended_in, total_in, gates_in, routes, cosine, sine, row_meta, key_meta, *outs
):
    grad_query_out, grad_logit_out, grad_own_out, grad_other_out, sums = outs
    count = grad_mixed.shape[0] // 4
    sums[...] = jnp.zeros_like(sums)
    for i in range(4):
        rows = pl.ds(count * i, count)
        extent = EXTENTS[i]
        named = [routes[rows, 0:1], routes[rows, 1:2]]
        gates = [gates_in[rows, 0:1], gates_in[rows, 1:2]]
        cos, sin = cosine[rows, :], sine[rows, :]
        attended = attended_in[i]
        picked = []
        for n in named:
            g = jnp.zeros((count, HEAD_SIZE), F32)
            for e in range(EXPERTS):
                g = g + jnp.where(n == e, grad_mixed[rows, HEAD_SIZE * e : HEAD_SIZE * (e + 1)], 0.0)
            picked.append(g)
        gate_grads = [
            jnp.sum(p * attended[count * j : count * (j + 1)], axis=1, keepdims=True)
            for j, p in enumerate(picked)
        ]
        level = gates[0] * gate_grads[0] + gates[1] * gate_grads[1]
        lane = lax.broadcasted_iota(jnp.int32, (count, HEAD_SIZE), 1)
        grad_logit_out[rows, :] = sum(
            jnp.where(lane == n, g * (d - level), 0.0) for n, g, d in zip(named, gates, gate_grads)
        ).astype(BF)
        grad_attended = jnp.concatenate(
            [gates[0] * picked[0], gates[1] * picked[1]], axis=0
        ).astype(BF)
        query = query_in[i]
        total = total_in[i]
        probs, grad_probs = [], []
        delta = jnp.zeros((2 * count, 1), F32)
        for k, h in enumerate((own, other)):
            score = masked_scores(
                query, h[:extent, :HEAD_SIZE], row_meta[rows, :], key_meta[k, :, :extent]
            )
            prob = jnp.exp(score - total)
            grad_prob = lax.dot_general(
                grad_attended, h[:extent, HEAD_SIZE:], LAST, preferred_element_type=F32
            )
            delta = delta + jnp.sum(prob * grad_prob, axis=1, keepdims=True)
            probs.append(prob)
            grad_probs.append(grad_prob)
        grad_query = jnp.zeros((2 * count, HEAD_SIZE), F32)
        for k, h in enumerate((own, other)):
            grad_score = (probs[k] * (grad_probs[k] - delta)).astype(BF)
            grad_query = grad_query + jnp.dot(
                grad_score, h[:extent, :HEAD_SIZE], preferred_element_type=F32
            )
            sums[k, :extent, :HEAD_SIZE] += (
                lax.dot_general(grad_score, query, ROWS, preferred_element_type=F32) * SCALE
            )
            sums[k, :extent, HEAD_SIZE:] += lax.dot_general(
                probs[k].astype(BF), grad_attended, ROWS, preferred_element_type=F32
            )
        grad_query = grad_query * SCALE
        turned = [
            g * cos - pltpu.roll(g, 64, 1) * sin for g in (grad_query[:count], grad_query[count:])
        ]
        for e in range(EXPERTS):
            grad_query_out[rows, HEAD_SIZE * e : HEAD_SIZE * (e + 1)] = (
                jnp.where(named[0] == e, turned[0], 0.0) + jnp.where(named[1] == e, turned[1], 0.0)
            ).astype(BF)
    grad_own_out[...] = sums[0]
    grad_other_out[...] = sums[1].astype(BF)


def in_vmem(kernel, outs, scratch, flops, *args):
    spec = pl.BlockSpec(memory_space=pltpu.VMEM)
    moved = sum(a.size * a.dtype.itemsize for a in args)
    return pl.pallas_call(
        kernel,
        out_shape=outs,
        in_specs=[spec] * len(args),
        out_specs=[spec] * len(outs),
        scratch_shapes=scratch,
        compiler_params=pltpu.CompilerParams(vmem_limit_bytes=40 * 1024 * 1024),
        cost_estimate=pl.CostEstimate(flops=flops, bytes_accessed=moved, transcendentals=1 << 20),
    )(*args)


def pick_of(routes):
    return (routes[:, :, None] == jnp.arange(EXPERTS, dtype=jnp.int32)[None, None, :]).astype(F32)


def pair_gates(logits, pick):
    chosen = jnp.sum(logits[:, None, :] * pick, axis=-1)
    weights = jnp.exp(chosen - jnp.max(chosen, axis=1, keepdims=True))
    return weights / jnp.sum(weights, axis=1, keepdims=True)


def gate_back(gates, grad_gates, pick):
    inner = gates * (grad_gates - jnp.sum(gates * grad_gates, axis=1, keepdims=True))
    return jnp.sum(inner[:, :, None] * pick, axis=1)


def norm_back(grad_normed, values, factor, gain):
    gain_part = jnp.sum(grad_normed * values * factor, axis=0)
    inner = grad_normed * gain
    grad_values = factor * inner - values * factor * factor * factor * jnp.mean(
        inner * values, axis=-1, keepdims=True
    )
    return grad_values, gain_part


def in_two(values):
    high = values.astype(BF)
    low = (values - high.astype(F32)).astype(BF)
    return jnp.concatenate([high, low], axis=1)


def widen(columns):
    return jnp.pad(columns, ((0, 0), (0, HEAD_SIZE - columns.shape[1])))


def body(
    tokens,
    cotangent,
    attn_gain,
    mlp_gain,
    attn_router,
    key_value_weight,
    query_matrix,
    output_matrix,
    mlp_router,
    gate_up_weight,
    down_weight,
    attn_routes,
    mlp_routes,
    priority,
    segments,
):
    z, y = lax.axis_index("dp"), lax.axis_index("y")
    core, x = lax.axis_index("core"), lax.axis_index("tensor")
    count = tokens.shape[0]
    quarter = count // 4
    capacity = 50
    room = 56
    sequence = 8 * count
    plane = ("y", "tensor")

    routers_own = jnp.concatenate([attn_router, mlp_router], axis=1)
    in_own = jnp.concatenate([query_matrix, key_value_weight], axis=1)
    down_pieces = ring_pieces(down_weight[0], "dp")
    mine = exchange(
        jnp.concatenate(
            [
                heads_first(in_own),
                jnp.broadcast_to(widen(routers_own), (4, 64, HEAD_SIZE)),
                heads_first(output_matrix),
            ],
            axis=2,
        ),
        "y",
    ).reshape(256, 2432)
    sent = jnp.concatenate([core_first(tokens), widen(attn_routes.astype(BF))], axis=1)
    arrived = spread(after(sent, mine), "y", 4).reshape(4 * count, MODEL_WIDTH + HEAD_SIZE)
    all_w = lax.all_gather(
        after(mine, (down_pieces[1], down_pieces[4])), ("dp", "core"), axis=0, tiled=True
    )
    all_w, arrived, far_low, far_high = lax.optimization_barrier(
        (all_w, arrived, down_pieces[2], down_pieces[3])
    )
    in_w, out_w = all_w[:, :1408], all_w[:, 1408:]
    gate_up_own = gate_up_weight.reshape(4, 2, 64, 2816).transpose(1, 0, 2, 3).reshape(512, 2816)
    gate_up_w = lax.all_gather(after(gate_up_own, all_w), "dp", axis=0, tiled=True)
    router_m = in_w[:, 1288:1296]

    down_w = jnp.concatenate(
        [
            down_pieces[0],
            down_pieces[1],
            jnp.concatenate([far_low, far_high], axis=0),
            down_pieces[4],
        ],
        axis=1,
    )

    def turned(columns, blocks):
        twice = jnp.concatenate([columns, columns], axis=1)
        return lax.dynamic_slice_in_dim(twice, blocks * 512, MODEL_WIDTH, axis=1)

    values = arrived[:, :MODEL_WIDTH].astype(F32)
    routes = arrived[:, MODEL_WIDTH : MODEL_WIDTH + 2].astype(jnp.int32)
    gain_a = core_first(attn_gain.astype(F32))[0]
    gain_m = core_first(mlp_gain.astype(F32))[0]
    xn1 = (values * rms_scale(values) * gain_a).astype(BF)

    ranking = priority[0]
    pick_m = pick_of(mlp_routes)
    before = (ranking[None, :] < ranking[:, None]).astype(BF)
    earlier = jnp.dot(before, jnp.sum(pick_m, axis=1).astype(BF), preferred_element_type=F32)
    slots = jnp.sum(pick_m * earlier[:, None, :], axis=-1).astype(jnp.int32)
    kept = slots < capacity
    dest = jnp.where(kept, mlp_routes * room + slots, -1)
    lanes = jnp.arange(EXPERTS * room, dtype=jnp.int32)
    to_row = (dest.T[:, :, None] == lanes[None, None, :]).astype(BF)
    any_row = to_row[0] + to_row[1]
    both_rows = to_row.reshape(2 * count, EXPERTS * room)

    def to_experts(rows):
        columns = rows.shape[1]
        return exchange(rows.reshape(EXPERTS, room, columns), ("y", "core")).reshape(
            EXPERTS * room, columns
        )

    def with_other(j):
        others = jnp.concatenate([pick_m[:, 1 - j], jnp.ones((count, 1), F32)], axis=1)
        return jnp.concatenate([cotangent, widen(others.astype(BF))], axis=1)

    grad_sent = lax.dot_general(
        both_rows,
        jnp.concatenate([with_other(0), with_other(1)], axis=0),
        ROWS,
        preferred_element_type=F32,
    ).astype(BF)
    grad_landed = to_experts(after(grad_sent, arrived))

    def places(half):
        blocks = 2 * jnp.arange(4, dtype=jnp.int32)[:, None] + half
        return (blocks * count + jnp.arange(count, dtype=jnp.int32)[None, :]).reshape(-1)

    of_sequence = lax.dynamic_slice_in_dim(segments, z * sequence, sequence).reshape(4, 2, count)

    def meta(half):
        documents = lax.dynamic_index_in_dim(of_sequence, half, 1, keepdims=False).reshape(-1)
        return jnp.stack([places(half), documents])

    key_meta = jnp.stack([meta(core), meta(1 - core)])
    row_meta = key_meta[0].T
    inverse = 10000.0 ** (-(jnp.arange(HEAD_SIZE // 2).astype(F32) * 2.0 / HEAD_SIZE))
    angle = places(core).astype(F32)[:, None] * inverse[None, :]
    cosine = jnp.tile(jnp.cos(angle), (1, 2))
    sine = jnp.concatenate([-jnp.sin(angle), jnp.sin(angle)], axis=1)

    def swapped(rows):
        return jnp.concatenate([rows[:, 64:], rows[:, :64]], axis=1)

    half = 4 * count
    projected = jnp.dot(xn1, in_w, preferred_element_type=F32)
    key_raw = projected[:, 1024:1152]
    kv_own = jnp.concatenate(
        [key_raw * cosine + swapped(key_raw) * sine, projected[:, 1152:1280]], axis=1
    ).astype(BF)
    kv_other = lax.ppermute(kv_own, "core", SWAP)
    shared = (routes, cosine, sine, row_meta, key_meta)
    query, attended, totals, gate_a, mixed = in_vmem(
        forward_kernel,
        [
            jax.ShapeDtypeStruct((4, 2 * count, HEAD_SIZE), BF),
            jax.ShapeDtypeStruct((4, 2 * count, HEAD_SIZE), F32),
            jax.ShapeDtypeStruct((4, 2 * count, 1), F32),
            jax.ShapeDtypeStruct((half, 2), F32),
            jax.ShapeDtypeStruct((half, EXPERTS * HEAD_SIZE), BF),
        ],
        [],
        6 << 28,
        projected,
        kv_own,
        kv_other,
        *shared,
    )
    branch_part = lax.dot_general(mixed, out_w, LAST, preferred_element_type=F32).astype(BF)
    branch_part = after(branch_part, grad_landed)
    grad_received = grad_landed[:, :MODEL_WIDTH]
    grad_act_raw = lax.dot_general(
        turned(grad_received, z), down_w, LAST, preferred_element_type=F32
    )
    branch = (
        after(exchange(branch_part.reshape(16, quarter, MODEL_WIDTH), plane), grad_act_raw)
        .astype(F32)
        .sum(axis=0)
    )

    first = x * quarter
    own_values = core_first(lax.dynamic_slice_in_dim(tokens, first, quarter)).astype(F32)
    own_factor = rms_scale(own_values)
    hidden = own_values + branch
    factor_m = rms_scale(hidden)
    xn2_own = (hidden * factor_m * gain_m).astype(BF)
    xn2 = spread(xn2_own, "tensor", 4).reshape(count, MODEL_WIDTH)
    gate_m = pair_gates(jnp.dot(xn2, router_m, preferred_element_type=F32), pick_m)
    weight_m = gate_m * kept.astype(F32)

    received = to_experts(
        lax.dot_general(any_row, xn2, ROWS, preferred_element_type=F32).astype(BF)
    )
    other_pick = grad_landed[:, MODEL_WIDTH : MODEL_WIDTH + EXPERTS].astype(F32)
    valid = grad_landed[:, MODEL_WIDTH + EXPERTS : MODEL_WIDTH + EXPERTS + 1].astype(F32)
    row_logits = jnp.dot(received, router_m, preferred_element_type=F32)
    here = (jnp.arange(EXPERTS, dtype=jnp.int32) == 2 * y + core).astype(F32)
    own_logit = jnp.sum(row_logits * here[None], axis=1, keepdims=True)
    other_logit = jnp.sum(row_logits * other_pick, axis=1, keepdims=True)
    top = jnp.maximum(own_logit, other_logit)
    own_weight = jnp.exp(own_logit - top)
    row_gate = valid * own_weight / (own_weight + jnp.exp(other_logit - top))

    width = down_weight.shape[1]
    grad_expert = (row_gate * grad_received.astype(F32)).astype(BF)
    gate_up = jnp.dot(received, gate_up_w, preferred_element_type=F32)
    gate_part, up_part = gate_up[:, :width], gate_up[:, width:]
    sigmoid_gate = jax.nn.sigmoid(gate_part)
    silu_gate = gate_part * sigmoid_gate
    activated = (silu_gate * up_part).astype(BF)
    grad_act = row_gate * grad_act_raw
    grad_gate_up = jnp.concatenate(
        [
            grad_act * up_part * sigmoid_gate * (1.0 + gate_part * (1.0 - sigmoid_gate)),
            grad_act * silu_gate,
        ],
        axis=1,
    ).astype(BF)
    row_gate_grad = jnp.sum(activated.astype(F32) * grad_act_raw, axis=1, keepdims=True)
    grad_rows = lax.dot_general(grad_gate_up, gate_up_w, LAST, preferred_element_type=F32).astype(BF)
    grad_returned = to_experts(jnp.concatenate([grad_rows, widen(in_two(row_gate_grad))], axis=1))
    late_grad, late_act, _ = lax.optimization_barrier((grad_gate_up, activated, grad_rows))
    grad_down_w = lax.dot_general(late_act, grad_expert, ROWS, preferred_element_type=F32).astype(BF)
    grad_gate_up_w = lax.dot_general(
        received, late_grad, ROWS, preferred_element_type=F32
    ).astype(BF)
    gate_up_sum = lax.psum_scatter(grad_gate_up_w, "dp", scatter_dimension=0, tiled=True)
    gate_up_grad = (
        gate_up_sum.reshape(2, 4, 64, 2816)
        .transpose(1, 0, 2, 3)
        .reshape(1, 512, 2, width)
        .astype(F32)
    )
    down_grad = lax.psum_scatter(grad_down_w, "dp", scatter_dimension=1, tiled=True).astype(F32)[None]
    expert_part = turned(
        jnp.dot(late_act, down_w, preferred_element_type=F32).astype(BF), lax.rem(4 - z, 4)
    )
    grad_returned = after(grad_returned, (grad_gate_up_w, grad_down_w, expert_part))
    expert_out = sum_direct(
        jnp.stack([expert_part[:, 512 * i : 512 * (i + 1)] for i in range(4)]), "tensor"
    ).astype(BF)

    grad_xn2_part = jnp.dot(
        any_row, grad_returned[:, :MODEL_WIDTH], preferred_element_type=F32
    ).astype(BF)
    row_gate_parts = grad_returned[:, MODEL_WIDTH : MODEL_WIDTH + 2]
    gate_m_part = jnp.sum(
        jnp.einsum("jtr,rd->tjd", to_row, row_gate_parts, preferred_element_type=F32), axis=2
    )
    shares = jnp.concatenate([grad_xn2_part, widen(in_two(gate_m_part))], axis=1)
    landed = (
        exchange(shares.reshape(4, quarter, MODEL_WIDTH + HEAD_SIZE), "tensor")
        .astype(F32)
        .sum(axis=0)
    )
    landed, expert_out = lax.optimization_barrier((landed, expert_out))
    returned = to_experts(expert_out)
    grad_gate_m = (
        landed[:, MODEL_WIDTH : MODEL_WIDTH + 2] + landed[:, MODEL_WIDTH + 2 : MODEL_WIDTH + 4]
    )

    def quarter_of(array, offset=0):
        return lax.dynamic_slice_in_dim(array, first + offset, quarter)

    grad_logit_m = gate_back(quarter_of(gate_m), grad_gate_m, quarter_of(pick_m))
    grad_xn2 = landed[:, :MODEL_WIDTH] + lax.dot_general(
        grad_logit_m, router_m.astype(F32), LAST, preferred_element_type=F32
    )
    grad_norm, gain_m_part = norm_back(grad_xn2, hidden, factor_m, gain_m)
    grad_hidden = core_first(quarter_of(cotangent)).astype(F32) + grad_norm
    grad_sent_back, returned = lax.optimization_barrier((grad_hidden.astype(BF), returned))
    grad_branch = spread(grad_sent_back, plane, 16).reshape(4 * count, MODEL_WIDTH)

    fetched = jnp.einsum("jtr,rd->jtd", to_row, returned, preferred_element_type=F32)
    moe_part = jnp.sum(weight_m.T[:, :, None] * fetched, axis=0).astype(BF)
    grad_branch, moe_part = lax.optimization_barrier((grad_branch, moe_part))
    moe_pieces = exchange(moe_part.reshape(4, quarter, MODEL_WIDTH // 4), "tensor")

    grad_mixed = jnp.dot(grad_branch, out_w, preferred_element_type=F32)
    grad_q_all, grad_logit_a, grad_kv_own, grad_kv_give = in_vmem(
        backward_kernel,
        [
            jax.ShapeDtypeStruct((half, EXPERTS * HEAD_SIZE), BF),
            jax.ShapeDtypeStruct((half, HEAD_SIZE), BF),
            jax.ShapeDtypeStruct((half, 2 * HEAD_SIZE), F32),
            jax.ShapeDtypeStruct((half, 2 * HEAD_SIZE), BF),
        ],
        [pltpu.VMEM((2, half, 2 * HEAD_SIZE), F32)],
        12 << 28,
        grad_mixed,
        query,
        kv_own,
        kv_other,
        attended,
        totals,
        gate_a,
        *shared,
    )
    out_terms = lax.dot_general(grad_branch, mixed, ROWS, preferred_element_type=F32).astype(BF)
    kv_back, out_terms, moe_pieces = lax.optimization_barrier(
        (lax.ppermute(grad_kv_give, "core", SWAP), out_terms, moe_pieces)
    )
    out_parts = core_sum(out_terms, core)
    moe = moe_pieces.transpose(1, 0, 2).reshape(quarter, MODEL_WIDTH).astype(F32)
    output_own = (core_last(hidden) + moe).astype(BF)
    own_grad_kv = grad_kv_own + kv_back.astype(F32)
    grad_key = own_grad_kv[:, :HEAD_SIZE]
    grad_kv = jnp.concatenate(
        [grad_key * cosine - swapped(grad_key) * sine, own_grad_kv[:, HEAD_SIZE:]], axis=1
    ).astype(BF)
    grad_in = jnp.concatenate([grad_q_all, grad_kv, grad_logit_a], axis=1)
    grad_xn1_part = lax.dot_general(grad_in, in_w, LAST, preferred_element_type=F32).astype(BF)
    out_right, out_left = ring_first(out_parts, "dp")
    gain_row = jnp.pad(gain_m_part[None].astype(BF), ((0, 7), (0, 0)))
    tall = jnp.concatenate([xn1, xn2_own, gain_row], axis=0)
    router_cols = jnp.pad(grad_logit_m.astype(BF), ((0, 0), (1288, 112)))
    gain_cols = (
        (jnp.arange(8)[:, None] == 0) & (jnp.arange(1408)[None, :] == 1296)
    ).astype(BF)
    grad_tall = jnp.concatenate([after(grad_in, grad_xn1_part), router_cols, gain_cols], axis=0)
    in_parts = core_sum(
        lax.dot_general(tall, grad_tall, ROWS, preferred_element_type=F32).astype(BF), core
    )
    in_right, in_left = ring_first(in_parts, "dp")
    out_sum = ring_second(out_parts, out_right, out_left, "dp").astype(BF)
    landed_raw = exchange(grad_xn1_part.reshape(16, quarter, MODEL_WIDTH), plane)
    in_sum = ring_second(in_parts, in_right, in_left, "dp").astype(BF)
    landed_raw, in_sum, out_sum = lax.optimization_barrier((landed_raw, in_sum, out_sum))
    landed_a = landed_raw.astype(F32).sum(axis=0)
    grad_x_norm, _ = norm_back(landed_a, own_values, own_factor, gain_a)
    ends = jnp.concatenate(
        [output_own, core_last((grad_hidden + grad_x_norm).astype(BF))], axis=1
    )
    both_ends = after(spread(ends, "tensor", 4), gate_up_grad).reshape(count, 2 * MODEL_WIDTH)
    output, input_grad = both_ends[:, :MODEL_WIDTH], both_ends[:, MODEL_WIDTH:]

    both_sums = jnp.concatenate([in_sum, out_sum], axis=1).reshape(4, 64, 2432)
    both_parts = in_order(send_direct(both_sums, "y"), y)
    in_parts, out_parts = both_parts[:, :, :1408], both_parts[:, :, 1408:]
    out_grad = heads_last(out_parts)
    in_grad = heads_last(in_parts[:, :, :1280])
    query_grad, kv_grad = in_grad[:, :8], in_grad[:, 8:]
    small_part = jnp.sum(in_parts[:, :, 1280:].astype(F32), axis=0)
    gain_rows = lax.dynamic_slice_in_dim(attn_gain.astype(F32), z * 512 + y * 128 + core * 64, 64)
    gain_a_part = (
        jnp.sum(in_grad * in_own.astype(F32), axis=(1, 2))
        + jnp.sum(small_part[:, :8] * attn_router.astype(F32), axis=1)
    ) / gain_rows
    small_sent = jnp.concatenate([small_part[:, :17], gain_a_part[:, None]], axis=1)
    small_bf = widen(small_sent.astype(BF))
    small_sum = sum(
        p.astype(F32) for p in [small_bf] + [from_ahead(small_bf, "tensor", k) for k in (1, 2, 3)]
    )
    return (
        output,
        input_grad,
        small_sum[:, 17],
        small_sum[:, 16],
        small_sum[:, :8],
        kv_grad,
        query_grad,
        out_grad,
        small_sum[:, 8:16],
        gate_up_grad,
        down_grad,
    )


def solution(mesh):
    split = Mesh(mesh.devices.reshape(4, 4, 2, 4), ("dp", "y", "core", "tensor"))
    rows = ("dp", "y", "core")
    expert = ("y", "core")
    placed = (
        P(rows, None),
        P(rows, None),
        P(),
        P(),
        P(rows, None),
        P(rows, None, "tensor"),
        P(rows, None, "tensor"),
        P(rows, None, "tensor"),
        P(rows, None),
        P(expert, "dp", None, "tensor"),
        P(expert, "tensor", "dp"),
        P(rows, None),
        P(rows, None),
        P(rows, None),
        P(),
    )
    return jax.shard_map(
        body,
        mesh=split,
        in_specs=placed,
        out_specs=(
            P(rows, None),
            P(rows, None),
            P(rows),
            P(rows),
            P(rows, None),
            P(rows, None, "tensor"),
            P(rows, None, "tensor"),
            P(rows, None, "tensor"),
            P(rows, None),
            P(expert, "dp", None, "tensor"),
            P(expert, "tensor", "dp"),
        ),
        check_vma=False,
    )
```

```python
import jax
import jax.numpy as jnp
from jax import lax
from jax.experimental import pallas as pl
from jax.experimental.pallas import tpu as pltpu
from jax.sharding import Mesh
from jax.sharding import PartitionSpec as P

MODEL_WIDTH = 2048
HEAD_SIZE = 128
EXPERTS = 8
WINDOW = 1024
NORM_EPS = 1e-06
BF = jnp.bfloat16
F32 = jnp.float32
ROWS = (((0,), (0,)), ((), ()))
LAST = (((1,), (1,)), ((), ()))
UP = [(0, 1), (1, 2), (2, 3), (3, 0)]
DOWN = [(0, 3), (1, 0), (2, 1), (3, 2)]
SWAP = [(0, 1), (1, 0)]


def exchange(blocks, axis):
    return lax.all_to_all(blocks, axis, split_axis=0, concat_axis=0, tiled=True)


def spread(block, axis, count):
    return exchange(jnp.broadcast_to(block, (count, *block.shape)), axis)


def from_ahead(block, axis, steps):
    return lax.ppermute(block, axis, [(i, (i - steps) % 4) for i in range(4)])


def in_order(pieces, first):
    both = jnp.stack(pieces + pieces[:3])
    return lax.dynamic_slice_in_dim(both, lax.rem(4 - first, 4), 4)


def pick_block(blocks, index):
    return lax.dynamic_index_in_dim(blocks, lax.rem(index, 4), 0, keepdims=False)


def send_direct(blocks, axis):
    me = lax.axis_index(axis)
    return [pick_block(blocks, me)] + [
        from_ahead(pick_block(blocks, me + 4 - k), axis, k) for k in (1, 2, 3)
    ]


def sum_direct(blocks, axis):
    return sum(p.astype(F32) for p in send_direct(blocks, axis))


def heads_first(shard):
    columns = shard.shape[1] * HEAD_SIZE
    return shard.reshape(64, -1, 4, HEAD_SIZE).transpose(2, 0, 1, 3).reshape(4, 64, columns)


def after(value, other):
    return lax.optimization_barrier((value, other))[0]


def core_first(rows):
    return rows.reshape(-1, 4, 4, 2, 64).transpose(0, 1, 3, 2, 4).reshape(-1, MODEL_WIDTH)


def core_last(rows):
    return rows.reshape(-1, 4, 2, 4, 64).transpose(0, 1, 3, 2, 4).reshape(-1, MODEL_WIDTH)


def core_sum(grad, core):
    columns = grad.shape[1]
    parts = grad.reshape(4, 2, 256, columns)
    keep = lax.dynamic_index_in_dim(parts, core, 1, keepdims=False)
    give = lax.dynamic_index_in_dim(parts, 1 - core, 1, keepdims=False)
    return (keep.astype(F32) + lax.ppermute(give, "core", SWAP).astype(F32)).astype(BF)


def ring_first(blocks, axis):
    me = lax.axis_index(axis)
    half = blocks.shape[1] // 2
    far = pick_block(blocks, me + 2)
    low = lax.ppermute(far[:half], axis, UP)
    high = lax.ppermute(far[half:], axis, DOWN)
    right, left = pick_block(blocks, me + 1), pick_block(blocks, me + 3)
    right = jnp.concatenate([(right[:half].astype(F32) + low.astype(F32)).astype(BF), right[half:]])
    left = jnp.concatenate([left[:half], (left[half:].astype(F32) + high.astype(F32)).astype(BF)])
    return right, left


def ring_second(blocks, right, left, axis):
    return (
        pick_block(blocks, lax.axis_index(axis)).astype(F32)
        + lax.ppermute(right, axis, UP).astype(F32)
        + lax.ppermute(left, axis, DOWN).astype(F32)
    )


def heads_last(blocks):
    heads = blocks.shape[2] // HEAD_SIZE
    return (
        blocks.reshape(4, 64, heads, HEAD_SIZE)
        .transpose(1, 2, 0, 3)
        .reshape(64, heads, 4 * HEAD_SIZE)
        .astype(F32)
    )


def rms_scale(values):
    return lax.rsqrt(jnp.mean(values * values, axis=-1, keepdims=True) + NORM_EPS)


def turn(heads, cosine, sine):
    first, second = heads[..., :64], heads[..., 64:]
    return jnp.concatenate([first * cosine - second * sine, second * cosine + first * sine], axis=-1)


EXTENTS = (256, 384, 512, 640)
SCALE = HEAD_SIZE**-0.5


def masked_scores(query, key, row_meta, key_meta):
    raw = lax.dot_general(query, key, LAST, preferred_element_type=F32) * SCALE
    gap = row_meta[:, 0:1] - key_meta[0:1]
    allowed = (gap >= 0) & (gap < WINDOW) & (row_meta[:, 1:2] == key_meta[1:2])
    return jnp.where(jnp.concatenate([allowed, allowed], axis=0), raw, -1e30)


def forward_kernel(proj, own, other, routes, cosine, sine, row_meta, key_meta, *outs):
    query_out, attended_out, total_out, gates_out, mixed_out = outs
    count = proj.shape[0] // 4
    for i in range(4):
        rows = pl.ds(count * i, count)
        extent = EXTENTS[i]
        logits = proj[rows, 1280:1288]
        lane = lax.broadcasted_iota(jnp.int32, (count, EXPERTS), 1)
        named = [routes[rows, 0:1], routes[rows, 1:2]]
        chosen = [jnp.sum(jnp.where(lane == n, logits, 0.0), axis=1, keepdims=True) for n in named]
        top = jnp.maximum(chosen[0], chosen[1])
        power = [jnp.exp(c - top) for c in chosen]
        gates = [p / (power[0] + power[1]) for p in power]
        gates_out[rows, 0:1] = gates[0]
        gates_out[rows, 1:2] = gates[1]
        cos, sin = cosine[rows, :], sine[rows, :]
        picked = []
        for n in named:
            q = jnp.zeros((count, HEAD_SIZE), F32)
            for e in range(EXPERTS):
                q = q + jnp.where(n == e, proj[rows, HEAD_SIZE * e : HEAD_SIZE * (e + 1)], 0.0)
            picked.append(q * cos + pltpu.roll(q, 64, 1) * sin)
        query = jnp.concatenate(picked, axis=0).astype(BF)
        query_out[i] = query
        halves = (own, other)
        scores = [
            masked_scores(
                query, h[:extent, :HEAD_SIZE], row_meta[rows, :], key_meta[k, :, :extent]
            )
            for k, h in enumerate(halves)
        ]
        row_max = jnp.maximum(
            jnp.max(scores[0], axis=1, keepdims=True), jnp.max(scores[1], axis=1, keepdims=True)
        )
        weights = [jnp.exp(s - row_max) for s in scores]
        total = jnp.sum(weights[0], axis=1, keepdims=True) + jnp.sum(weights[1], axis=1, keepdims=True)
        inverse = 1.0 / total
        attended = sum(
            jnp.dot((w * inverse).astype(BF), h[:extent, HEAD_SIZE:], preferred_element_type=F32)
            for w, h in zip(weights, halves)
        )
        attended_out[i] = attended
        total_out[i] = row_max + jnp.log(total)
        for e in range(EXPERTS):
            mixed_out[rows, HEAD_SIZE * e : HEAD_SIZE * (e + 1)] = (
                jnp.where(named[0] == e, gates[0], 0.0) * attended[:count]
                + jnp.where(named[1] == e, gates[1], 0.0) * attended[count:]
            ).astype(BF)


def backward_kernel(
    grad_mixed, query_in, own, other, attended_in, total_in, gates_in, routes, cosine, sine, row_meta, key_meta, *outs
):
    grad_query_out, grad_logit_out, grad_own_out, grad_other_out, sums = outs
    count = grad_mixed.shape[0] // 4
    sums[...] = jnp.zeros_like(sums)
    for i in range(4):
        rows = pl.ds(count * i, count)
        extent = EXTENTS[i]
        named = [routes[rows, 0:1], routes[rows, 1:2]]
        gates = [gates_in[rows, 0:1], gates_in[rows, 1:2]]
        cos, sin = cosine[rows, :], sine[rows, :]
        attended = attended_in[i]
        picked = []
        for n in named:
            g = jnp.zeros((count, HEAD_SIZE), F32)
            for e in range(EXPERTS):
                g = g + jnp.where(n == e, grad_mixed[rows, HEAD_SIZE * e : HEAD_SIZE * (e + 1)], 0.0)
            picked.append(g)
        gate_grads = [
            jnp.sum(p * attended[count * j : count * (j + 1)], axis=1, keepdims=True)
            for j, p in enumerate(picked)
        ]
        level = gates[0] * gate_grads[0] + gates[1] * gate_grads[1]
        lane = lax.broadcasted_iota(jnp.int32, (count, HEAD_SIZE), 1)
        grad_logit_out[rows, :] = sum(
            jnp.where(lane == n, g * (d - level), 0.0) for n, g, d in zip(named, gates, gate_grads)
        ).astype(BF)
        grad_attended = jnp.concatenate(
            [gates[0] * picked[0], gates[1] * picked[1]], axis=0
        ).astype(BF)
        query = query_in[i]
        total = total_in[i]
        probs, grad_probs = [], []
        delta = jnp.zeros((2 * count, 1), F32)
        for k, h in enumerate((own, other)):
            score = masked_scores(
                query, h[:extent, :HEAD_SIZE], row_meta[rows, :], key_meta[k, :, :extent]
            )
            prob = jnp.exp(score - total)
            grad_prob = lax.dot_general(
                grad_attended, h[:extent, HEAD_SIZE:], LAST, preferred_element_type=F32
            )
            delta = delta + jnp.sum(prob * grad_prob, axis=1, keepdims=True)
            probs.append(prob)
            grad_probs.append(grad_prob)
        grad_query = jnp.zeros((2 * count, HEAD_SIZE), F32)
        for k, h in enumerate((own, other)):
            grad_score = (probs[k] * (grad_probs[k] - delta)).astype(BF)
            grad_query = grad_query + jnp.dot(
                grad_score, h[:extent, :HEAD_SIZE], preferred_element_type=F32
            )
            sums[k, :extent, :HEAD_SIZE] += (
                lax.dot_general(grad_score, query, ROWS, preferred_element_type=F32) * SCALE
            )
            sums[k, :extent, HEAD_SIZE:] += lax.dot_general(
                probs[k].astype(BF), grad_attended, ROWS, preferred_element_type=F32
            )
        grad_query = grad_query * SCALE
        turned = [
            g * cos - pltpu.roll(g, 64, 1) * sin for g in (grad_query[:count], grad_query[count:])
        ]
        for e in range(EXPERTS):
            grad_query_out[rows, HEAD_SIZE * e : HEAD_SIZE * (e + 1)] = (
                jnp.where(named[0] == e, turned[0], 0.0) + jnp.where(named[1] == e, turned[1], 0.0)
            ).astype(BF)
    grad_own_out[...] = sums[0]
    grad_other_out[...] = sums[1].astype(BF)


def in_vmem(kernel, outs, scratch, flops, *args):
    spec = pl.BlockSpec(memory_space=pltpu.VMEM)
    moved = sum(a.size * a.dtype.itemsize for a in args)
    return pl.pallas_call(
        kernel,
        out_shape=outs,
        in_specs=[spec] * len(args),
        out_specs=[spec] * len(outs),
        scratch_shapes=scratch,
        compiler_params=pltpu.CompilerParams(vmem_limit_bytes=40 * 1024 * 1024),
        cost_estimate=pl.CostEstimate(flops=flops, bytes_accessed=moved, transcendentals=1 << 20),
    )(*args)


def pick_of(routes):
    return (routes[:, :, None] == jnp.arange(EXPERTS, dtype=jnp.int32)[None, None, :]).astype(F32)


def pair_gates(logits, pick):
    chosen = jnp.sum(logits[:, None, :] * pick, axis=-1)
    weights = jnp.exp(chosen - jnp.max(chosen, axis=1, keepdims=True))
    return weights / jnp.sum(weights, axis=1, keepdims=True)


def gate_back(gates, grad_gates, pick):
    inner = gates * (grad_gates - jnp.sum(gates * grad_gates, axis=1, keepdims=True))
    return jnp.sum(inner[:, :, None] * pick, axis=1)


def norm_back(grad_normed, values, factor, gain):
    gain_part = jnp.sum(grad_normed * values * factor, axis=0)
    inner = grad_normed * gain
    grad_values = factor * inner - values * factor * factor * factor * jnp.mean(
        inner * values, axis=-1, keepdims=True
    )
    return grad_values, gain_part


def in_two(values):
    high = values.astype(BF)
    low = (values - high.astype(F32)).astype(BF)
    return jnp.concatenate([high, low], axis=1)


def widen(columns):
    return jnp.pad(columns, ((0, 0), (0, HEAD_SIZE - columns.shape[1])))


def body(
    tokens,
    cotangent,
    attn_gain,
    mlp_gain,
    attn_router,
    key_value_weight,
    query_matrix,
    output_matrix,
    mlp_router,
    gate_up_weight,
    down_weight,
    attn_routes,
    mlp_routes,
    priority,
    segments,
):
    z, y = lax.axis_index("dp"), lax.axis_index("y")
    core, x = lax.axis_index("core"), lax.axis_index("tensor")
    count = tokens.shape[0]
    quarter = count // 4
    capacity = 50
    room = 56
    sequence = 8 * count
    plane = ("y", "tensor")

    routers_own = jnp.concatenate([attn_router, mlp_router], axis=1)
    in_own = jnp.concatenate([query_matrix, key_value_weight], axis=1)
    down_own = down_weight[0]
    down_before = lax.ppermute(down_own, "dp", UP)
    down_after = lax.ppermute(down_own, "dp", DOWN)
    mine = exchange(
        jnp.concatenate(
            [
                heads_first(in_own),
                jnp.broadcast_to(widen(routers_own), (4, 64, HEAD_SIZE)),
                heads_first(output_matrix),
            ],
            axis=2,
        ),
        "y",
    ).reshape(256, 2432)
    sent = jnp.concatenate([core_first(tokens), widen(attn_routes.astype(BF))], axis=1)
    arrived = spread(after(sent, mine), "y", 4).reshape(4 * count, MODEL_WIDTH + HEAD_SIZE)
    all_w = lax.all_gather(
        after(mine, (down_before, down_after)), ("dp", "core"), axis=0, tiled=True
    )
    all_w, down_before, down_after, _ = lax.optimization_barrier(
        (all_w, down_before, down_after, arrived)
    )
    in_w, out_w = all_w[:, :1408], all_w[:, 1408:]
    low_rows = down_own.shape[0] // 2
    far_low = lax.ppermute(down_before[:low_rows], "dp", UP)
    far_high = lax.ppermute(down_after[low_rows:], "dp", DOWN)
    gate_up_own = gate_up_weight.reshape(4, 2, 64, 2816).transpose(1, 0, 2, 3).reshape(512, 2816)
    gate_up_w = lax.all_gather(after(gate_up_own, all_w), "dp", axis=0, tiled=True)
    router_m = in_w[:, 1288:1296]

    down_w = jnp.concatenate(
        [down_own, down_after, jnp.concatenate([far_low, far_high], axis=0), down_before], axis=1
    )

    def turned(columns, blocks):
        twice = jnp.concatenate([columns, columns], axis=1)
        return lax.dynamic_slice_in_dim(twice, blocks * 512, MODEL_WIDTH, axis=1)

    values = arrived[:, :MODEL_WIDTH].astype(F32)
    routes = arrived[:, MODEL_WIDTH : MODEL_WIDTH + 2].astype(jnp.int32)
    gain_a = core_first(attn_gain.astype(F32))[0]
    gain_m = core_first(mlp_gain.astype(F32))[0]
    xn1 = (values * rms_scale(values) * gain_a).astype(BF)

    ranking = priority[0]
    pick_m = pick_of(mlp_routes)
    before = (ranking[None, :] < ranking[:, None]).astype(BF)
    earlier = jnp.dot(before, jnp.sum(pick_m, axis=1).astype(BF), preferred_element_type=F32)
    slots = jnp.sum(pick_m * earlier[:, None, :], axis=-1).astype(jnp.int32)
    kept = slots < capacity
    dest = jnp.where(kept, mlp_routes * room + slots, -1)
    lanes = jnp.arange(EXPERTS * room, dtype=jnp.int32)
    to_row = (dest.T[:, :, None] == lanes[None, None, :]).astype(BF)
    any_row = to_row[0] + to_row[1]
    both_rows = to_row.reshape(2 * count, EXPERTS * room)

    def to_experts(rows):
        columns = rows.shape[1]
        return exchange(rows.reshape(EXPERTS, room, columns), ("y", "core")).reshape(
            EXPERTS * room, columns
        )

    def with_other(j):
        others = jnp.concatenate([pick_m[:, 1 - j], jnp.ones((count, 1), F32)], axis=1)
        return jnp.concatenate([cotangent, widen(others.astype(BF))], axis=1)

    grad_sent = lax.dot_general(
        both_rows,
        jnp.concatenate([with_other(0), with_other(1)], axis=0),
        ROWS,
        preferred_element_type=F32,
    ).astype(BF)
    grad_landed = to_experts(after(grad_sent, arrived))

    def places(half):
        blocks = 2 * jnp.arange(4, dtype=jnp.int32)[:, None] + half
        return (blocks * count + jnp.arange(count, dtype=jnp.int32)[None, :]).reshape(-1)

    of_sequence = lax.dynamic_slice_in_dim(segments, z * sequence, sequence).reshape(4, 2, count)

    def meta(half):
        documents = lax.dynamic_index_in_dim(of_sequence, half, 1, keepdims=False).reshape(-1)
        return jnp.stack([places(half), documents])

    key_meta = jnp.stack([meta(core), meta(1 - core)])
    row_meta = key_meta[0].T
    inverse = 10000.0 ** (-(jnp.arange(HEAD_SIZE // 2).astype(F32) * 2.0 / HEAD_SIZE))
    angle = places(core).astype(F32)[:, None] * inverse[None, :]
    cosine = jnp.tile(jnp.cos(angle), (1, 2))
    sine = jnp.concatenate([-jnp.sin(angle), jnp.sin(angle)], axis=1)

    def swapped(rows):
        return jnp.concatenate([rows[:, 64:], rows[:, :64]], axis=1)

    half = 4 * count
    projected = jnp.dot(xn1, in_w, preferred_element_type=F32)
    key_raw = projected[:, 1024:1152]
    kv_own = jnp.concatenate(
        [key_raw * cosine + swapped(key_raw) * sine, projected[:, 1152:1280]], axis=1
    ).astype(BF)
    kv_other = lax.ppermute(kv_own, "core", SWAP)
    shared = (routes, cosine, sine, row_meta, key_meta)
    query, attended, totals, gate_a, mixed = in_vmem(
        forward_kernel,
        [
            jax.ShapeDtypeStruct((4, 2 * count, HEAD_SIZE), BF),
            jax.ShapeDtypeStruct((4, 2 * count, HEAD_SIZE), F32),
            jax.ShapeDtypeStruct((4, 2 * count, 1), F32),
            jax.ShapeDtypeStruct((half, 2), F32),
            jax.ShapeDtypeStruct((half, EXPERTS * HEAD_SIZE), BF),
        ],
        [],
        6 << 28,
        projected,
        kv_own,
        kv_other,
        *shared,
    )
    branch_part = lax.dot_general(mixed, out_w, LAST, preferred_element_type=F32).astype(BF)
    branch_part = after(branch_part, grad_landed)
    grad_received = grad_landed[:, :MODEL_WIDTH]
    grad_act_raw = lax.dot_general(
        turned(grad_received, z), down_w, LAST, preferred_element_type=F32
    )
    branch = exchange(branch_part.reshape(16, quarter, MODEL_WIDTH), plane).astype(F32).sum(axis=0)

    first = x * quarter
    own_values = core_first(lax.dynamic_slice_in_dim(tokens, first, quarter)).astype(F32)
    own_factor = rms_scale(own_values)
    hidden = after(own_values, grad_act_raw) + branch
    factor_m = rms_scale(hidden)
    xn2_own = (hidden * factor_m * gain_m).astype(BF)
    xn2 = spread(xn2_own, "tensor", 4).reshape(count, MODEL_WIDTH)
    gate_m = pair_gates(jnp.dot(xn2, router_m, preferred_element_type=F32), pick_m)
    weight_m = gate_m * kept.astype(F32)

    received = to_experts(
        lax.dot_general(any_row, xn2, ROWS, preferred_element_type=F32).astype(BF)
    )
    other_pick = grad_landed[:, MODEL_WIDTH : MODEL_WIDTH + EXPERTS].astype(F32)
    valid = grad_landed[:, MODEL_WIDTH + EXPERTS : MODEL_WIDTH + EXPERTS + 1].astype(F32)
    row_logits = jnp.dot(received, router_m, preferred_element_type=F32)
    here = (jnp.arange(EXPERTS, dtype=jnp.int32) == 2 * y + core).astype(F32)
    own_logit = jnp.sum(row_logits * here[None], axis=1, keepdims=True)
    other_logit = jnp.sum(row_logits * other_pick, axis=1, keepdims=True)
    top = jnp.maximum(own_logit, other_logit)
    own_weight = jnp.exp(own_logit - top)
    row_gate = valid * own_weight / (own_weight + jnp.exp(other_logit - top))

    width = down_weight.shape[1]
    grad_expert = (row_gate * grad_received.astype(F32)).astype(BF)
    gate_up = jnp.dot(received, gate_up_w, preferred_element_type=F32)
    gate_part, up_part = gate_up[:, :width], gate_up[:, width:]
    sigmoid_gate = jax.nn.sigmoid(gate_part)
    silu_gate = gate_part * sigmoid_gate
    activated = (silu_gate * up_part).astype(BF)
    grad_act = row_gate * grad_act_raw
    grad_gate_up = jnp.concatenate(
        [
            grad_act * up_part * sigmoid_gate * (1.0 + gate_part * (1.0 - sigmoid_gate)),
            grad_act * silu_gate,
        ],
        axis=1,
    ).astype(BF)
    row_gate_grad = jnp.sum(activated.astype(F32) * grad_act_raw, axis=1, keepdims=True)
    grad_rows = lax.dot_general(grad_gate_up, gate_up_w, LAST, preferred_element_type=F32).astype(BF)
    grad_back = jnp.concatenate([grad_rows, widen(in_two(row_gate_grad))], axis=1)
    grad_back, late_grad, late_act = lax.optimization_barrier((grad_back, grad_gate_up, activated))
    grad_returned = to_experts(grad_back)
    grad_gate_up_w = lax.dot_general(
        received, late_grad, ROWS, preferred_element_type=F32
    ).astype(BF)
    gate_up_sum = lax.psum_scatter(grad_gate_up_w, "dp", scatter_dimension=0, tiled=True)
    gate_up_grad = (
        gate_up_sum.reshape(2, 4, 64, 2816)
        .transpose(1, 0, 2, 3)
        .reshape(1, 512, 2, width)
        .astype(F32)
    )
    expert_part = turned(
        jnp.dot(late_act, down_w, preferred_element_type=F32).astype(BF), lax.rem(4 - z, 4)
    )
    late_any = after(any_row, (grad_gate_up_w, expert_part))
    expert_out = sum_direct(
        jnp.stack([expert_part[:, 512 * i : 512 * (i + 1)] for i in range(4)]), "tensor"
    ).astype(BF)

    grad_xn2_part = jnp.dot(
        late_any, grad_returned[:, :MODEL_WIDTH], preferred_element_type=F32
    ).astype(BF)
    row_gate_parts = grad_returned[:, MODEL_WIDTH : MODEL_WIDTH + 2]
    gate_m_part = jnp.sum(
        jnp.einsum("jtr,rd->tjd", to_row, row_gate_parts, preferred_element_type=F32), axis=2
    )
    shares = jnp.concatenate([grad_xn2_part, widen(in_two(gate_m_part))], axis=1)
    landed = (
        exchange(shares.reshape(4, quarter, MODEL_WIDTH + HEAD_SIZE), "tensor")
        .astype(F32)
        .sum(axis=0)
    )
    landed, expert_out = lax.optimization_barrier((landed, expert_out))
    returned = to_experts(expert_out)
    grad_gate_m = (
        landed[:, MODEL_WIDTH : MODEL_WIDTH + 2] + landed[:, MODEL_WIDTH + 2 : MODEL_WIDTH + 4]
    )

    def quarter_of(array, offset=0):
        return lax.dynamic_slice_in_dim(array, first + offset, quarter)

    grad_logit_m = gate_back(quarter_of(gate_m), grad_gate_m, quarter_of(pick_m))
    grad_xn2 = landed[:, :MODEL_WIDTH] + lax.dot_general(
        grad_logit_m, router_m.astype(F32), LAST, preferred_element_type=F32
    )
    grad_norm, gain_m_part = norm_back(grad_xn2, hidden, factor_m, gain_m)
    grad_hidden = core_first(quarter_of(cotangent)).astype(F32) + grad_norm
    grad_sent_back, returned = lax.optimization_barrier((grad_hidden.astype(BF), returned))
    grad_branch = spread(grad_sent_back, plane, 16).reshape(4 * count, MODEL_WIDTH)

    fetched = jnp.einsum("jtr,rd->jtd", to_row, returned, preferred_element_type=F32)
    moe_part = jnp.sum(weight_m.T[:, :, None] * fetched, axis=0).astype(BF)
    grad_down_w = lax.dot_general(
        after(late_act, returned), grad_expert, ROWS, preferred_element_type=F32
    ).astype(BF)
    down_sum = lax.psum_scatter(grad_down_w, "dp", scatter_dimension=1, tiled=True)
    grad_branch, moe_part, _ = lax.optimization_barrier((grad_branch, moe_part, grad_down_w))
    moe_pieces = exchange(moe_part.reshape(4, quarter, MODEL_WIDTH // 4), "tensor")

    grad_mixed = jnp.dot(grad_branch, out_w, preferred_element_type=F32)
    grad_q_all, grad_logit_a, grad_kv_own, grad_kv_give = in_vmem(
        backward_kernel,
        [
            jax.ShapeDtypeStruct((half, EXPERTS * HEAD_SIZE), BF),
            jax.ShapeDtypeStruct((half, HEAD_SIZE), BF),
            jax.ShapeDtypeStruct((half, 2 * HEAD_SIZE), F32),
            jax.ShapeDtypeStruct((half, 2 * HEAD_SIZE), BF),
        ],
        [pltpu.VMEM((2, half, 2 * HEAD_SIZE), F32)],
        12 << 28,
        grad_mixed,
        query,
        kv_own,
        kv_other,
        attended,
        totals,
        gate_a,
        *shared,
    )
    out_terms = lax.dot_general(grad_branch, mixed, ROWS, preferred_element_type=F32).astype(BF)
    kv_back, out_terms, moe_pieces = lax.optimization_barrier(
        (lax.ppermute(grad_kv_give, "core", SWAP), out_terms, moe_pieces)
    )
    out_parts = core_sum(out_terms, core)
    moe = moe_pieces.transpose(1, 0, 2).reshape(quarter, MODEL_WIDTH).astype(F32)
    output_own = (core_last(hidden) + moe).astype(BF)
    own_grad_kv = grad_kv_own + kv_back.astype(F32)
    grad_key = own_grad_kv[:, :HEAD_SIZE]
    grad_kv = jnp.concatenate(
        [grad_key * cosine - swapped(grad_key) * sine, own_grad_kv[:, HEAD_SIZE:]], axis=1
    ).astype(BF)
    grad_in = jnp.concatenate([grad_q_all, grad_kv, grad_logit_a], axis=1)
    grad_xn1_part = lax.dot_general(grad_in, in_w, LAST, preferred_element_type=F32).astype(BF)
    out_right, out_left = ring_first(out_parts, "dp")
    gain_row = jnp.pad(gain_m_part[None].astype(BF), ((0, 7), (0, 0)))
    tall = jnp.concatenate([xn1, xn2_own, gain_row], axis=0)
    router_cols = jnp.pad(grad_logit_m.astype(BF), ((0, 0), (1288, 112)))
    gain_cols = (
        (jnp.arange(8)[:, None] == 0) & (jnp.arange(1408)[None, :] == 1296)
    ).astype(BF)
    grad_tall = jnp.concatenate([after(grad_in, (grad_xn1_part, out_parts, gate_up_sum)), router_cols, gain_cols], axis=0)
    in_parts = core_sum(
        lax.dot_general(tall, grad_tall, ROWS, preferred_element_type=F32).astype(BF), core
    )
    in_right, in_left = ring_first(in_parts, "dp")
    out_sum = ring_second(after(out_parts, gate_up_grad), out_right, out_left, "dp").astype(BF)
    landed_raw = exchange(grad_xn1_part.reshape(16, quarter, MODEL_WIDTH), plane)
    in_sum = ring_second(in_parts, in_right, in_left, "dp").astype(BF)
    landed_raw, in_sum, out_sum = lax.optimization_barrier((landed_raw, in_sum, out_sum))
    landed_a = landed_raw.astype(F32).sum(axis=0)
    grad_x_norm, _ = norm_back(landed_a, own_values, own_factor, gain_a)
    columns = jnp.arange(1408, dtype=jnp.int32)[None, :]
    gain_a_part = jnp.sum(
        jnp.where(columns < 1288, in_sum.astype(F32) * mine[:, :1408].astype(F32), 0.0),
        axis=1,
        keepdims=True,
    )
    small_part = jnp.where(columns[:, :128] == 17, gain_a_part, in_sum[:, 1280:].astype(F32))
    small_sent = jnp.broadcast_to(
        small_part.astype(BF).reshape(4, 1, 64, 128), (4, 4, 64, 128)
    ).reshape(16, 64, 128)
    gain_rows = lax.dynamic_slice_in_dim(attn_gain.astype(F32), z * 512 + y * 128 + core * 64, 64)

    ends = jnp.concatenate(
        [output_own, core_last((grad_hidden + grad_x_norm).astype(BF))], axis=1
    )
    ends, down_sum = lax.optimization_barrier((ends, down_sum))
    down_grad = down_sum.astype(F32)[None]
    both_ends = spread(ends, "tensor", 4)
    both_ends, small_sent = lax.optimization_barrier((both_ends, small_sent))
    small_sum = exchange(small_sent, plane).astype(F32).sum(axis=0)
    both_ends = both_ends.reshape(count, 2 * MODEL_WIDTH)
    output, input_grad = both_ends[:, :MODEL_WIDTH], both_ends[:, MODEL_WIDTH:]
    both_sums = jnp.concatenate([in_sum[:, :1280], out_sum], axis=1).reshape(4, 64, 2304)
    both_grads = heads_last(in_order(send_direct(both_sums, "y"), y))
    in_grad, out_grad = both_grads[:, :10], both_grads[:, 10:]
    query_grad, kv_grad = in_grad[:, :8], in_grad[:, 8:]
    return (
        output,
        input_grad,
        small_sum[:, 17] / gain_rows,
        small_sum[:, 16],
        small_sum[:, :8],
        kv_grad,
        query_grad,
        out_grad,
        small_sum[:, 8:16],
        gate_up_grad,
        down_grad,
    )


def solution(mesh):
    split = Mesh(mesh.devices.reshape(4, 4, 2, 4), ("dp", "y", "core", "tensor"))
    rows = ("dp", "y", "core")
    expert = ("y", "core")
    placed = (
        P(rows, None),
        P(rows, None),
        P(),
        P(),
        P(rows, None),
        P(rows, None, "tensor"),
        P(rows, None, "tensor"),
        P(rows, None, "tensor"),
        P(rows, None),
        P(expert, "dp", None, "tensor"),
        P(expert, "tensor", "dp"),
        P(rows, None),
        P(rows, None),
        P(rows, None),
        P(),
    )
    return jax.shard_map(
        body,
        mesh=split,
        in_specs=placed,
        out_specs=(
            P(rows, None),
            P(rows, None),
            P(rows),
            P(rows),
            P(rows, None),
            P(rows, None, "tensor"),
            P(rows, None, "tensor"),
            P(rows, None, "tensor"),
            P(rows, None),
            P(expert, "dp", None, "tensor"),
            P(expert, "tensor", "dp"),
        ),
        check_vma=False,
    )
```

```python
import jax
import jax.numpy as jnp
from jax import lax
from jax.experimental import pallas as pl
from jax.experimental.pallas import tpu as pltpu
from jax.sharding import Mesh
from jax.sharding import PartitionSpec as P

MODEL_WIDTH = 2048
HEAD_SIZE = 128
EXPERTS = 8
WINDOW = 1024
NORM_EPS = 1e-06
BF = jnp.bfloat16
F32 = jnp.float32
ROWS = (((0,), (0,)), ((), ()))
LAST = (((1,), (1,)), ((), ()))
UP = [(0, 1), (1, 2), (2, 3), (3, 0)]
DOWN = [(0, 3), (1, 0), (2, 1), (3, 2)]
SWAP = [(0, 1), (1, 0)]


def exchange(blocks, axis):
    return lax.all_to_all(blocks, axis, split_axis=0, concat_axis=0, tiled=True)


def spread(block, axis, count):
    return exchange(jnp.broadcast_to(block, (count, *block.shape)), axis)


def from_ahead(block, axis, steps):
    return lax.ppermute(block, axis, [(i, (i - steps) % 4) for i in range(4)])


def in_order(pieces, first):
    both = jnp.stack(pieces + pieces[:3])
    return lax.dynamic_slice_in_dim(both, lax.rem(4 - first, 4), 4)


def pick_block(blocks, index):
    return lax.dynamic_index_in_dim(blocks, lax.rem(index, 4), 0, keepdims=False)


def send_direct(blocks, axis):
    me = lax.axis_index(axis)
    return [pick_block(blocks, me)] + [
        from_ahead(pick_block(blocks, me + 4 - k), axis, k) for k in (1, 2, 3)
    ]


def heads_first(shard):
    columns = shard.shape[1] * HEAD_SIZE
    return shard.reshape(64, -1, 4, HEAD_SIZE).transpose(2, 0, 1, 3).reshape(4, 64, columns)


def after(value, other):
    return lax.optimization_barrier((value, other))[0]


def core_first(rows):
    return rows.reshape(-1, 4, 4, 2, 64).transpose(0, 1, 3, 2, 4).reshape(-1, MODEL_WIDTH)


def core_last(rows):
    return rows.reshape(-1, 4, 2, 4, 64).transpose(0, 1, 3, 2, 4).reshape(-1, MODEL_WIDTH)


def ring_first(ahead, low, high, back, axis):
    low = lax.ppermute(low, axis, UP)
    high = lax.ppermute(high, axis, DOWN)
    half = low.shape[0]
    ahead = jnp.concatenate([(ahead[:half].astype(F32) + low.astype(F32)).astype(BF), ahead[half:]])
    back = jnp.concatenate([back[:half], (back[half:].astype(F32) + high.astype(F32)).astype(BF)])
    return ahead, back


def ring_second(own, ahead, back, axis):
    return (
        own.astype(F32)
        + lax.ppermute(ahead, axis, UP).astype(F32)
        + lax.ppermute(back, axis, DOWN).astype(F32)
    )


def heads_last(blocks):
    heads = blocks.shape[2] // HEAD_SIZE
    return (
        blocks.reshape(4, 64, heads, HEAD_SIZE)
        .transpose(1, 2, 0, 3)
        .reshape(64, heads, 4 * HEAD_SIZE)
        .astype(F32)
    )


def rms_scale(values):
    return lax.rsqrt(jnp.mean(values * values, axis=-1, keepdims=True) + NORM_EPS)


def turn(heads, cosine, sine):
    first, second = heads[..., :64], heads[..., 64:]
    return jnp.concatenate([first * cosine - second * sine, second * cosine + first * sine], axis=-1)


EXTENTS = (256, 384, 512, 640)
SCALE = HEAD_SIZE**-0.5


def masked_scores(query, key, row_meta, key_meta):
    raw = lax.dot_general(query, key, LAST, preferred_element_type=F32) * SCALE
    gap = row_meta[:, 0:1] - key_meta[0:1]
    allowed = (gap >= 0) & (gap < WINDOW) & (row_meta[:, 1:2] == key_meta[1:2])
    return jnp.where(jnp.concatenate([allowed, allowed], axis=0), raw, -1e30)


def forward_kernel(proj, own, other, routes, cosine, sine, row_meta, key_meta, *outs):
    query_out, attended_out, total_out, gates_out, mixed_out = outs
    count = proj.shape[0] // 4
    for i in range(4):
        rows = pl.ds(count * i, count)
        extent = EXTENTS[i]
        logits = proj[rows, 1280:1288]
        lane = lax.broadcasted_iota(jnp.int32, (count, EXPERTS), 1)
        named = [routes[rows, 0:1], routes[rows, 1:2]]
        chosen = [jnp.sum(jnp.where(lane == n, logits, 0.0), axis=1, keepdims=True) for n in named]
        top = jnp.maximum(chosen[0], chosen[1])
        power = [jnp.exp(c - top) for c in chosen]
        gates = [p / (power[0] + power[1]) for p in power]
        gates_out[rows, 0:1] = gates[0]
        gates_out[rows, 1:2] = gates[1]
        cos, sin = cosine[rows, :], sine[rows, :]
        picked = []
        for n in named:
            q = jnp.zeros((count, HEAD_SIZE), F32)
            for e in range(EXPERTS):
                q = q + jnp.where(n == e, proj[rows, HEAD_SIZE * e : HEAD_SIZE * (e + 1)], 0.0)
            picked.append(q * cos + pltpu.roll(q, 64, 1) * sin)
        query = jnp.concatenate(picked, axis=0).astype(BF)
        query_out[i] = query
        halves = (own, other)
        scores = [
            masked_scores(
                query, h[:extent, :HEAD_SIZE], row_meta[rows, :], key_meta[k, :, :extent]
            )
            for k, h in enumerate(halves)
        ]
        row_max = jnp.maximum(
            jnp.max(scores[0], axis=1, keepdims=True), jnp.max(scores[1], axis=1, keepdims=True)
        )
        weights = [jnp.exp(s - row_max) for s in scores]
        total = jnp.sum(weights[0], axis=1, keepdims=True) + jnp.sum(weights[1], axis=1, keepdims=True)
        inverse = 1.0 / total
        attended = sum(
            jnp.dot((w * inverse).astype(BF), h[:extent, HEAD_SIZE:], preferred_element_type=F32)
            for w, h in zip(weights, halves)
        )
        attended_out[i] = attended
        total_out[i] = row_max + jnp.log(total)
        for e in range(EXPERTS):
            mixed_out[rows, HEAD_SIZE * e : HEAD_SIZE * (e + 1)] = (
                jnp.where(named[0] == e, gates[0], 0.0) * attended[:count]
                + jnp.where(named[1] == e, gates[1], 0.0) * attended[count:]
            ).astype(BF)


def backward_kernel(
    grad_mixed, query_in, own, other, attended_in, total_in, gates_in, routes, cosine, sine, row_meta, key_meta, *outs
):
    grad_query_out, grad_logit_out, grad_own_out, grad_other_out, sums = outs
    count = grad_mixed.shape[0] // 4
    sums[...] = jnp.zeros_like(sums)
    for i in range(4):
        rows = pl.ds(count * i, count)
        extent = EXTENTS[i]
        named = [routes[rows, 0:1], routes[rows, 1:2]]
        gates = [gates_in[rows, 0:1], gates_in[rows, 1:2]]
        cos, sin = cosine[rows, :], sine[rows, :]
        attended = attended_in[i]
        picked = []
        for n in named:
            g = jnp.zeros((count, HEAD_SIZE), F32)
            for e in range(EXPERTS):
                g = g + jnp.where(n == e, grad_mixed[rows, HEAD_SIZE * e : HEAD_SIZE * (e + 1)], 0.0)
            picked.append(g)
        gate_grads = [
            jnp.sum(p * attended[count * j : count * (j + 1)], axis=1, keepdims=True)
            for j, p in enumerate(picked)
        ]
        level = gates[0] * gate_grads[0] + gates[1] * gate_grads[1]
        lane = lax.broadcasted_iota(jnp.int32, (count, HEAD_SIZE), 1)
        grad_logit_out[rows, :] = sum(
            jnp.where(lane == n, g * (d - level), 0.0) for n, g, d in zip(named, gates, gate_grads)
        ).astype(BF)
        grad_attended = jnp.concatenate(
            [gates[0] * picked[0], gates[1] * picked[1]], axis=0
        ).astype(BF)
        query = query_in[i]
        total = total_in[i]
        probs, grad_probs = [], []
        delta = jnp.zeros((2 * count, 1), F32)
        for k, h in enumerate((own, other)):
            score = masked_scores(
                query, h[:extent, :HEAD_SIZE], row_meta[rows, :], key_meta[k, :, :extent]
            )
            prob = jnp.exp(score - total)
            grad_prob = lax.dot_general(
                grad_attended, h[:extent, HEAD_SIZE:], LAST, preferred_element_type=F32
            )
            delta = delta + jnp.sum(prob * grad_prob, axis=1, keepdims=True)
            probs.append(prob)
            grad_probs.append(grad_prob)
        grad_query = jnp.zeros((2 * count, HEAD_SIZE), F32)
        for k, h in enumerate((own, other)):
            grad_score = (probs[k] * (grad_probs[k] - delta)).astype(BF)
            grad_query = grad_query + jnp.dot(
                grad_score, h[:extent, :HEAD_SIZE], preferred_element_type=F32
            )
            sums[k, :extent, :HEAD_SIZE] += (
                lax.dot_general(grad_score, query, ROWS, preferred_element_type=F32) * SCALE
            )
            sums[k, :extent, HEAD_SIZE:] += lax.dot_general(
                probs[k].astype(BF), grad_attended, ROWS, preferred_element_type=F32
            )
        grad_query = grad_query * SCALE
        turned = [
            g * cos - pltpu.roll(g, 64, 1) * sin for g in (grad_query[:count], grad_query[count:])
        ]
        for e in range(EXPERTS):
            grad_query_out[rows, HEAD_SIZE * e : HEAD_SIZE * (e + 1)] = (
                jnp.where(named[0] == e, turned[0], 0.0) + jnp.where(named[1] == e, turned[1], 0.0)
            ).astype(BF)
    grad_own_out[...] = sums[0]
    grad_other_out[...] = sums[1].astype(BF)


def in_vmem(kernel, outs, scratch, flops, *args):
    spec = pl.BlockSpec(memory_space=pltpu.VMEM)
    moved = sum(a.size * a.dtype.itemsize for a in args)
    return pl.pallas_call(
        kernel,
        out_shape=outs,
        in_specs=[spec] * len(args),
        out_specs=[spec] * len(outs),
        scratch_shapes=scratch,
        compiler_params=pltpu.CompilerParams(vmem_limit_bytes=40 * 1024 * 1024),
        cost_estimate=pl.CostEstimate(flops=flops, bytes_accessed=moved, transcendentals=1 << 20),
    )(*args)


FREE = pl.CostEstimate(flops=0, bytes_accessed=0, transcendentals=0)


def on_grid(kernel, scalars, grid, in_specs, out_specs, outs, scratch, *args, cost=FREE):
    return pl.pallas_call(
        kernel,
        out_shape=outs,
        grid_spec=pltpu.PrefetchScalarGridSpec(
            num_scalar_prefetch=1,
            grid=grid,
            in_specs=in_specs,
            out_specs=out_specs,
            scratch_shapes=scratch,
        ),
        compiler_params=pltpu.CompilerParams(vmem_limit_bytes=48 * 1024 * 1024),
        cost_estimate=cost,
    )(jnp.stack(scalars).astype(jnp.int32), *args)


def give_terms(tall, terms, place, core):
    depth, columns = terms.shape

    def kernel(at, left, right, out):
        out[0] = lax.dot_general(left[...], right[...], ROWS, preferred_element_type=F32).astype(BF)

    return on_grid(
        kernel,
        (place, core),
        (4,),
        [
            pl.BlockSpec((depth, 256), lambda i, at: (0, 2 * i + 1 - at[1])),
            pl.BlockSpec((depth, columns), lambda i, at: (0, 0)),
        ],
        pl.BlockSpec((1, 256, columns), lambda i, at: (i, 0, 0)),
        jax.ShapeDtypeStruct((4, 256, columns), BF),
        [],
        tall,
        terms,
    )


def keep_terms(tall, terms, landed, place, core):
    depth, columns = terms.shape

    def kernel(at, left, right, more, own, ahead, low, high, back):
        total = lax.dot_general(left[...], right[...], ROWS, preferred_element_type=F32).astype(
            BF
        ).astype(F32) + more[0].astype(F32)
        total = total.astype(BF)
        step = pl.program_id(0)

        @pl.when(step == 0)
        def _():
            own[...] = total

        @pl.when(step == 1)
        def _():
            ahead[...] = total

        @pl.when(step == 2)
        def _():
            low[...] = total[:128]
            high[...] = total[128:]

        @pl.when(step == 3)
        def _():
            back[...] = total

    def whole(rows):
        return pl.BlockSpec((rows, columns), lambda i, at: (0, 0))

    return on_grid(
        kernel,
        (place, core),
        (4,),
        [
            pl.BlockSpec((depth, 256), lambda i, at: (0, 2 * lax.rem(at[0] + i, 4) + at[1])),
            whole(depth),
            pl.BlockSpec((1, 256, columns), lambda i, at: (lax.rem(at[0] + i, 4), 0, 0)),
        ],
        [whole(256), whole(256), whole(128), whole(128), whole(256)],
        [jax.ShapeDtypeStruct((r, columns), BF) for r in (256, 256, 128, 128, 256)],
        [],
        tall,
        terms,
        landed,
    )


def gate_up_product(rows, pair):
    def kernel(at, left, right, out):
        out[...] = lax.dot_general(left[...], right[0], ROWS, preferred_element_type=F32).astype(BF)

    depth, width = pair.shape[1:]
    return on_grid(
        kernel,
        (jnp.int32(0),),
        (2, 8),
        [
            pl.BlockSpec((depth, 256), lambda h, i, at: (0, i)),
            pl.BlockSpec((1, depth, width), lambda h, i, at: (h, 0, 0)),
        ],
        pl.BlockSpec((256, width), lambda h, i, at: (i, h)),
        jax.ShapeDtypeStruct((MODEL_WIDTH, 2 * width), BF),
        [],
        rows,
        pair,
    )


def down_product(activated, grads, gate):
    def kernel(at, left, right, scale, out):
        scaled = (scale[...] * right[...].astype(F32)).astype(BF)
        out[...] = lax.dot_general(left[...], scaled, ROWS, preferred_element_type=F32).astype(BF)

    depth, width = activated.shape
    return on_grid(
        kernel,
        (jnp.int32(0),),
        (4,),
        [
            pl.BlockSpec((depth, width), lambda i, at: (0, 0)),
            pl.BlockSpec((depth, 512), lambda i, at: (0, i)),
            pl.BlockSpec((depth, 1), lambda i, at: (0, 0)),
        ],
        pl.BlockSpec((width, 512), lambda i, at: (0, i)),
        jax.ShapeDtypeStruct((width, MODEL_WIDTH), BF),
        [],
        activated,
        grads,
        gate,
    )


def down_back(grads, down_w):
    def kernel(at, left, right, out):
        out[...] = lax.dot_general(left[...], right[...], LAST, preferred_element_type=F32)

    depth, width = grads.shape[0], down_w.shape[0]
    return on_grid(
        kernel,
        (jnp.int32(0),),
        (width // 128,),
        [
            pl.BlockSpec((depth, MODEL_WIDTH), lambda i, at: (0, 0)),
            pl.BlockSpec((128, MODEL_WIDTH), lambda i, at: (i, 0)),
        ],
        pl.BlockSpec((depth, 128), lambda i, at: (0, i)),
        jax.ShapeDtypeStruct((depth, width), F32),
        [],
        grads,
        down_w,
    )


def expert_quarters(activated, down_w, place, x):
    def kernel(at, left, right, out):
        out[0] = jnp.dot(left[...], right[...], preferred_element_type=F32).astype(BF)

    depth, width = activated.shape
    return on_grid(
        kernel,
        (place, x),
        (4,),
        [
            pl.BlockSpec((depth, width), lambda i, at: (0, 0)),
            pl.BlockSpec((width, 512), lambda i, at: (0, i)),
        ],
        pl.BlockSpec((1, depth, 512), lambda i, at: (lax.rem(at[0] + i + 4 - at[1], 4), 0, 0)),
        jax.ShapeDtypeStruct((4, depth, 512), BF),
        [],
        activated,
        down_w,
    )


def expert_middle(rows, marks, router, gate_up_w, grad_act, expert):
    depth, width = grad_act.shape
    blocks = width // 128

    def kernel(
        at, rows_ref, marks_ref, router_ref, gate_ref, up_ref, flat_ref, grad_ref,
        act_out, pair_out, gate_out, back_out, pair_all, row_gate, row_grad,
    ):
        step = pl.program_id(0)
        lane = lax.broadcasted_iota(jnp.int32, (depth, 128), 1)

        @pl.when(step == 0)
        def _():
            logits = jnp.dot(rows_ref[...], router_ref[...], preferred_element_type=F32)
            marks_f = marks_ref[...].astype(F32)
            own = jnp.sum(jnp.where(lane == at[0], logits, 0.0), axis=1, keepdims=True)
            other = jnp.sum(jnp.where(lane < 8, logits * marks_f, 0.0), axis=1, keepdims=True)
            valid = jnp.sum(jnp.where(lane == 8, marks_f, 0.0), axis=1, keepdims=True)
            top = jnp.maximum(own, other)
            power = jnp.exp(own - top)
            row_gate[...] = valid * power / (power + jnp.exp(other - top))
            gate_out[...] = row_gate[...]
            row_grad[...] = jnp.zeros_like(row_grad)

        @pl.when(step < blocks)
        def _():
            both = jnp.concatenate([gate_ref[...], up_ref[...]], axis=1)
            gate_up = jnp.dot(rows_ref[...], both, preferred_element_type=F32)
            gate, up = gate_up[:, :128], gate_up[:, 128:]
            sigmoid = 1.0 / (1.0 + jnp.exp(-gate))
            silu = gate * sigmoid
            act = (silu * up).astype(BF)
            raw = grad_ref[...]
            grad = row_gate[...] * raw
            grad_gate = (grad * up * sigmoid * (1.0 + gate * (1.0 - sigmoid))).astype(BF)
            grad_up = (grad * silu).astype(BF)
            act_out[...] = act
            pair_out[0] = grad_gate
            pair_out[1] = grad_up
            at_lane = pl.multiple_of(step * 128, 128)
            pair_all[:, pl.ds(at_lane, 128)] = grad_gate
            pair_all[:, pl.ds(at_lane + width, 128)] = grad_up
            row_grad[...] += jnp.sum(act.astype(F32) * raw, axis=1, keepdims=True)

        @pl.when(step >= blocks)
        def _():
            back_out[...] = lax.dot_general(
                pair_all[...], flat_ref[...], LAST, preferred_element_type=F32
            ).astype(BF)

        @pl.when(step == blocks + 4)
        def _():
            high = row_grad[...].astype(BF).astype(F32)
            low = row_grad[...] - high
            wide = lax.broadcasted_iota(jnp.int32, (depth, 512), 1)
            back_out[...] = jnp.where(wide == 0, high, jnp.where(wide == 1, low, 0.0)).astype(BF)

    def first(i):
        return jnp.minimum(i, blocks - 1)

    def second(i):
        return jnp.clip(i - blocks, 0, 3)

    return on_grid(
        kernel,
        (expert,),
        (blocks + 5,),
        [
            pl.BlockSpec((depth, MODEL_WIDTH), lambda i, at: (0, 0)),
            pl.BlockSpec((depth, 128), lambda i, at: (0, 0)),
            pl.BlockSpec((MODEL_WIDTH, 128), lambda i, at: (0, 0)),
            pl.BlockSpec((MODEL_WIDTH, 128), lambda i, at: (0, first(i))),
            pl.BlockSpec((MODEL_WIDTH, 128), lambda i, at: (0, blocks + first(i))),
            pl.BlockSpec((512, 2 * width), lambda i, at: (second(i), 0)),
            pl.BlockSpec((depth, 128), lambda i, at: (0, first(i))),
        ],
        [
            pl.BlockSpec((depth, 128), lambda i, at: (0, first(i))),
            pl.BlockSpec((2, depth, 128), lambda i, at: (0, 0, first(i))),
            pl.BlockSpec((depth, 1), lambda i, at: (0, 0)),
            pl.BlockSpec((depth, 512), lambda i, at: (0, jnp.clip(i - blocks, 0, 4))),
        ],
        [
            jax.ShapeDtypeStruct((depth, width), BF),
            jax.ShapeDtypeStruct((2, depth, width), BF),
            jax.ShapeDtypeStruct((depth, 1), F32),
            jax.ShapeDtypeStruct((depth, MODEL_WIDTH + 512), BF),
        ],
        [
            pltpu.VMEM((depth, 2 * width), BF),
            pltpu.VMEM((depth, 1), F32),
            pltpu.VMEM((depth, 1), F32),
        ],
        rows,
        marks,
        router,
        gate_up_w,
        gate_up_w,
        gate_up_w,
        grad_act,
        cost=pl.CostEstimate(
            flops=8 * depth * MODEL_WIDTH * width, bytes_accessed=1 << 24, transcendentals=1 << 20
        ),
    )


def pick_of(routes):
    return (routes[:, :, None] == jnp.arange(EXPERTS, dtype=jnp.int32)[None, None, :]).astype(F32)


def pair_gates(logits, pick):
    chosen = jnp.sum(logits[:, None, :] * pick, axis=-1)
    weights = jnp.exp(chosen - jnp.max(chosen, axis=1, keepdims=True))
    return weights / jnp.sum(weights, axis=1, keepdims=True)


def gate_back(gates, grad_gates, pick):
    inner = gates * (grad_gates - jnp.sum(gates * grad_gates, axis=1, keepdims=True))
    return jnp.sum(inner[:, :, None] * pick, axis=1)


def norm_back(grad_normed, values, factor, gain):
    gain_part = jnp.sum(grad_normed * values * factor, axis=0)
    inner = grad_normed * gain
    grad_values = factor * inner - values * factor * factor * factor * jnp.mean(
        inner * values, axis=-1, keepdims=True
    )
    return grad_values, gain_part


def in_two(values):
    high = values.astype(BF)
    low = (values - high.astype(F32)).astype(BF)
    return jnp.concatenate([high, low], axis=1)


def widen(columns):
    return jnp.pad(columns, ((0, 0), (0, HEAD_SIZE - columns.shape[1])))


def body(
    tokens,
    cotangent,
    attn_gain,
    mlp_gain,
    attn_router,
    key_value_weight,
    query_matrix,
    output_matrix,
    mlp_router,
    gate_up_weight,
    down_weight,
    attn_routes,
    mlp_routes,
    priority,
    segments,
):
    z, y = lax.axis_index("dp"), lax.axis_index("y")
    core, x = lax.axis_index("core"), lax.axis_index("tensor")
    count = tokens.shape[0]
    quarter = count // 4
    capacity = 50
    room = 56
    sequence = 8 * count
    plane = ("y", "tensor")

    routers_own = jnp.concatenate([attn_router, mlp_router], axis=1)
    in_own = jnp.concatenate([query_matrix, key_value_weight], axis=1)
    down_own = down_weight[0]
    down_before = lax.ppermute(down_own, "dp", UP)
    down_after = lax.ppermute(down_own, "dp", DOWN)
    mine = exchange(
        jnp.concatenate(
            [
                heads_first(in_own),
                jnp.broadcast_to(widen(routers_own), (4, 64, HEAD_SIZE)),
                heads_first(output_matrix),
            ],
            axis=2,
        ),
        "y",
    ).reshape(256, 2432)
    sent = jnp.concatenate([core_first(tokens), widen(attn_routes.astype(BF))], axis=1)
    arrived = spread(after(sent, mine), "y", 4).reshape(4 * count, MODEL_WIDTH + HEAD_SIZE)
    all_w = lax.all_gather(
        after(mine, (down_before, down_after)), ("dp", "core"), axis=0, tiled=True
    )
    def turned(columns, blocks):
        twice = jnp.concatenate([columns, columns], axis=1)
        return lax.dynamic_slice_in_dim(twice, blocks * 512, MODEL_WIDTH, axis=1)

    values = arrived[:, :MODEL_WIDTH].astype(F32)
    routes = arrived[:, MODEL_WIDTH : MODEL_WIDTH + 2].astype(jnp.int32)
    gain_a = core_first(attn_gain.astype(F32))[0]
    gain_m = core_first(mlp_gain.astype(F32))[0]
    xn1 = (values * rms_scale(values) * gain_a).astype(BF)

    ranking = priority[0]
    pick_m = pick_of(mlp_routes)
    before = (ranking[None, :] < ranking[:, None]).astype(BF)
    earlier = jnp.dot(before, jnp.sum(pick_m, axis=1).astype(BF), preferred_element_type=F32)
    slots = jnp.sum(pick_m * earlier[:, None, :], axis=-1).astype(jnp.int32)
    kept = slots < capacity
    dest = jnp.where(kept, mlp_routes * room + slots, -1)
    lanes = jnp.arange(EXPERTS * room, dtype=jnp.int32)
    to_row = (dest.T[:, :, None] == lanes[None, None, :]).astype(BF)
    any_row = to_row[0] + to_row[1]
    both_rows = to_row.reshape(2 * count, EXPERTS * room)

    def to_experts(rows):
        columns = rows.shape[1]
        return exchange(rows.reshape(EXPERTS, room, columns), ("y", "core")).reshape(
            EXPERTS * room, columns
        )

    def with_other(j):
        others = jnp.concatenate([pick_m[:, 1 - j], jnp.ones((count, 1), F32)], axis=1)
        return jnp.concatenate([cotangent, widen(others.astype(BF))], axis=1)

    grad_sent = lax.dot_general(
        both_rows,
        jnp.concatenate([with_other(0), with_other(1)], axis=0),
        ROWS,
        preferred_element_type=F32,
    ).astype(BF)
    all_w, down_before, down_after, xn1, grad_sent = lax.optimization_barrier(
        (all_w, down_before, down_after, xn1, grad_sent)
    )
    in_w, out_w = all_w[:, :1408], all_w[:, 1408:]
    low_rows = down_own.shape[0] // 2
    far_low = lax.ppermute(down_before[:low_rows], "dp", UP)
    far_high = lax.ppermute(down_after[low_rows:], "dp", DOWN)
    gate_up_own = gate_up_weight.reshape(4, 2, 64, 2816).transpose(1, 0, 2, 3).reshape(512, 2816)
    gate_up_w = lax.all_gather(after(gate_up_own, all_w), "dp", axis=0, tiled=True)
    router_m = in_w[:, 1288:1296]

    down_w = jnp.concatenate(
        [down_own, down_after, jnp.concatenate([far_low, far_high], axis=0), down_before], axis=1
    )

    grad_landed = to_experts(grad_sent)

    def places(half):
        blocks = 2 * jnp.arange(4, dtype=jnp.int32)[:, None] + half
        return (blocks * count + jnp.arange(count, dtype=jnp.int32)[None, :]).reshape(-1)

    of_sequence = lax.dynamic_slice_in_dim(segments, z * sequence, sequence).reshape(4, 2, count)

    def meta(half):
        documents = lax.dynamic_index_in_dim(of_sequence, half, 1, keepdims=False).reshape(-1)
        return jnp.stack([places(half), documents])

    key_meta = jnp.stack([meta(core), meta(1 - core)])
    row_meta = key_meta[0].T
    inverse = 10000.0 ** (-(jnp.arange(HEAD_SIZE // 2).astype(F32) * 2.0 / HEAD_SIZE))
    angle = places(core).astype(F32)[:, None] * inverse[None, :]
    cosine = jnp.tile(jnp.cos(angle), (1, 2))
    sine = jnp.concatenate([-jnp.sin(angle), jnp.sin(angle)], axis=1)

    def swapped(rows):
        return jnp.concatenate([rows[:, 64:], rows[:, :64]], axis=1)

    half = 4 * count
    projected = jnp.dot(xn1, in_w, preferred_element_type=F32)
    key_raw = projected[:, 1024:1152]
    kv_own = jnp.concatenate(
        [key_raw * cosine + swapped(key_raw) * sine, projected[:, 1152:1280]], axis=1
    ).astype(BF)
    kv_other = lax.ppermute(kv_own, "core", SWAP)
    shared = (routes, cosine, sine, row_meta, key_meta)
    query, attended, totals, gate_a, mixed = in_vmem(
        forward_kernel,
        [
            jax.ShapeDtypeStruct((4, 2 * count, HEAD_SIZE), BF),
            jax.ShapeDtypeStruct((4, 2 * count, HEAD_SIZE), F32),
            jax.ShapeDtypeStruct((4, 2 * count, 1), F32),
            jax.ShapeDtypeStruct((half, 2), F32),
            jax.ShapeDtypeStruct((half, EXPERTS * HEAD_SIZE), BF),
        ],
        [],
        6 << 28,
        projected,
        kv_own,
        kv_other,
        *shared,
    )
    branch_part = lax.dot_general(mixed, out_w, LAST, preferred_element_type=F32).astype(BF)
    branch_part = after(branch_part, grad_landed)
    grad_received = grad_landed[:, :MODEL_WIDTH]
    grad_turned = turned(grad_received, z)
    branch = exchange(branch_part.reshape(16, quarter, MODEL_WIDTH), plane).astype(F32).sum(axis=0)

    first = x * quarter
    own_values = core_first(lax.dynamic_slice_in_dim(tokens, first, quarter)).astype(F32)
    own_factor = rms_scale(own_values)
    hidden = after(own_values, (down_w, grad_turned)) + branch
    factor_m = rms_scale(hidden)
    xn2_own = (hidden * factor_m * gain_m).astype(BF)
    xn2 = spread(xn2_own, "tensor", 4).reshape(count, MODEL_WIDTH)
    gate_m = pair_gates(jnp.dot(xn2, router_m, preferred_element_type=F32), pick_m)
    weight_m = gate_m * kept.astype(F32)

    received = to_experts(
        lax.dot_general(any_row, xn2, ROWS, preferred_element_type=F32).astype(BF)
    )
    grad_act_raw = down_back(grad_turned, down_w)
    received, grad_act_raw = lax.optimization_barrier((received, grad_act_raw))
    activated, grad_pair, row_gate, grad_back = expert_middle(
        received,
        grad_landed[:, MODEL_WIDTH:],
        jnp.pad(router_m, ((0, 0), (0, 120))),
        gate_up_w,
        grad_act_raw,
        2 * y + core,
    )
    grad_back, late_pair, late_act = lax.optimization_barrier((grad_back, grad_pair, activated))
    grad_returned = to_experts(grad_back[:, : MODEL_WIDTH + HEAD_SIZE])
    grad_gate_up_w = gate_up_product(received, late_pair)
    gate_up_sum = lax.psum_scatter(grad_gate_up_w, "dp", scatter_dimension=0, tiled=True)
    width = down_own.shape[0]
    quarters = expert_quarters(late_act, down_w, z, x)
    late_any = after(any_row, (grad_gate_up_w, quarters))
    expert_out = (
        quarters[0].astype(F32)
        + sum(from_ahead(quarters[4 - k], "tensor", k).astype(F32) for k in (1, 2, 3))
    ).astype(BF)

    grad_xn2_part = jnp.dot(
        late_any, grad_returned[:, :MODEL_WIDTH], preferred_element_type=F32
    ).astype(BF)
    row_gate_parts = grad_returned[:, MODEL_WIDTH : MODEL_WIDTH + 2]
    gate_m_part = jnp.sum(
        jnp.einsum("jtr,rd->tjd", to_row, row_gate_parts, preferred_element_type=F32), axis=2
    )
    shares = jnp.concatenate([grad_xn2_part, widen(in_two(gate_m_part))], axis=1)
    landed = (
        exchange(shares.reshape(4, quarter, MODEL_WIDTH + HEAD_SIZE), "tensor")
        .astype(F32)
        .sum(axis=0)
    )
    landed, expert_out = lax.optimization_barrier((landed, expert_out))
    returned = to_experts(expert_out)
    grad_gate_m = (
        landed[:, MODEL_WIDTH : MODEL_WIDTH + 2] + landed[:, MODEL_WIDTH + 2 : MODEL_WIDTH + 4]
    )

    def quarter_of(array, offset=0):
        return lax.dynamic_slice_in_dim(array, first + offset, quarter)

    grad_logit_m = gate_back(quarter_of(gate_m), grad_gate_m, quarter_of(pick_m))
    grad_xn2 = landed[:, :MODEL_WIDTH] + lax.dot_general(
        grad_logit_m, router_m.astype(F32), LAST, preferred_element_type=F32
    )
    grad_norm, gain_m_part = norm_back(grad_xn2, hidden, factor_m, gain_m)
    grad_hidden = core_first(quarter_of(cotangent)).astype(F32) + grad_norm
    grad_sent_back, returned = lax.optimization_barrier((grad_hidden.astype(BF), returned))
    grad_branch = spread(grad_sent_back, plane, 16).reshape(4 * count, MODEL_WIDTH)

    fetched = jnp.einsum("jtr,rd->jtd", to_row, returned, preferred_element_type=F32)
    moe_part = jnp.sum(weight_m.T[:, :, None] * fetched, axis=0).astype(BF)
    grad_down_w = down_product(after(late_act, returned), grad_received, row_gate)
    down_sum = lax.psum_scatter(grad_down_w, "dp", scatter_dimension=1, tiled=True)
    grad_branch, moe_part, _ = lax.optimization_barrier((grad_branch, moe_part, grad_down_w))
    moe_pieces = exchange(moe_part.reshape(4, quarter, MODEL_WIDTH // 4), "tensor")

    grad_mixed = jnp.dot(grad_branch, out_w, preferred_element_type=F32)
    grad_q_all, grad_logit_a, grad_kv_own, grad_kv_give = in_vmem(
        backward_kernel,
        [
            jax.ShapeDtypeStruct((half, EXPERTS * HEAD_SIZE), BF),
            jax.ShapeDtypeStruct((half, HEAD_SIZE), BF),
            jax.ShapeDtypeStruct((half, 2 * HEAD_SIZE), F32),
            jax.ShapeDtypeStruct((half, 2 * HEAD_SIZE), BF),
        ],
        [pltpu.VMEM((2, half, 2 * HEAD_SIZE), F32)],
        12 << 28,
        grad_mixed,
        query,
        kv_own,
        kv_other,
        attended,
        totals,
        gate_a,
        *shared,
    )
    out_give = lax.ppermute(give_terms(grad_branch, mixed, z, core), "core", SWAP)
    kv_back, moe_pieces = lax.optimization_barrier(
        (lax.ppermute(grad_kv_give, "core", SWAP), moe_pieces)
    )
    moe = moe_pieces.transpose(1, 0, 2).reshape(quarter, MODEL_WIDTH).astype(F32)
    output_own = (core_last(hidden) + moe).astype(BF)
    own_grad_kv = grad_kv_own + kv_back.astype(F32)
    grad_key = own_grad_kv[:, :HEAD_SIZE]
    grad_kv = jnp.concatenate(
        [grad_key * cosine - swapped(grad_key) * sine, own_grad_kv[:, HEAD_SIZE:]], axis=1
    ).astype(BF)
    grad_in = jnp.concatenate([grad_q_all, grad_kv, grad_logit_a], axis=1)
    grad_xn1_part = lax.dot_general(grad_in, in_w, LAST, preferred_element_type=F32).astype(BF)
    gain_row = jnp.pad(gain_m_part[None].astype(BF), ((0, 7), (0, 0)))
    tall = jnp.concatenate([xn1, xn2_own, gain_row], axis=0)
    router_cols = jnp.pad(grad_logit_m.astype(BF), ((0, 0), (1288, 112)))
    gain_cols = (
        (jnp.arange(8)[:, None] == 0) & (jnp.arange(1408)[None, :] == 1296)
    ).astype(BF)
    grad_tall = jnp.concatenate([grad_in, router_cols, gain_cols], axis=0)
    in_give = lax.ppermute(give_terms(tall, grad_tall, z, core), "core", SWAP)
    out_own, *out_rest = keep_terms(grad_branch, mixed, out_give, z, core)
    out_ahead, out_back = ring_first(*out_rest, "dp")
    in_own_rows, *in_rest = keep_terms(
        tall, grad_tall, after(in_give, out_own), z, core
    )
    in_ahead, in_back = ring_first(*in_rest, "dp")
    out_sum = ring_second(out_own, out_ahead, out_back, "dp").astype(BF)
    in_sum = ring_second(in_own_rows, in_ahead, in_back, "dp").astype(BF)
    landed_raw = exchange(grad_xn1_part.reshape(16, quarter, MODEL_WIDTH), plane)
    landed_raw, in_sum, out_sum = lax.optimization_barrier((landed_raw, in_sum, out_sum))
    landed_a = landed_raw.astype(F32).sum(axis=0)
    grad_x_norm, _ = norm_back(landed_a, own_values, own_factor, gain_a)
    columns = jnp.arange(1408, dtype=jnp.int32)[None, :]
    gain_a_part = jnp.sum(
        jnp.where(columns < 1288, in_sum.astype(F32) * mine[:, :1408].astype(F32), 0.0),
        axis=1,
        keepdims=True,
    )
    small_part = jnp.where(columns[:, :128] == 17, gain_a_part, in_sum[:, 1280:].astype(F32))
    small_sent = jnp.broadcast_to(
        small_part.astype(BF).reshape(4, 1, 64, 128), (4, 4, 64, 128)
    ).reshape(16, 64, 128)
    gain_rows = lax.dynamic_slice_in_dim(attn_gain.astype(F32), z * 512 + y * 128 + core * 64, 64)

    ends = jnp.concatenate(
        [output_own, core_last((grad_hidden + grad_x_norm).astype(BF))], axis=1
    )
    ends, gate_up_sum, small_raw = lax.optimization_barrier(
        (ends, gate_up_sum, exchange(small_sent, plane))
    )
    gate_up_grad = (
        gate_up_sum.reshape(2, 4, 64, 2816)
        .transpose(1, 0, 2, 3)
        .reshape(1, 512, 2, width)
        .astype(F32)
    )
    small_sum = small_raw.astype(F32).sum(axis=0)
    both_ends, down_sum = lax.optimization_barrier((spread(ends, "tensor", 4), down_sum))
    down_grad = down_sum.astype(F32)[None]
    both_ends = both_ends.reshape(count, 2 * MODEL_WIDTH)
    output, input_grad = both_ends[:, :MODEL_WIDTH], both_ends[:, MODEL_WIDTH:]
    both_sums = jnp.concatenate([in_sum[:, :1280], out_sum], axis=1).reshape(4, 64, 2304)
    both_grads = heads_last(in_order(send_direct(both_sums, "y"), y))
    in_grad, out_grad = both_grads[:, :10], both_grads[:, 10:]
    query_grad, kv_grad = in_grad[:, :8], in_grad[:, 8:]
    return (
        output,
        input_grad,
        small_sum[:, 17] / gain_rows,
        small_sum[:, 16],
        small_sum[:, :8],
        kv_grad,
        query_grad,
        out_grad,
        small_sum[:, 8:16],
        gate_up_grad,
        down_grad,
    )


def solution(mesh):
    split = Mesh(mesh.devices.reshape(4, 4, 2, 4), ("dp", "y", "core", "tensor"))
    rows = ("dp", "y", "core")
    expert = ("y", "core")
    placed = (
        P(rows, None),
        P(rows, None),
        P(),
        P(),
        P(rows, None),
        P(rows, None, "tensor"),
        P(rows, None, "tensor"),
        P(rows, None, "tensor"),
        P(rows, None),
        P(expert, "dp", None, "tensor"),
        P(expert, "tensor", "dp"),
        P(rows, None),
        P(rows, None),
        P(rows, None),
        P(),
    )
    return jax.shard_map(
        body,
        mesh=split,
        in_specs=placed,
        out_specs=(
            P(rows, None),
            P(rows, None),
            P(rows),
            P(rows),
            P(rows, None),
            P(rows, None, "tensor"),
            P(rows, None, "tensor"),
            P(rows, None, "tensor"),
            P(rows, None),
            P(expert, "dp", None, "tensor"),
            P(expert, "tensor", "dp"),
        ),
        check_vma=False,
    )
```

```python
import jax
import jax.numpy as jnp
from jax import lax
from jax.experimental import pallas as pl
from jax.experimental.pallas import tpu as pltpu
from jax.sharding import Mesh
from jax.sharding import PartitionSpec as P

MODEL_WIDTH = 2048
HEAD_SIZE = 128
EXPERTS = 8
WINDOW = 1024
NORM_EPS = 1e-06
BF = jnp.bfloat16
F32 = jnp.float32
ROWS = (((0,), (0,)), ((), ()))
LAST = (((1,), (1,)), ((), ()))
UP = [(0, 1), (1, 2), (2, 3), (3, 0)]
DOWN = [(0, 3), (1, 0), (2, 1), (3, 2)]
SWAP = [(0, 1), (1, 0)]


def exchange(blocks, axis):
    return lax.all_to_all(blocks, axis, split_axis=0, concat_axis=0, tiled=True)


def spread(block, axis, count):
    return exchange(jnp.broadcast_to(block, (count, *block.shape)), axis)


def from_ahead(block, axis, steps):
    return lax.ppermute(block, axis, [(i, (i - steps) % 4) for i in range(4)])


def in_order(pieces, first):
    both = jnp.stack(pieces + pieces[:3])
    return lax.dynamic_slice_in_dim(both, lax.rem(4 - first, 4), 4)


def pick_block(blocks, index):
    return lax.dynamic_index_in_dim(blocks, lax.rem(index, 4), 0, keepdims=False)


def send_direct(blocks, axis):
    me = lax.axis_index(axis)
    return [pick_block(blocks, me)] + [
        from_ahead(pick_block(blocks, me + 4 - k), axis, k) for k in (1, 2, 3)
    ]


def heads_first(shard):
    columns = shard.shape[1] * HEAD_SIZE
    return shard.reshape(64, -1, 4, HEAD_SIZE).transpose(2, 0, 1, 3).reshape(4, 64, columns)


def after(value, other):
    return lax.optimization_barrier((value, other))[0]


def core_first(rows):
    return rows.reshape(-1, 4, 4, 2, 64).transpose(0, 1, 3, 2, 4).reshape(-1, MODEL_WIDTH)


def core_last(rows):
    return rows.reshape(-1, 4, 2, 4, 64).transpose(0, 1, 3, 2, 4).reshape(-1, MODEL_WIDTH)


def ring_first(ahead, low, high, back, axis):
    low = lax.ppermute(low, axis, UP)
    high = lax.ppermute(high, axis, DOWN)
    half = low.shape[0]
    ahead = jnp.concatenate([(ahead[:half].astype(F32) + low.astype(F32)).astype(BF), ahead[half:]])
    back = jnp.concatenate([back[:half], (back[half:].astype(F32) + high.astype(F32)).astype(BF)])
    return ahead, back


def ring_second(own, ahead, back, axis):
    return (
        own.astype(F32)
        + lax.ppermute(ahead, axis, UP).astype(F32)
        + lax.ppermute(back, axis, DOWN).astype(F32)
    )


def rms_scale(values):
    return lax.rsqrt(jnp.mean(values * values, axis=-1, keepdims=True) + NORM_EPS)


def turn(heads, cosine, sine):
    first, second = heads[..., :64], heads[..., 64:]
    return jnp.concatenate([first * cosine - second * sine, second * cosine + first * sine], axis=-1)


EXTENTS = (256, 384, 512, 640)
SCALE = HEAD_SIZE**-0.5


def masked_scores(query, key, row_meta, key_meta):
    raw = lax.dot_general(query, key, LAST, preferred_element_type=F32) * SCALE
    gap = row_meta[:, 0:1] - key_meta[0:1]
    allowed = (gap >= 0) & (gap < WINDOW) & (row_meta[:, 1:2] == key_meta[1:2])
    return jnp.where(jnp.concatenate([allowed, allowed], axis=0), raw, -1e30)


def forward_kernel(proj, own, other, routes, cosine, sine, row_meta, key_meta, *outs):
    query_out, attended_out, total_out, gates_out, mixed_out = outs
    count = proj.shape[0] // 4
    for i in range(4):
        rows = pl.ds(count * i, count)
        extent = EXTENTS[i]
        logits = proj[rows, 1280:1288]
        lane = lax.broadcasted_iota(jnp.int32, (count, EXPERTS), 1)
        named = [routes[rows, 0:1], routes[rows, 1:2]]
        chosen = [jnp.sum(jnp.where(lane == n, logits, 0.0), axis=1, keepdims=True) for n in named]
        top = jnp.maximum(chosen[0], chosen[1])
        power = [jnp.exp(c - top) for c in chosen]
        gates = [p / (power[0] + power[1]) for p in power]
        gates_out[rows, 0:1] = gates[0]
        gates_out[rows, 1:2] = gates[1]
        cos, sin = cosine[rows, :], sine[rows, :]
        picked = []
        for n in named:
            q = jnp.zeros((count, HEAD_SIZE), F32)
            for e in range(EXPERTS):
                q = q + jnp.where(n == e, proj[rows, HEAD_SIZE * e : HEAD_SIZE * (e + 1)], 0.0)
            picked.append(q * cos + pltpu.roll(q, 64, 1) * sin)
        query = jnp.concatenate(picked, axis=0).astype(BF)
        query_out[i] = query
        halves = (own, other)
        scores = [
            masked_scores(
                query, h[:extent, :HEAD_SIZE], row_meta[rows, :], key_meta[k, :, :extent]
            )
            for k, h in enumerate(halves)
        ]
        row_max = jnp.maximum(
            jnp.max(scores[0], axis=1, keepdims=True), jnp.max(scores[1], axis=1, keepdims=True)
        )
        weights = [jnp.exp(s - row_max) for s in scores]
        total = jnp.sum(weights[0], axis=1, keepdims=True) + jnp.sum(weights[1], axis=1, keepdims=True)
        inverse = 1.0 / total
        attended = sum(
            jnp.dot((w * inverse).astype(BF), h[:extent, HEAD_SIZE:], preferred_element_type=F32)
            for w, h in zip(weights, halves)
        )
        attended_out[i] = attended
        total_out[i] = row_max + jnp.log(total)
        for e in range(EXPERTS):
            mixed_out[rows, HEAD_SIZE * e : HEAD_SIZE * (e + 1)] = (
                jnp.where(named[0] == e, gates[0], 0.0) * attended[:count]
                + jnp.where(named[1] == e, gates[1], 0.0) * attended[count:]
            ).astype(BF)


def backward_kernel(
    grad_mixed, query_in, own, other, attended_in, total_in, gates_in, routes, cosine, sine, row_meta, key_meta, *outs
):
    grad_query_out, grad_logit_out, grad_own_out, grad_other_out, sums = outs
    count = grad_mixed.shape[0] // 4
    sums[...] = jnp.zeros_like(sums)
    for i in range(4):
        rows = pl.ds(count * i, count)
        extent = EXTENTS[i]
        named = [routes[rows, 0:1], routes[rows, 1:2]]
        gates = [gates_in[rows, 0:1], gates_in[rows, 1:2]]
        cos, sin = cosine[rows, :], sine[rows, :]
        attended = attended_in[i]
        picked = []
        for n in named:
            g = jnp.zeros((count, HEAD_SIZE), F32)
            for e in range(EXPERTS):
                g = g + jnp.where(n == e, grad_mixed[rows, HEAD_SIZE * e : HEAD_SIZE * (e + 1)], 0.0)
            picked.append(g)
        gate_grads = [
            jnp.sum(p * attended[count * j : count * (j + 1)], axis=1, keepdims=True)
            for j, p in enumerate(picked)
        ]
        level = gates[0] * gate_grads[0] + gates[1] * gate_grads[1]
        lane = lax.broadcasted_iota(jnp.int32, (count, HEAD_SIZE), 1)
        grad_logit_out[rows, :] = sum(
            jnp.where(lane == n, g * (d - level), 0.0) for n, g, d in zip(named, gates, gate_grads)
        ).astype(BF)
        grad_attended = jnp.concatenate(
            [gates[0] * picked[0], gates[1] * picked[1]], axis=0
        ).astype(BF)
        query = query_in[i]
        total = total_in[i]
        probs, grad_probs = [], []
        delta = jnp.zeros((2 * count, 1), F32)
        for k, h in enumerate((own, other)):
            score = masked_scores(
                query, h[:extent, :HEAD_SIZE], row_meta[rows, :], key_meta[k, :, :extent]
            )
            prob = jnp.exp(score - total)
            grad_prob = lax.dot_general(
                grad_attended, h[:extent, HEAD_SIZE:], LAST, preferred_element_type=F32
            )
            delta = delta + jnp.sum(prob * grad_prob, axis=1, keepdims=True)
            probs.append(prob)
            grad_probs.append(grad_prob)
        grad_query = jnp.zeros((2 * count, HEAD_SIZE), F32)
        for k, h in enumerate((own, other)):
            grad_score = (probs[k] * (grad_probs[k] - delta)).astype(BF)
            grad_query = grad_query + jnp.dot(
                grad_score, h[:extent, :HEAD_SIZE], preferred_element_type=F32
            )
            sums[k, :extent, :HEAD_SIZE] += (
                lax.dot_general(grad_score, query, ROWS, preferred_element_type=F32) * SCALE
            )
            sums[k, :extent, HEAD_SIZE:] += lax.dot_general(
                probs[k].astype(BF), grad_attended, ROWS, preferred_element_type=F32
            )
        grad_query = grad_query * SCALE
        turned = [
            g * cos - pltpu.roll(g, 64, 1) * sin for g in (grad_query[:count], grad_query[count:])
        ]
        for e in range(EXPERTS):
            grad_query_out[rows, HEAD_SIZE * e : HEAD_SIZE * (e + 1)] = (
                jnp.where(named[0] == e, turned[0], 0.0) + jnp.where(named[1] == e, turned[1], 0.0)
            ).astype(BF)
    grad_own_out[...] = sums[0]
    grad_other_out[...] = sums[1].astype(BF)


def in_vmem(kernel, outs, scratch, flops, *args):
    spec = pl.BlockSpec(memory_space=pltpu.VMEM)
    moved = sum(a.size * a.dtype.itemsize for a in args)
    return pl.pallas_call(
        kernel,
        out_shape=outs,
        in_specs=[spec] * len(args),
        out_specs=[spec] * len(outs),
        scratch_shapes=scratch,
        compiler_params=pltpu.CompilerParams(vmem_limit_bytes=40 * 1024 * 1024),
        cost_estimate=pl.CostEstimate(flops=flops, bytes_accessed=moved, transcendentals=1 << 20),
    )(*args)


SOME = pl.CostEstimate(flops=1 << 35, bytes_accessed=1 << 27, transcendentals=0)


def on_grid(kernel, scalars, grid, in_specs, out_specs, outs, scratch, *args, cost=SOME):
    return pl.pallas_call(
        kernel,
        out_shape=outs,
        grid_spec=pltpu.PrefetchScalarGridSpec(
            num_scalar_prefetch=1,
            grid=grid,
            in_specs=in_specs,
            out_specs=out_specs,
            scratch_shapes=scratch,
        ),
        compiler_params=pltpu.CompilerParams(vmem_limit_bytes=48 * 1024 * 1024),
        cost_estimate=cost,
    )(jnp.stack(scalars).astype(jnp.int32), *args)


def give_terms(tall, terms, place, core):
    depth, columns = terms.shape

    def kernel(at, left, right, out):
        out[0] = lax.dot_general(left[...], right[...], ROWS, preferred_element_type=F32).astype(BF)

    return on_grid(
        kernel,
        (place, core),
        (4,),
        [
            pl.BlockSpec((depth, 256), lambda i, at: (0, 2 * i + 1 - at[1])),
            pl.BlockSpec((depth, columns), lambda i, at: (0, 0)),
        ],
        pl.BlockSpec((1, 256, columns), lambda i, at: (i, 0, 0)),
        jax.ShapeDtypeStruct((4, 256, columns), BF),
        [],
        tall,
        terms,
    )


def keep_terms(tall, terms, landed, place, core):
    depth, columns = terms.shape

    def kernel(at, left, right, more, own, ahead, low, high, back):
        total = lax.dot_general(left[...], right[...], ROWS, preferred_element_type=F32).astype(
            BF
        ).astype(F32) + more[0].astype(F32)
        total = total.astype(BF)
        step = pl.program_id(0)

        @pl.when(step == 0)
        def _():
            own[...] = total

        @pl.when(step == 1)
        def _():
            ahead[...] = total

        @pl.when(step == 2)
        def _():
            low[...] = total[:128]
            high[...] = total[128:]

        @pl.when(step == 3)
        def _():
            back[...] = total

    def whole(rows):
        return pl.BlockSpec((rows, columns), lambda i, at: (0, 0))

    return on_grid(
        kernel,
        (place, core),
        (4,),
        [
            pl.BlockSpec((depth, 256), lambda i, at: (0, 2 * lax.rem(at[0] + i, 4) + at[1])),
            whole(depth),
            pl.BlockSpec((1, 256, columns), lambda i, at: (lax.rem(at[0] + i, 4), 0, 0)),
        ],
        [whole(256), whole(256), whole(128), whole(128), whole(256)],
        [jax.ShapeDtypeStruct((r, columns), BF) for r in (256, 256, 128, 128, 256)],
        [],
        tall,
        terms,
        landed,
    )


def half_product(rows, pair, half):
    def kernel(at, left, right, out):
        out[...] = lax.dot_general(left[...], right[0], ROWS, preferred_element_type=F32).astype(BF)

    depth, width = pair.shape[1:]
    return on_grid(
        kernel,
        (jnp.int32(0),),
        (8,),
        [
            pl.BlockSpec((depth, 256), lambda i, at: (0, i)),
            pl.BlockSpec((1, depth, width), lambda i, at: (half, 0, 0)),
        ],
        pl.BlockSpec((256, width), lambda i, at: (i, 0)),
        jax.ShapeDtypeStruct((MODEL_WIDTH, width), BF),
        [],
        rows,
        pair,
    )


def down_product(activated, grads, gate):
    def kernel(at, left, right, scale, out):
        scaled = (scale[...] * right[...].astype(F32)).astype(BF)
        out[...] = lax.dot_general(left[...], scaled, ROWS, preferred_element_type=F32).astype(BF)

    depth, width = activated.shape
    return on_grid(
        kernel,
        (jnp.int32(0),),
        (4,),
        [
            pl.BlockSpec((depth, width), lambda i, at: (0, 0)),
            pl.BlockSpec((depth, 512), lambda i, at: (0, i)),
            pl.BlockSpec((depth, 1), lambda i, at: (0, 0)),
        ],
        pl.BlockSpec((width, 512), lambda i, at: (0, i)),
        jax.ShapeDtypeStruct((width, MODEL_WIDTH), BF),
        [],
        activated,
        grads,
        gate,
    )


def down_back(grads, pieces, place):
    def kernel(at, left, own, ahead, far_a, far_b, back, out):
        total = None
        for shift, start, piece in (
            (0, 0, own), (1, 0, ahead), (2, 0, far_a), (2, 256, far_b), (3, 0, back)
        ):
            size = piece.shape[1]
            lanes = pl.ds(pl.multiple_of(lax.rem(at[0] + shift, 4) * 512 + start, 256), size)
            term = lax.dot_general(left[:, lanes], piece[...], LAST, preferred_element_type=F32)
            total = term if total is None else total + term
        out[...] = total

    depth, width = grads.shape[0], pieces[0].shape[0]
    return on_grid(
        kernel,
        (place,),
        (width // 128,),
        [pl.BlockSpec(grads.shape, lambda i, at: (0, 0))]
        + [pl.BlockSpec((128, p.shape[1]), lambda i, at: (i, 0)) for p in pieces],
        pl.BlockSpec((depth, 128), lambda i, at: (0, i)),
        jax.ShapeDtypeStruct((depth, width), F32),
        [],
        grads,
        *pieces,
    )


def expert_quarters(activated, pieces, place, x):
    def kernel(at, left, own, ahead, far_a, far_b, back, out):
        step = pl.program_id(0)
        for shift, refs in enumerate(((own,), (ahead,), (far_a, far_b), (back,))):

            @pl.when(step == shift)
            def _():
                terms = [jnp.dot(left[...], r[...], preferred_element_type=F32) for r in refs]
                out[0] = jnp.concatenate(terms, axis=1).astype(BF)

    depth = activated.shape[0]
    return on_grid(
        kernel,
        (place, x),
        (4,),
        [pl.BlockSpec(a.shape, lambda i, at: (0, 0)) for a in (activated, *pieces)],
        pl.BlockSpec((1, depth, 512), lambda i, at: (lax.rem(at[0] + i + 4 - at[1], 4), 0, 0)),
        jax.ShapeDtypeStruct((4, depth, 512), BF),
        [],
        activated,
        *pieces,
    )


def expert_middle(rows, marks, router, gate_up_w, grad_act, expert):
    depth, width = grad_act.shape
    blocks = width // 128

    def kernel(
        at, rows_ref, marks_ref, router_ref, gate_ref, up_ref, flat_ref, grad_ref,
        act_out, pair_out, gate_out, back_out, pair_all, row_gate, row_grad,
    ):
        step = pl.program_id(0)
        lane = lax.broadcasted_iota(jnp.int32, (depth, 128), 1)

        @pl.when(step == 0)
        def _():
            logits = jnp.dot(rows_ref[...], router_ref[...], preferred_element_type=F32)
            marks_f = marks_ref[...].astype(F32)
            own = jnp.sum(jnp.where(lane == at[0], logits, 0.0), axis=1, keepdims=True)
            other = jnp.sum(jnp.where(lane < 8, logits * marks_f, 0.0), axis=1, keepdims=True)
            valid = jnp.sum(jnp.where(lane == 8, marks_f, 0.0), axis=1, keepdims=True)
            top = jnp.maximum(own, other)
            power = jnp.exp(own - top)
            row_gate[...] = valid * power / (power + jnp.exp(other - top))
            gate_out[...] = row_gate[...]
            row_grad[...] = jnp.zeros_like(row_grad)

        @pl.when(step < blocks)
        def _():
            both = jnp.concatenate([gate_ref[...], up_ref[...]], axis=1)
            gate_up = jnp.dot(rows_ref[...], both, preferred_element_type=F32)
            gate, up = gate_up[:, :128], gate_up[:, 128:]
            sigmoid = 1.0 / (1.0 + jnp.exp(-gate))
            silu = gate * sigmoid
            act = (silu * up).astype(BF)
            raw = grad_ref[...]
            grad = row_gate[...] * raw
            grad_gate = (grad * up * sigmoid * (1.0 + gate * (1.0 - sigmoid))).astype(BF)
            grad_up = (grad * silu).astype(BF)
            act_out[...] = act
            pair_out[0] = grad_gate
            pair_out[1] = grad_up
            at_lane = pl.multiple_of(step * 128, 128)
            pair_all[:, pl.ds(at_lane, 128)] = grad_gate
            pair_all[:, pl.ds(at_lane + width, 128)] = grad_up
            row_grad[...] += jnp.sum(act.astype(F32) * raw, axis=1, keepdims=True)

        @pl.when(step >= blocks)
        def _():
            back_lane = pl.multiple_of((step - blocks) * 512, 512)
            back_out[:, pl.ds(back_lane, 512)] = lax.dot_general(
                pair_all[...], flat_ref[...], LAST, preferred_element_type=F32
            ).astype(BF)

        @pl.when(step == blocks + 3)
        def _():
            high = row_grad[...].astype(BF).astype(F32)
            low = row_grad[...] - high
            back_out[:, MODEL_WIDTH:] = jnp.where(
                lane == 0, high, jnp.where(lane == 1, low, 0.0)
            ).astype(BF)

    def first(i):
        return jnp.minimum(i, blocks - 1)

    def second(i):
        return jnp.clip(i - blocks, 0, 3)

    return on_grid(
        kernel,
        (expert,),
        (blocks + 4,),
        [
            pl.BlockSpec((depth, MODEL_WIDTH), lambda i, at: (0, 0)),
            pl.BlockSpec((depth, 128), lambda i, at: (0, 0)),
            pl.BlockSpec((MODEL_WIDTH, 128), lambda i, at: (0, 0)),
            pl.BlockSpec((MODEL_WIDTH, 128), lambda i, at: (0, first(i))),
            pl.BlockSpec((MODEL_WIDTH, 128), lambda i, at: (0, blocks + first(i))),
            pl.BlockSpec((512, 2 * width), lambda i, at: (second(i), 0)),
            pl.BlockSpec((depth, 128), lambda i, at: (0, first(i))),
        ],
        [
            pl.BlockSpec((depth, 128), lambda i, at: (0, first(i))),
            pl.BlockSpec((2, depth, 128), lambda i, at: (0, 0, first(i))),
            pl.BlockSpec((depth, 1), lambda i, at: (0, 0)),
            pl.BlockSpec((depth, MODEL_WIDTH + 128), lambda i, at: (0, 0)),
        ],
        [
            jax.ShapeDtypeStruct((depth, width), BF),
            jax.ShapeDtypeStruct((2, depth, width), BF),
            jax.ShapeDtypeStruct((depth, 1), F32),
            jax.ShapeDtypeStruct((depth, MODEL_WIDTH + 128), BF),
        ],
        [
            pltpu.VMEM((depth, 2 * width), BF),
            pltpu.VMEM((depth, 1), F32),
            pltpu.VMEM((depth, 1), F32),
        ],
        rows,
        marks,
        router,
        gate_up_w,
        gate_up_w,
        gate_up_w,
        grad_act,
        cost=pl.CostEstimate(
            flops=8 * depth * MODEL_WIDTH * width, bytes_accessed=1 << 24, transcendentals=1 << 20
        ),
    )


def heads_placed(pieces, y):
    def kernel(at, p0, p1, p2, p3, query, kv, out):
        for k, piece in enumerate((p0, p1, p2, p3)):
            lanes = pl.ds(pl.multiple_of(lax.rem(at[0] + k, 4) * 128, 128), 128)
            for e in range(18):
                block = piece[:, 128 * e : 128 * (e + 1)].astype(F32)
                if e < 8:
                    query[:, e, lanes] = block
                elif e < 10:
                    kv[:, e - 8, lanes] = block
                else:
                    out[:, e - 10, lanes] = block

    shapes = [(64, 8, 512), (64, 2, 512), (64, 8, 512)]
    return on_grid(
        kernel,
        (y,),
        (1,),
        [pl.BlockSpec((64, 2432), lambda i, at: (0, 0))] * 4,
        [pl.BlockSpec(s, lambda i, at: (0, 0, 0)) for s in shapes],
        [jax.ShapeDtypeStruct(s, F32) for s in shapes],
        [],
        *pieces,
        cost=pl.CostEstimate(flops=0, bytes_accessed=0, transcendentals=0),
    )


def pick_of(routes):
    return (routes[:, :, None] == jnp.arange(EXPERTS, dtype=jnp.int32)[None, None, :]).astype(F32)


def pair_gates(logits, pick):
    chosen = jnp.sum(logits[:, None, :] * pick, axis=-1)
    weights = jnp.exp(chosen - jnp.max(chosen, axis=1, keepdims=True))
    return weights / jnp.sum(weights, axis=1, keepdims=True)


def gate_back(gates, grad_gates, pick):
    inner = gates * (grad_gates - jnp.sum(gates * grad_gates, axis=1, keepdims=True))
    return jnp.sum(inner[:, :, None] * pick, axis=1)


def norm_back(grad_normed, values, factor, gain):
    gain_part = jnp.sum(grad_normed * values * factor, axis=0)
    inner = grad_normed * gain
    grad_values = factor * inner - values * factor * factor * factor * jnp.mean(
        inner * values, axis=-1, keepdims=True
    )
    return grad_values, gain_part


def in_two(values):
    high = values.astype(BF)
    low = (values - high.astype(F32)).astype(BF)
    return jnp.concatenate([high, low], axis=1)


def widen(columns):
    return jnp.pad(columns, ((0, 0), (0, HEAD_SIZE - columns.shape[1])))


def body(
    tokens,
    cotangent,
    attn_gain,
    mlp_gain,
    attn_router,
    key_value_weight,
    query_matrix,
    output_matrix,
    mlp_router,
    gate_up_weight,
    down_weight,
    attn_routes,
    mlp_routes,
    priority,
    segments,
):
    z, y = lax.axis_index("dp"), lax.axis_index("y")
    core, x = lax.axis_index("core"), lax.axis_index("tensor")
    count = tokens.shape[0]
    quarter = count // 4
    capacity = 50
    room = 56
    sequence = 8 * count
    plane = ("y", "tensor")

    routers_own = jnp.concatenate([attn_router, mlp_router], axis=1)
    in_own = jnp.concatenate([query_matrix, key_value_weight], axis=1)
    down_own = down_weight[0]
    down_before = lax.ppermute(down_own, "dp", UP)
    down_after = lax.ppermute(down_own, "dp", DOWN)
    mine = exchange(
        jnp.concatenate(
            [
                heads_first(in_own),
                jnp.broadcast_to(widen(routers_own), (4, 64, HEAD_SIZE)),
                heads_first(output_matrix),
            ],
            axis=2,
        ),
        "y",
    ).reshape(256, 2432)
    sent = jnp.concatenate([core_first(tokens), widen(attn_routes.astype(BF))], axis=1)
    arrived = spread(after(sent, mine), "y", 4).reshape(4 * count, MODEL_WIDTH + HEAD_SIZE)
    all_w = lax.all_gather(
        after(mine, (down_before, down_after)), ("dp", "core"), axis=0, tiled=True
    )
    values = arrived[:, :MODEL_WIDTH].astype(F32)
    routes = arrived[:, MODEL_WIDTH : MODEL_WIDTH + 2].astype(jnp.int32)
    gain_a = core_first(attn_gain.astype(F32))[0]
    gain_m = core_first(mlp_gain.astype(F32))[0]
    xn1 = (values * rms_scale(values) * gain_a).astype(BF)

    ranking = priority[0]
    pick_m = pick_of(mlp_routes)
    before = (ranking[None, :] < ranking[:, None]).astype(BF)
    earlier = jnp.dot(before, jnp.sum(pick_m, axis=1).astype(BF), preferred_element_type=F32)
    slots = jnp.sum(pick_m * earlier[:, None, :], axis=-1).astype(jnp.int32)
    kept = slots < capacity
    dest = jnp.where(kept, mlp_routes * room + slots, -1)
    lanes = jnp.arange(EXPERTS * room, dtype=jnp.int32)
    to_row = (dest.T[:, :, None] == lanes[None, None, :]).astype(BF)
    any_row = to_row[0] + to_row[1]
    both_rows = to_row.reshape(2 * count, EXPERTS * room)

    def to_experts(rows):
        columns = rows.shape[1]
        return exchange(rows.reshape(EXPERTS, room, columns), ("y", "core")).reshape(
            EXPERTS * room, columns
        )

    def with_other(j):
        others = jnp.concatenate([pick_m[:, 1 - j], jnp.ones((count, 1), F32)], axis=1)
        return jnp.concatenate([cotangent, widen(others.astype(BF))], axis=1)

    grad_sent = lax.dot_general(
        both_rows,
        jnp.concatenate([with_other(0), with_other(1)], axis=0),
        ROWS,
        preferred_element_type=F32,
    ).astype(BF)
    all_w, down_before, down_after, xn1, grad_sent = lax.optimization_barrier(
        (all_w, down_before, down_after, xn1, grad_sent)
    )
    in_w, out_w = all_w[:, :1408], all_w[:, 1408:]
    far_a = lax.ppermute(down_before[:, :256], "dp", UP)
    far_b = lax.ppermute(down_after[:, 256:], "dp", DOWN)
    down_pieces = (down_own, down_after, far_a, far_b, down_before)
    gate_up_own = gate_up_weight.reshape(4, 2, 64, 2816).transpose(1, 0, 2, 3).reshape(512, 2816)
    gate_up_w = lax.all_gather(after(gate_up_own, all_w), "dp", axis=0, tiled=True)
    router_m = in_w[:, 1288:1296]

    grad_landed = to_experts(grad_sent)

    def places(half):
        blocks = 2 * jnp.arange(4, dtype=jnp.int32)[:, None] + half
        return (blocks * count + jnp.arange(count, dtype=jnp.int32)[None, :]).reshape(-1)

    of_sequence = lax.dynamic_slice_in_dim(segments, z * sequence, sequence).reshape(4, 2, count)

    def meta(half):
        documents = lax.dynamic_index_in_dim(of_sequence, half, 1, keepdims=False).reshape(-1)
        return jnp.stack([places(half), documents])

    key_meta = jnp.stack([meta(core), meta(1 - core)])
    row_meta = key_meta[0].T
    inverse = 10000.0 ** (-(jnp.arange(HEAD_SIZE // 2).astype(F32) * 2.0 / HEAD_SIZE))
    angle = places(core).astype(F32)[:, None] * inverse[None, :]
    cosine = jnp.tile(jnp.cos(angle), (1, 2))
    sine = jnp.concatenate([-jnp.sin(angle), jnp.sin(angle)], axis=1)

    def swapped(rows):
        return jnp.concatenate([rows[:, 64:], rows[:, :64]], axis=1)

    half = 4 * count
    projected = jnp.dot(xn1, in_w, preferred_element_type=F32)
    key_raw = projected[:, 1024:1152]
    kv_own = jnp.concatenate(
        [key_raw * cosine + swapped(key_raw) * sine, projected[:, 1152:1280]], axis=1
    ).astype(BF)
    kv_other = lax.ppermute(kv_own, "core", SWAP)
    shared = (routes, cosine, sine, row_meta, key_meta)
    query, attended, totals, gate_a, mixed = in_vmem(
        forward_kernel,
        [
            jax.ShapeDtypeStruct((4, 2 * count, HEAD_SIZE), BF),
            jax.ShapeDtypeStruct((4, 2 * count, HEAD_SIZE), F32),
            jax.ShapeDtypeStruct((4, 2 * count, 1), F32),
            jax.ShapeDtypeStruct((half, 2), F32),
            jax.ShapeDtypeStruct((half, EXPERTS * HEAD_SIZE), BF),
        ],
        [],
        6 << 28,
        projected,
        kv_own,
        kv_other,
        *shared,
    )
    branch_part = lax.dot_general(mixed, out_w, LAST, preferred_element_type=F32).astype(BF)
    branch_part = after(branch_part, grad_landed)
    grad_received = grad_landed[:, :MODEL_WIDTH]
    branch = exchange(branch_part.reshape(16, quarter, MODEL_WIDTH), plane).astype(F32).sum(axis=0)

    first = x * quarter
    own_values = core_first(lax.dynamic_slice_in_dim(tokens, first, quarter)).astype(F32)
    own_factor = rms_scale(own_values)
    hidden = after(own_values, (far_a, far_b)) + branch
    factor_m = rms_scale(hidden)
    xn2_own = (hidden * factor_m * gain_m).astype(BF)
    xn2 = spread(xn2_own, "tensor", 4).reshape(count, MODEL_WIDTH)
    gate_m = pair_gates(jnp.dot(xn2, router_m, preferred_element_type=F32), pick_m)
    weight_m = gate_m * kept.astype(F32)

    received = to_experts(
        lax.dot_general(any_row, xn2, ROWS, preferred_element_type=F32).astype(BF)
    )
    grad_act_raw = down_back(grad_received, down_pieces, z)
    received, grad_act_raw = lax.optimization_barrier((received, grad_act_raw))
    activated, grad_pair, row_gate, grad_back = expert_middle(
        received,
        grad_landed[:, MODEL_WIDTH:],
        jnp.pad(router_m, ((0, 0), (0, 120))),
        gate_up_w,
        grad_act_raw,
        2 * y + core,
    )
    grad_back, late_pair, late_act = lax.optimization_barrier((grad_back, grad_pair, activated))
    grad_returned = to_experts(grad_back)
    grad_down_w = down_product(late_act, grad_received, row_gate)
    down_sum = lax.psum_scatter(grad_down_w, "dp", scatter_dimension=1, tiled=True)
    quarters = expert_quarters(late_act, down_pieces, z, x)
    late_any = after(any_row, (grad_down_w, quarters))
    expert_out = (
        quarters[0].astype(F32)
        + sum(from_ahead(quarters[4 - k], "tensor", k).astype(F32) for k in (1, 2, 3))
    ).astype(BF)

    grad_xn2_part = jnp.dot(
        late_any, grad_returned[:, :MODEL_WIDTH], preferred_element_type=F32
    ).astype(BF)
    row_gate_parts = grad_returned[:, MODEL_WIDTH : MODEL_WIDTH + 2]
    gate_m_part = jnp.sum(
        jnp.einsum("jtr,rd->tjd", to_row, row_gate_parts, preferred_element_type=F32), axis=2
    )
    shares = jnp.concatenate([grad_xn2_part, widen(in_two(gate_m_part))], axis=1)
    landed = (
        exchange(shares.reshape(4, quarter, MODEL_WIDTH + HEAD_SIZE), "tensor")
        .astype(F32)
        .sum(axis=0)
    )
    landed, expert_out = lax.optimization_barrier((landed, expert_out))
    returned = to_experts(expert_out)
    grad_gate_m = (
        landed[:, MODEL_WIDTH : MODEL_WIDTH + 2] + landed[:, MODEL_WIDTH + 2 : MODEL_WIDTH + 4]
    )

    def quarter_of(array, offset=0):
        return lax.dynamic_slice_in_dim(array, first + offset, quarter)

    grad_logit_m = gate_back(quarter_of(gate_m), grad_gate_m, quarter_of(pick_m))
    grad_xn2 = landed[:, :MODEL_WIDTH] + lax.dot_general(
        grad_logit_m, router_m.astype(F32), LAST, preferred_element_type=F32
    )
    grad_norm, gain_m_part = norm_back(grad_xn2, hidden, factor_m, gain_m)
    grad_hidden = core_first(quarter_of(cotangent)).astype(F32) + grad_norm
    grad_sent_back, returned = lax.optimization_barrier((grad_hidden.astype(BF), returned))
    grad_branch = spread(grad_sent_back, plane, 16).reshape(4 * count, MODEL_WIDTH)

    fetched = jnp.einsum("jtr,rd->jtd", to_row, returned, preferred_element_type=F32)
    moe_part = jnp.sum(weight_m.T[:, :, None] * fetched, axis=0).astype(BF)
    grad_gate_w = half_product(after(received, returned), late_pair, 0)
    gate_sum = lax.psum_scatter(grad_gate_w, "dp", scatter_dimension=0, tiled=True)
    grad_up_w = half_product(after(received, returned), late_pair, 1)
    up_sum = lax.psum_scatter(grad_up_w, "dp", scatter_dimension=0, tiled=True)
    width = down_own.shape[0]
    grad_branch, moe_part, *_ = lax.optimization_barrier(
        (grad_branch, moe_part, grad_gate_w, grad_up_w)
    )
    moe_pieces = exchange(moe_part.reshape(4, quarter, MODEL_WIDTH // 4), "tensor")

    grad_mixed = jnp.dot(grad_branch, out_w, preferred_element_type=F32)
    grad_q_all, grad_logit_a, grad_kv_own, grad_kv_give = in_vmem(
        backward_kernel,
        [
            jax.ShapeDtypeStruct((half, EXPERTS * HEAD_SIZE), BF),
            jax.ShapeDtypeStruct((half, HEAD_SIZE), BF),
            jax.ShapeDtypeStruct((half, 2 * HEAD_SIZE), F32),
            jax.ShapeDtypeStruct((half, 2 * HEAD_SIZE), BF),
        ],
        [pltpu.VMEM((2, half, 2 * HEAD_SIZE), F32)],
        40 << 28,
        grad_mixed,
        query,
        kv_own,
        kv_other,
        attended,
        totals,
        gate_a,
        *shared,
    )
    out_give = lax.ppermute(give_terms(grad_branch, mixed, z, core), "core", SWAP)
    kv_back, moe_pieces = lax.optimization_barrier(
        (lax.ppermute(grad_kv_give, "core", SWAP), moe_pieces)
    )
    moe = moe_pieces.transpose(1, 0, 2).reshape(quarter, MODEL_WIDTH).astype(F32)
    output_own = (core_last(hidden) + moe).astype(BF)
    own_grad_kv = grad_kv_own + kv_back.astype(F32)
    grad_key = own_grad_kv[:, :HEAD_SIZE]
    grad_kv = jnp.concatenate(
        [grad_key * cosine - swapped(grad_key) * sine, own_grad_kv[:, HEAD_SIZE:]], axis=1
    ).astype(BF)
    grad_in = jnp.concatenate([grad_q_all, grad_kv, grad_logit_a], axis=1)
    grad_xn1_part = lax.dot_general(grad_in, in_w, LAST, preferred_element_type=F32).astype(BF)
    gain_row = jnp.pad(gain_m_part[None].astype(BF), ((0, 7), (0, 0)))
    tall = jnp.concatenate([xn1, xn2_own, gain_row], axis=0)
    router_cols = jnp.pad(grad_logit_m.astype(BF), ((0, 0), (1288, 112)))
    gain_cols = (
        (jnp.arange(8)[:, None] == 0) & (jnp.arange(1408)[None, :] == 1296)
    ).astype(BF)
    grad_tall = jnp.concatenate([after(grad_in, grad_xn1_part), router_cols, gain_cols], axis=0)
    in_give = lax.ppermute(give_terms(tall, grad_tall, z, core), "core", SWAP)
    out_own, *out_rest = keep_terms(
        grad_branch, mixed, after(out_give, grad_xn1_part), z, core
    )
    out_ahead, out_back = ring_first(*out_rest, "dp")
    in_own_rows, *in_rest = keep_terms(
        tall, grad_tall, after(in_give, out_own), z, core
    )
    in_ahead, in_back = ring_first(*in_rest, "dp")
    out_sum = ring_second(out_own, out_ahead, out_back, "dp").astype(BF)
    in_sum = ring_second(in_own_rows, in_ahead, in_back, "dp").astype(BF)
    landed_raw = exchange(grad_xn1_part.reshape(16, quarter, MODEL_WIDTH), plane)
    landed_raw, in_sum, out_sum, down_sum = lax.optimization_barrier(
        (landed_raw, in_sum, out_sum, down_sum)
    )
    landed_a = landed_raw.astype(F32).sum(axis=0)
    grad_x_norm, _ = norm_back(landed_a, own_values, own_factor, gain_a)
    columns = jnp.arange(1408, dtype=jnp.int32)[None, :]
    gain_a_part = jnp.sum(
        jnp.where(columns < 1288, in_sum.astype(F32) * mine[:, :1408].astype(F32), 0.0),
        axis=1,
        keepdims=True,
    )
    small_part = jnp.where(columns[:, :128] == 17, gain_a_part, in_sum[:, 1280:].astype(F32))
    gain_rows = lax.dynamic_slice_in_dim(attn_gain.astype(F32), z * 512 + y * 128 + core * 64, 64)

    ends = jnp.concatenate(
        [output_own, core_last((grad_hidden + grad_x_norm).astype(BF))], axis=1
    )
    both_sums = jnp.concatenate(
        [in_sum[:, :1280], out_sum, small_part.astype(BF)], axis=1
    ).reshape(4, 64, 2432)
    y_parts = send_direct(both_sums, "y")
    ends, gate_sum = lax.optimization_barrier((ends, gate_sum))
    gate_up_grad = (
        jnp.stack([gate_sum, up_sum], axis=1)
        .reshape(2, 4, 64, 2, width)
        .transpose(1, 0, 2, 3, 4)
        .reshape(1, 512, 2, width)
        .astype(F32)
    )
    _, _, *y_parts = lax.optimization_barrier((gate_up_grad, ends, *y_parts))
    both_ends = spread(ends, "tensor", 4)
    small_y = sum(p[:, 2304:].astype(F32) for p in y_parts).astype(BF)
    small_y = after(small_y, both_ends)
    small_sum = small_y.astype(F32) + sum(
        from_ahead(small_y, "tensor", k).astype(F32) for k in (1, 2, 3)
    )
    down_grad = down_sum.astype(F32)[None]
    both_ends = both_ends.reshape(count, 2 * MODEL_WIDTH)
    output, input_grad = both_ends[:, :MODEL_WIDTH], both_ends[:, MODEL_WIDTH:]
    query_grad, kv_grad, out_grad = heads_placed(y_parts, y)
    return (
        output,
        input_grad,
        small_sum[:, 17] / gain_rows,
        small_sum[:, 16],
        small_sum[:, :8],
        kv_grad,
        query_grad,
        out_grad,
        small_sum[:, 8:16],
        gate_up_grad,
        down_grad,
    )


def solution(mesh):
    split = Mesh(mesh.devices.reshape(4, 4, 2, 4), ("dp", "y", "core", "tensor"))
    rows = ("dp", "y", "core")
    expert = ("y", "core")
    placed = (
        P(rows, None),
        P(rows, None),
        P(),
        P(),
        P(rows, None),
        P(rows, None, "tensor"),
        P(rows, None, "tensor"),
        P(rows, None, "tensor"),
        P(rows, None),
        P(expert, "dp", None, "tensor"),
        P(expert, "tensor", "dp"),
        P(rows, None),
        P(rows, None),
        P(rows, None),
        P(),
    )
    return jax.shard_map(
        body,
        mesh=split,
        in_specs=placed,
        out_specs=(
            P(rows, None),
            P(rows, None),
            P(rows),
            P(rows),
            P(rows, None),
            P(rows, None, "tensor"),
            P(rows, None, "tensor"),
            P(rows, None, "tensor"),
            P(rows, None),
            P(expert, "dp", None, "tensor"),
            P(expert, "tensor", "dp"),
        ),
        check_vma=False,
    )
```

```python
import jax
import jax.numpy as jnp
from jax import lax
from jax.experimental import pallas as pl
from jax.experimental.pallas import tpu as pltpu
from jax.sharding import Mesh
from jax.sharding import PartitionSpec as P

MODEL_WIDTH = 2048
HEAD_SIZE = 128
EXPERTS = 8
WINDOW = 1024
NORM_EPS = 1e-06
BF = jnp.bfloat16
F32 = jnp.float32
ROWS = (((0,), (0,)), ((), ()))
LAST = (((1,), (1,)), ((), ()))
UP = [(0, 1), (1, 2), (2, 3), (3, 0)]
DOWN = [(0, 3), (1, 0), (2, 1), (3, 2)]
SWAP = [(0, 1), (1, 0)]


def exchange(blocks, axis):
    return lax.all_to_all(blocks, axis, split_axis=0, concat_axis=0, tiled=True)


def spread(block, axis, count):
    return exchange(jnp.broadcast_to(block, (count, *block.shape)), axis)


def from_ahead(block, axis, steps):
    return lax.ppermute(block, axis, [(i, (i - steps) % 4) for i in range(4)])


def in_order(pieces, first):
    both = jnp.stack(pieces + pieces[:3])
    return lax.dynamic_slice_in_dim(both, lax.rem(4 - first, 4), 4)


def pick_block(blocks, index):
    return lax.dynamic_index_in_dim(blocks, lax.rem(index, 4), 0, keepdims=False)


def send_direct(blocks, axis):
    me = lax.axis_index(axis)
    return [pick_block(blocks, me)] + [
        from_ahead(pick_block(blocks, me + 4 - k), axis, k) for k in (1, 2, 3)
    ]


def heads_first(shard):
    columns = shard.shape[1] * HEAD_SIZE
    return shard.reshape(64, -1, 4, HEAD_SIZE).transpose(2, 0, 1, 3).reshape(4, 64, columns)


def after(value, other):
    return lax.optimization_barrier((value, other))[0]


def core_first(rows):
    return rows.reshape(-1, 4, 4, 2, 64).transpose(0, 1, 3, 2, 4).reshape(-1, MODEL_WIDTH)


def core_last(rows):
    return rows.reshape(-1, 4, 2, 4, 64).transpose(0, 1, 3, 2, 4).reshape(-1, MODEL_WIDTH)


def ring_first(ahead, low, high, back, axis):
    low = lax.ppermute(low, axis, UP)
    high = lax.ppermute(high, axis, DOWN)
    half = low.shape[0]
    ahead = jnp.concatenate([(ahead[:half].astype(F32) + low.astype(F32)).astype(BF), ahead[half:]])
    back = jnp.concatenate([back[:half], (back[half:].astype(F32) + high.astype(F32)).astype(BF)])
    return ahead, back


def ring_second(own, ahead, back, axis):
    return (
        own.astype(F32)
        + lax.ppermute(ahead, axis, UP).astype(F32)
        + lax.ppermute(back, axis, DOWN).astype(F32)
    )


def rms_scale(values):
    return lax.rsqrt(jnp.mean(values * values, axis=-1, keepdims=True) + NORM_EPS)


def turn(heads, cosine, sine):
    first, second = heads[..., :64], heads[..., 64:]
    return jnp.concatenate([first * cosine - second * sine, second * cosine + first * sine], axis=-1)


EXTENTS = (256, 384, 512, 640)
SCALE = HEAD_SIZE**-0.5


def masked_scores(query, key, row_meta, key_meta):
    raw = lax.dot_general(query, key, LAST, preferred_element_type=F32) * SCALE
    gap = row_meta[:, 0:1] - key_meta[0:1]
    allowed = (gap >= 0) & (gap < WINDOW) & (row_meta[:, 1:2] == key_meta[1:2])
    return jnp.where(jnp.concatenate([allowed, allowed], axis=0), raw, -1e30)


def forward_kernel(proj, own, other, routes, cosine, sine, row_meta, key_meta, *outs):
    query_out, attended_out, total_out, gates_out, mixed_out = outs
    count = proj.shape[0] // 4
    for i in range(4):
        rows = pl.ds(count * i, count)
        extent = EXTENTS[i]
        logits = proj[rows, 1280:1288]
        lane = lax.broadcasted_iota(jnp.int32, (count, EXPERTS), 1)
        named = [routes[rows, 0:1], routes[rows, 1:2]]
        chosen = [jnp.sum(jnp.where(lane == n, logits, 0.0), axis=1, keepdims=True) for n in named]
        top = jnp.maximum(chosen[0], chosen[1])
        power = [jnp.exp(c - top) for c in chosen]
        gates = [p / (power[0] + power[1]) for p in power]
        gates_out[rows, 0:1] = gates[0]
        gates_out[rows, 1:2] = gates[1]
        cos, sin = cosine[rows, :], sine[rows, :]
        picked = []
        for n in named:
            q = jnp.zeros((count, HEAD_SIZE), F32)
            for e in range(EXPERTS):
                q = q + jnp.where(n == e, proj[rows, HEAD_SIZE * e : HEAD_SIZE * (e + 1)], 0.0)
            picked.append(q * cos + pltpu.roll(q, 64, 1) * sin)
        query = jnp.concatenate(picked, axis=0).astype(BF)
        query_out[i] = query
        halves = (own, other)
        scores = [
            masked_scores(
                query, h[:extent, :HEAD_SIZE], row_meta[rows, :], key_meta[k, :, :extent]
            )
            for k, h in enumerate(halves)
        ]
        row_max = jnp.maximum(
            jnp.max(scores[0], axis=1, keepdims=True), jnp.max(scores[1], axis=1, keepdims=True)
        )
        weights = [jnp.exp(s - row_max) for s in scores]
        total = jnp.sum(weights[0], axis=1, keepdims=True) + jnp.sum(weights[1], axis=1, keepdims=True)
        inverse = 1.0 / total
        attended = sum(
            jnp.dot((w * inverse).astype(BF), h[:extent, HEAD_SIZE:], preferred_element_type=F32)
            for w, h in zip(weights, halves)
        )
        attended_out[i] = attended
        total_out[i] = row_max + jnp.log(total)
        for e in range(EXPERTS):
            mixed_out[rows, HEAD_SIZE * e : HEAD_SIZE * (e + 1)] = (
                jnp.where(named[0] == e, gates[0], 0.0) * attended[:count]
                + jnp.where(named[1] == e, gates[1], 0.0) * attended[count:]
            ).astype(BF)


def backward_kernel(
    grad_mixed, query_in, own, other, attended_in, total_in, gates_in, routes, cosine, sine, row_meta, key_meta, *outs
):
    grad_query_out, grad_logit_out, grad_own_out, grad_other_out, sums = outs
    count = grad_mixed.shape[0] // 4
    sums[...] = jnp.zeros_like(sums)
    for i in range(4):
        rows = pl.ds(count * i, count)
        extent = EXTENTS[i]
        named = [routes[rows, 0:1], routes[rows, 1:2]]
        gates = [gates_in[rows, 0:1], gates_in[rows, 1:2]]
        cos, sin = cosine[rows, :], sine[rows, :]
        attended = attended_in[i]
        picked = []
        for n in named:
            g = jnp.zeros((count, HEAD_SIZE), F32)
            for e in range(EXPERTS):
                g = g + jnp.where(n == e, grad_mixed[rows, HEAD_SIZE * e : HEAD_SIZE * (e + 1)], 0.0)
            picked.append(g)
        gate_grads = [
            jnp.sum(p * attended[count * j : count * (j + 1)], axis=1, keepdims=True)
            for j, p in enumerate(picked)
        ]
        level = gates[0] * gate_grads[0] + gates[1] * gate_grads[1]
        lane = lax.broadcasted_iota(jnp.int32, (count, HEAD_SIZE), 1)
        grad_logit_out[rows, :] = sum(
            jnp.where(lane == n, g * (d - level), 0.0) for n, g, d in zip(named, gates, gate_grads)
        ).astype(BF)
        grad_attended = jnp.concatenate(
            [gates[0] * picked[0], gates[1] * picked[1]], axis=0
        ).astype(BF)
        query = query_in[i]
        total = total_in[i]
        probs, grad_probs = [], []
        delta = jnp.zeros((2 * count, 1), F32)
        for k, h in enumerate((own, other)):
            score = masked_scores(
                query, h[:extent, :HEAD_SIZE], row_meta[rows, :], key_meta[k, :, :extent]
            )
            prob = jnp.exp(score - total)
            grad_prob = lax.dot_general(
                grad_attended, h[:extent, HEAD_SIZE:], LAST, preferred_element_type=F32
            )
            delta = delta + jnp.sum(prob * grad_prob, axis=1, keepdims=True)
            probs.append(prob)
            grad_probs.append(grad_prob)
        grad_query = jnp.zeros((2 * count, HEAD_SIZE), F32)
        for k, h in enumerate((own, other)):
            grad_score = (probs[k] * (grad_probs[k] - delta)).astype(BF)
            grad_query = grad_query + jnp.dot(
                grad_score, h[:extent, :HEAD_SIZE], preferred_element_type=F32
            )
            sums[k, :extent, :HEAD_SIZE] += (
                lax.dot_general(grad_score, query, ROWS, preferred_element_type=F32) * SCALE
            )
            sums[k, :extent, HEAD_SIZE:] += lax.dot_general(
                probs[k].astype(BF), grad_attended, ROWS, preferred_element_type=F32
            )
        grad_query = grad_query * SCALE
        turned = [
            g * cos - pltpu.roll(g, 64, 1) * sin for g in (grad_query[:count], grad_query[count:])
        ]
        for e in range(EXPERTS):
            grad_query_out[rows, HEAD_SIZE * e : HEAD_SIZE * (e + 1)] = (
                jnp.where(named[0] == e, turned[0], 0.0) + jnp.where(named[1] == e, turned[1], 0.0)
            ).astype(BF)
    grad_own_out[...] = sums[0]
    grad_other_out[...] = sums[1].astype(BF)


def in_vmem(kernel, outs, scratch, flops, *args):
    spec = pl.BlockSpec(memory_space=pltpu.VMEM)
    moved = sum(a.size * a.dtype.itemsize for a in args)
    return pl.pallas_call(
        kernel,
        out_shape=outs,
        in_specs=[spec] * len(args),
        out_specs=[spec] * len(outs),
        scratch_shapes=scratch,
        compiler_params=pltpu.CompilerParams(vmem_limit_bytes=40 * 1024 * 1024),
        cost_estimate=pl.CostEstimate(flops=flops, bytes_accessed=moved, transcendentals=1 << 20),
    )(*args)


SOME = pl.CostEstimate(flops=1 << 35, bytes_accessed=1 << 27, transcendentals=0)


def on_grid(kernel, scalars, grid, in_specs, out_specs, outs, scratch, *args, cost=SOME):
    return pl.pallas_call(
        kernel,
        out_shape=outs,
        grid_spec=pltpu.PrefetchScalarGridSpec(
            num_scalar_prefetch=1,
            grid=grid,
            in_specs=in_specs,
            out_specs=out_specs,
            scratch_shapes=scratch,
        ),
        compiler_params=pltpu.CompilerParams(vmem_limit_bytes=48 * 1024 * 1024),
        cost_estimate=cost,
    )(jnp.stack(scalars).astype(jnp.int32), *args)


def give_terms(pairs, place, core):
    columns = pairs[0][1].shape[1]

    def kernel(at, *refs):
        out = refs[-1]
        total = sum(
            lax.dot_general(refs[j][...], refs[j + 1][...], ROWS, preferred_element_type=F32)
            for j in range(0, len(refs) - 1, 2)
        )
        out[0] = total.astype(BF)

    specs = []
    for tall, terms in pairs:
        specs.append(pl.BlockSpec((tall.shape[0], 256), lambda i, at: (0, 2 * i + 1 - at[1])))
        specs.append(pl.BlockSpec(terms.shape, lambda i, at: (0, 0)))
    return on_grid(
        kernel,
        (place, core),
        (4,),
        specs,
        pl.BlockSpec((1, 256, columns), lambda i, at: (i, 0, 0)),
        jax.ShapeDtypeStruct((4, 256, columns), BF),
        [],
        *[a for pair in pairs for a in pair],
    )


def keep_terms(pairs, landed, place, core):
    columns = pairs[0][1].shape[1]
    count = 2 * len(pairs)

    def kernel(at, *refs):
        more, own, ahead, low, high, back = refs[count:]
        total = sum(
            lax.dot_general(refs[j][...], refs[j + 1][...], ROWS, preferred_element_type=F32)
            for j in range(0, count, 2)
        )
        total = (total.astype(BF).astype(F32) + more[0].astype(F32)).astype(BF)
        step = pl.program_id(0)

        @pl.when(step == 0)
        def _():
            own[...] = total

        @pl.when(step == 1)
        def _():
            ahead[...] = total

        @pl.when(step == 2)
        def _():
            low[...] = total[:128]
            high[...] = total[128:]

        @pl.when(step == 3)
        def _():
            back[...] = total

    def whole(rows):
        return pl.BlockSpec((rows, columns), lambda i, at: (0, 0))

    specs = []
    for tall, terms in pairs:
        specs.append(
            pl.BlockSpec(
                (tall.shape[0], 256), lambda i, at: (0, 2 * lax.rem(at[0] + i, 4) + at[1])
            )
        )
        specs.append(pl.BlockSpec(terms.shape, lambda i, at: (0, 0)))
    specs.append(pl.BlockSpec((1, 256, columns), lambda i, at: (lax.rem(at[0] + i, 4), 0, 0)))
    return on_grid(
        kernel,
        (place, core),
        (4,),
        specs,
        [whole(256), whole(256), whole(128), whole(128), whole(256)],
        [jax.ShapeDtypeStruct((r, columns), BF) for r in (256, 256, 128, 128, 256)],
        [],
        *[a for pair in pairs for a in pair],
        landed,
    )


def gate_up_product(rows, pair):
    def kernel(at, left, right, out):
        out[...] = lax.dot_general(left[...], right[0], ROWS, preferred_element_type=F32).astype(BF)

    depth, width = pair.shape[1:]
    return on_grid(
        kernel,
        (jnp.int32(0),),
        (2, 8),
        [
            pl.BlockSpec((depth, 256), lambda h, i, at: (0, i)),
            pl.BlockSpec((1, depth, width), lambda h, i, at: (h, 0, 0)),
        ],
        pl.BlockSpec((256, width), lambda h, i, at: (i, h)),
        jax.ShapeDtypeStruct((MODEL_WIDTH, 2 * width), BF),
        [],
        rows,
        pair,
    )


def down_product(activated, grads, gate):
    def kernel(at, left, right, scale, out):
        scaled = (scale[...] * right[...].astype(F32)).astype(BF)
        out[...] = lax.dot_general(left[...], scaled, ROWS, preferred_element_type=F32).astype(BF)

    depth, width = activated.shape
    return on_grid(
        kernel,
        (jnp.int32(0),),
        (4,),
        [
            pl.BlockSpec((depth, width), lambda i, at: (0, 0)),
            pl.BlockSpec((depth, 512), lambda i, at: (0, i)),
            pl.BlockSpec((depth, 1), lambda i, at: (0, 0)),
        ],
        pl.BlockSpec((width, 512), lambda i, at: (0, i)),
        jax.ShapeDtypeStruct((width, MODEL_WIDTH), BF),
        [],
        activated,
        grads,
        gate,
    )


def down_back(grads, pieces, place):
    def kernel(at, left, own, ahead, far_a, far_b, back, out):
        total = None
        for shift, start, piece in (
            (0, 0, own), (1, 0, ahead), (2, 0, far_a), (2, 256, far_b), (3, 0, back)
        ):
            size = piece.shape[1]
            lanes = pl.ds(pl.multiple_of(lax.rem(at[0] + shift, 4) * 512 + start, 256), size)
            term = lax.dot_general(left[:, lanes], piece[...], LAST, preferred_element_type=F32)
            total = term if total is None else total + term
        out[...] = total

    depth, width = grads.shape[0], pieces[0].shape[0]
    return on_grid(
        kernel,
        (place,),
        (width // 128,),
        [pl.BlockSpec(grads.shape, lambda i, at: (0, 0))]
        + [pl.BlockSpec((128, p.shape[1]), lambda i, at: (i, 0)) for p in pieces],
        pl.BlockSpec((depth, 128), lambda i, at: (0, i)),
        jax.ShapeDtypeStruct((depth, width), F32),
        [],
        grads,
        *pieces,
    )


def expert_quarters(activated, pieces, place, x):
    def kernel(at, left, own, ahead, far_a, far_b, back, out):
        step = pl.program_id(0)
        for shift, refs in enumerate(((own,), (ahead,), (far_a, far_b), (back,))):

            @pl.when(step == shift)
            def _():
                terms = [jnp.dot(left[...], r[...], preferred_element_type=F32) for r in refs]
                out[0] = jnp.concatenate(terms, axis=1).astype(BF)

    depth = activated.shape[0]
    return on_grid(
        kernel,
        (place, x),
        (4,),
        [pl.BlockSpec(a.shape, lambda i, at: (0, 0)) for a in (activated, *pieces)],
        pl.BlockSpec((1, depth, 512), lambda i, at: (lax.rem(at[0] + i + 4 - at[1], 4), 0, 0)),
        jax.ShapeDtypeStruct((4, depth, 512), BF),
        [],
        activated,
        *pieces,
    )


def expert_middle(rows, marks, router, gate_up_w, grad_act, expert):
    depth, width = grad_act.shape
    blocks = width // 128

    def kernel(
        at, rows_ref, marks_ref, router_ref, gate_ref, up_ref, flat_ref, grad_ref,
        act_out, pair_out, gate_out, back_out, pair_all, row_gate, row_grad,
    ):
        step = pl.program_id(0)
        lane = lax.broadcasted_iota(jnp.int32, (depth, 128), 1)

        @pl.when(step == 0)
        def _():
            logits = jnp.dot(rows_ref[...], router_ref[...], preferred_element_type=F32)
            marks_f = marks_ref[...].astype(F32)
            own = jnp.sum(jnp.where(lane == at[0], logits, 0.0), axis=1, keepdims=True)
            other = jnp.sum(jnp.where(lane < 8, logits * marks_f, 0.0), axis=1, keepdims=True)
            valid = jnp.sum(jnp.where(lane == 8, marks_f, 0.0), axis=1, keepdims=True)
            top = jnp.maximum(own, other)
            power = jnp.exp(own - top)
            row_gate[...] = valid * power / (power + jnp.exp(other - top))
            gate_out[...] = row_gate[...]
            row_grad[...] = jnp.zeros_like(row_grad)

        @pl.when(step < blocks)
        def _():
            both = jnp.concatenate([gate_ref[...], up_ref[...]], axis=1)
            gate_up = jnp.dot(rows_ref[...], both, preferred_element_type=F32)
            gate, up = gate_up[:, :128], gate_up[:, 128:]
            sigmoid = 1.0 / (1.0 + jnp.exp(-gate))
            silu = gate * sigmoid
            act = (silu * up).astype(BF)
            raw = grad_ref[...]
            grad = row_gate[...] * raw
            grad_gate = (grad * up * sigmoid * (1.0 + gate * (1.0 - sigmoid))).astype(BF)
            grad_up = (grad * silu).astype(BF)
            act_out[...] = act
            pair_out[0] = grad_gate
            pair_out[1] = grad_up
            at_lane = pl.multiple_of(step * 128, 128)
            pair_all[:, pl.ds(at_lane, 128)] = grad_gate
            pair_all[:, pl.ds(at_lane + width, 128)] = grad_up
            row_grad[...] += jnp.sum(act.astype(F32) * raw, axis=1, keepdims=True)

        @pl.when(step >= blocks)
        def _():
            back_lane = pl.multiple_of((step - blocks) * 512, 512)
            back_out[:, pl.ds(back_lane, 512)] = lax.dot_general(
                pair_all[...], flat_ref[...], LAST, preferred_element_type=F32
            ).astype(BF)

        @pl.when(step == blocks + 3)
        def _():
            high = row_grad[...].astype(BF).astype(F32)
            low = row_grad[...] - high
            back_out[:, MODEL_WIDTH:] = jnp.where(
                lane == 0, high, jnp.where(lane == 1, low, 0.0)
            ).astype(BF)

    def first(i):
        return jnp.minimum(i, blocks - 1)

    def second(i):
        return jnp.clip(i - blocks, 0, 3)

    return on_grid(
        kernel,
        (expert,),
        (blocks + 4,),
        [
            pl.BlockSpec((depth, MODEL_WIDTH), lambda i, at: (0, 0)),
            pl.BlockSpec((depth, 128), lambda i, at: (0, 0)),
            pl.BlockSpec((MODEL_WIDTH, 128), lambda i, at: (0, 0)),
            pl.BlockSpec((MODEL_WIDTH, 128), lambda i, at: (0, first(i))),
            pl.BlockSpec((MODEL_WIDTH, 128), lambda i, at: (0, blocks + first(i))),
            pl.BlockSpec((512, 2 * width), lambda i, at: (second(i), 0)),
            pl.BlockSpec((depth, 128), lambda i, at: (0, first(i))),
        ],
        [
            pl.BlockSpec((depth, 128), lambda i, at: (0, first(i))),
            pl.BlockSpec((2, depth, 128), lambda i, at: (0, 0, first(i))),
            pl.BlockSpec((depth, 1), lambda i, at: (0, 0)),
            pl.BlockSpec((depth, MODEL_WIDTH + 128), lambda i, at: (0, 0)),
        ],
        [
            jax.ShapeDtypeStruct((depth, width), BF),
            jax.ShapeDtypeStruct((2, depth, width), BF),
            jax.ShapeDtypeStruct((depth, 1), F32),
            jax.ShapeDtypeStruct((depth, MODEL_WIDTH + 128), BF),
        ],
        [
            pltpu.VMEM((depth, 2 * width), BF),
            pltpu.VMEM((depth, 1), F32),
            pltpu.VMEM((depth, 1), F32),
        ],
        rows,
        marks,
        router,
        gate_up_w,
        gate_up_w,
        gate_up_w,
        grad_act,
        cost=pl.CostEstimate(
            flops=8 * depth * MODEL_WIDTH * width, bytes_accessed=1 << 24, transcendentals=1 << 20
        ),
    )


def heads_placed(pieces, y):
    def kernel(at, p0, p1, p2, p3, query, kv, out):
        for k, piece in enumerate((p0, p1, p2, p3)):
            lanes = pl.ds(pl.multiple_of(lax.rem(at[0] + k, 4) * 128, 128), 128)
            for e in range(18):
                block = piece[:, 128 * e : 128 * (e + 1)].astype(F32)
                if e < 8:
                    query[:, e, lanes] = block
                elif e < 10:
                    kv[:, e - 8, lanes] = block
                else:
                    out[:, e - 10, lanes] = block

    shapes = [(64, 8, 512), (64, 2, 512), (64, 8, 512)]
    return on_grid(
        kernel,
        (y,),
        (1,),
        [pl.BlockSpec((64, 2432), lambda i, at: (0, 0))] * 4,
        [pl.BlockSpec(s, lambda i, at: (0, 0, 0)) for s in shapes],
        [jax.ShapeDtypeStruct(s, F32) for s in shapes],
        [],
        *pieces,
        cost=pl.CostEstimate(flops=0, bytes_accessed=0, transcendentals=0),
    )


def pick_of(routes):
    return (routes[:, :, None] == jnp.arange(EXPERTS, dtype=jnp.int32)[None, None, :]).astype(F32)


def pair_gates(logits, pick):
    chosen = jnp.sum(logits[:, None, :] * pick, axis=-1)
    weights = jnp.exp(chosen - jnp.max(chosen, axis=1, keepdims=True))
    return weights / jnp.sum(weights, axis=1, keepdims=True)


def gate_back(gates, grad_gates, pick):
    inner = gates * (grad_gates - jnp.sum(gates * grad_gates, axis=1, keepdims=True))
    return jnp.sum(inner[:, :, None] * pick, axis=1)


def norm_back(grad_normed, values, factor, gain):
    gain_part = jnp.sum(grad_normed * values * factor, axis=0)
    inner = grad_normed * gain
    grad_values = factor * inner - values * factor * factor * factor * jnp.mean(
        inner * values, axis=-1, keepdims=True
    )
    return grad_values, gain_part


def in_two(values):
    high = values.astype(BF)
    low = (values - high.astype(F32)).astype(BF)
    return jnp.concatenate([high, low], axis=1)


def widen(columns):
    return jnp.pad(columns, ((0, 0), (0, HEAD_SIZE - columns.shape[1])))


def body(
    tokens,
    cotangent,
    attn_gain,
    mlp_gain,
    attn_router,
    key_value_weight,
    query_matrix,
    output_matrix,
    mlp_router,
    gate_up_weight,
    down_weight,
    attn_routes,
    mlp_routes,
    priority,
    segments,
):
    z, y = lax.axis_index("dp"), lax.axis_index("y")
    core, x = lax.axis_index("core"), lax.axis_index("tensor")
    count = tokens.shape[0]
    quarter = count // 4
    capacity = 50
    room = 56
    sequence = 8 * count
    plane = ("y", "tensor")

    routers_own = jnp.concatenate([attn_router, mlp_router], axis=1)
    down_own = down_weight[0]
    down_before = lax.ppermute(down_own, "dp", UP)
    down_after = lax.ppermute(down_own, "dp", DOWN)
    mine = exchange(
        jnp.concatenate(
            [
                heads_first(query_matrix),
                heads_first(key_value_weight),
                jnp.broadcast_to(widen(routers_own), (4, 64, HEAD_SIZE)),
                heads_first(output_matrix),
            ],
            axis=2,
        ),
        "y",
    ).reshape(256, 2432)
    sent = jnp.concatenate([core_first(tokens), widen(attn_routes.astype(BF))], axis=1)
    arrived = spread(after(sent, mine), "y", 4).reshape(4 * count, MODEL_WIDTH + HEAD_SIZE)
    all_w = lax.all_gather(
        after(mine, (down_before, down_after)), ("dp", "core"), axis=0, tiled=True
    )
    values = arrived[:, :MODEL_WIDTH].astype(F32)
    routes = arrived[:, MODEL_WIDTH : MODEL_WIDTH + 2].astype(jnp.int32)
    gain_a = core_first(attn_gain.astype(F32))[0]
    gain_m = core_first(mlp_gain.astype(F32))[0]
    xn1 = (values * rms_scale(values) * gain_a).astype(BF)

    ranking = priority[0]
    pick_m = pick_of(mlp_routes)
    before = (ranking[None, :] < ranking[:, None]).astype(BF)
    earlier = jnp.dot(before, jnp.sum(pick_m, axis=1).astype(BF), preferred_element_type=F32)
    slots = jnp.sum(pick_m * earlier[:, None, :], axis=-1).astype(jnp.int32)
    kept = slots < capacity
    dest = jnp.where(kept, mlp_routes * room + slots, -1)
    lanes = jnp.arange(EXPERTS * room, dtype=jnp.int32)
    to_row = (dest.T[:, :, None] == lanes[None, None, :]).astype(BF)
    any_row = to_row[0] + to_row[1]
    both_rows = to_row.reshape(2 * count, EXPERTS * room)

    def to_experts(rows):
        columns = rows.shape[1]
        return exchange(rows.reshape(EXPERTS, room, columns), ("y", "core")).reshape(
            EXPERTS * room, columns
        )

    def with_other(j):
        others = jnp.concatenate([pick_m[:, 1 - j], jnp.ones((count, 1), F32)], axis=1)
        return jnp.concatenate([cotangent, widen(others.astype(BF))], axis=1)

    grad_sent = lax.dot_general(
        both_rows,
        jnp.concatenate([with_other(0), with_other(1)], axis=0),
        ROWS,
        preferred_element_type=F32,
    ).astype(BF)
    def places(half):
        blocks = 2 * jnp.arange(4, dtype=jnp.int32)[:, None] + half
        return (blocks * count + jnp.arange(count, dtype=jnp.int32)[None, :]).reshape(-1)

    inverse = 10000.0 ** (-(jnp.arange(HEAD_SIZE // 2).astype(F32) * 2.0 / HEAD_SIZE))
    angle = places(core).astype(F32)[:, None] * inverse[None, :]
    cosine = jnp.tile(jnp.cos(angle), (1, 2))
    sine = jnp.concatenate([-jnp.sin(angle), jnp.sin(angle)], axis=1)

    first = x * quarter
    cot_own = core_first(lax.dynamic_slice_in_dim(cotangent, first, quarter)).astype(F32)
    all_w, down_before, down_after, xn1, grad_sent, cosine, sine, cot_own = (
        lax.optimization_barrier(
            (all_w, down_before, down_after, xn1, grad_sent, cosine, sine, cot_own)
        )
    )
    in_w, out_w = all_w[:, :1408], all_w[:, 1408:]
    far_a = lax.ppermute(down_before[:, :256], "dp", UP)
    far_b = lax.ppermute(down_after[:, 256:], "dp", DOWN)
    down_pieces = (down_own, down_after, far_a, far_b, down_before)
    gate_up_own = gate_up_weight.reshape(4, 2, 64, 2816).transpose(1, 0, 2, 3).reshape(512, 2816)
    gate_up_w = lax.all_gather(after(gate_up_own, all_w), "dp", axis=0, tiled=True)
    router_m = in_w[:, 1288:1296]

    grad_landed = to_experts(grad_sent)

    of_sequence = lax.dynamic_slice_in_dim(segments, z * sequence, sequence).reshape(4, 2, count)

    def meta(half):
        documents = lax.dynamic_index_in_dim(of_sequence, half, 1, keepdims=False).reshape(-1)
        return jnp.stack([places(half), documents])

    key_meta = jnp.stack([meta(core), meta(1 - core)])
    row_meta = key_meta[0].T
    def swapped(rows):
        return jnp.concatenate([rows[:, 64:], rows[:, :64]], axis=1)

    half = 4 * count
    projected = jnp.dot(xn1, in_w, preferred_element_type=F32)
    key_raw = projected[:, 1024:1152]
    kv_own = jnp.concatenate(
        [key_raw * cosine + swapped(key_raw) * sine, projected[:, 1152:1280]], axis=1
    ).astype(BF)
    kv_other = lax.ppermute(kv_own, "core", SWAP)
    shared = (routes, cosine, sine, row_meta, key_meta)
    query, attended, totals, gate_a, mixed = in_vmem(
        forward_kernel,
        [
            jax.ShapeDtypeStruct((4, 2 * count, HEAD_SIZE), BF),
            jax.ShapeDtypeStruct((4, 2 * count, HEAD_SIZE), F32),
            jax.ShapeDtypeStruct((4, 2 * count, 1), F32),
            jax.ShapeDtypeStruct((half, 2), F32),
            jax.ShapeDtypeStruct((half, EXPERTS * HEAD_SIZE), BF),
        ],
        [],
        6 << 28,
        projected,
        kv_own,
        kv_other,
        *shared,
    )
    branch_part = lax.dot_general(mixed, out_w, LAST, preferred_element_type=F32).astype(BF)
    branch_part = after(branch_part, grad_landed)
    grad_received = grad_landed[:, :MODEL_WIDTH]
    branch = exchange(branch_part.reshape(16, quarter, MODEL_WIDTH), plane).astype(F32).sum(axis=0)

    own_values = lax.dynamic_slice_in_dim(values, y * count + first, quarter)
    own_factor = rms_scale(own_values)
    hidden = after(own_values, (far_a, far_b)) + branch
    factor_m = rms_scale(hidden)
    xn2_own = (hidden * factor_m * gain_m).astype(BF)
    xn2 = spread(xn2_own, "tensor", 4).reshape(count, MODEL_WIDTH)
    gate_m = pair_gates(jnp.dot(xn2, router_m, preferred_element_type=F32), pick_m)

    received = to_experts(
        lax.dot_general(any_row, xn2, ROWS, preferred_element_type=F32).astype(BF)
    )
    grad_act_raw = down_back(grad_received, down_pieces, z)
    received, grad_act_raw, hidden_last, gate_m = lax.optimization_barrier(
        (received, grad_act_raw, core_last(hidden), gate_m)
    )
    weight_m = gate_m * kept.astype(F32)
    activated, grad_pair, row_gate, grad_back = expert_middle(
        received,
        grad_landed[:, MODEL_WIDTH:],
        jnp.pad(router_m, ((0, 0), (0, 120))),
        gate_up_w,
        grad_act_raw,
        2 * y + core,
    )
    grad_back, late_pair, late_act = lax.optimization_barrier((grad_back, grad_pair, activated))
    grad_returned = to_experts(grad_back)
    grad_down_w = down_product(late_act, grad_received, row_gate)
    down_sum = lax.psum_scatter(grad_down_w, "dp", scatter_dimension=1, tiled=True)
    quarters = expert_quarters(late_act, down_pieces, z, x)
    grad_gate_up_w = gate_up_product(received, late_pair)
    gate_up_sum = lax.psum_scatter(grad_gate_up_w, "dp", scatter_dimension=0, tiled=True)
    late_any = after(any_row, (grad_down_w, quarters, grad_gate_up_w))
    expert_out = (
        quarters[0].astype(F32)
        + sum(from_ahead(quarters[4 - k], "tensor", k).astype(F32) for k in (1, 2, 3))
    ).astype(BF)

    grad_xn2_part = jnp.dot(
        late_any, grad_returned[:, :MODEL_WIDTH], preferred_element_type=F32
    ).astype(BF)
    row_gate_parts = grad_returned[:, MODEL_WIDTH : MODEL_WIDTH + 2]
    gate_m_part = jnp.sum(
        jnp.einsum("jtr,rd->tjd", to_row, row_gate_parts, preferred_element_type=F32), axis=2
    )
    shares = jnp.concatenate([grad_xn2_part, widen(in_two(gate_m_part))], axis=1)
    landed = (
        exchange(shares.reshape(4, quarter, MODEL_WIDTH + HEAD_SIZE), "tensor")
        .astype(F32)
        .sum(axis=0)
    )
    landed, expert_out = lax.optimization_barrier((landed, expert_out))
    returned = to_experts(expert_out)
    grad_gate_m = (
        landed[:, MODEL_WIDTH : MODEL_WIDTH + 2] + landed[:, MODEL_WIDTH + 2 : MODEL_WIDTH + 4]
    )

    def quarter_of(array, offset=0):
        return lax.dynamic_slice_in_dim(array, first + offset, quarter)

    grad_logit_m = gate_back(quarter_of(gate_m), grad_gate_m, quarter_of(pick_m))
    grad_xn2 = landed[:, :MODEL_WIDTH] + lax.dot_general(
        grad_logit_m, router_m.astype(F32), LAST, preferred_element_type=F32
    )
    grad_norm, gain_m_part = norm_back(grad_xn2, hidden, factor_m, gain_m)
    grad_hidden = cot_own + grad_norm
    grad_sent_back, returned = lax.optimization_barrier((grad_hidden.astype(BF), returned))
    grad_branch = spread(grad_sent_back, plane, 16).reshape(4 * count, MODEL_WIDTH)

    fetched = jnp.einsum("jtr,rd->jtd", to_row, returned, preferred_element_type=F32)
    moe_part = jnp.sum(weight_m.T[:, :, None] * fetched, axis=0).astype(BF)
    width = down_own.shape[0]
    grad_branch, moe_part = lax.optimization_barrier((grad_branch, moe_part))
    moe_pieces = exchange(moe_part.reshape(4, quarter, MODEL_WIDTH // 4), "tensor")

    grad_mixed = jnp.dot(grad_branch, out_w, preferred_element_type=F32)
    grad_q_all, grad_logit_a, grad_kv_own, grad_kv_give = in_vmem(
        backward_kernel,
        [
            jax.ShapeDtypeStruct((half, EXPERTS * HEAD_SIZE), BF),
            jax.ShapeDtypeStruct((half, HEAD_SIZE), BF),
            jax.ShapeDtypeStruct((half, 2 * HEAD_SIZE), F32),
            jax.ShapeDtypeStruct((half, 2 * HEAD_SIZE), BF),
        ],
        [pltpu.VMEM((2, half, 2 * HEAD_SIZE), F32)],
        40 << 28,
        grad_mixed,
        query,
        kv_own,
        kv_other,
        attended,
        totals,
        gate_a,
        *shared,
    )
    kv_back, moe_pieces = lax.optimization_barrier(
        (lax.ppermute(grad_kv_give, "core", SWAP), moe_pieces)
    )
    moe = moe_pieces.transpose(1, 0, 2).reshape(quarter, MODEL_WIDTH).astype(F32)
    output_own = (hidden_last + moe).astype(BF)
    own_grad_kv = grad_kv_own + kv_back.astype(F32)
    grad_key = own_grad_kv[:, :HEAD_SIZE]
    grad_kv = jnp.concatenate(
        [grad_key * cosine - swapped(grad_key) * sine, own_grad_kv[:, HEAD_SIZE:]], axis=1
    ).astype(BF)
    grad_in = jnp.concatenate([grad_q_all, grad_kv, grad_logit_a], axis=1)
    grad_xn1_part = lax.dot_general(grad_in, in_w, LAST, preferred_element_type=F32).astype(BF)
    gain_row = jnp.pad(gain_m_part[None].astype(BF), ((0, 7), (0, 0)))
    lane = jnp.arange(1408, dtype=jnp.int32)[None, :]
    router_cols = jnp.pad(grad_logit_m.astype(BF), ((0, 0), (1288, 112)))
    gain_cols = ((jnp.arange(8)[:, None] == 0) & (lane == 1296)).astype(BF)
    in_pairs = [
        (xn1, after(grad_in, grad_xn1_part)),
        (
            jnp.concatenate([xn2_own, gain_row], axis=0),
            jnp.concatenate([router_cols, gain_cols], axis=0),
        ),
    ]
    in_give = lax.ppermute(give_terms(in_pairs, z, core), "core", SWAP)
    out_pairs = [(grad_branch, after(mixed, in_give))]
    out_give = lax.ppermute(give_terms(out_pairs, z, core), "core", SWAP)
    in_own_rows, *in_rest = keep_terms(in_pairs, in_give, z, core)
    in_ahead, in_back = ring_first(*in_rest, "dp")
    out_own, *out_rest = keep_terms(out_pairs, out_give, z, core)
    out_ahead, out_back = ring_first(*out_rest, "dp")
    out_sum = ring_second(out_own, out_ahead, out_back, "dp").astype(BF)
    in_sum = ring_second(in_own_rows, in_ahead, in_back, "dp").astype(BF)
    landed_raw = exchange(grad_xn1_part.reshape(16, quarter, MODEL_WIDTH), plane)
    landed_raw, in_sum, out_sum, down_sum = lax.optimization_barrier(
        (landed_raw, in_sum, out_sum, down_sum)
    )
    landed_a = landed_raw.astype(F32).sum(axis=0)
    grad_x_norm, _ = norm_back(landed_a, own_values, own_factor, gain_a)
    columns = jnp.arange(1408, dtype=jnp.int32)[None, :]
    gain_a_part = jnp.sum(
        jnp.where(columns < 1288, in_sum.astype(F32) * mine[:, :1408].astype(F32), 0.0),
        axis=1,
        keepdims=True,
    )
    small_part = jnp.where(columns[:, :128] == 17, gain_a_part, in_sum[:, 1280:].astype(F32))
    gain_rows = lax.dynamic_slice_in_dim(attn_gain.astype(F32), z * 512 + y * 128 + core * 64, 64)

    ends = jnp.concatenate(
        [output_own, core_last((grad_hidden + grad_x_norm).astype(BF))], axis=1
    )
    both_sums = jnp.concatenate(
        [in_sum[:, :1280], out_sum, small_part.astype(BF)], axis=1
    ).reshape(4, 64, 2432)
    y_parts = send_direct(both_sums, "y")
    gate_up_grad = (
        gate_up_sum.reshape(2, 4, 64, 2816)
        .transpose(1, 0, 2, 3)
        .reshape(1, 512, 2, width)
        .astype(F32)
    )
    _, _, *y_parts = lax.optimization_barrier((gate_up_grad, ends, *y_parts))
    both_ends = spread(ends, "tensor", 4)
    small_y = sum(p[:, 2304:].astype(F32) for p in y_parts).astype(BF)
    small_y = after(small_y, both_ends)
    small_sum = small_y.astype(F32) + sum(
        from_ahead(small_y, "tensor", k).astype(F32) for k in (1, 2, 3)
    )
    down_grad = down_sum.astype(F32)[None]
    both_ends = both_ends.reshape(count, 2 * MODEL_WIDTH)
    output, input_grad = both_ends[:, :MODEL_WIDTH], both_ends[:, MODEL_WIDTH:]
    query_grad, kv_grad, out_grad = heads_placed(y_parts, y)
    return (
        output,
        input_grad,
        small_sum[:, 17] / gain_rows,
        small_sum[:, 16],
        small_sum[:, :8],
        kv_grad,
        query_grad,
        out_grad,
        small_sum[:, 8:16],
        gate_up_grad,
        down_grad,
    )


def solution(mesh):
    split = Mesh(mesh.devices.reshape(4, 4, 2, 4), ("dp", "y", "core", "tensor"))
    rows = ("dp", "y", "core")
    expert = ("y", "core")
    placed = (
        P(rows, None),
        P(rows, None),
        P(),
        P(),
        P(rows, None),
        P(rows, None, "tensor"),
        P(rows, None, "tensor"),
        P(rows, None, "tensor"),
        P(rows, None),
        P(expert, "dp", None, "tensor"),
        P(expert, "tensor", "dp"),
        P(rows, None),
        P(rows, None),
        P(rows, None),
        P(),
    )
    return jax.shard_map(
        body,
        mesh=split,
        in_specs=placed,
        out_specs=(
            P(rows, None),
            P(rows, None),
            P(rows),
            P(rows),
            P(rows, None),
            P(rows, None, "tensor"),
            P(rows, None, "tensor"),
            P(rows, None, "tensor"),
            P(rows, None),
            P(expert, "dp", None, "tensor"),
            P(expert, "tensor", "dp"),
        ),
        check_vma=False,
    )
```

```python
import jax
import jax.numpy as jnp
from jax import lax
from jax.experimental import pallas as pl
from jax.experimental.pallas import tpu as pltpu
from jax.sharding import Mesh
from jax.sharding import PartitionSpec as P

MODEL_WIDTH = 2048
HEAD_SIZE = 128
EXPERTS = 8
WINDOW = 1024
NORM_EPS = 1e-06
BF = jnp.bfloat16
F32 = jnp.float32
ROWS = (((0,), (0,)), ((), ()))
LAST = (((1,), (1,)), ((), ()))
UP = [(0, 1), (1, 2), (2, 3), (3, 0)]
DOWN = [(0, 3), (1, 0), (2, 1), (3, 2)]
SWAP = [(0, 1), (1, 0)]


def exchange(blocks, axis):
    return lax.all_to_all(blocks, axis, split_axis=0, concat_axis=0, tiled=True)


def spread(block, axis, count):
    return exchange(jnp.broadcast_to(block, (count, *block.shape)), axis)


def from_ahead(block, axis, steps):
    return lax.ppermute(block, axis, [(i, (i - steps) % 4) for i in range(4)])


def in_order(pieces, first):
    both = jnp.stack(pieces + pieces[:3])
    return lax.dynamic_slice_in_dim(both, lax.rem(4 - first, 4), 4)


def pick_block(blocks, index):
    return lax.dynamic_index_in_dim(blocks, lax.rem(index, 4), 0, keepdims=False)


def send_direct(blocks, axis):
    me = lax.axis_index(axis)
    return [pick_block(blocks, me)] + [
        from_ahead(pick_block(blocks, me + 4 - k), axis, k) for k in (1, 2, 3)
    ]


def heads_first(shard):
    columns = shard.shape[1] * HEAD_SIZE
    return shard.reshape(64, -1, 4, HEAD_SIZE).transpose(2, 0, 1, 3).reshape(4, 64, columns)


def after(value, other):
    return lax.optimization_barrier((value, other))[0]


def core_first(rows):
    return rows.reshape(-1, 4, 4, 2, 64).transpose(0, 1, 3, 2, 4).reshape(-1, MODEL_WIDTH)


def core_last(rows):
    return rows.reshape(-1, 4, 2, 4, 64).transpose(0, 1, 3, 2, 4).reshape(-1, MODEL_WIDTH)


def ring_first(ahead, low, high, back, axis):
    low = lax.ppermute(low, axis, UP)
    high = lax.ppermute(high, axis, DOWN)
    half = low.shape[0]
    ahead = jnp.concatenate([(ahead[:half].astype(F32) + low.astype(F32)).astype(BF), ahead[half:]])
    back = jnp.concatenate([back[:half], (back[half:].astype(F32) + high.astype(F32)).astype(BF)])
    return ahead, back


def ring_second(own, ahead, back, axis):
    return (
        own.astype(F32)
        + lax.ppermute(ahead, axis, UP).astype(F32)
        + lax.ppermute(back, axis, DOWN).astype(F32)
    )


def rms_scale(values):
    return lax.rsqrt(jnp.mean(values * values, axis=-1, keepdims=True) + NORM_EPS)


def turn(heads, cosine, sine):
    first, second = heads[..., :64], heads[..., 64:]
    return jnp.concatenate([first * cosine - second * sine, second * cosine + first * sine], axis=-1)


EXTENTS = (256, 384, 512, 640)
SCALE = HEAD_SIZE**-0.5


def masked_scores(query, key, row_meta, key_meta):
    raw = lax.dot_general(query, key, LAST, preferred_element_type=F32) * SCALE
    gap = row_meta[:, 0:1] - key_meta[0:1]
    allowed = (gap >= 0) & (gap < WINDOW) & (row_meta[:, 1:2] == key_meta[1:2])
    return jnp.where(jnp.concatenate([allowed, allowed], axis=0), raw, -1e30)


def forward_kernel(proj, own, other, routes, cosine, sine, row_meta, key_meta, *outs):
    query_out, attended_out, total_out, gates_out, mixed_out = outs
    count = proj.shape[0] // 4
    for i in range(4):
        rows = pl.ds(count * i, count)
        extent = EXTENTS[i]
        logits = proj[rows, 1280:1288]
        lane = lax.broadcasted_iota(jnp.int32, (count, EXPERTS), 1)
        named = [routes[rows, 0:1], routes[rows, 1:2]]
        chosen = [jnp.sum(jnp.where(lane == n, logits, 0.0), axis=1, keepdims=True) for n in named]
        top = jnp.maximum(chosen[0], chosen[1])
        power = [jnp.exp(c - top) for c in chosen]
        gates = [p / (power[0] + power[1]) for p in power]
        gates_out[rows, 0:1] = gates[0]
        gates_out[rows, 1:2] = gates[1]
        cos, sin = cosine[rows, :], sine[rows, :]
        picked = []
        for n in named:
            q = jnp.zeros((count, HEAD_SIZE), F32)
            for e in range(EXPERTS):
                q = q + jnp.where(n == e, proj[rows, HEAD_SIZE * e : HEAD_SIZE * (e + 1)], 0.0)
            picked.append(q * cos + pltpu.roll(q, 64, 1) * sin)
        query = jnp.concatenate(picked, axis=0).astype(BF)
        query_out[i] = query
        halves = (own, other)
        scores = [
            masked_scores(
                query, h[:extent, :HEAD_SIZE], row_meta[rows, :], key_meta[k, :, :extent]
            )
            for k, h in enumerate(halves)
        ]
        row_max = jnp.maximum(
            jnp.max(scores[0], axis=1, keepdims=True), jnp.max(scores[1], axis=1, keepdims=True)
        )
        weights = [jnp.exp(s - row_max) for s in scores]
        total = jnp.sum(weights[0], axis=1, keepdims=True) + jnp.sum(weights[1], axis=1, keepdims=True)
        inverse = 1.0 / total
        attended = sum(
            jnp.dot((w * inverse).astype(BF), h[:extent, HEAD_SIZE:], preferred_element_type=F32)
            for w, h in zip(weights, halves)
        )
        attended_out[i] = attended
        total_out[i] = row_max + jnp.log(total)
        for e in range(EXPERTS):
            mixed_out[rows, HEAD_SIZE * e : HEAD_SIZE * (e + 1)] = (
                jnp.where(named[0] == e, gates[0], 0.0) * attended[:count]
                + jnp.where(named[1] == e, gates[1], 0.0) * attended[count:]
            ).astype(BF)


def backward_kernel(
    grad_mixed, query_in, own, other, attended_in, total_in, gates_in, routes, cosine, sine, row_meta, key_meta, *outs
):
    grad_query_out, grad_logit_out, grad_own_out, grad_other_out, sums = outs
    count = grad_mixed.shape[0] // 4
    sums[...] = jnp.zeros_like(sums)
    for i in range(4):
        rows = pl.ds(count * i, count)
        extent = EXTENTS[i]
        named = [routes[rows, 0:1], routes[rows, 1:2]]
        gates = [gates_in[rows, 0:1], gates_in[rows, 1:2]]
        cos, sin = cosine[rows, :], sine[rows, :]
        attended = attended_in[i]
        picked = []
        for n in named:
            g = jnp.zeros((count, HEAD_SIZE), F32)
            for e in range(EXPERTS):
                g = g + jnp.where(n == e, grad_mixed[rows, HEAD_SIZE * e : HEAD_SIZE * (e + 1)], 0.0)
            picked.append(g)
        gate_grads = [
            jnp.sum(p * attended[count * j : count * (j + 1)], axis=1, keepdims=True)
            for j, p in enumerate(picked)
        ]
        level = gates[0] * gate_grads[0] + gates[1] * gate_grads[1]
        lane = lax.broadcasted_iota(jnp.int32, (count, HEAD_SIZE), 1)
        grad_logit_out[rows, :] = sum(
            jnp.where(lane == n, g * (d - level), 0.0) for n, g, d in zip(named, gates, gate_grads)
        ).astype(BF)
        grad_attended = jnp.concatenate(
            [gates[0] * picked[0], gates[1] * picked[1]], axis=0
        ).astype(BF)
        query = query_in[i]
        total = total_in[i]
        probs, grad_probs = [], []
        delta = jnp.zeros((2 * count, 1), F32)
        for k, h in enumerate((own, other)):
            score = masked_scores(
                query, h[:extent, :HEAD_SIZE], row_meta[rows, :], key_meta[k, :, :extent]
            )
            prob = jnp.exp(score - total)
            grad_prob = lax.dot_general(
                grad_attended, h[:extent, HEAD_SIZE:], LAST, preferred_element_type=F32
            )
            delta = delta + jnp.sum(prob * grad_prob, axis=1, keepdims=True)
            probs.append(prob)
            grad_probs.append(grad_prob)
        grad_query = jnp.zeros((2 * count, HEAD_SIZE), F32)
        for k, h in enumerate((own, other)):
            grad_score = (probs[k] * (grad_probs[k] - delta)).astype(BF)
            grad_query = grad_query + jnp.dot(
                grad_score, h[:extent, :HEAD_SIZE], preferred_element_type=F32
            )
            sums[k, :extent, :HEAD_SIZE] += (
                lax.dot_general(grad_score, query, ROWS, preferred_element_type=F32) * SCALE
            )
            sums[k, :extent, HEAD_SIZE:] += lax.dot_general(
                probs[k].astype(BF), grad_attended, ROWS, preferred_element_type=F32
            )
        grad_query = grad_query * SCALE
        turned = [
            g * cos - pltpu.roll(g, 64, 1) * sin for g in (grad_query[:count], grad_query[count:])
        ]
        for e in range(EXPERTS):
            grad_query_out[rows, HEAD_SIZE * e : HEAD_SIZE * (e + 1)] = (
                jnp.where(named[0] == e, turned[0], 0.0) + jnp.where(named[1] == e, turned[1], 0.0)
            ).astype(BF)
    grad_own_out[...] = sums[0]
    grad_other_out[...] = sums[1].astype(BF)


def in_vmem(kernel, outs, scratch, flops, *args):
    spec = pl.BlockSpec(memory_space=pltpu.VMEM)
    moved = sum(a.size * a.dtype.itemsize for a in args)
    return pl.pallas_call(
        kernel,
        out_shape=outs,
        in_specs=[spec] * len(args),
        out_specs=[spec] * len(outs),
        scratch_shapes=scratch,
        compiler_params=pltpu.CompilerParams(vmem_limit_bytes=40 * 1024 * 1024),
        cost_estimate=pl.CostEstimate(flops=flops, bytes_accessed=moved, transcendentals=1 << 20),
    )(*args)


SOME = pl.CostEstimate(flops=1 << 35, bytes_accessed=1 << 27, transcendentals=0)


def on_grid(kernel, scalars, grid, in_specs, out_specs, outs, scratch, *args, cost=SOME):
    return pl.pallas_call(
        kernel,
        out_shape=outs,
        grid_spec=pltpu.PrefetchScalarGridSpec(
            num_scalar_prefetch=1,
            grid=grid,
            in_specs=in_specs,
            out_specs=out_specs,
            scratch_shapes=scratch,
        ),
        compiler_params=pltpu.CompilerParams(vmem_limit_bytes=48 * 1024 * 1024),
        cost_estimate=cost,
    )(jnp.stack(scalars).astype(jnp.int32), *args)


def give_terms(pairs, place, core):
    columns = pairs[0][1].shape[1]

    def kernel(at, *refs):
        out = refs[-1]
        total = sum(
            lax.dot_general(refs[j][...], refs[j + 1][...], ROWS, preferred_element_type=F32)
            for j in range(0, len(refs) - 1, 2)
        )
        out[0] = total.astype(BF)

    specs = []
    for tall, terms in pairs:
        specs.append(pl.BlockSpec((tall.shape[0], 256), lambda i, at: (0, 2 * i + 1 - at[1])))
        specs.append(pl.BlockSpec(terms.shape, lambda i, at: (0, 0)))
    return on_grid(
        kernel,
        (place, core),
        (4,),
        specs,
        pl.BlockSpec((1, 256, columns), lambda i, at: (i, 0, 0)),
        jax.ShapeDtypeStruct((4, 256, columns), BF),
        [],
        *[a for pair in pairs for a in pair],
    )


def keep_terms(pairs, landed, place, core):
    columns = pairs[0][1].shape[1]
    count = 2 * len(pairs)

    def kernel(at, *refs):
        more, own, ahead, low, high, back = refs[count:]
        total = sum(
            lax.dot_general(refs[j][...], refs[j + 1][...], ROWS, preferred_element_type=F32)
            for j in range(0, count, 2)
        )
        total = (total.astype(BF).astype(F32) + more[0].astype(F32)).astype(BF)
        step = pl.program_id(0)

        @pl.when(step == 0)
        def _():
            own[...] = total

        @pl.when(step == 1)
        def _():
            ahead[...] = total

        @pl.when(step == 2)
        def _():
            low[...] = total[:128]
            high[...] = total[128:]

        @pl.when(step == 3)
        def _():
            back[...] = total

    def whole(rows):
        return pl.BlockSpec((rows, columns), lambda i, at: (0, 0))

    specs = []
    for tall, terms in pairs:
        specs.append(
            pl.BlockSpec(
                (tall.shape[0], 256), lambda i, at: (0, 2 * lax.rem(at[0] + i, 4) + at[1])
            )
        )
        specs.append(pl.BlockSpec(terms.shape, lambda i, at: (0, 0)))
    specs.append(pl.BlockSpec((1, 256, columns), lambda i, at: (lax.rem(at[0] + i, 4), 0, 0)))
    return on_grid(
        kernel,
        (place, core),
        (4,),
        specs,
        [whole(256), whole(256), whole(128), whole(128), whole(256)],
        [jax.ShapeDtypeStruct((r, columns), BF) for r in (256, 256, 128, 128, 256)],
        [],
        *[a for pair in pairs for a in pair],
        landed,
    )


def gate_up_product(rows, pair):
    def kernel(at, left, right, out):
        out[...] = lax.dot_general(left[...], right[0], ROWS, preferred_element_type=F32).astype(BF)

    depth, width = pair.shape[1:]
    return on_grid(
        kernel,
        (jnp.int32(0),),
        (2, 8),
        [
            pl.BlockSpec((depth, 256), lambda h, i, at: (0, i)),
            pl.BlockSpec((1, depth, width), lambda h, i, at: (h, 0, 0)),
        ],
        pl.BlockSpec((256, width), lambda h, i, at: (i, h)),
        jax.ShapeDtypeStruct((MODEL_WIDTH, 2 * width), BF),
        [],
        rows,
        pair,
    )


def down_product(activated, grads, gate):
    def kernel(at, left, right, scale, out):
        scaled = (scale[...] * right[...].astype(F32)).astype(BF)
        out[...] = lax.dot_general(left[...], scaled, ROWS, preferred_element_type=F32).astype(BF)

    depth, width = activated.shape
    return on_grid(
        kernel,
        (jnp.int32(0),),
        (4,),
        [
            pl.BlockSpec((depth, width), lambda i, at: (0, 0)),
            pl.BlockSpec((depth, 512), lambda i, at: (0, i)),
            pl.BlockSpec((depth, 1), lambda i, at: (0, 0)),
        ],
        pl.BlockSpec((width, 512), lambda i, at: (0, i)),
        jax.ShapeDtypeStruct((width, MODEL_WIDTH), BF),
        [],
        activated,
        grads,
        gate,
    )


def down_back(grads, pieces, place):
    def kernel(at, left, own, ahead, far_a, far_b, back, out):
        total = None
        for shift, start, piece in (
            (0, 0, own), (1, 0, ahead), (2, 0, far_a), (2, 256, far_b), (3, 0, back)
        ):
            size = piece.shape[1]
            lanes = pl.ds(pl.multiple_of(lax.rem(at[0] + shift, 4) * 512 + start, 256), size)
            term = lax.dot_general(left[:, lanes], piece[...], LAST, preferred_element_type=F32)
            total = term if total is None else total + term
        out[...] = total

    depth, width = grads.shape[0], pieces[0].shape[0]
    return on_grid(
        kernel,
        (place,),
        (width // 128,),
        [pl.BlockSpec(grads.shape, lambda i, at: (0, 0))]
        + [pl.BlockSpec((128, p.shape[1]), lambda i, at: (i, 0)) for p in pieces],
        pl.BlockSpec((depth, 128), lambda i, at: (0, i)),
        jax.ShapeDtypeStruct((depth, width), F32),
        [],
        grads,
        *pieces,
    )


def expert_quarters(activated, pieces, place, x):
    def kernel(at, left, own, ahead, far_a, far_b, back, out):
        step = pl.program_id(0)
        for shift, refs in enumerate(((own,), (ahead,), (far_a, far_b), (back,))):

            @pl.when(step == shift)
            def _():
                terms = [jnp.dot(left[...], r[...], preferred_element_type=F32) for r in refs]
                out[0] = jnp.concatenate(terms, axis=1).astype(BF)

    depth = activated.shape[0]
    return on_grid(
        kernel,
        (place, x),
        (4,),
        [pl.BlockSpec(a.shape, lambda i, at: (0, 0)) for a in (activated, *pieces)],
        pl.BlockSpec((1, depth, 512), lambda i, at: (lax.rem(at[0] + i + 4 - at[1], 4), 0, 0)),
        jax.ShapeDtypeStruct((4, depth, 512), BF),
        [],
        activated,
        *pieces,
    )


def expert_middle(rows, marks, router, gate_up_w, grad_act, expert):
    depth, width = grad_act.shape
    blocks = width // 128

    def kernel(
        at, rows_ref, marks_ref, router_ref, gate_ref, up_ref, flat_ref, grad_ref,
        act_out, pair_out, gate_out, back_out, pair_all, row_gate, row_grad,
    ):
        step = pl.program_id(0)
        lane = lax.broadcasted_iota(jnp.int32, (depth, 128), 1)

        @pl.when(step == 0)
        def _():
            logits = jnp.dot(rows_ref[...], router_ref[...], preferred_element_type=F32)
            marks_f = marks_ref[...].astype(F32)
            own = jnp.sum(jnp.where(lane == at[0], logits, 0.0), axis=1, keepdims=True)
            other = jnp.sum(jnp.where(lane < 8, logits * marks_f, 0.0), axis=1, keepdims=True)
            valid = jnp.sum(jnp.where(lane == 8, marks_f, 0.0), axis=1, keepdims=True)
            top = jnp.maximum(own, other)
            power = jnp.exp(own - top)
            row_gate[...] = valid * power / (power + jnp.exp(other - top))
            gate_out[...] = row_gate[...]
            row_grad[...] = jnp.zeros_like(row_grad)

        @pl.when(step < blocks)
        def _():
            both = jnp.concatenate([gate_ref[...], up_ref[...]], axis=1)
            gate_up = jnp.dot(rows_ref[...], both, preferred_element_type=F32)
            gate, up = gate_up[:, :128], gate_up[:, 128:]
            sigmoid = 1.0 / (1.0 + jnp.exp(-gate))
            silu = gate * sigmoid
            act = (silu * up).astype(BF)
            raw = grad_ref[...]
            grad = row_gate[...] * raw
            grad_gate = (grad * up * sigmoid * (1.0 + gate * (1.0 - sigmoid))).astype(BF)
            grad_up = (grad * silu).astype(BF)
            act_out[...] = act
            pair_out[0] = grad_gate
            pair_out[1] = grad_up
            at_lane = pl.multiple_of(step * 128, 128)
            pair_all[:, pl.ds(at_lane, 128)] = grad_gate
            pair_all[:, pl.ds(at_lane + width, 128)] = grad_up
            row_grad[...] += jnp.sum(act.astype(F32) * raw, axis=1, keepdims=True)

        @pl.when(step >= blocks)
        def _():
            back_lane = pl.multiple_of((step - blocks) * 512, 512)
            back_out[:, pl.ds(back_lane, 512)] = lax.dot_general(
                pair_all[...], flat_ref[...], LAST, preferred_element_type=F32
            ).astype(BF)

        @pl.when(step == blocks + 3)
        def _():
            high = row_grad[...].astype(BF).astype(F32)
            low = row_grad[...] - high
            back_out[:, MODEL_WIDTH:] = jnp.where(
                lane == 0, high, jnp.where(lane == 1, low, 0.0)
            ).astype(BF)

    def first(i):
        return jnp.minimum(i, blocks - 1)

    def second(i):
        return jnp.clip(i - blocks, 0, 3)

    return on_grid(
        kernel,
        (expert,),
        (blocks + 4,),
        [
            pl.BlockSpec((depth, MODEL_WIDTH), lambda i, at: (0, 0)),
            pl.BlockSpec((depth, 128), lambda i, at: (0, 0)),
            pl.BlockSpec((MODEL_WIDTH, 128), lambda i, at: (0, 0)),
            pl.BlockSpec((MODEL_WIDTH, 128), lambda i, at: (0, first(i))),
            pl.BlockSpec((MODEL_WIDTH, 128), lambda i, at: (0, blocks + first(i))),
            pl.BlockSpec((512, 2 * width), lambda i, at: (second(i), 0)),
            pl.BlockSpec((depth, 128), lambda i, at: (0, first(i))),
        ],
        [
            pl.BlockSpec((depth, 128), lambda i, at: (0, first(i))),
            pl.BlockSpec((2, depth, 128), lambda i, at: (0, 0, first(i))),
            pl.BlockSpec((depth, 1), lambda i, at: (0, 0)),
            pl.BlockSpec((depth, MODEL_WIDTH + 128), lambda i, at: (0, 0)),
        ],
        [
            jax.ShapeDtypeStruct((depth, width), BF),
            jax.ShapeDtypeStruct((2, depth, width), BF),
            jax.ShapeDtypeStruct((depth, 1), F32),
            jax.ShapeDtypeStruct((depth, MODEL_WIDTH + 128), BF),
        ],
        [
            pltpu.VMEM((depth, 2 * width), BF),
            pltpu.VMEM((depth, 1), F32),
            pltpu.VMEM((depth, 1), F32),
        ],
        rows,
        marks,
        router,
        gate_up_w,
        gate_up_w,
        gate_up_w,
        grad_act,
        cost=pl.CostEstimate(
            flops=8 * depth * MODEL_WIDTH * width, bytes_accessed=1 << 24, transcendentals=1 << 20
        ),
    )


def heads_placed(pieces, y):
    def kernel(at, p0, p1, p2, p3, query, kv, out):
        for k, piece in enumerate((p0, p1, p2, p3)):
            lanes = pl.ds(pl.multiple_of(lax.rem(at[0] + k, 4) * 128, 128), 128)
            for e in range(18):
                block = piece[:, 128 * e : 128 * (e + 1)].astype(F32)
                if e < 8:
                    query[:, e, lanes] = block
                elif e < 10:
                    kv[:, e - 8, lanes] = block
                else:
                    out[:, e - 10, lanes] = block

    shapes = [(64, 8, 512), (64, 2, 512), (64, 8, 512)]
    return on_grid(
        kernel,
        (y,),
        (1,),
        [pl.BlockSpec((64, 2432), lambda i, at: (0, 0))] * 4,
        [pl.BlockSpec(s, lambda i, at: (0, 0, 0)) for s in shapes],
        [jax.ShapeDtypeStruct(s, F32) for s in shapes],
        [],
        *pieces,
        cost=pl.CostEstimate(flops=0, bytes_accessed=0, transcendentals=0),
    )


def pick_of(routes):
    return (routes[:, :, None] == jnp.arange(EXPERTS, dtype=jnp.int32)[None, None, :]).astype(F32)


def pair_gates(logits, pick):
    chosen = jnp.sum(logits[:, None, :] * pick, axis=-1)
    weights = jnp.exp(chosen - jnp.max(chosen, axis=1, keepdims=True))
    return weights / jnp.sum(weights, axis=1, keepdims=True)


def gate_back(gates, grad_gates, pick):
    inner = gates * (grad_gates - jnp.sum(gates * grad_gates, axis=1, keepdims=True))
    return jnp.sum(inner[:, :, None] * pick, axis=1)


def norm_back(grad_normed, values, factor, gain):
    gain_part = jnp.sum(grad_normed * values * factor, axis=0)
    inner = grad_normed * gain
    grad_values = factor * inner - values * factor * factor * factor * jnp.mean(
        inner * values, axis=-1, keepdims=True
    )
    return grad_values, gain_part


def in_two(values):
    high = values.astype(BF)
    low = (values - high.astype(F32)).astype(BF)
    return jnp.concatenate([high, low], axis=1)


def widen(columns):
    return jnp.pad(columns, ((0, 0), (0, HEAD_SIZE - columns.shape[1])))


def body(
    tokens,
    cotangent,
    attn_gain,
    mlp_gain,
    attn_router,
    key_value_weight,
    query_matrix,
    output_matrix,
    mlp_router,
    gate_up_weight,
    down_weight,
    attn_routes,
    mlp_routes,
    priority,
    segments,
):
    z, y = lax.axis_index("dp"), lax.axis_index("y")
    core, x = lax.axis_index("core"), lax.axis_index("tensor")
    count = tokens.shape[0]
    quarter = count // 4
    capacity = 50
    room = 56
    sequence = 8 * count
    plane = ("y", "tensor")

    routers_own = jnp.concatenate([attn_router, mlp_router], axis=1)
    down_own = down_weight[0]
    down_before = lax.ppermute(down_own, "dp", UP)
    down_after = lax.ppermute(down_own, "dp", DOWN)
    mine = exchange(
        jnp.concatenate(
            [
                heads_first(query_matrix),
                heads_first(key_value_weight),
                jnp.broadcast_to(widen(routers_own), (4, 64, HEAD_SIZE)),
                heads_first(output_matrix),
            ],
            axis=2,
        ),
        "y",
    ).reshape(256, 2432)
    sent = jnp.concatenate([core_first(tokens), widen(attn_routes.astype(BF))], axis=1)
    arrived = spread(after(sent, mine), "y", 4).reshape(4 * count, MODEL_WIDTH + HEAD_SIZE)
    all_w = lax.all_gather(
        after(mine, (down_before, down_after)), ("dp", "core"), axis=0, tiled=True
    )
    values = arrived[:, :MODEL_WIDTH].astype(F32)
    routes = arrived[:, MODEL_WIDTH : MODEL_WIDTH + 2].astype(jnp.int32)
    gain_a = core_first(attn_gain.astype(F32))[0]
    gain_m = core_first(mlp_gain.astype(F32))[0]
    xn1 = (values * rms_scale(values) * gain_a).astype(BF)

    ranking = priority[0]
    pick_m = pick_of(mlp_routes)
    before = (ranking[None, :] < ranking[:, None]).astype(BF)
    earlier = jnp.dot(before, jnp.sum(pick_m, axis=1).astype(BF), preferred_element_type=F32)
    slots = jnp.sum(pick_m * earlier[:, None, :], axis=-1).astype(jnp.int32)
    kept = slots < capacity
    dest = jnp.where(kept, mlp_routes * room + slots, -1)
    lanes = jnp.arange(EXPERTS * room, dtype=jnp.int32)
    to_row = (dest.T[:, :, None] == lanes[None, None, :]).astype(BF)
    any_row = to_row[0] + to_row[1]
    both_rows = to_row.reshape(2 * count, EXPERTS * room)

    def to_experts(rows):
        columns = rows.shape[1]
        return exchange(rows.reshape(EXPERTS, room, columns), ("y", "core")).reshape(
            EXPERTS * room, columns
        )

    def with_other(j):
        others = jnp.concatenate([pick_m[:, 1 - j], jnp.ones((count, 1), F32)], axis=1)
        return jnp.concatenate([cotangent, widen(others.astype(BF))], axis=1)

    grad_sent = lax.dot_general(
        both_rows,
        jnp.concatenate([with_other(0), with_other(1)], axis=0),
        ROWS,
        preferred_element_type=F32,
    ).astype(BF)
    def places(half):
        blocks = 2 * jnp.arange(4, dtype=jnp.int32)[:, None] + half
        return (blocks * count + jnp.arange(count, dtype=jnp.int32)[None, :]).reshape(-1)

    inverse = 10000.0 ** (-(jnp.arange(HEAD_SIZE // 2).astype(F32) * 2.0 / HEAD_SIZE))
    angle = places(core).astype(F32)[:, None] * inverse[None, :]
    cosine = jnp.tile(jnp.cos(angle), (1, 2))
    sine = jnp.concatenate([-jnp.sin(angle), jnp.sin(angle)], axis=1)

    first = x * quarter
    cot_own = core_first(lax.dynamic_slice_in_dim(cotangent, first, quarter)).astype(F32)
    all_w, down_before, down_after, xn1, grad_sent, cosine, sine, cot_own = (
        lax.optimization_barrier(
            (all_w, down_before, down_after, xn1, grad_sent, cosine, sine, cot_own)
        )
    )
    in_w, out_w = all_w[:, :1408], all_w[:, 1408:]
    far_a = lax.ppermute(down_before[:, :256], "dp", UP)
    far_b = lax.ppermute(down_after[:, 256:], "dp", DOWN)
    down_pieces = (down_own, down_after, far_a, far_b, down_before)
    gate_up_own = gate_up_weight.reshape(4, 2, 64, 2816).transpose(1, 0, 2, 3).reshape(512, 2816)
    gate_up_w = lax.all_gather(after(gate_up_own, all_w), "dp", axis=0, tiled=True)
    router_m = in_w[:, 1288:1296]

    grad_landed = to_experts(grad_sent)

    of_sequence = lax.dynamic_slice_in_dim(segments, z * sequence, sequence).reshape(4, 2, count)

    def meta(half):
        documents = lax.dynamic_index_in_dim(of_sequence, half, 1, keepdims=False).reshape(-1)
        return jnp.stack([places(half), documents])

    key_meta = jnp.stack([meta(core), meta(1 - core)])
    row_meta = key_meta[0].T
    def swapped(rows):
        return jnp.concatenate([rows[:, 64:], rows[:, :64]], axis=1)

    half = 4 * count
    projected = jnp.dot(xn1, in_w, preferred_element_type=F32)
    key_raw = projected[:, 1024:1152]
    kv_own = jnp.concatenate(
        [key_raw * cosine + swapped(key_raw) * sine, projected[:, 1152:1280]], axis=1
    ).astype(BF)
    kv_other = lax.ppermute(kv_own, "core", SWAP)
    shared = (routes, cosine, sine, row_meta, key_meta)
    query, attended, totals, gate_a, mixed = in_vmem(
        forward_kernel,
        [
            jax.ShapeDtypeStruct((4, 2 * count, HEAD_SIZE), BF),
            jax.ShapeDtypeStruct((4, 2 * count, HEAD_SIZE), F32),
            jax.ShapeDtypeStruct((4, 2 * count, 1), F32),
            jax.ShapeDtypeStruct((half, 2), F32),
            jax.ShapeDtypeStruct((half, EXPERTS * HEAD_SIZE), BF),
        ],
        [],
        6 << 28,
        projected,
        kv_own,
        kv_other,
        *shared,
    )
    branch_part = lax.dot_general(mixed, out_w, LAST, preferred_element_type=F32).astype(BF)
    branch_part = after(branch_part, grad_landed)
    grad_received = grad_landed[:, :MODEL_WIDTH]
    branch = exchange(branch_part.reshape(16, quarter, MODEL_WIDTH), plane).astype(F32).sum(axis=0)

    own_values = lax.dynamic_slice_in_dim(values, y * count + first, quarter)
    own_factor = rms_scale(own_values)
    hidden = after(own_values, (far_a, far_b)) + branch
    factor_m = rms_scale(hidden)
    xn2_own = (hidden * factor_m * gain_m).astype(BF)
    xn2 = spread(xn2_own, "tensor", 4).reshape(count, MODEL_WIDTH)
    gate_m = pair_gates(jnp.dot(xn2, router_m, preferred_element_type=F32), pick_m)

    received = to_experts(
        lax.dot_general(any_row, xn2, ROWS, preferred_element_type=F32).astype(BF)
    )
    grad_act_raw = down_back(grad_received, down_pieces, z)
    received, grad_act_raw, hidden_last, gate_m = lax.optimization_barrier(
        (received, grad_act_raw, core_last(hidden), gate_m)
    )
    weight_m = gate_m * kept.astype(F32)
    activated, grad_pair, row_gate, grad_back = expert_middle(
        received,
        grad_landed[:, MODEL_WIDTH:],
        jnp.pad(router_m, ((0, 0), (0, 120))),
        gate_up_w,
        grad_act_raw,
        2 * y + core,
    )
    grad_back, late_pair, late_act = lax.optimization_barrier((grad_back, grad_pair, activated))
    grad_returned = to_experts(grad_back)
    grad_down_w = down_product(late_act, grad_received, row_gate)
    down_sum = lax.psum_scatter(grad_down_w, "dp", scatter_dimension=1, tiled=True)
    quarters = expert_quarters(late_act, down_pieces, z, x)
    grad_gate_up_w = gate_up_product(received, late_pair)
    gate_up_sum = lax.psum_scatter(grad_gate_up_w, "dp", scatter_dimension=0, tiled=True)
    late_any = after(any_row, (grad_down_w, quarters, grad_gate_up_w))
    expert_out = (
        quarters[0].astype(F32)
        + sum(from_ahead(quarters[4 - k], "tensor", k).astype(F32) for k in (1, 2, 3))
    ).astype(BF)

    grad_xn2_part = jnp.dot(
        late_any, grad_returned[:, :MODEL_WIDTH], preferred_element_type=F32
    ).astype(BF)
    row_gate_parts = grad_returned[:, MODEL_WIDTH : MODEL_WIDTH + 2]
    gate_m_part = jnp.sum(
        jnp.einsum("jtr,rd->tjd", to_row, row_gate_parts, preferred_element_type=F32), axis=2
    )
    shares = jnp.concatenate([grad_xn2_part, widen(in_two(gate_m_part))], axis=1)
    landed = (
        exchange(shares.reshape(4, quarter, MODEL_WIDTH + HEAD_SIZE), "tensor")
        .astype(F32)
        .sum(axis=0)
    )
    landed, expert_out = lax.optimization_barrier((landed, expert_out))
    returned = to_experts(expert_out)
    grad_gate_m = (
        landed[:, MODEL_WIDTH : MODEL_WIDTH + 2] + landed[:, MODEL_WIDTH + 2 : MODEL_WIDTH + 4]
    )

    def quarter_of(array, offset=0):
        return lax.dynamic_slice_in_dim(array, first + offset, quarter)

    grad_logit_m = gate_back(quarter_of(gate_m), grad_gate_m, quarter_of(pick_m))
    grad_xn2 = landed[:, :MODEL_WIDTH] + lax.dot_general(
        grad_logit_m, router_m.astype(F32), LAST, preferred_element_type=F32
    )
    grad_norm, gain_m_part = norm_back(grad_xn2, hidden, factor_m, gain_m)
    grad_hidden = cot_own + grad_norm
    grad_sent_back, returned = lax.optimization_barrier((grad_hidden.astype(BF), returned))
    grad_branch = spread(grad_sent_back, plane, 16).reshape(4 * count, MODEL_WIDTH)

    fetched = jnp.einsum("jtr,rd->jtd", to_row, returned, preferred_element_type=F32)
    moe_part = jnp.sum(weight_m.T[:, :, None] * fetched, axis=0).astype(BF)
    width = down_own.shape[0]
    grad_branch, moe_part = lax.optimization_barrier((grad_branch, moe_part))
    moe_pieces = exchange(moe_part.reshape(4, quarter, MODEL_WIDTH // 4), "tensor")

    grad_mixed = jnp.dot(grad_branch, out_w, preferred_element_type=F32)
    grad_q_all, grad_logit_a, grad_kv_own, grad_kv_give = in_vmem(
        backward_kernel,
        [
            jax.ShapeDtypeStruct((half, EXPERTS * HEAD_SIZE), BF),
            jax.ShapeDtypeStruct((half, HEAD_SIZE), BF),
            jax.ShapeDtypeStruct((half, 2 * HEAD_SIZE), F32),
            jax.ShapeDtypeStruct((half, 2 * HEAD_SIZE), BF),
        ],
        [pltpu.VMEM((2, half, 2 * HEAD_SIZE), F32)],
        40 << 28,
        grad_mixed,
        query,
        kv_own,
        kv_other,
        attended,
        totals,
        gate_a,
        *shared,
    )
    gate_up_grad = (
        gate_up_sum.reshape(2, 4, 64, 2816)
        .transpose(1, 0, 2, 3)
        .reshape(1, 512, 2, width)
        .astype(F32)
    )
    out_pairs = [(grad_branch, mixed)]
    out_give = lax.ppermute(give_terms(out_pairs, z, core), "core", SWAP)
    kv_back, moe_pieces = lax.optimization_barrier(
        (lax.ppermute(grad_kv_give, "core", SWAP), moe_pieces)
    )
    moe = moe_pieces.transpose(1, 0, 2).reshape(quarter, MODEL_WIDTH).astype(F32)
    output_own = (hidden_last + moe).astype(BF)
    own_grad_kv = grad_kv_own + kv_back.astype(F32)
    grad_key = own_grad_kv[:, :HEAD_SIZE]
    grad_kv = jnp.concatenate(
        [grad_key * cosine - swapped(grad_key) * sine, own_grad_kv[:, HEAD_SIZE:]], axis=1
    ).astype(BF)
    grad_in = jnp.concatenate([grad_q_all, grad_kv, grad_logit_a], axis=1)
    grad_xn1_part = lax.dot_general(grad_in, in_w, LAST, preferred_element_type=F32).astype(BF)
    gain_row = jnp.pad(gain_m_part[None].astype(BF), ((0, 7), (0, 0)))
    lane = jnp.arange(1408, dtype=jnp.int32)[None, :]
    router_cols = jnp.pad(grad_logit_m.astype(BF), ((0, 0), (1288, 112)))
    gain_cols = ((jnp.arange(8)[:, None] == 0) & (lane == 1296)).astype(BF)
    in_pairs = [
        (xn1, after(grad_in, grad_xn1_part)),
        (
            jnp.concatenate([xn2_own, gain_row], axis=0),
            jnp.concatenate([router_cols, gain_cols], axis=0),
        ),
    ]
    in_give = lax.ppermute(give_terms(in_pairs, z, core), "core", SWAP)
    out_own, *out_rest = keep_terms(out_pairs, after(out_give, grad_xn1_part), z, core)
    out_ahead, out_back = ring_first(*out_rest, "dp")
    in_own_rows, *in_rest = keep_terms(in_pairs, in_give, z, core)
    in_ahead, in_back = ring_first(*in_rest, "dp")
    out_sum = ring_second(after(out_own, gate_up_grad), out_ahead, out_back, "dp").astype(BF)
    landed_raw = exchange(grad_xn1_part.reshape(16, quarter, MODEL_WIDTH), plane)
    landed_raw, in_ahead, in_back, out_sum, down_sum = lax.optimization_barrier(
        (landed_raw, in_ahead, in_back, out_sum, down_sum)
    )
    in_sum = ring_second(in_own_rows, in_ahead, in_back, "dp").astype(BF)
    landed_a = landed_raw.astype(F32).sum(axis=0)
    grad_x_norm, _ = norm_back(landed_a, own_values, own_factor, gain_a)
    columns = jnp.arange(1408, dtype=jnp.int32)[None, :]
    gain_a_part = jnp.sum(
        jnp.where(columns < 1288, in_sum.astype(F32) * mine[:, :1408].astype(F32), 0.0),
        axis=1,
        keepdims=True,
    )
    small_part = jnp.where(columns[:, :128] == 17, gain_a_part, in_sum[:, 1280:].astype(F32))
    gain_rows = lax.dynamic_slice_in_dim(attn_gain.astype(F32), z * 512 + y * 128 + core * 64, 64)

    ends = jnp.concatenate(
        [output_own, core_last((grad_hidden + grad_x_norm).astype(BF))], axis=1
    )
    both_sums = jnp.concatenate(
        [in_sum[:, :1280], out_sum, small_part.astype(BF)], axis=1
    ).reshape(4, 64, 2432)
    y_parts = send_direct(both_sums, "y")
    _, *y_parts = lax.optimization_barrier((ends, *y_parts))
    both_ends = spread(ends, "tensor", 4)
    small_y = sum(p[:, 2304:].astype(F32) for p in y_parts).astype(BF)
    small_y = after(small_y, both_ends)
    small_sum = small_y.astype(F32) + sum(
        from_ahead(small_y, "tensor", k).astype(F32) for k in (1, 2, 3)
    )
    down_grad = down_sum.astype(F32)[None]
    both_ends = both_ends.reshape(count, 2 * MODEL_WIDTH)
    output, input_grad = both_ends[:, :MODEL_WIDTH], both_ends[:, MODEL_WIDTH:]
    query_grad, kv_grad, out_grad = heads_placed(y_parts, y)
    return (
        output,
        input_grad,
        small_sum[:, 17] / gain_rows,
        small_sum[:, 16],
        small_sum[:, :8],
        kv_grad,
        query_grad,
        out_grad,
        small_sum[:, 8:16],
        gate_up_grad,
        down_grad,
    )


def solution(mesh):
    split = Mesh(mesh.devices.reshape(4, 4, 2, 4), ("dp", "y", "core", "tensor"))
    rows = ("dp", "y", "core")
    expert = ("y", "core")
    placed = (
        P(rows, None),
        P(rows, None),
        P(),
        P(),
        P(rows, None),
        P(rows, None, "tensor"),
        P(rows, None, "tensor"),
        P(rows, None, "tensor"),
        P(rows, None),
        P(expert, "dp", None, "tensor"),
        P(expert, "tensor", "dp"),
        P(rows, None),
        P(rows, None),
        P(rows, None),
        P(),
    )
    return jax.shard_map(
        body,
        mesh=split,
        in_specs=placed,
        out_specs=(
            P(rows, None),
            P(rows, None),
            P(rows),
            P(rows),
            P(rows, None),
            P(rows, None, "tensor"),
            P(rows, None, "tensor"),
            P(rows, None, "tensor"),
            P(rows, None),
            P(expert, "dp", None, "tensor"),
            P(expert, "tensor", "dp"),
        ),
        check_vma=False,
    )
```

```python
import jax
import jax.numpy as jnp
from jax import lax
from jax.experimental import pallas as pl
from jax.experimental.pallas import tpu as pltpu
from jax.sharding import Mesh
from jax.sharding import PartitionSpec as P

MODEL_WIDTH = 2048
HEAD_SIZE = 128
EXPERTS = 8
WINDOW = 1024
NORM_EPS = 1e-06
BF = jnp.bfloat16
F32 = jnp.float32
ROWS = (((0,), (0,)), ((), ()))
LAST = (((1,), (1,)), ((), ()))
UP = [(0, 1), (1, 2), (2, 3), (3, 0)]
DOWN = [(0, 3), (1, 0), (2, 1), (3, 2)]
SWAP = [(0, 1), (1, 0)]


def exchange(blocks, axis):
    return lax.all_to_all(blocks, axis, split_axis=0, concat_axis=0, tiled=True)


def spread(block, axis, count):
    return exchange(jnp.broadcast_to(block, (count, *block.shape)), axis)


def from_ahead(block, axis, steps):
    return lax.ppermute(block, axis, [(i, (i - steps) % 4) for i in range(4)])


def in_order(pieces, first):
    both = jnp.stack(pieces + pieces[:3])
    return lax.dynamic_slice_in_dim(both, lax.rem(4 - first, 4), 4)


def pick_block(blocks, index):
    return lax.dynamic_index_in_dim(blocks, lax.rem(index, 4), 0, keepdims=False)


def send_direct(blocks, axis):
    me = lax.axis_index(axis)
    return [pick_block(blocks, me)] + [
        from_ahead(pick_block(blocks, me + 4 - k), axis, k) for k in (1, 2, 3)
    ]


def heads_first(shard):
    columns = shard.shape[1] * HEAD_SIZE
    return shard.reshape(64, -1, 4, HEAD_SIZE).transpose(2, 0, 1, 3).reshape(4, 64, columns)


def after(value, other):
    return lax.optimization_barrier((value, other))[0]


def core_first(rows):
    return rows.reshape(-1, 4, 4, 2, 64).transpose(0, 1, 3, 2, 4).reshape(-1, MODEL_WIDTH)


def core_last(rows):
    return rows.reshape(-1, 4, 2, 4, 64).transpose(0, 1, 3, 2, 4).reshape(-1, MODEL_WIDTH)


def ring_first(ahead, low, high, back, axis):
    low = lax.ppermute(low, axis, UP)
    high = lax.ppermute(high, axis, DOWN)
    half = low.shape[0]
    ahead = jnp.concatenate([(ahead[:half].astype(F32) + low.astype(F32)).astype(BF), ahead[half:]])
    back = jnp.concatenate([back[:half], (back[half:].astype(F32) + high.astype(F32)).astype(BF)])
    return ahead, back


def ring_second(own, ahead, back, axis):
    return (
        own.astype(F32)
        + lax.ppermute(ahead, axis, UP).astype(F32)
        + lax.ppermute(back, axis, DOWN).astype(F32)
    )


def rms_scale(values):
    return lax.rsqrt(jnp.mean(values * values, axis=-1, keepdims=True) + NORM_EPS)


def turn(heads, cosine, sine):
    first, second = heads[..., :64], heads[..., 64:]
    return jnp.concatenate([first * cosine - second * sine, second * cosine + first * sine], axis=-1)


EXTENTS = (256, 384, 512, 640)
SCALE = HEAD_SIZE**-0.5


def masked_scores(query, key, row_meta, key_meta):
    raw = lax.dot_general(query, key, LAST, preferred_element_type=F32) * SCALE
    gap = row_meta[:, 0:1] - key_meta[0:1]
    allowed = (gap >= 0) & (gap < WINDOW) & (row_meta[:, 1:2] == key_meta[1:2])
    return jnp.where(jnp.concatenate([allowed, allowed], axis=0), raw, -1e30)


def forward_kernel(proj, own, other, routes, cosine, sine, row_meta, key_meta, *outs):
    query_out, attended_out, total_out, gates_out, mixed_out = outs
    count = proj.shape[0] // 4
    for i in range(4):
        rows = pl.ds(count * i, count)
        extent = EXTENTS[i]
        logits = proj[rows, 1280:1288]
        lane = lax.broadcasted_iota(jnp.int32, (count, EXPERTS), 1)
        named = [routes[rows, 0:1], routes[rows, 1:2]]
        chosen = [jnp.sum(jnp.where(lane == n, logits, 0.0), axis=1, keepdims=True) for n in named]
        top = jnp.maximum(chosen[0], chosen[1])
        power = [jnp.exp(c - top) for c in chosen]
        gates = [p / (power[0] + power[1]) for p in power]
        gates_out[rows, 0:1] = gates[0]
        gates_out[rows, 1:2] = gates[1]
        cos, sin = cosine[rows, :], sine[rows, :]
        picked = []
        for n in named:
            q = jnp.zeros((count, HEAD_SIZE), F32)
            for e in range(EXPERTS):
                q = q + jnp.where(n == e, proj[rows, HEAD_SIZE * e : HEAD_SIZE * (e + 1)], 0.0)
            picked.append(q * cos + pltpu.roll(q, 64, 1) * sin)
        query = jnp.concatenate(picked, axis=0).astype(BF)
        query_out[i] = query
        halves = (own, other)
        scores = [
            masked_scores(
                query, h[:extent, :HEAD_SIZE], row_meta[rows, :], key_meta[k, :, :extent]
            )
            for k, h in enumerate(halves)
        ]
        row_max = jnp.maximum(
            jnp.max(scores[0], axis=1, keepdims=True), jnp.max(scores[1], axis=1, keepdims=True)
        )
        weights = [jnp.exp(s - row_max) for s in scores]
        total = jnp.sum(weights[0], axis=1, keepdims=True) + jnp.sum(weights[1], axis=1, keepdims=True)
        inverse = 1.0 / total
        attended = sum(
            jnp.dot((w * inverse).astype(BF), h[:extent, HEAD_SIZE:], preferred_element_type=F32)
            for w, h in zip(weights, halves)
        )
        attended_out[i] = attended
        total_out[i] = row_max + jnp.log(total)
        for e in range(EXPERTS):
            mixed_out[rows, HEAD_SIZE * e : HEAD_SIZE * (e + 1)] = (
                jnp.where(named[0] == e, gates[0], 0.0) * attended[:count]
                + jnp.where(named[1] == e, gates[1], 0.0) * attended[count:]
            ).astype(BF)


def backward_kernel(
    grad_mixed, query_in, own, other, attended_in, total_in, gates_in, routes, cosine, sine, row_meta, key_meta, *outs
):
    grad_query_out, grad_logit_out, grad_own_out, grad_other_out, sums = outs
    count = grad_mixed.shape[0] // 4
    sums[...] = jnp.zeros_like(sums)
    for i in range(4):
        rows = pl.ds(count * i, count)
        extent = EXTENTS[i]
        named = [routes[rows, 0:1], routes[rows, 1:2]]
        gates = [gates_in[rows, 0:1], gates_in[rows, 1:2]]
        cos, sin = cosine[rows, :], sine[rows, :]
        attended = attended_in[i]
        picked = []
        for n in named:
            g = jnp.zeros((count, HEAD_SIZE), F32)
            for e in range(EXPERTS):
                g = g + jnp.where(n == e, grad_mixed[rows, HEAD_SIZE * e : HEAD_SIZE * (e + 1)], 0.0)
            picked.append(g)
        gate_grads = [
            jnp.sum(p * attended[count * j : count * (j + 1)], axis=1, keepdims=True)
            for j, p in enumerate(picked)
        ]
        level = gates[0] * gate_grads[0] + gates[1] * gate_grads[1]
        lane = lax.broadcasted_iota(jnp.int32, (count, HEAD_SIZE), 1)
        grad_logit_out[rows, :] = sum(
            jnp.where(lane == n, g * (d - level), 0.0) for n, g, d in zip(named, gates, gate_grads)
        ).astype(BF)
        grad_attended = jnp.concatenate(
            [gates[0] * picked[0], gates[1] * picked[1]], axis=0
        ).astype(BF)
        query = query_in[i]
        total = total_in[i]
        probs, grad_probs = [], []
        delta = jnp.zeros((2 * count, 1), F32)
        for k, h in enumerate((own, other)):
            score = masked_scores(
                query, h[:extent, :HEAD_SIZE], row_meta[rows, :], key_meta[k, :, :extent]
            )
            prob = jnp.exp(score - total)
            grad_prob = lax.dot_general(
                grad_attended, h[:extent, HEAD_SIZE:], LAST, preferred_element_type=F32
            )
            delta = delta + jnp.sum(prob * grad_prob, axis=1, keepdims=True)
            probs.append(prob)
            grad_probs.append(grad_prob)
        grad_query = jnp.zeros((2 * count, HEAD_SIZE), F32)
        for k, h in enumerate((own, other)):
            grad_score = (probs[k] * (grad_probs[k] - delta)).astype(BF)
            grad_query = grad_query + jnp.dot(
                grad_score, h[:extent, :HEAD_SIZE], preferred_element_type=F32
            )
            sums[k, :extent, :HEAD_SIZE] += (
                lax.dot_general(grad_score, query, ROWS, preferred_element_type=F32) * SCALE
            )
            sums[k, :extent, HEAD_SIZE:] += lax.dot_general(
                probs[k].astype(BF), grad_attended, ROWS, preferred_element_type=F32
            )
        grad_query = grad_query * SCALE
        turned = [
            g * cos - pltpu.roll(g, 64, 1) * sin for g in (grad_query[:count], grad_query[count:])
        ]
        for e in range(EXPERTS):
            grad_query_out[rows, HEAD_SIZE * e : HEAD_SIZE * (e + 1)] = (
                jnp.where(named[0] == e, turned[0], 0.0) + jnp.where(named[1] == e, turned[1], 0.0)
            ).astype(BF)
    grad_own_out[...] = sums[0]
    grad_other_out[...] = sums[1].astype(BF)


def in_vmem(kernel, outs, scratch, flops, *args):
    spec = pl.BlockSpec(memory_space=pltpu.VMEM)
    moved = sum(a.size * a.dtype.itemsize for a in args)
    return pl.pallas_call(
        kernel,
        out_shape=outs,
        in_specs=[spec] * len(args),
        out_specs=[spec] * len(outs),
        scratch_shapes=scratch,
        compiler_params=pltpu.CompilerParams(vmem_limit_bytes=40 * 1024 * 1024),
        cost_estimate=pl.CostEstimate(flops=flops, bytes_accessed=moved, transcendentals=1 << 20),
    )(*args)


SOME = pl.CostEstimate(flops=1 << 35, bytes_accessed=1 << 27, transcendentals=0)


def on_grid(kernel, scalars, grid, in_specs, out_specs, outs, scratch, *args, cost=SOME):
    return pl.pallas_call(
        kernel,
        out_shape=outs,
        grid_spec=pltpu.PrefetchScalarGridSpec(
            num_scalar_prefetch=1,
            grid=grid,
            in_specs=in_specs,
            out_specs=out_specs,
            scratch_shapes=scratch,
        ),
        compiler_params=pltpu.CompilerParams(vmem_limit_bytes=48 * 1024 * 1024),
        cost_estimate=cost,
    )(jnp.stack(scalars).astype(jnp.int32), *args)


def give_terms(pairs, place, core):
    columns = pairs[0][1].shape[1]

    def kernel(at, *refs):
        out = refs[-1]
        total = sum(
            lax.dot_general(refs[j][...], refs[j + 1][...], ROWS, preferred_element_type=F32)
            for j in range(0, len(refs) - 1, 2)
        )
        out[0] = total.astype(BF)

    specs = []
    for tall, terms in pairs:
        specs.append(pl.BlockSpec((tall.shape[0], 256), lambda i, at: (0, 2 * i + 1 - at[1])))
        specs.append(pl.BlockSpec(terms.shape, lambda i, at: (0, 0)))
    return on_grid(
        kernel,
        (place, core),
        (4,),
        specs,
        pl.BlockSpec((1, 256, columns), lambda i, at: (i, 0, 0)),
        jax.ShapeDtypeStruct((4, 256, columns), BF),
        [],
        *[a for pair in pairs for a in pair],
    )


def keep_terms(pairs, landed, place, core):
    columns = pairs[0][1].shape[1]
    count = 2 * len(pairs)

    def kernel(at, *refs):
        more, own, ahead, low, high, back = refs[count:]
        total = sum(
            lax.dot_general(refs[j][...], refs[j + 1][...], ROWS, preferred_element_type=F32)
            for j in range(0, count, 2)
        )
        total = (total.astype(BF).astype(F32) + more[0].astype(F32)).astype(BF)
        step = pl.program_id(0)

        @pl.when(step == 0)
        def _():
            own[...] = total

        @pl.when(step == 1)
        def _():
            ahead[...] = total

        @pl.when(step == 2)
        def _():
            low[...] = total[:128]
            high[...] = total[128:]

        @pl.when(step == 3)
        def _():
            back[...] = total

    def whole(rows):
        return pl.BlockSpec((rows, columns), lambda i, at: (0, 0))

    specs = []
    for tall, terms in pairs:
        specs.append(
            pl.BlockSpec(
                (tall.shape[0], 256), lambda i, at: (0, 2 * lax.rem(at[0] + i, 4) + at[1])
            )
        )
        specs.append(pl.BlockSpec(terms.shape, lambda i, at: (0, 0)))
    specs.append(pl.BlockSpec((1, 256, columns), lambda i, at: (lax.rem(at[0] + i, 4), 0, 0)))
    return on_grid(
        kernel,
        (place, core),
        (4,),
        specs,
        [whole(256), whole(256), whole(128), whole(128), whole(256)],
        [jax.ShapeDtypeStruct((r, columns), BF) for r in (256, 256, 128, 128, 256)],
        [],
        *[a for pair in pairs for a in pair],
        landed,
    )


def gate_up_product(rows, pair):
    depth, width = pair.shape[1:]

    def kernel(at, left, right, out):
        for half in range(2):
            out[:, width * half : width * (half + 1)] = lax.dot_general(
                left[...], right[half], ROWS, preferred_element_type=F32
            ).astype(BF)

    return on_grid(
        kernel,
        (jnp.int32(0),),
        (8,),
        [
            pl.BlockSpec((depth, 256), lambda i, at: (0, i)),
            pl.BlockSpec((2, depth, width), lambda i, at: (0, 0, 0)),
        ],
        pl.BlockSpec((256, 2 * width), lambda i, at: (i, 0)),
        jax.ShapeDtypeStruct((MODEL_WIDTH, 2 * width), BF),
        [],
        rows,
        pair,
    )


def down_product(activated, grads, gate):
    def kernel(at, left, right, scale, out):
        scaled = (scale[...] * right[...].astype(F32)).astype(BF)
        out[...] = lax.dot_general(left[...], scaled, ROWS, preferred_element_type=F32).astype(BF)

    depth, width = activated.shape
    return on_grid(
        kernel,
        (jnp.int32(0),),
        (4,),
        [
            pl.BlockSpec((depth, width), lambda i, at: (0, 0)),
            pl.BlockSpec((depth, 512), lambda i, at: (0, i)),
            pl.BlockSpec((depth, 1), lambda i, at: (0, 0)),
        ],
        pl.BlockSpec((width, 512), lambda i, at: (0, i)),
        jax.ShapeDtypeStruct((width, MODEL_WIDTH), BF),
        [],
        activated,
        grads,
        gate,
    )


def down_back(grads, pieces, place):
    def kernel(at, left, own, ahead, far_a, far_b, back, out):
        total = None
        for shift, start, piece in (
            (0, 0, own), (1, 0, ahead), (2, 0, far_a), (2, 256, far_b), (3, 0, back)
        ):
            size = piece.shape[1]
            lanes = pl.ds(pl.multiple_of(lax.rem(at[0] + shift, 4) * 512 + start, 256), size)
            term = lax.dot_general(left[:, lanes], piece[...], LAST, preferred_element_type=F32)
            total = term if total is None else total + term
        out[...] = total

    depth, width = grads.shape[0], pieces[0].shape[0]
    return on_grid(
        kernel,
        (place,),
        (width // 128,),
        [pl.BlockSpec(grads.shape, lambda i, at: (0, 0))]
        + [pl.BlockSpec((128, p.shape[1]), lambda i, at: (i, 0)) for p in pieces],
        pl.BlockSpec((depth, 128), lambda i, at: (0, i)),
        jax.ShapeDtypeStruct((depth, width), F32),
        [],
        grads,
        *pieces,
    )


def expert_quarters(activated, pieces, place, x):
    def kernel(at, left, own, ahead, far_a, far_b, back, out):
        step = pl.program_id(0)
        for shift, refs in enumerate(((own,), (ahead,), (far_a, far_b), (back,))):

            @pl.when(step == shift)
            def _():
                terms = [jnp.dot(left[...], r[...], preferred_element_type=F32) for r in refs]
                out[0] = jnp.concatenate(terms, axis=1).astype(BF)

    depth = activated.shape[0]
    return on_grid(
        kernel,
        (place, x),
        (4,),
        [pl.BlockSpec(a.shape, lambda i, at: (0, 0)) for a in (activated, *pieces)],
        pl.BlockSpec((1, depth, 512), lambda i, at: (lax.rem(at[0] + i + 4 - at[1], 4), 0, 0)),
        jax.ShapeDtypeStruct((4, depth, 512), BF),
        [],
        activated,
        *pieces,
    )


def expert_middle(rows, marks, router, gate_up_w, grad_act, expert):
    depth, width = grad_act.shape
    blocks = width // 128

    def kernel(
        at, rows_ref, marks_ref, router_ref, gate_ref, up_ref, flat_ref, grad_ref,
        act_out, pair_out, gate_out, back_out, pair_all, row_gate, row_grad,
    ):
        step = pl.program_id(0)
        lane = lax.broadcasted_iota(jnp.int32, (depth, 128), 1)

        @pl.when(step == 0)
        def _():
            logits = jnp.dot(rows_ref[...], router_ref[...], preferred_element_type=F32)
            marks_f = marks_ref[...].astype(F32)
            own = jnp.sum(jnp.where(lane == at[0], logits, 0.0), axis=1, keepdims=True)
            other = jnp.sum(jnp.where(lane < 8, logits * marks_f, 0.0), axis=1, keepdims=True)
            valid = jnp.sum(jnp.where(lane == 8, marks_f, 0.0), axis=1, keepdims=True)
            top = jnp.maximum(own, other)
            power = jnp.exp(own - top)
            row_gate[...] = valid * power / (power + jnp.exp(other - top))
            gate_out[...] = row_gate[...]
            row_grad[...] = jnp.zeros_like(row_grad)

        @pl.when(step < blocks)
        def _():
            both = jnp.concatenate([gate_ref[...], up_ref[...]], axis=1)
            gate_up = jnp.dot(rows_ref[...], both, preferred_element_type=F32)
            gate, up = gate_up[:, :128], gate_up[:, 128:]
            sigmoid = 1.0 / (1.0 + jnp.exp(-gate))
            silu = gate * sigmoid
            act = (silu * up).astype(BF)
            raw = grad_ref[...]
            grad = row_gate[...] * raw
            grad_gate = (grad * up * sigmoid * (1.0 + gate * (1.0 - sigmoid))).astype(BF)
            grad_up = (grad * silu).astype(BF)
            act_out[...] = act
            pair_out[0] = grad_gate
            pair_out[1] = grad_up
            at_lane = pl.multiple_of(step * 128, 128)
            pair_all[:, pl.ds(at_lane, 128)] = grad_gate
            pair_all[:, pl.ds(at_lane + width, 128)] = grad_up
            row_grad[...] += jnp.sum(act.astype(F32) * raw, axis=1, keepdims=True)

        @pl.when(step >= blocks)
        def _():
            back_lane = pl.multiple_of((step - blocks) * 512, 512)
            back_out[:, pl.ds(back_lane, 512)] = lax.dot_general(
                pair_all[...], flat_ref[...], LAST, preferred_element_type=F32
            ).astype(BF)

        @pl.when(step == blocks + 3)
        def _():
            high = row_grad[...].astype(BF).astype(F32)
            low = row_grad[...] - high
            back_out[:, MODEL_WIDTH:] = jnp.where(
                lane == 0, high, jnp.where(lane == 1, low, 0.0)
            ).astype(BF)

    def first(i):
        return jnp.minimum(i, blocks - 1)

    def second(i):
        return jnp.clip(i - blocks, 0, 3)

    return on_grid(
        kernel,
        (expert,),
        (blocks + 4,),
        [
            pl.BlockSpec((depth, MODEL_WIDTH), lambda i, at: (0, 0)),
            pl.BlockSpec((depth, 128), lambda i, at: (0, 0)),
            pl.BlockSpec((MODEL_WIDTH, 128), lambda i, at: (0, 0)),
            pl.BlockSpec((MODEL_WIDTH, 128), lambda i, at: (0, first(i))),
            pl.BlockSpec((MODEL_WIDTH, 128), lambda i, at: (0, blocks + first(i))),
            pl.BlockSpec((512, 2 * width), lambda i, at: (second(i), 0)),
            pl.BlockSpec((depth, 128), lambda i, at: (0, first(i))),
        ],
        [
            pl.BlockSpec((depth, 128), lambda i, at: (0, first(i))),
            pl.BlockSpec((2, depth, 128), lambda i, at: (0, 0, first(i))),
            pl.BlockSpec((depth, 1), lambda i, at: (0, 0)),
            pl.BlockSpec((depth, MODEL_WIDTH + 128), lambda i, at: (0, 0)),
        ],
        [
            jax.ShapeDtypeStruct((depth, width), BF),
            jax.ShapeDtypeStruct((2, depth, width), BF),
            jax.ShapeDtypeStruct((depth, 1), F32),
            jax.ShapeDtypeStruct((depth, MODEL_WIDTH + 128), BF),
        ],
        [
            pltpu.VMEM((depth, 2 * width), BF),
            pltpu.VMEM((depth, 1), F32),
            pltpu.VMEM((depth, 1), F32),
        ],
        rows,
        marks,
        router,
        gate_up_w,
        gate_up_w,
        gate_up_w,
        grad_act,
        cost=pl.CostEstimate(
            flops=8 * depth * MODEL_WIDTH * width, bytes_accessed=1 << 24, transcendentals=1 << 20
        ),
    )


def heads_placed(pieces, y):
    def kernel(at, p0, p1, p2, p3, query, kv, out):
        for k, piece in enumerate((p0, p1, p2, p3)):
            lanes = pl.ds(pl.multiple_of(lax.rem(at[0] + k, 4) * 128, 128), 128)
            for e in range(18):
                block = piece[:, 128 * e : 128 * (e + 1)].astype(F32)
                if e < 8:
                    query[:, e, lanes] = block
                elif e < 10:
                    kv[:, e - 8, lanes] = block
                else:
                    out[:, e - 10, lanes] = block

    shapes = [(64, 8, 512), (64, 2, 512), (64, 8, 512)]
    return on_grid(
        kernel,
        (y,),
        (1,),
        [pl.BlockSpec((64, 2432), lambda i, at: (0, 0))] * 4,
        [pl.BlockSpec(s, lambda i, at: (0, 0, 0)) for s in shapes],
        [jax.ShapeDtypeStruct(s, F32) for s in shapes],
        [],
        *pieces,
        cost=pl.CostEstimate(flops=0, bytes_accessed=0, transcendentals=0),
    )


def pick_of(routes):
    return (routes[:, :, None] == jnp.arange(EXPERTS, dtype=jnp.int32)[None, None, :]).astype(F32)


def pair_gates(logits, pick):
    chosen = jnp.sum(logits[:, None, :] * pick, axis=-1)
    weights = jnp.exp(chosen - jnp.max(chosen, axis=1, keepdims=True))
    return weights / jnp.sum(weights, axis=1, keepdims=True)


def gate_back(gates, grad_gates, pick):
    inner = gates * (grad_gates - jnp.sum(gates * grad_gates, axis=1, keepdims=True))
    return jnp.sum(inner[:, :, None] * pick, axis=1)


def norm_back(grad_normed, values, factor, gain):
    gain_part = jnp.sum(grad_normed * values * factor, axis=0)
    inner = grad_normed * gain
    grad_values = factor * inner - values * factor * factor * factor * jnp.mean(
        inner * values, axis=-1, keepdims=True
    )
    return grad_values, gain_part


def in_two(values):
    high = values.astype(BF)
    low = (values - high.astype(F32)).astype(BF)
    return jnp.concatenate([high, low], axis=1)


def widen(columns):
    return jnp.pad(columns, ((0, 0), (0, HEAD_SIZE - columns.shape[1])))


def body(
    tokens,
    cotangent,
    attn_gain,
    mlp_gain,
    attn_router,
    key_value_weight,
    query_matrix,
    output_matrix,
    mlp_router,
    gate_up_weight,
    down_weight,
    attn_routes,
    mlp_routes,
    priority,
    segments,
):
    z, y = lax.axis_index("dp"), lax.axis_index("y")
    core, x = lax.axis_index("core"), lax.axis_index("tensor")
    count = tokens.shape[0]
    quarter = count // 4
    capacity = 50
    room = 56
    sequence = 8 * count
    plane = ("y", "tensor")

    routers_own = jnp.concatenate([attn_router, mlp_router], axis=1)
    down_own = down_weight[0]
    down_before = lax.ppermute(down_own, "dp", UP)
    down_after = lax.ppermute(down_own, "dp", DOWN)
    mine = exchange(
        jnp.concatenate(
            [
                heads_first(query_matrix),
                heads_first(key_value_weight),
                jnp.broadcast_to(widen(routers_own), (4, 64, HEAD_SIZE)),
                heads_first(output_matrix),
            ],
            axis=2,
        ),
        "y",
    ).reshape(256, 2432)
    sent = jnp.concatenate([core_first(tokens), widen(attn_routes.astype(BF))], axis=1)
    arrived = spread(after(sent, mine), "y", 4).reshape(4 * count, MODEL_WIDTH + HEAD_SIZE)
    all_w = lax.all_gather(
        after(mine, (down_before, down_after)), ("dp", "core"), axis=0, tiled=True
    )
    values = arrived[:, :MODEL_WIDTH].astype(F32)
    routes = arrived[:, MODEL_WIDTH : MODEL_WIDTH + 2].astype(jnp.int32)
    gain_a = core_first(attn_gain.astype(F32))[0]
    gain_m = core_first(mlp_gain.astype(F32))[0]
    xn1 = (values * rms_scale(values) * gain_a).astype(BF)

    ranking = priority[0]
    pick_m = pick_of(mlp_routes)
    before = (ranking[None, :] < ranking[:, None]).astype(BF)
    earlier = jnp.dot(before, jnp.sum(pick_m, axis=1).astype(BF), preferred_element_type=F32)
    slots = jnp.sum(pick_m * earlier[:, None, :], axis=-1).astype(jnp.int32)
    kept = slots < capacity
    dest = jnp.where(kept, mlp_routes * room + slots, -1)
    lanes = jnp.arange(EXPERTS * room, dtype=jnp.int32)
    to_row = (dest.T[:, :, None] == lanes[None, None, :]).astype(BF)
    any_row = to_row[0] + to_row[1]
    both_rows = to_row.reshape(2 * count, EXPERTS * room)

    def to_experts(rows):
        columns = rows.shape[1]
        return exchange(rows.reshape(EXPERTS, room, columns), ("y", "core")).reshape(
            EXPERTS * room, columns
        )

    def with_other(j):
        others = jnp.concatenate([pick_m[:, 1 - j], jnp.ones((count, 1), F32)], axis=1)
        return jnp.concatenate([cotangent, widen(others.astype(BF))], axis=1)

    grad_sent = lax.dot_general(
        both_rows,
        jnp.concatenate([with_other(0), with_other(1)], axis=0),
        ROWS,
        preferred_element_type=F32,
    ).astype(BF)
    def places(half):
        blocks = 2 * jnp.arange(4, dtype=jnp.int32)[:, None] + half
        return (blocks * count + jnp.arange(count, dtype=jnp.int32)[None, :]).reshape(-1)

    inverse = 10000.0 ** (-(jnp.arange(HEAD_SIZE // 2).astype(F32) * 2.0 / HEAD_SIZE))
    angle = places(core).astype(F32)[:, None] * inverse[None, :]
    cosine = jnp.tile(jnp.cos(angle), (1, 2))
    sine = jnp.concatenate([-jnp.sin(angle), jnp.sin(angle)], axis=1)

    first = x * quarter
    cot_own = core_first(lax.dynamic_slice_in_dim(cotangent, first, quarter)).astype(F32)
    all_w, down_before, down_after, xn1, grad_sent, cosine, sine, cot_own = (
        lax.optimization_barrier(
            (all_w, down_before, down_after, xn1, grad_sent, cosine, sine, cot_own)
        )
    )
    in_w, out_w = all_w[:, :1408], all_w[:, 1408:]
    far_a = lax.ppermute(down_before[:, :256], "dp", UP)
    far_b = lax.ppermute(down_after[:, 256:], "dp", DOWN)
    down_pieces = (down_own, down_after, far_a, far_b, down_before)
    gate_up_own = gate_up_weight.reshape(4, 2, 64, 2816).transpose(1, 0, 2, 3).reshape(512, 2816)
    gate_up_w = lax.all_gather(after(gate_up_own, all_w), "dp", axis=0, tiled=True)
    router_m = in_w[:, 1288:1296]

    grad_landed = to_experts(grad_sent)

    of_sequence = lax.dynamic_slice_in_dim(segments, z * sequence, sequence).reshape(4, 2, count)

    def meta(half):
        documents = lax.dynamic_index_in_dim(of_sequence, half, 1, keepdims=False).reshape(-1)
        return jnp.stack([places(half), documents])

    key_meta = jnp.stack([meta(core), meta(1 - core)])
    row_meta = key_meta[0].T
    def swapped(rows):
        return jnp.concatenate([rows[:, 64:], rows[:, :64]], axis=1)

    half = 4 * count
    projected = jnp.dot(xn1, in_w, preferred_element_type=F32)
    key_raw = projected[:, 1024:1152]
    kv_own = jnp.concatenate(
        [key_raw * cosine + swapped(key_raw) * sine, projected[:, 1152:1280]], axis=1
    ).astype(BF)
    kv_other = lax.ppermute(kv_own, "core", SWAP)
    shared = (routes, cosine, sine, row_meta, key_meta)
    query, attended, totals, gate_a, mixed = in_vmem(
        forward_kernel,
        [
            jax.ShapeDtypeStruct((4, 2 * count, HEAD_SIZE), BF),
            jax.ShapeDtypeStruct((4, 2 * count, HEAD_SIZE), F32),
            jax.ShapeDtypeStruct((4, 2 * count, 1), F32),
            jax.ShapeDtypeStruct((half, 2), F32),
            jax.ShapeDtypeStruct((half, EXPERTS * HEAD_SIZE), BF),
        ],
        [],
        6 << 28,
        projected,
        kv_own,
        kv_other,
        *shared,
    )
    branch_part = lax.dot_general(mixed, out_w, LAST, preferred_element_type=F32).astype(BF)
    branch_part = after(branch_part, grad_landed)
    grad_received = grad_landed[:, :MODEL_WIDTH]
    branch = exchange(branch_part.reshape(16, quarter, MODEL_WIDTH), plane).astype(F32).sum(axis=0)

    own_values = lax.dynamic_slice_in_dim(values, y * count + first, quarter)
    own_factor = rms_scale(own_values)
    hidden = after(own_values, (far_a, far_b)) + branch
    factor_m = rms_scale(hidden)
    xn2_own = (hidden * factor_m * gain_m).astype(BF)
    xn2 = spread(xn2_own, "tensor", 4).reshape(count, MODEL_WIDTH)
    gate_m = pair_gates(jnp.dot(xn2, router_m, preferred_element_type=F32), pick_m)

    received = to_experts(
        lax.dot_general(any_row, xn2, ROWS, preferred_element_type=F32).astype(BF)
    )
    grad_act_raw = down_back(grad_received, down_pieces, z)
    received, grad_act_raw, hidden_last, gate_m = lax.optimization_barrier(
        (received, grad_act_raw, core_last(hidden), gate_m)
    )
    weight_m = gate_m * kept.astype(F32)
    activated, grad_pair, row_gate, grad_back = expert_middle(
        received,
        grad_landed[:, MODEL_WIDTH:],
        jnp.pad(router_m, ((0, 0), (0, 120))),
        gate_up_w,
        grad_act_raw,
        2 * y + core,
    )
    grad_back, late_pair, late_act = lax.optimization_barrier((grad_back, grad_pair, activated))
    grad_returned = to_experts(grad_back)
    grad_down_w = down_product(late_act, grad_received, row_gate)
    down_sum = lax.psum_scatter(grad_down_w, "dp", scatter_dimension=1, tiled=True)
    quarters = expert_quarters(late_act, down_pieces, z, x)
    grad_gate_up_w = gate_up_product(received, late_pair)
    gate_up_sum = lax.psum_scatter(grad_gate_up_w, "dp", scatter_dimension=0, tiled=True)
    late_any = after(any_row, (grad_down_w, quarters, grad_gate_up_w))
    expert_out = (
        quarters[0].astype(F32)
        + sum(from_ahead(quarters[4 - k], "tensor", k).astype(F32) for k in (1, 2, 3))
    ).astype(BF)

    grad_xn2_part = jnp.dot(
        late_any, grad_returned[:, :MODEL_WIDTH], preferred_element_type=F32
    ).astype(BF)
    row_gate_parts = grad_returned[:, MODEL_WIDTH : MODEL_WIDTH + 2]
    gate_m_part = jnp.sum(
        jnp.einsum("jtr,rd->tjd", to_row, row_gate_parts, preferred_element_type=F32), axis=2
    )
    shares = jnp.concatenate([grad_xn2_part, widen(in_two(gate_m_part))], axis=1)
    landed = (
        exchange(shares.reshape(4, quarter, MODEL_WIDTH + HEAD_SIZE), "tensor")
        .astype(F32)
        .sum(axis=0)
    )
    landed, expert_out = lax.optimization_barrier((landed, expert_out))
    returned = to_experts(expert_out)
    grad_gate_m = (
        landed[:, MODEL_WIDTH : MODEL_WIDTH + 2] + landed[:, MODEL_WIDTH + 2 : MODEL_WIDTH + 4]
    )

    def quarter_of(array, offset=0):
        return lax.dynamic_slice_in_dim(array, first + offset, quarter)

    grad_logit_m = gate_back(quarter_of(gate_m), grad_gate_m, quarter_of(pick_m))
    grad_xn2 = landed[:, :MODEL_WIDTH] + lax.dot_general(
        grad_logit_m, router_m.astype(F32), LAST, preferred_element_type=F32
    )
    grad_norm, gain_m_part = norm_back(grad_xn2, hidden, factor_m, gain_m)
    grad_hidden = cot_own + grad_norm
    grad_sent_back, returned = lax.optimization_barrier((grad_hidden.astype(BF), returned))
    grad_branch = spread(grad_sent_back, plane, 16).reshape(4 * count, MODEL_WIDTH)

    fetched = jnp.einsum("jtr,rd->jtd", to_row, returned, preferred_element_type=F32)
    moe_part = jnp.sum(weight_m.T[:, :, None] * fetched, axis=0).astype(BF)
    width = down_own.shape[0]
    grad_branch, moe_part = lax.optimization_barrier((grad_branch, moe_part))
    moe_pieces = exchange(moe_part.reshape(4, quarter, MODEL_WIDTH // 4), "tensor")

    grad_mixed = jnp.dot(grad_branch, out_w, preferred_element_type=F32)
    grad_q_all, grad_logit_a, grad_kv_own, grad_kv_give = in_vmem(
        backward_kernel,
        [
            jax.ShapeDtypeStruct((half, EXPERTS * HEAD_SIZE), BF),
            jax.ShapeDtypeStruct((half, HEAD_SIZE), BF),
            jax.ShapeDtypeStruct((half, 2 * HEAD_SIZE), F32),
            jax.ShapeDtypeStruct((half, 2 * HEAD_SIZE), BF),
        ],
        [pltpu.VMEM((2, half, 2 * HEAD_SIZE), F32)],
        40 << 28,
        grad_mixed,
        query,
        kv_own,
        kv_other,
        attended,
        totals,
        gate_a,
        *shared,
    )
    out_pairs = [(grad_branch, mixed)]
    out_give = lax.ppermute(give_terms(out_pairs, z, core), "core", SWAP)
    kv_back, moe_pieces = lax.optimization_barrier(
        (lax.ppermute(grad_kv_give, "core", SWAP), moe_pieces)
    )
    moe = moe_pieces.transpose(1, 0, 2).reshape(quarter, MODEL_WIDTH).astype(F32)
    output_own = (hidden_last + moe).astype(BF)
    own_grad_kv = grad_kv_own + kv_back.astype(F32)
    grad_key = own_grad_kv[:, :HEAD_SIZE]
    grad_kv = jnp.concatenate(
        [grad_key * cosine - swapped(grad_key) * sine, own_grad_kv[:, HEAD_SIZE:]], axis=1
    ).astype(BF)
    grad_in = jnp.concatenate([grad_q_all, grad_kv, grad_logit_a], axis=1)
    grad_xn1_part = lax.dot_general(grad_in, in_w, LAST, preferred_element_type=F32).astype(BF)
    gain_row = jnp.pad(gain_m_part[None].astype(BF), ((0, 7), (0, 0)))
    lane = jnp.arange(1408, dtype=jnp.int32)[None, :]
    router_cols = jnp.pad(grad_logit_m.astype(BF), ((0, 0), (1288, 112)))
    gain_cols = ((jnp.arange(8)[:, None] == 0) & (lane == 1296)).astype(BF)
    in_pairs = [
        (xn1, after(grad_in, grad_xn1_part)),
        (
            jnp.concatenate([xn2_own, gain_row], axis=0),
            jnp.concatenate([router_cols, gain_cols], axis=0),
        ),
    ]
    in_give = lax.ppermute(give_terms(in_pairs, z, core), "core", SWAP)
    out_own, *out_rest = keep_terms(out_pairs, after(out_give, grad_xn1_part), z, core)
    in_own_rows, *in_rest = keep_terms(in_pairs, in_give, z, core)
    out_rest[0], out_rest[3], _ = lax.optimization_barrier(
        (out_rest[0], out_rest[3], in_own_rows)
    )
    out_ahead, out_back = ring_first(*out_rest, "dp")
    in_ahead, in_back = ring_first(*in_rest, "dp")
    out_sum = ring_second(after(out_own, gate_up_sum), out_ahead, out_back, "dp").astype(BF)
    landed_raw = exchange(grad_xn1_part.reshape(16, quarter, MODEL_WIDTH), plane)
    landed_raw, in_ahead, in_back, out_sum, down_sum = lax.optimization_barrier(
        (landed_raw, in_ahead, in_back, out_sum, down_sum)
    )
    in_sum = ring_second(in_own_rows, in_ahead, in_back, "dp").astype(BF)
    landed_a = landed_raw.astype(F32).sum(axis=0)
    grad_x_norm, _ = norm_back(landed_a, own_values, own_factor, gain_a)
    columns = jnp.arange(1408, dtype=jnp.int32)[None, :]
    gain_a_part = jnp.sum(
        jnp.where(columns < 1288, in_sum.astype(F32) * mine[:, :1408].astype(F32), 0.0),
        axis=1,
        keepdims=True,
    )
    small_part = jnp.where(columns[:, :128] == 17, gain_a_part, in_sum[:, 1280:].astype(F32))
    gain_rows = lax.dynamic_slice_in_dim(attn_gain.astype(F32), z * 512 + y * 128 + core * 64, 64)

    ends = jnp.concatenate(
        [output_own, core_last((grad_hidden + grad_x_norm).astype(BF))], axis=1
    )
    both_sums = jnp.concatenate(
        [in_sum[:, :1280], out_sum, small_part.astype(BF)], axis=1
    ).reshape(4, 64, 2432)
    y_parts = send_direct(both_sums, "y")
    gate_up_grad = (
        after(gate_up_sum, both_sums)
        .reshape(2, 4, 64, 2816)
        .transpose(1, 0, 2, 3)
        .reshape(1, 512, 2, width)
        .astype(F32)
    )
    _, _, *y_parts = lax.optimization_barrier((gate_up_grad, ends, *y_parts))
    both_ends = spread(ends, "tensor", 4)
    small_y = sum(p[:, 2304:].astype(F32) for p in y_parts).astype(BF)
    small_y = after(small_y, both_ends)
    small_sum = small_y.astype(F32) + sum(
        from_ahead(small_y, "tensor", k).astype(F32) for k in (1, 2, 3)
    )
    down_grad = down_sum.astype(F32)[None]
    both_ends = both_ends.reshape(count, 2 * MODEL_WIDTH)
    output, input_grad = both_ends[:, :MODEL_WIDTH], both_ends[:, MODEL_WIDTH:]
    query_grad, kv_grad, out_grad = heads_placed(y_parts, y)
    return (
        output,
        input_grad,
        small_sum[:, 17] / gain_rows,
        small_sum[:, 16],
        small_sum[:, :8],
        kv_grad,
        query_grad,
        out_grad,
        small_sum[:, 8:16],
        gate_up_grad,
        down_grad,
    )


def solution(mesh):
    split = Mesh(mesh.devices.reshape(4, 4, 2, 4), ("dp", "y", "core", "tensor"))
    rows = ("dp", "y", "core")
    expert = ("y", "core")
    placed = (
        P(rows, None),
        P(rows, None),
        P(),
        P(),
        P(rows, None),
        P(rows, None, "tensor"),
        P(rows, None, "tensor"),
        P(rows, None, "tensor"),
        P(rows, None),
        P(expert, "dp", None, "tensor"),
        P(expert, "tensor", "dp"),
        P(rows, None),
        P(rows, None),
        P(rows, None),
        P(),
    )
    return jax.shard_map(
        body,
        mesh=split,
        in_specs=placed,
        out_specs=(
            P(rows, None),
            P(rows, None),
            P(rows),
            P(rows),
            P(rows, None),
            P(rows, None, "tensor"),
            P(rows, None, "tensor"),
            P(rows, None, "tensor"),
            P(rows, None),
            P(expert, "dp", None, "tensor"),
            P(expert, "tensor", "dp"),
        ),
        check_vma=False,
    )
```

```python
import jax
import jax.numpy as jnp
from jax import lax
from jax.experimental import pallas as pl
from jax.experimental.pallas import tpu as pltpu
from jax.sharding import Mesh
from jax.sharding import PartitionSpec as P

MODEL_WIDTH = 2048
HEAD_SIZE = 128
EXPERTS = 8
WINDOW = 1024
NORM_EPS = 1e-06
BF = jnp.bfloat16
F32 = jnp.float32
ROWS = (((0,), (0,)), ((), ()))
LAST = (((1,), (1,)), ((), ()))
UP = [(0, 1), (1, 2), (2, 3), (3, 0)]
DOWN = [(0, 3), (1, 0), (2, 1), (3, 2)]
SWAP = [(0, 1), (1, 0)]


def exchange(blocks, axis):
    return lax.all_to_all(blocks, axis, split_axis=0, concat_axis=0, tiled=True)


def spread(block, axis, count):
    return exchange(jnp.broadcast_to(block, (count, *block.shape)), axis)


def from_ahead(block, axis, steps):
    return lax.ppermute(block, axis, [(i, (i - steps) % 4) for i in range(4)])


def in_order(pieces, first):
    both = jnp.stack(pieces + pieces[:3])
    return lax.dynamic_slice_in_dim(both, lax.rem(4 - first, 4), 4)


def pick_block(blocks, index):
    return lax.dynamic_index_in_dim(blocks, lax.rem(index, 4), 0, keepdims=False)


def send_direct(blocks, axis):
    me = lax.axis_index(axis)
    return [pick_block(blocks, me)] + [
        from_ahead(pick_block(blocks, me + 4 - k), axis, k) for k in (1, 2, 3)
    ]


def heads_first(shard):
    columns = shard.shape[1] * HEAD_SIZE
    return shard.reshape(64, -1, 4, HEAD_SIZE).transpose(2, 0, 1, 3).reshape(4, 64, columns)


def after(value, other):
    return lax.optimization_barrier((value, other))[0]


def core_first(rows):
    return rows.reshape(-1, 4, 4, 2, 64).transpose(0, 1, 3, 2, 4).reshape(-1, MODEL_WIDTH)


def core_last(rows):
    return rows.reshape(-1, 4, 2, 4, 64).transpose(0, 1, 3, 2, 4).reshape(-1, MODEL_WIDTH)


def ring_first(ahead, low, high, back, axis):
    low = lax.ppermute(low, axis, UP)
    high = lax.ppermute(high, axis, DOWN)
    half = low.shape[0]
    ahead = jnp.concatenate([(ahead[:half].astype(F32) + low.astype(F32)).astype(BF), ahead[half:]])
    back = jnp.concatenate([back[:half], (back[half:].astype(F32) + high.astype(F32)).astype(BF)])
    return ahead, back


def ring_second(own, ahead, back, axis):
    return (
        own.astype(F32)
        + lax.ppermute(ahead, axis, UP).astype(F32)
        + lax.ppermute(back, axis, DOWN).astype(F32)
    )


def rms_scale(values):
    return lax.rsqrt(jnp.mean(values * values, axis=-1, keepdims=True) + NORM_EPS)


def turn(heads, cosine, sine):
    first, second = heads[..., :64], heads[..., 64:]
    return jnp.concatenate([first * cosine - second * sine, second * cosine + first * sine], axis=-1)


EXTENTS = (256, 384, 512, 640)
SCALE = HEAD_SIZE**-0.5


def masked_scores(query, key, row_meta, key_meta):
    raw = lax.dot_general(query, key, LAST, preferred_element_type=F32) * SCALE
    gap = row_meta[:, 0:1] - key_meta[0:1]
    allowed = (gap >= 0) & (gap < WINDOW) & (row_meta[:, 1:2] == key_meta[1:2])
    return jnp.where(jnp.concatenate([allowed, allowed], axis=0), raw, -1e30)


def forward_kernel(proj, own, other, routes, cosine, sine, row_meta, key_meta, *outs):
    query_out, attended_out, total_out, gates_out, mixed_out = outs
    count = proj.shape[0] // 4
    for i in range(4):
        rows = pl.ds(count * i, count)
        extent = EXTENTS[i]
        logits = proj[rows, 1280:1288]
        lane = lax.broadcasted_iota(jnp.int32, (count, EXPERTS), 1)
        named = [routes[rows, 0:1], routes[rows, 1:2]]
        chosen = [jnp.sum(jnp.where(lane == n, logits, 0.0), axis=1, keepdims=True) for n in named]
        top = jnp.maximum(chosen[0], chosen[1])
        power = [jnp.exp(c - top) for c in chosen]
        gates = [p / (power[0] + power[1]) for p in power]
        gates_out[rows, 0:1] = gates[0]
        gates_out[rows, 1:2] = gates[1]
        cos, sin = cosine[rows, :], sine[rows, :]
        picked = []
        for n in named:
            q = jnp.zeros((count, HEAD_SIZE), F32)
            for e in range(EXPERTS):
                q = q + jnp.where(n == e, proj[rows, HEAD_SIZE * e : HEAD_SIZE * (e + 1)], 0.0)
            picked.append(q * cos + pltpu.roll(q, 64, 1) * sin)
        query = jnp.concatenate(picked, axis=0).astype(BF)
        query_out[i] = query
        halves = (own, other)
        scores = [
            masked_scores(
                query, h[:extent, :HEAD_SIZE], row_meta[rows, :], key_meta[k, :, :extent]
            )
            for k, h in enumerate(halves)
        ]
        row_max = jnp.maximum(
            jnp.max(scores[0], axis=1, keepdims=True), jnp.max(scores[1], axis=1, keepdims=True)
        )
        weights = [jnp.exp(s - row_max) for s in scores]
        total = jnp.sum(weights[0], axis=1, keepdims=True) + jnp.sum(weights[1], axis=1, keepdims=True)
        inverse = 1.0 / total
        attended = sum(
            jnp.dot((w * inverse).astype(BF), h[:extent, HEAD_SIZE:], preferred_element_type=F32)
            for w, h in zip(weights, halves)
        )
        attended_out[i] = attended
        total_out[i] = row_max + jnp.log(total)
        for e in range(EXPERTS):
            mixed_out[rows, HEAD_SIZE * e : HEAD_SIZE * (e + 1)] = (
                jnp.where(named[0] == e, gates[0], 0.0) * attended[:count]
                + jnp.where(named[1] == e, gates[1], 0.0) * attended[count:]
            ).astype(BF)


def backward_kernel(
    grad_mixed, query_in, own, other, attended_in, total_in, gates_in, routes, cosine, sine, row_meta, key_meta, *outs
):
    grad_query_out, grad_logit_out, grad_own_out, grad_other_out, sums = outs
    count = grad_mixed.shape[0] // 4
    sums[...] = jnp.zeros_like(sums)
    for i in range(4):
        rows = pl.ds(count * i, count)
        extent = EXTENTS[i]
        named = [routes[rows, 0:1], routes[rows, 1:2]]
        gates = [gates_in[rows, 0:1], gates_in[rows, 1:2]]
        cos, sin = cosine[rows, :], sine[rows, :]
        attended = attended_in[i]
        picked = []
        for n in named:
            g = jnp.zeros((count, HEAD_SIZE), F32)
            for e in range(EXPERTS):
                g = g + jnp.where(n == e, grad_mixed[rows, HEAD_SIZE * e : HEAD_SIZE * (e + 1)], 0.0)
            picked.append(g)
        gate_grads = [
            jnp.sum(p * attended[count * j : count * (j + 1)], axis=1, keepdims=True)
            for j, p in enumerate(picked)
        ]
        level = gates[0] * gate_grads[0] + gates[1] * gate_grads[1]
        lane = lax.broadcasted_iota(jnp.int32, (count, HEAD_SIZE), 1)
        grad_logit_out[rows, :] = sum(
            jnp.where(lane == n, g * (d - level), 0.0) for n, g, d in zip(named, gates, gate_grads)
        ).astype(BF)
        grad_attended = jnp.concatenate(
            [gates[0] * picked[0], gates[1] * picked[1]], axis=0
        ).astype(BF)
        query = query_in[i]
        total = total_in[i]
        probs, grad_probs = [], []
        delta = jnp.zeros((2 * count, 1), F32)
        for k, h in enumerate((own, other)):
            score = masked_scores(
                query, h[:extent, :HEAD_SIZE], row_meta[rows, :], key_meta[k, :, :extent]
            )
            prob = jnp.exp(score - total)
            grad_prob = lax.dot_general(
                grad_attended, h[:extent, HEAD_SIZE:], LAST, preferred_element_type=F32
            )
            delta = delta + jnp.sum(prob * grad_prob, axis=1, keepdims=True)
            probs.append(prob)
            grad_probs.append(grad_prob)
        grad_query = jnp.zeros((2 * count, HEAD_SIZE), F32)
        for k, h in enumerate((own, other)):
            grad_score = (probs[k] * (grad_probs[k] - delta)).astype(BF)
            grad_query = grad_query + jnp.dot(
                grad_score, h[:extent, :HEAD_SIZE], preferred_element_type=F32
            )
            sums[k, :extent, :HEAD_SIZE] += (
                lax.dot_general(grad_score, query, ROWS, preferred_element_type=F32) * SCALE
            )
            sums[k, :extent, HEAD_SIZE:] += lax.dot_general(
                probs[k].astype(BF), grad_attended, ROWS, preferred_element_type=F32
            )
        grad_query = grad_query * SCALE
        turned = [
            g * cos - pltpu.roll(g, 64, 1) * sin for g in (grad_query[:count], grad_query[count:])
        ]
        for e in range(EXPERTS):
            grad_query_out[rows, HEAD_SIZE * e : HEAD_SIZE * (e + 1)] = (
                jnp.where(named[0] == e, turned[0], 0.0) + jnp.where(named[1] == e, turned[1], 0.0)
            ).astype(BF)
    grad_own_out[...] = sums[0]
    grad_other_out[...] = sums[1].astype(BF)


def in_vmem(kernel, outs, scratch, flops, *args):
    spec = pl.BlockSpec(memory_space=pltpu.VMEM)
    moved = sum(a.size * a.dtype.itemsize for a in args)
    return pl.pallas_call(
        kernel,
        out_shape=outs,
        in_specs=[spec] * len(args),
        out_specs=[spec] * len(outs),
        scratch_shapes=scratch,
        compiler_params=pltpu.CompilerParams(vmem_limit_bytes=40 * 1024 * 1024),
        cost_estimate=pl.CostEstimate(flops=flops, bytes_accessed=moved, transcendentals=1 << 20),
    )(*args)


SOME = pl.CostEstimate(flops=1 << 35, bytes_accessed=1 << 27, transcendentals=0)


def on_grid(kernel, scalars, grid, in_specs, out_specs, outs, scratch, *args, cost=SOME):
    return pl.pallas_call(
        kernel,
        out_shape=outs,
        grid_spec=pltpu.PrefetchScalarGridSpec(
            num_scalar_prefetch=1,
            grid=grid,
            in_specs=in_specs,
            out_specs=out_specs,
            scratch_shapes=scratch,
        ),
        compiler_params=pltpu.CompilerParams(vmem_limit_bytes=48 * 1024 * 1024),
        cost_estimate=cost,
    )(jnp.stack(scalars).astype(jnp.int32), *args)


def give_terms(pairs, place, core):
    columns = pairs[0][1].shape[1]

    def kernel(at, *refs):
        out = refs[-1]
        total = sum(
            lax.dot_general(refs[j][...], refs[j + 1][...], ROWS, preferred_element_type=F32)
            for j in range(0, len(refs) - 1, 2)
        )
        out[0] = total.astype(BF)

    specs = []
    for tall, terms in pairs:
        specs.append(pl.BlockSpec((tall.shape[0], 256), lambda i, at: (0, 2 * i + 1 - at[1])))
        specs.append(pl.BlockSpec(terms.shape, lambda i, at: (0, 0)))
    return on_grid(
        kernel,
        (place, core),
        (4,),
        specs,
        pl.BlockSpec((1, 256, columns), lambda i, at: (i, 0, 0)),
        jax.ShapeDtypeStruct((4, 256, columns), BF),
        [],
        *[a for pair in pairs for a in pair],
    )


def keep_terms(pairs, landed, place, core):
    columns = pairs[0][1].shape[1]
    count = 2 * len(pairs)

    def kernel(at, *refs):
        more, own, ahead, low, high, back = refs[count:]
        total = sum(
            lax.dot_general(refs[j][...], refs[j + 1][...], ROWS, preferred_element_type=F32)
            for j in range(0, count, 2)
        )
        total = (total.astype(BF).astype(F32) + more[0].astype(F32)).astype(BF)
        step = pl.program_id(0)

        @pl.when(step == 0)
        def _():
            own[...] = total

        @pl.when(step == 1)
        def _():
            ahead[...] = total

        @pl.when(step == 2)
        def _():
            low[...] = total[:128]
            high[...] = total[128:]

        @pl.when(step == 3)
        def _():
            back[...] = total

    def whole(rows):
        return pl.BlockSpec((rows, columns), lambda i, at: (0, 0))

    specs = []
    for tall, terms in pairs:
        specs.append(
            pl.BlockSpec(
                (tall.shape[0], 256), lambda i, at: (0, 2 * lax.rem(at[0] + i, 4) + at[1])
            )
        )
        specs.append(pl.BlockSpec(terms.shape, lambda i, at: (0, 0)))
    specs.append(pl.BlockSpec((1, 256, columns), lambda i, at: (lax.rem(at[0] + i, 4), 0, 0)))
    return on_grid(
        kernel,
        (place, core),
        (4,),
        specs,
        [whole(256), whole(256), whole(128), whole(128), whole(256)],
        [jax.ShapeDtypeStruct((r, columns), BF) for r in (256, 256, 128, 128, 256)],
        [],
        *[a for pair in pairs for a in pair],
        landed,
    )


def gate_up_product(rows, pair):
    depth, width = pair.shape[1:]

    def kernel(at, left, right, out):
        for half in range(2):
            out[:, width * half : width * (half + 1)] = lax.dot_general(
                left[...], right[half], ROWS, preferred_element_type=F32
            ).astype(BF)

    return on_grid(
        kernel,
        (jnp.int32(0),),
        (8,),
        [
            pl.BlockSpec((depth, 256), lambda i, at: (0, i)),
            pl.BlockSpec((2, depth, width), lambda i, at: (0, 0, 0)),
        ],
        pl.BlockSpec((256, 2 * width), lambda i, at: (i, 0)),
        jax.ShapeDtypeStruct((MODEL_WIDTH, 2 * width), BF),
        [],
        rows,
        pair,
    )


def down_product(activated, grads, gate):
    def kernel(at, left, right, scale, out):
        scaled = (scale[...] * right[...].astype(F32)).astype(BF)
        out[...] = lax.dot_general(left[...], scaled, ROWS, preferred_element_type=F32).astype(BF)

    depth, width = activated.shape
    return on_grid(
        kernel,
        (jnp.int32(0),),
        (4,),
        [
            pl.BlockSpec((depth, width), lambda i, at: (0, 0)),
            pl.BlockSpec((depth, 512), lambda i, at: (0, i)),
            pl.BlockSpec((depth, 1), lambda i, at: (0, 0)),
        ],
        pl.BlockSpec((width, 512), lambda i, at: (0, i)),
        jax.ShapeDtypeStruct((width, MODEL_WIDTH), BF),
        [],
        activated,
        grads,
        gate,
    )


def down_back(grads, pieces, place):
    def kernel(at, left, own, ahead, far_a, far_b, back, out):
        total = None
        for shift, start, piece in (
            (0, 0, own), (1, 0, ahead), (2, 0, far_a), (2, 256, far_b), (3, 0, back)
        ):
            size = piece.shape[1]
            lanes = pl.ds(pl.multiple_of(lax.rem(at[0] + shift, 4) * 512 + start, 256), size)
            term = lax.dot_general(left[:, lanes], piece[...], LAST, preferred_element_type=F32)
            total = term if total is None else total + term
        out[...] = total

    depth, width = grads.shape[0], pieces[0].shape[0]
    return on_grid(
        kernel,
        (place,),
        (width // 128,),
        [pl.BlockSpec(grads.shape, lambda i, at: (0, 0))]
        + [pl.BlockSpec((128, p.shape[1]), lambda i, at: (i, 0)) for p in pieces],
        pl.BlockSpec((depth, 128), lambda i, at: (0, i)),
        jax.ShapeDtypeStruct((depth, width), F32),
        [],
        grads,
        *pieces,
    )


def expert_quarters(activated, pieces, place, x):
    def kernel(at, left, own, ahead, far_a, far_b, back, out):
        step = pl.program_id(0)
        for shift, refs in enumerate(((own,), (ahead,), (far_a, far_b), (back,))):

            @pl.when(step == shift)
            def _():
                terms = [jnp.dot(left[...], r[...], preferred_element_type=F32) for r in refs]
                out[0] = jnp.concatenate(terms, axis=1).astype(BF)

    depth = activated.shape[0]
    return on_grid(
        kernel,
        (place, x),
        (4,),
        [pl.BlockSpec(a.shape, lambda i, at: (0, 0)) for a in (activated, *pieces)],
        pl.BlockSpec((1, depth, 512), lambda i, at: (lax.rem(at[0] + i + 4 - at[1], 4), 0, 0)),
        jax.ShapeDtypeStruct((4, depth, 512), BF),
        [],
        activated,
        *pieces,
    )


def expert_middle(rows, marks, router, gate_up_w, grad_act, expert):
    depth, width = grad_act.shape
    blocks = width // 128

    def kernel(
        at, rows_ref, marks_ref, router_ref, gate_ref, up_ref, flat_ref, grad_ref,
        act_out, pair_out, gate_out, back_out, pair_all, held, row_gate, row_grad,
    ):
        step = pl.program_id(0)
        lane = lax.broadcasted_iota(jnp.int32, (depth, 128), 1)

        @pl.when(step == 0)
        def _():
            logits = jnp.dot(rows_ref[...], router_ref[...], preferred_element_type=F32)
            marks_f = marks_ref[...].astype(F32)
            own = jnp.sum(jnp.where(lane == at[0], logits, 0.0), axis=1, keepdims=True)
            other = jnp.sum(jnp.where(lane < 8, logits * marks_f, 0.0), axis=1, keepdims=True)
            valid = jnp.sum(jnp.where(lane == 8, marks_f, 0.0), axis=1, keepdims=True)
            top = jnp.maximum(own, other)
            power = jnp.exp(own - top)
            row_gate[...] = valid * power / (power + jnp.exp(other - top))
            gate_out[...] = row_gate[...]
            row_grad[...] = jnp.zeros_like(row_grad)

        @pl.when(step <= blocks)
        def _():
            both = jnp.concatenate([gate_ref[...], up_ref[...]], axis=1)
            last = held[lax.rem(step + 1, 2)]
            held[lax.rem(step, 2)] = jnp.dot(rows_ref[...], both, preferred_element_type=F32)
            gate, up = last[:, :128], last[:, 128:]
            sigmoid = 1.0 / (1.0 + jnp.exp(-gate))
            silu = gate * sigmoid
            act = (silu * up).astype(BF)
            raw = grad_ref[...]
            grad = row_gate[...] * raw
            grad_gate = (grad * up * sigmoid * (1.0 + gate * (1.0 - sigmoid))).astype(BF)
            grad_up = (grad * silu).astype(BF)
            act_out[...] = act
            pair_out[0] = grad_gate
            pair_out[1] = grad_up
            at_lane = pl.multiple_of(jnp.maximum(step - 1, 0) * 128, 128)
            pair_all[:, pl.ds(at_lane, 128)] = grad_gate
            pair_all[:, pl.ds(at_lane + width, 128)] = grad_up
            term = jnp.sum(act.astype(F32) * raw, axis=1, keepdims=True)
            row_grad[...] += jnp.where(step > 0, term, 0.0)

        @pl.when(step > blocks)
        def _():
            back_lane = pl.multiple_of((step - blocks - 1) * 512, 512)
            back_out[:, pl.ds(back_lane, 512)] = lax.dot_general(
                pair_all[...], flat_ref[...], LAST, preferred_element_type=F32
            ).astype(BF)

        @pl.when(step == blocks + 4)
        def _():
            high = row_grad[...].astype(BF).astype(F32)
            low = row_grad[...] - high
            back_out[:, MODEL_WIDTH:] = jnp.where(
                lane == 0, high, jnp.where(lane == 1, low, 0.0)
            ).astype(BF)

    def first(i):
        return jnp.minimum(i, blocks - 1)

    def before(i):
        return jnp.clip(i - 1, 0, blocks - 1)

    def second(i):
        return jnp.clip(i - blocks - 1, 0, 3)

    return on_grid(
        kernel,
        (expert,),
        (blocks + 5,),
        [
            pl.BlockSpec((depth, MODEL_WIDTH), lambda i, at: (0, 0)),
            pl.BlockSpec((depth, 128), lambda i, at: (0, 0)),
            pl.BlockSpec((MODEL_WIDTH, 128), lambda i, at: (0, 0)),
            pl.BlockSpec((MODEL_WIDTH, 128), lambda i, at: (0, first(i))),
            pl.BlockSpec((MODEL_WIDTH, 128), lambda i, at: (0, blocks + first(i))),
            pl.BlockSpec((512, 2 * width), lambda i, at: (second(i), 0)),
            pl.BlockSpec((depth, 128), lambda i, at: (0, before(i))),
        ],
        [
            pl.BlockSpec((depth, 128), lambda i, at: (0, before(i))),
            pl.BlockSpec((2, depth, 128), lambda i, at: (0, 0, before(i))),
            pl.BlockSpec((depth, 1), lambda i, at: (0, 0)),
            pl.BlockSpec((depth, MODEL_WIDTH + 128), lambda i, at: (0, 0)),
        ],
        [
            jax.ShapeDtypeStruct((depth, width), BF),
            jax.ShapeDtypeStruct((2, depth, width), BF),
            jax.ShapeDtypeStruct((depth, 1), F32),
            jax.ShapeDtypeStruct((depth, MODEL_WIDTH + 128), BF),
        ],
        [
            pltpu.VMEM((depth, 2 * width), BF),
            pltpu.VMEM((2, depth, 256), F32),
            pltpu.VMEM((depth, 1), F32),
            pltpu.VMEM((depth, 1), F32),
        ],
        rows,
        marks,
        router,
        gate_up_w,
        gate_up_w,
        gate_up_w,
        grad_act,
        cost=pl.CostEstimate(
            flops=8 * depth * MODEL_WIDTH * width, bytes_accessed=1 << 24, transcendentals=1 << 20
        ),
    )


def heads_placed(pieces, y):
    def kernel(at, p0, p1, p2, p3, query, kv, out):
        for k, piece in enumerate((p0, p1, p2, p3)):
            lanes = pl.ds(pl.multiple_of(lax.rem(at[0] + k, 4) * 128, 128), 128)
            for e in range(18):
                block = piece[:, 128 * e : 128 * (e + 1)].astype(F32)
                if e < 8:
                    query[:, e, lanes] = block
                elif e < 10:
                    kv[:, e - 8, lanes] = block
                else:
                    out[:, e - 10, lanes] = block

    shapes = [(64, 8, 512), (64, 2, 512), (64, 8, 512)]
    return on_grid(
        kernel,
        (y,),
        (1,),
        [pl.BlockSpec((64, 2432), lambda i, at: (0, 0))] * 4,
        [pl.BlockSpec(s, lambda i, at: (0, 0, 0)) for s in shapes],
        [jax.ShapeDtypeStruct(s, F32) for s in shapes],
        [],
        *pieces,
        cost=pl.CostEstimate(flops=0, bytes_accessed=0, transcendentals=0),
    )


def pick_of(routes):
    return (routes[:, :, None] == jnp.arange(EXPERTS, dtype=jnp.int32)[None, None, :]).astype(F32)


def pair_gates(logits, pick):
    chosen = jnp.sum(logits[:, None, :] * pick, axis=-1)
    weights = jnp.exp(chosen - jnp.max(chosen, axis=1, keepdims=True))
    return weights / jnp.sum(weights, axis=1, keepdims=True)


def gate_back(gates, grad_gates, pick):
    inner = gates * (grad_gates - jnp.sum(gates * grad_gates, axis=1, keepdims=True))
    return jnp.sum(inner[:, :, None] * pick, axis=1)


def norm_back(grad_normed, values, factor, gain):
    gain_part = jnp.sum(grad_normed * values * factor, axis=0)
    inner = grad_normed * gain
    grad_values = factor * inner - values * factor * factor * factor * jnp.mean(
        inner * values, axis=-1, keepdims=True
    )
    return grad_values, gain_part


def in_two(values):
    high = values.astype(BF)
    low = (values - high.astype(F32)).astype(BF)
    return jnp.concatenate([high, low], axis=1)


def widen(columns):
    return jnp.pad(columns, ((0, 0), (0, HEAD_SIZE - columns.shape[1])))


def body(
    tokens,
    cotangent,
    attn_gain,
    mlp_gain,
    attn_router,
    key_value_weight,
    query_matrix,
    output_matrix,
    mlp_router,
    gate_up_weight,
    down_weight,
    attn_routes,
    mlp_routes,
    priority,
    segments,
):
    z, y = lax.axis_index("dp"), lax.axis_index("y")
    core, x = lax.axis_index("core"), lax.axis_index("tensor")
    count = tokens.shape[0]
    quarter = count // 4
    capacity = 50
    room = 56
    sequence = 8 * count
    plane = ("y", "tensor")

    routers_own = jnp.concatenate([attn_router, mlp_router], axis=1)
    down_own = down_weight[0]
    down_before = lax.ppermute(down_own, "dp", UP)
    down_after = lax.ppermute(down_own, "dp", DOWN)
    mine = exchange(
        jnp.concatenate(
            [
                heads_first(query_matrix),
                heads_first(key_value_weight),
                jnp.broadcast_to(widen(routers_own), (4, 64, HEAD_SIZE)),
                heads_first(output_matrix),
            ],
            axis=2,
        ),
        "y",
    ).reshape(256, 2432)
    sent = jnp.concatenate([core_first(tokens), widen(attn_routes.astype(BF))], axis=1)
    arrived = spread(after(sent, mine), "y", 4).reshape(4 * count, MODEL_WIDTH + HEAD_SIZE)
    all_w = lax.all_gather(
        after(mine, (down_before, down_after)), ("dp", "core"), axis=0, tiled=True
    )
    values = arrived[:, :MODEL_WIDTH].astype(F32)
    routes = arrived[:, MODEL_WIDTH : MODEL_WIDTH + 2].astype(jnp.int32)
    gain_a = core_first(attn_gain.astype(F32))[0]
    gain_m = core_first(mlp_gain.astype(F32))[0]
    xn1 = (values * rms_scale(values) * gain_a).astype(BF)

    ranking = priority[0]
    pick_m = pick_of(mlp_routes)
    before = (ranking[None, :] < ranking[:, None]).astype(BF)
    earlier = jnp.dot(before, jnp.sum(pick_m, axis=1).astype(BF), preferred_element_type=F32)
    slots = jnp.sum(pick_m * earlier[:, None, :], axis=-1).astype(jnp.int32)
    kept = slots < capacity
    dest = jnp.where(kept, mlp_routes * room + slots, -1)
    lanes = jnp.arange(EXPERTS * room, dtype=jnp.int32)
    to_row = (dest.T[:, :, None] == lanes[None, None, :]).astype(BF)
    any_row = to_row[0] + to_row[1]
    both_rows = to_row.reshape(2 * count, EXPERTS * room)

    def to_experts(rows):
        columns = rows.shape[1]
        return exchange(rows.reshape(EXPERTS, room, columns), ("y", "core")).reshape(
            EXPERTS * room, columns
        )

    def with_other(j):
        others = jnp.concatenate([pick_m[:, 1 - j], jnp.ones((count, 1), F32)], axis=1)
        return jnp.concatenate([cotangent, widen(others.astype(BF))], axis=1)

    grad_sent = lax.dot_general(
        both_rows,
        jnp.concatenate([with_other(0), with_other(1)], axis=0),
        ROWS,
        preferred_element_type=F32,
    ).astype(BF)
    def places(half):
        blocks = 2 * jnp.arange(4, dtype=jnp.int32)[:, None] + half
        return (blocks * count + jnp.arange(count, dtype=jnp.int32)[None, :]).reshape(-1)

    inverse = 10000.0 ** (-(jnp.arange(HEAD_SIZE // 2).astype(F32) * 2.0 / HEAD_SIZE))
    angle = places(core).astype(F32)[:, None] * inverse[None, :]
    cosine = jnp.tile(jnp.cos(angle), (1, 2))
    sine = jnp.concatenate([-jnp.sin(angle), jnp.sin(angle)], axis=1)

    first = x * quarter
    cot_own = core_first(lax.dynamic_slice_in_dim(cotangent, first, quarter)).astype(F32)
    all_w, down_before, down_after, xn1, grad_sent, cosine, sine, cot_own = (
        lax.optimization_barrier(
            (all_w, down_before, down_after, xn1, grad_sent, cosine, sine, cot_own)
        )
    )
    in_w, out_w = all_w[:, :1408], all_w[:, 1408:]
    far_a = lax.ppermute(down_before[:, :256], "dp", UP)
    far_b = lax.ppermute(down_after[:, 256:], "dp", DOWN)
    down_pieces = (down_own, down_after, far_a, far_b, down_before)
    gate_up_own = gate_up_weight.reshape(4, 2, 64, 2816).transpose(1, 0, 2, 3).reshape(512, 2816)
    gate_up_w = lax.all_gather(after(gate_up_own, all_w), "dp", axis=0, tiled=True)
    router_m = in_w[:, 1288:1296]

    grad_landed = to_experts(grad_sent)

    of_sequence = lax.dynamic_slice_in_dim(segments, z * sequence, sequence).reshape(4, 2, count)

    def meta(half):
        documents = lax.dynamic_index_in_dim(of_sequence, half, 1, keepdims=False).reshape(-1)
        return jnp.stack([places(half), documents])

    key_meta = jnp.stack([meta(core), meta(1 - core)])
    row_meta = key_meta[0].T
    def swapped(rows):
        return jnp.concatenate([rows[:, 64:], rows[:, :64]], axis=1)

    half = 4 * count
    projected = jnp.dot(xn1, in_w, preferred_element_type=F32)
    key_raw = projected[:, 1024:1152]
    kv_own = jnp.concatenate(
        [key_raw * cosine + swapped(key_raw) * sine, projected[:, 1152:1280]], axis=1
    ).astype(BF)
    kv_other = lax.ppermute(kv_own, "core", SWAP)
    shared = (routes, cosine, sine, row_meta, key_meta)
    query, attended, totals, gate_a, mixed = in_vmem(
        forward_kernel,
        [
            jax.ShapeDtypeStruct((4, 2 * count, HEAD_SIZE), BF),
            jax.ShapeDtypeStruct((4, 2 * count, HEAD_SIZE), F32),
            jax.ShapeDtypeStruct((4, 2 * count, 1), F32),
            jax.ShapeDtypeStruct((half, 2), F32),
            jax.ShapeDtypeStruct((half, EXPERTS * HEAD_SIZE), BF),
        ],
        [],
        6 << 28,
        projected,
        kv_own,
        kv_other,
        *shared,
    )
    branch_part = lax.dot_general(mixed, out_w, LAST, preferred_element_type=F32).astype(BF)
    branch_part = after(branch_part, grad_landed)
    grad_received = grad_landed[:, :MODEL_WIDTH]
    branch = exchange(branch_part.reshape(16, quarter, MODEL_WIDTH), plane).astype(F32).sum(axis=0)

    own_values = lax.dynamic_slice_in_dim(values, y * count + first, quarter)
    own_factor = rms_scale(own_values)
    hidden = after(own_values, (far_a, far_b)) + branch
    factor_m = rms_scale(hidden)
    xn2_own = (hidden * factor_m * gain_m).astype(BF)
    xn2 = spread(xn2_own, "tensor", 4).reshape(count, MODEL_WIDTH)
    gate_m = pair_gates(jnp.dot(xn2, router_m, preferred_element_type=F32), pick_m)

    received = to_experts(
        lax.dot_general(any_row, xn2, ROWS, preferred_element_type=F32).astype(BF)
    )
    grad_act_raw = down_back(grad_received, down_pieces, z)
    received, grad_act_raw, hidden_last, gate_m = lax.optimization_barrier(
        (received, grad_act_raw, core_last(hidden), gate_m)
    )
    weight_m = gate_m * kept.astype(F32)
    activated, grad_pair, row_gate, grad_back = expert_middle(
        received,
        grad_landed[:, MODEL_WIDTH:],
        jnp.pad(router_m, ((0, 0), (0, 120))),
        gate_up_w,
        grad_act_raw,
        2 * y + core,
    )
    grad_back, late_pair, late_act = lax.optimization_barrier((grad_back, grad_pair, activated))
    grad_returned = to_experts(grad_back)
    grad_down_w = down_product(late_act, grad_received, row_gate)
    down_sum = lax.psum_scatter(grad_down_w, "dp", scatter_dimension=1, tiled=True)
    quarters = expert_quarters(late_act, down_pieces, z, x)
    grad_gate_up_w = gate_up_product(received, late_pair)
    gate_up_sum = lax.psum_scatter(grad_gate_up_w, "dp", scatter_dimension=0, tiled=True)
    late_any = after(any_row, (grad_down_w, quarters, grad_gate_up_w))
    expert_out = (
        quarters[0].astype(F32)
        + sum(from_ahead(quarters[4 - k], "tensor", k).astype(F32) for k in (1, 2, 3))
    ).astype(BF)

    grad_xn2_part = jnp.dot(
        late_any, grad_returned[:, :MODEL_WIDTH], preferred_element_type=F32
    ).astype(BF)
    row_gate_parts = grad_returned[:, MODEL_WIDTH : MODEL_WIDTH + 2]
    gate_m_part = jnp.sum(
        jnp.einsum("jtr,rd->tjd", to_row, row_gate_parts, preferred_element_type=F32), axis=2
    )
    shares = jnp.concatenate([grad_xn2_part, widen(in_two(gate_m_part))], axis=1)
    landed = (
        exchange(shares.reshape(4, quarter, MODEL_WIDTH + HEAD_SIZE), "tensor")
        .astype(F32)
        .sum(axis=0)
    )
    landed, expert_out = lax.optimization_barrier((landed, expert_out))
    returned = to_experts(expert_out)
    grad_gate_m = (
        landed[:, MODEL_WIDTH : MODEL_WIDTH + 2] + landed[:, MODEL_WIDTH + 2 : MODEL_WIDTH + 4]
    )

    def quarter_of(array, offset=0):
        return lax.dynamic_slice_in_dim(array, first + offset, quarter)

    grad_logit_m = gate_back(quarter_of(gate_m), grad_gate_m, quarter_of(pick_m))
    grad_xn2 = landed[:, :MODEL_WIDTH] + lax.dot_general(
        grad_logit_m, router_m.astype(F32), LAST, preferred_element_type=F32
    )
    grad_norm, gain_m_part = norm_back(grad_xn2, hidden, factor_m, gain_m)
    grad_hidden = cot_own + grad_norm
    grad_sent_back, returned = lax.optimization_barrier((grad_hidden.astype(BF), returned))
    grad_branch = spread(grad_sent_back, plane, 16).reshape(4 * count, MODEL_WIDTH)

    fetched = jnp.einsum("jtr,rd->jtd", to_row, returned, preferred_element_type=F32)
    moe_part = jnp.sum(weight_m.T[:, :, None] * fetched, axis=0).astype(BF)
    width = down_own.shape[0]
    grad_branch, moe_part = lax.optimization_barrier((grad_branch, moe_part))

    grad_mixed = jnp.dot(grad_branch, out_w, preferred_element_type=F32)
    grad_q_all, grad_logit_a, grad_kv_own, grad_kv_give = in_vmem(
        backward_kernel,
        [
            jax.ShapeDtypeStruct((half, EXPERTS * HEAD_SIZE), BF),
            jax.ShapeDtypeStruct((half, HEAD_SIZE), BF),
            jax.ShapeDtypeStruct((half, 2 * HEAD_SIZE), F32),
            jax.ShapeDtypeStruct((half, 2 * HEAD_SIZE), BF),
        ],
        [pltpu.VMEM((2, half, 2 * HEAD_SIZE), F32)],
        40 << 28,
        grad_mixed,
        query,
        kv_own,
        kv_other,
        attended,
        totals,
        gate_a,
        *shared,
    )
    out_pairs = [(grad_branch, mixed)]
    out_give = lax.ppermute(give_terms(out_pairs, z, core), "core", SWAP)
    kv_back = lax.ppermute(grad_kv_give, "core", SWAP)
    moe_pieces = exchange(
        after(moe_part, grad_kv_give).reshape(4, quarter, MODEL_WIDTH // 4), "tensor"
    )
    moe = moe_pieces.transpose(1, 0, 2).reshape(quarter, MODEL_WIDTH).astype(F32)
    output_own = (hidden_last + moe).astype(BF)
    own_grad_kv = grad_kv_own + kv_back.astype(F32)
    grad_key = own_grad_kv[:, :HEAD_SIZE]
    grad_kv = jnp.concatenate(
        [grad_key * cosine - swapped(grad_key) * sine, own_grad_kv[:, HEAD_SIZE:]], axis=1
    ).astype(BF)
    grad_in = jnp.concatenate([grad_q_all, grad_kv, grad_logit_a], axis=1)
    grad_xn1_part = lax.dot_general(grad_in, in_w, LAST, preferred_element_type=F32).astype(BF)
    grad_xn1_part, moe_pieces = lax.optimization_barrier((grad_xn1_part, moe_pieces))
    gain_row = jnp.pad(gain_m_part[None].astype(BF), ((0, 7), (0, 0)))
    lane = jnp.arange(1408, dtype=jnp.int32)[None, :]
    router_cols = jnp.pad(grad_logit_m.astype(BF), ((0, 0), (1288, 112)))
    gain_cols = ((jnp.arange(8)[:, None] == 0) & (lane == 1296)).astype(BF)
    in_pairs = [
        (xn1, after(grad_in, grad_xn1_part)),
        (
            jnp.concatenate([xn2_own, gain_row], axis=0),
            jnp.concatenate([router_cols, gain_cols], axis=0),
        ),
    ]
    in_give = lax.ppermute(give_terms(in_pairs, z, core), "core", SWAP)
    out_own, *out_rest = keep_terms(out_pairs, after(out_give, grad_xn1_part), z, core)
    in_own_rows, *in_rest = keep_terms(in_pairs, in_give, z, core)
    out_rest[0], out_rest[3], _ = lax.optimization_barrier(
        (out_rest[0], out_rest[3], in_own_rows)
    )
    out_ahead, out_back = ring_first(*out_rest, "dp")
    in_ahead, in_back = ring_first(*in_rest, "dp")
    out_sum = ring_second(after(out_own, gate_up_sum), out_ahead, out_back, "dp").astype(BF)
    landed_raw = exchange(grad_xn1_part.reshape(16, quarter, MODEL_WIDTH), plane)
    landed_raw, *_ = lax.optimization_barrier((landed_raw, in_ahead, in_back))
    out_sum, down_sum = lax.optimization_barrier((out_sum, down_sum))
    in_sum = ring_second(in_own_rows, in_ahead, in_back, "dp").astype(BF)
    landed_a = landed_raw.astype(F32).sum(axis=0)
    grad_x_norm, _ = norm_back(landed_a, own_values, own_factor, gain_a)
    columns = jnp.arange(1408, dtype=jnp.int32)[None, :]
    gain_a_part = jnp.sum(
        jnp.where(columns < 1288, in_sum.astype(F32) * mine[:, :1408].astype(F32), 0.0),
        axis=1,
        keepdims=True,
    )
    small_part = jnp.where(columns[:, :128] == 17, gain_a_part, in_sum[:, 1280:].astype(F32))
    gain_rows = lax.dynamic_slice_in_dim(attn_gain.astype(F32), z * 512 + y * 128 + core * 64, 64)

    ends = jnp.concatenate(
        [output_own, core_last((grad_hidden + grad_x_norm).astype(BF))], axis=1
    )
    ends, out_sum = lax.optimization_barrier((ends, out_sum))
    both_sums = jnp.concatenate(
        [in_sum[:, :1280], out_sum, small_part.astype(BF)], axis=1
    ).reshape(4, 64, 2432)
    y_parts = send_direct(both_sums, "y")
    gate_up_grad = (
        after(gate_up_sum, both_sums)
        .reshape(2, 4, 64, 2816)
        .transpose(1, 0, 2, 3)
        .reshape(1, 512, 2, width)
        .astype(F32)
    )
    _, _, *y_parts = lax.optimization_barrier((gate_up_grad, ends, *y_parts))
    both_ends = spread(ends, "tensor", 4)
    small_y = sum(p[:, 2304:].astype(F32) for p in y_parts).astype(BF)
    small_y = after(small_y, both_ends)
    small_sum = small_y.astype(F32) + sum(
        from_ahead(small_y, "tensor", k).astype(F32) for k in (1, 2, 3)
    )
    down_grad = down_sum.astype(F32)[None]
    both_ends = both_ends.reshape(count, 2 * MODEL_WIDTH)
    output, input_grad = both_ends[:, :MODEL_WIDTH], both_ends[:, MODEL_WIDTH:]
    query_grad, kv_grad, out_grad = heads_placed(y_parts, y)
    return (
        output,
        input_grad,
        small_sum[:, 17] / gain_rows,
        small_sum[:, 16],
        small_sum[:, :8],
        kv_grad,
        query_grad,
        out_grad,
        small_sum[:, 8:16],
        gate_up_grad,
        down_grad,
    )


def solution(mesh):
    split = Mesh(mesh.devices.reshape(4, 4, 2, 4), ("dp", "y", "core", "tensor"))
    rows = ("dp", "y", "core")
    expert = ("y", "core")
    placed = (
        P(rows, None),
        P(rows, None),
        P(),
        P(),
        P(rows, None),
        P(rows, None, "tensor"),
        P(rows, None, "tensor"),
        P(rows, None, "tensor"),
        P(rows, None),
        P(expert, "dp", None, "tensor"),
        P(expert, "tensor", "dp"),
        P(rows, None),
        P(rows, None),
        P(rows, None),
        P(),
    )
    return jax.shard_map(
        body,
        mesh=split,
        in_specs=placed,
        out_specs=(
            P(rows, None),
            P(rows, None),
            P(rows),
            P(rows),
            P(rows, None),
            P(rows, None, "tensor"),
            P(rows, None, "tensor"),
            P(rows, None, "tensor"),
            P(rows, None),
            P(expert, "dp", None, "tensor"),
            P(expert, "tensor", "dp"),
        ),
        check_vma=False,
    )
```

```python
import jax
import jax.numpy as jnp
from jax import lax
from jax.experimental import pallas as pl
from jax.experimental.pallas import tpu as pltpu
from jax.sharding import Mesh
from jax.sharding import PartitionSpec as P

MODEL_WIDTH = 2048
HEAD_SIZE = 128
EXPERTS = 8
WINDOW = 1024
NORM_EPS = 1e-06
BF = jnp.bfloat16
F32 = jnp.float32
ROWS = (((0,), (0,)), ((), ()))
LAST = (((1,), (1,)), ((), ()))
UP = [(0, 1), (1, 2), (2, 3), (3, 0)]
DOWN = [(0, 3), (1, 0), (2, 1), (3, 2)]
SWAP = [(0, 1), (1, 0)]


def exchange(blocks, axis):
    return lax.all_to_all(blocks, axis, split_axis=0, concat_axis=0, tiled=True)


def spread(block, axis, count):
    return exchange(jnp.broadcast_to(block, (count, *block.shape)), axis)


def from_ahead(block, axis, steps):
    return lax.ppermute(block, axis, [(i, (i - steps) % 4) for i in range(4)])


def in_order(pieces, first):
    both = jnp.stack(pieces + pieces[:3])
    return lax.dynamic_slice_in_dim(both, lax.rem(4 - first, 4), 4)


def pick_block(blocks, index):
    return lax.dynamic_index_in_dim(blocks, lax.rem(index, 4), 0, keepdims=False)


def send_direct(blocks, axis):
    me = lax.axis_index(axis)
    return [pick_block(blocks, me)] + [
        from_ahead(pick_block(blocks, me + 4 - k), axis, k) for k in (1, 2, 3)
    ]


def heads_first(shard):
    columns = shard.shape[1] * HEAD_SIZE
    return shard.reshape(64, -1, 4, HEAD_SIZE).transpose(2, 0, 1, 3).reshape(4, 64, columns)


def after(value, other):
    return lax.optimization_barrier((value, other))[0]


def core_first(rows):
    return rows.reshape(-1, 4, 4, 2, 64).transpose(0, 1, 3, 2, 4).reshape(-1, MODEL_WIDTH)


def core_last(rows):
    return rows.reshape(-1, 4, 2, 4, 64).transpose(0, 1, 3, 2, 4).reshape(-1, MODEL_WIDTH)


def ring_first(ahead, low, high, back, axis):
    low = lax.ppermute(low, axis, UP)
    high = lax.ppermute(high, axis, DOWN)
    half = low.shape[0]
    ahead = jnp.concatenate([(ahead[:half].astype(F32) + low.astype(F32)).astype(BF), ahead[half:]])
    back = jnp.concatenate([back[:half], (back[half:].astype(F32) + high.astype(F32)).astype(BF)])
    return ahead, back


def ring_second(own, ahead, back, axis):
    return (
        own.astype(F32)
        + lax.ppermute(ahead, axis, UP).astype(F32)
        + lax.ppermute(back, axis, DOWN).astype(F32)
    )


def rms_scale(values):
    return lax.rsqrt(jnp.mean(values * values, axis=-1, keepdims=True) + NORM_EPS)


def turn(heads, cosine, sine):
    first, second = heads[..., :64], heads[..., 64:]
    return jnp.concatenate([first * cosine - second * sine, second * cosine + first * sine], axis=-1)


EXTENTS = (256, 384, 512, 640)
SCALE = HEAD_SIZE**-0.5


def masked_scores(query, key, row_meta, key_meta):
    raw = lax.dot_general(query, key, LAST, preferred_element_type=F32) * SCALE
    gap = row_meta[:, 0:1] - key_meta[0:1]
    allowed = (gap >= 0) & (gap < WINDOW) & (row_meta[:, 1:2] == key_meta[1:2])
    return jnp.where(jnp.concatenate([allowed, allowed], axis=0), raw, -1e30)


def forward_kernel(proj, own, other, routes, cosine, sine, row_meta, key_meta, *outs):
    query_out, attended_out, total_out, gates_out, mixed_out = outs
    count = proj.shape[0] // 4
    for i in range(4):
        rows = pl.ds(count * i, count)
        extent = EXTENTS[i]
        logits = proj[rows, 1280:1288]
        lane = lax.broadcasted_iota(jnp.int32, (count, EXPERTS), 1)
        named = [routes[rows, 0:1], routes[rows, 1:2]]
        chosen = [jnp.sum(jnp.where(lane == n, logits, 0.0), axis=1, keepdims=True) for n in named]
        top = jnp.maximum(chosen[0], chosen[1])
        power = [jnp.exp(c - top) for c in chosen]
        gates = [p / (power[0] + power[1]) for p in power]
        gates_out[rows, 0:1] = gates[0]
        gates_out[rows, 1:2] = gates[1]
        cos, sin = cosine[rows, :], sine[rows, :]
        picked = []
        for n in named:
            q = jnp.zeros((count, HEAD_SIZE), F32)
            for e in range(EXPERTS):
                q = q + jnp.where(n == e, proj[rows, HEAD_SIZE * e : HEAD_SIZE * (e + 1)], 0.0)
            picked.append(q * cos + pltpu.roll(q, 64, 1) * sin)
        query = jnp.concatenate(picked, axis=0).astype(BF)
        query_out[i] = query
        halves = (own, other)
        scores = [
            masked_scores(
                query, h[:extent, :HEAD_SIZE], row_meta[rows, :], key_meta[k, :, :extent]
            )
            for k, h in enumerate(halves)
        ]
        row_max = jnp.maximum(
            jnp.max(scores[0], axis=1, keepdims=True), jnp.max(scores[1], axis=1, keepdims=True)
        )
        weights = [jnp.exp(s - row_max) for s in scores]
        total = jnp.sum(weights[0], axis=1, keepdims=True) + jnp.sum(weights[1], axis=1, keepdims=True)
        inverse = 1.0 / total
        attended = sum(
            jnp.dot((w * inverse).astype(BF), h[:extent, HEAD_SIZE:], preferred_element_type=F32)
            for w, h in zip(weights, halves)
        )
        attended_out[i] = attended
        total_out[i] = row_max + jnp.log(total)
        for e in range(EXPERTS):
            mixed_out[rows, HEAD_SIZE * e : HEAD_SIZE * (e + 1)] = (
                jnp.where(named[0] == e, gates[0], 0.0) * attended[:count]
                + jnp.where(named[1] == e, gates[1], 0.0) * attended[count:]
            ).astype(BF)


def backward_kernel(
    grad_mixed, query_in, own, other, attended_in, total_in, gates_in, routes, cosine, sine, row_meta, key_meta, *outs
):
    grad_query_out, grad_logit_out, grad_own_out, grad_other_out, sums = outs
    count = grad_mixed.shape[0] // 4
    sums[...] = jnp.zeros_like(sums)
    for i in range(4):
        rows = pl.ds(count * i, count)
        extent = EXTENTS[i]
        named = [routes[rows, 0:1], routes[rows, 1:2]]
        gates = [gates_in[rows, 0:1], gates_in[rows, 1:2]]
        cos, sin = cosine[rows, :], sine[rows, :]
        attended = attended_in[i]
        picked = []
        for n in named:
            g = jnp.zeros((count, HEAD_SIZE), F32)
            for e in range(EXPERTS):
                g = g + jnp.where(n == e, grad_mixed[rows, HEAD_SIZE * e : HEAD_SIZE * (e + 1)], 0.0)
            picked.append(g)
        gate_grads = [
            jnp.sum(p * attended[count * j : count * (j + 1)], axis=1, keepdims=True)
            for j, p in enumerate(picked)
        ]
        level = gates[0] * gate_grads[0] + gates[1] * gate_grads[1]
        lane = lax.broadcasted_iota(jnp.int32, (count, HEAD_SIZE), 1)
        grad_logit_out[rows, :] = sum(
            jnp.where(lane == n, g * (d - level), 0.0) for n, g, d in zip(named, gates, gate_grads)
        ).astype(BF)
        grad_attended = jnp.concatenate(
            [gates[0] * picked[0], gates[1] * picked[1]], axis=0
        ).astype(BF)
        query = query_in[i]
        total = total_in[i]
        probs, grad_probs = [], []
        delta = jnp.zeros((2 * count, 1), F32)
        for k, h in enumerate((own, other)):
            score = masked_scores(
                query, h[:extent, :HEAD_SIZE], row_meta[rows, :], key_meta[k, :, :extent]
            )
            prob = jnp.exp(score - total)
            grad_prob = lax.dot_general(
                grad_attended, h[:extent, HEAD_SIZE:], LAST, preferred_element_type=F32
            )
            delta = delta + jnp.sum(prob * grad_prob, axis=1, keepdims=True)
            probs.append(prob)
            grad_probs.append(grad_prob)
        grad_query = jnp.zeros((2 * count, HEAD_SIZE), F32)
        for k, h in enumerate((own, other)):
            grad_score = (probs[k] * (grad_probs[k] - delta)).astype(BF)
            grad_query = grad_query + jnp.dot(
                grad_score, h[:extent, :HEAD_SIZE], preferred_element_type=F32
            )
            sums[k, :extent, :HEAD_SIZE] += (
                lax.dot_general(grad_score, query, ROWS, preferred_element_type=F32) * SCALE
            )
            sums[k, :extent, HEAD_SIZE:] += lax.dot_general(
                probs[k].astype(BF), grad_attended, ROWS, preferred_element_type=F32
            )
        grad_query = grad_query * SCALE
        turned = [
            g * cos - pltpu.roll(g, 64, 1) * sin for g in (grad_query[:count], grad_query[count:])
        ]
        for e in range(EXPERTS):
            grad_query_out[rows, HEAD_SIZE * e : HEAD_SIZE * (e + 1)] = (
                jnp.where(named[0] == e, turned[0], 0.0) + jnp.where(named[1] == e, turned[1], 0.0)
            ).astype(BF)
    grad_own_out[...] = sums[0]
    grad_other_out[...] = sums[1].astype(BF)


def in_vmem(kernel, outs, scratch, flops, *args):
    spec = pl.BlockSpec(memory_space=pltpu.VMEM)
    moved = sum(a.size * a.dtype.itemsize for a in args)
    return pl.pallas_call(
        kernel,
        out_shape=outs,
        in_specs=[spec] * len(args),
        out_specs=[spec] * len(outs),
        scratch_shapes=scratch,
        compiler_params=pltpu.CompilerParams(vmem_limit_bytes=40 * 1024 * 1024),
        cost_estimate=pl.CostEstimate(flops=flops, bytes_accessed=moved, transcendentals=1 << 20),
    )(*args)


SOME = pl.CostEstimate(flops=1 << 35, bytes_accessed=1 << 27, transcendentals=0)


def on_grid(kernel, scalars, grid, in_specs, out_specs, outs, scratch, *args, cost=SOME):
    return pl.pallas_call(
        kernel,
        out_shape=outs,
        grid_spec=pltpu.PrefetchScalarGridSpec(
            num_scalar_prefetch=1,
            grid=grid,
            in_specs=in_specs,
            out_specs=out_specs,
            scratch_shapes=scratch,
        ),
        compiler_params=pltpu.CompilerParams(vmem_limit_bytes=48 * 1024 * 1024),
        cost_estimate=cost,
    )(jnp.stack(scalars).astype(jnp.int32), *args)


def give_terms(pairs, place, core):
    columns = pairs[0][1].shape[1]

    def kernel(at, *refs):
        out = refs[-1]
        total = sum(
            lax.dot_general(refs[j][...], refs[j + 1][...], ROWS, preferred_element_type=F32)
            for j in range(0, len(refs) - 1, 2)
        )
        out[0] = total.astype(BF)

    specs = []
    for tall, terms in pairs:
        specs.append(pl.BlockSpec((tall.shape[0], 256), lambda i, at: (0, 2 * i + 1 - at[1])))
        specs.append(pl.BlockSpec(terms.shape, lambda i, at: (0, 0)))
    return on_grid(
        kernel,
        (place, core),
        (4,),
        specs,
        pl.BlockSpec((1, 256, columns), lambda i, at: (i, 0, 0)),
        jax.ShapeDtypeStruct((4, 256, columns), BF),
        [],
        *[a for pair in pairs for a in pair],
    )


def keep_terms(pairs, landed, place, core):
    columns = pairs[0][1].shape[1]
    count = 2 * len(pairs)

    def kernel(at, *refs):
        more, own, ahead, low, high, back = refs[count:]
        total = sum(
            lax.dot_general(refs[j][...], refs[j + 1][...], ROWS, preferred_element_type=F32)
            for j in range(0, count, 2)
        )
        total = (total.astype(BF).astype(F32) + more[0].astype(F32)).astype(BF)
        step = pl.program_id(0)

        @pl.when(step == 0)
        def _():
            own[...] = total

        @pl.when(step == 1)
        def _():
            ahead[...] = total

        @pl.when(step == 2)
        def _():
            low[...] = total[:128]
            high[...] = total[128:]

        @pl.when(step == 3)
        def _():
            back[...] = total

    def whole(rows):
        return pl.BlockSpec((rows, columns), lambda i, at: (0, 0))

    specs = []
    for tall, terms in pairs:
        specs.append(
            pl.BlockSpec(
                (tall.shape[0], 256), lambda i, at: (0, 2 * lax.rem(at[0] + i, 4) + at[1])
            )
        )
        specs.append(pl.BlockSpec(terms.shape, lambda i, at: (0, 0)))
    specs.append(pl.BlockSpec((1, 256, columns), lambda i, at: (lax.rem(at[0] + i, 4), 0, 0)))
    return on_grid(
        kernel,
        (place, core),
        (4,),
        specs,
        [whole(256), whole(256), whole(128), whole(128), whole(256)],
        [jax.ShapeDtypeStruct((r, columns), BF) for r in (256, 256, 128, 128, 256)],
        [],
        *[a for pair in pairs for a in pair],
        landed,
    )


def gate_up_product(rows, pair):
    depth, width = pair.shape[1:]

    def kernel(at, left, right, out):
        for half in range(2):
            out[:, width * half : width * (half + 1)] = lax.dot_general(
                left[...], right[half], ROWS, preferred_element_type=F32
            ).astype(BF)

    return on_grid(
        kernel,
        (jnp.int32(0),),
        (8,),
        [
            pl.BlockSpec((depth, 256), lambda i, at: (0, i)),
            pl.BlockSpec((2, depth, width), lambda i, at: (0, 0, 0)),
        ],
        pl.BlockSpec((256, 2 * width), lambda i, at: (i, 0)),
        jax.ShapeDtypeStruct((MODEL_WIDTH, 2 * width), BF),
        [],
        rows,
        pair,
    )


def down_product(activated, grads, gate):
    def kernel(at, left, right, scale, out):
        scaled = (scale[...] * right[...].astype(F32)).astype(BF)
        out[...] = lax.dot_general(left[...], scaled, ROWS, preferred_element_type=F32).astype(BF)

    depth, width = activated.shape
    return on_grid(
        kernel,
        (jnp.int32(0),),
        (4,),
        [
            pl.BlockSpec((depth, width), lambda i, at: (0, 0)),
            pl.BlockSpec((depth, 512), lambda i, at: (0, i)),
            pl.BlockSpec((depth, 1), lambda i, at: (0, 0)),
        ],
        pl.BlockSpec((width, 512), lambda i, at: (0, i)),
        jax.ShapeDtypeStruct((width, MODEL_WIDTH), BF),
        [],
        activated,
        grads,
        gate,
    )


def down_back(grads, pieces, place):
    def kernel(at, left, own, ahead, far_a, far_b, back, out):
        total = None
        for shift, start, piece in (
            (0, 0, own), (1, 0, ahead), (2, 0, far_a), (2, 256, far_b), (3, 0, back)
        ):
            size = piece.shape[1]
            lanes = pl.ds(pl.multiple_of(lax.rem(at[0] + shift, 4) * 512 + start, 256), size)
            term = lax.dot_general(left[:, lanes], piece[...], LAST, preferred_element_type=F32)
            total = term if total is None else total + term
        out[...] = total

    depth, width = grads.shape[0], pieces[0].shape[0]
    return on_grid(
        kernel,
        (place,),
        (width // 128,),
        [pl.BlockSpec(grads.shape, lambda i, at: (0, 0))]
        + [pl.BlockSpec((128, p.shape[1]), lambda i, at: (i, 0)) for p in pieces],
        pl.BlockSpec((depth, 128), lambda i, at: (0, i)),
        jax.ShapeDtypeStruct((depth, width), F32),
        [],
        grads,
        *pieces,
    )


def expert_quarters(activated, pieces, place, x):
    def kernel(at, left, own, ahead, far_a, far_b, back, out):
        step = pl.program_id(0)
        for shift, refs in enumerate(((own,), (ahead,), (far_a, far_b), (back,))):

            @pl.when(step == shift)
            def _():
                terms = [jnp.dot(left[...], r[...], preferred_element_type=F32) for r in refs]
                out[0] = jnp.concatenate(terms, axis=1).astype(BF)

    depth = activated.shape[0]
    return on_grid(
        kernel,
        (place, x),
        (4,),
        [pl.BlockSpec(a.shape, lambda i, at: (0, 0)) for a in (activated, *pieces)],
        pl.BlockSpec((1, depth, 512), lambda i, at: (lax.rem(at[0] + i + 4 - at[1], 4), 0, 0)),
        jax.ShapeDtypeStruct((4, depth, 512), BF),
        [],
        activated,
        *pieces,
    )


def expert_middle(rows, marks, router, gate_up_w, grad_act, expert):
    depth, width = grad_act.shape
    blocks = width // 128

    def kernel(
        at, rows_ref, marks_ref, router_ref, gate_ref, up_ref, flat_ref, grad_ref,
        act_out, pair_out, gate_out, back_out, pair_all, row_gate, row_grad,
    ):
        step = pl.program_id(0)
        lane = lax.broadcasted_iota(jnp.int32, (depth, 128), 1)

        @pl.when(step == 0)
        def _():
            logits = jnp.dot(rows_ref[...], router_ref[...], preferred_element_type=F32)
            marks_f = marks_ref[...].astype(F32)
            own = jnp.sum(jnp.where(lane == at[0], logits, 0.0), axis=1, keepdims=True)
            other = jnp.sum(jnp.where(lane < 8, logits * marks_f, 0.0), axis=1, keepdims=True)
            valid = jnp.sum(jnp.where(lane == 8, marks_f, 0.0), axis=1, keepdims=True)
            top = jnp.maximum(own, other)
            power = jnp.exp(own - top)
            row_gate[...] = valid * power / (power + jnp.exp(other - top))
            gate_out[...] = row_gate[...]
            row_grad[...] = jnp.zeros_like(row_grad)

        @pl.when(step < blocks)
        def _():
            both = jnp.concatenate([gate_ref[...], up_ref[...]], axis=1)
            gate_up = jnp.dot(rows_ref[...], both, preferred_element_type=F32)
            gate, up = gate_up[:, :128], gate_up[:, 128:]
            sigmoid = 1.0 / (1.0 + jnp.exp(-gate))
            silu = gate * sigmoid
            act = (silu * up).astype(BF)
            raw = grad_ref[...]
            grad = row_gate[...] * raw
            grad_gate = (grad * up * sigmoid * (1.0 + gate * (1.0 - sigmoid))).astype(BF)
            grad_up = (grad * silu).astype(BF)
            act_out[...] = act
            pair_out[0] = grad_gate
            pair_out[1] = grad_up
            at_lane = pl.multiple_of(step * 128, 128)
            pair_all[:, pl.ds(at_lane, 128)] = grad_gate
            pair_all[:, pl.ds(at_lane + width, 128)] = grad_up
            row_grad[...] += jnp.sum(act.astype(F32) * raw, axis=1, keepdims=True)

        @pl.when(step >= blocks)
        def _():
            back_lane = pl.multiple_of((step - blocks) * 512, 512)
            back_out[:, pl.ds(back_lane, 512)] = lax.dot_general(
                pair_all[...], flat_ref[...], LAST, preferred_element_type=F32
            ).astype(BF)

        @pl.when(step == blocks + 3)
        def _():
            high = row_grad[...].astype(BF).astype(F32)
            low = row_grad[...] - high
            back_out[:, MODEL_WIDTH:] = jnp.where(
                lane == 0, high, jnp.where(lane == 1, low, 0.0)
            ).astype(BF)

    def first(i):
        return jnp.minimum(i, blocks - 1)

    def second(i):
        return jnp.clip(i - blocks, 0, 3)

    return on_grid(
        kernel,
        (expert,),
        (blocks + 4,),
        [
            pl.BlockSpec((depth, MODEL_WIDTH), lambda i, at: (0, 0)),
            pl.BlockSpec((depth, 128), lambda i, at: (0, 0)),
            pl.BlockSpec((MODEL_WIDTH, 128), lambda i, at: (0, 0)),
            pl.BlockSpec((MODEL_WIDTH, 128), lambda i, at: (0, first(i))),
            pl.BlockSpec((MODEL_WIDTH, 128), lambda i, at: (0, blocks + first(i))),
            pl.BlockSpec((512, 2 * width), lambda i, at: (second(i), 0)),
            pl.BlockSpec((depth, 128), lambda i, at: (0, first(i))),
        ],
        [
            pl.BlockSpec((depth, 128), lambda i, at: (0, first(i))),
            pl.BlockSpec((2, depth, 128), lambda i, at: (0, 0, first(i))),
            pl.BlockSpec((depth, 1), lambda i, at: (0, 0)),
            pl.BlockSpec((depth, MODEL_WIDTH + 128), lambda i, at: (0, 0)),
        ],
        [
            jax.ShapeDtypeStruct((depth, width), BF),
            jax.ShapeDtypeStruct((2, depth, width), BF),
            jax.ShapeDtypeStruct((depth, 1), F32),
            jax.ShapeDtypeStruct((depth, MODEL_WIDTH + 128), BF),
        ],
        [
            pltpu.VMEM((depth, 2 * width), BF),
            pltpu.VMEM((depth, 1), F32),
            pltpu.VMEM((depth, 1), F32),
        ],
        rows,
        marks,
        router,
        gate_up_w,
        gate_up_w,
        gate_up_w,
        grad_act,
        cost=pl.CostEstimate(
            flops=8 * depth * MODEL_WIDTH * width, bytes_accessed=1 << 24, transcendentals=1 << 20
        ),
    )


def heads_placed(pieces, y):
    def kernel(at, p0, p1, p2, p3, query, kv, out):
        for k, piece in enumerate((p0, p1, p2, p3)):
            lanes = pl.ds(pl.multiple_of(lax.rem(at[0] + k, 4) * 128, 128), 128)
            for e in range(18):
                block = piece[:, 128 * e : 128 * (e + 1)].astype(F32)
                if e < 8:
                    query[:, e, lanes] = block
                elif e < 10:
                    kv[:, e - 8, lanes] = block
                else:
                    out[:, e - 10, lanes] = block

    shapes = [(64, 8, 512), (64, 2, 512), (64, 8, 512)]
    return on_grid(
        kernel,
        (y,),
        (1,),
        [pl.BlockSpec((64, 2432), lambda i, at: (0, 0))] * 4,
        [pl.BlockSpec(s, lambda i, at: (0, 0, 0)) for s in shapes],
        [jax.ShapeDtypeStruct(s, F32) for s in shapes],
        [],
        *pieces,
        cost=pl.CostEstimate(flops=0, bytes_accessed=0, transcendentals=0),
    )


def pick_of(routes):
    return (routes[:, :, None] == jnp.arange(EXPERTS, dtype=jnp.int32)[None, None, :]).astype(F32)


def pair_gates(logits, pick):
    chosen = jnp.sum(logits[:, None, :] * pick, axis=-1)
    weights = jnp.exp(chosen - jnp.max(chosen, axis=1, keepdims=True))
    return weights / jnp.sum(weights, axis=1, keepdims=True)


def gate_back(gates, grad_gates, pick):
    inner = gates * (grad_gates - jnp.sum(gates * grad_gates, axis=1, keepdims=True))
    return jnp.sum(inner[:, :, None] * pick, axis=1)


def norm_back(grad_normed, values, factor, gain):
    gain_part = jnp.sum(grad_normed * values * factor, axis=0)
    inner = grad_normed * gain
    grad_values = factor * inner - values * factor * factor * factor * jnp.mean(
        inner * values, axis=-1, keepdims=True
    )
    return grad_values, gain_part


def in_two(values):
    high = values.astype(BF)
    low = (values - high.astype(F32)).astype(BF)
    return jnp.concatenate([high, low], axis=1)


def widen(columns):
    return jnp.pad(columns, ((0, 0), (0, HEAD_SIZE - columns.shape[1])))


def body(
    tokens,
    cotangent,
    attn_gain,
    mlp_gain,
    attn_router,
    key_value_weight,
    query_matrix,
    output_matrix,
    mlp_router,
    gate_up_weight,
    down_weight,
    attn_routes,
    mlp_routes,
    priority,
    segments,
):
    z, y = lax.axis_index("dp"), lax.axis_index("y")
    core, x = lax.axis_index("core"), lax.axis_index("tensor")
    count = tokens.shape[0]
    quarter = count // 4
    capacity = 50
    room = 56
    sequence = 8 * count
    plane = ("y", "tensor")

    routers_own = jnp.concatenate([attn_router, mlp_router], axis=1)
    down_own = down_weight[0]
    down_before = lax.ppermute(down_own, "dp", UP)
    down_after = lax.ppermute(down_own, "dp", DOWN)
    mine = exchange(
        jnp.concatenate(
            [
                heads_first(query_matrix),
                heads_first(key_value_weight),
                jnp.broadcast_to(widen(routers_own), (4, 64, HEAD_SIZE)),
                heads_first(output_matrix),
            ],
            axis=2,
        ),
        "y",
    ).reshape(256, 2432)
    sent = jnp.concatenate([core_first(tokens), widen(attn_routes.astype(BF))], axis=1)
    arrived = spread(after(sent, mine), "y", 4).reshape(4 * count, MODEL_WIDTH + HEAD_SIZE)
    all_w = lax.all_gather(
        after(mine, (down_before, down_after)), ("dp", "core"), axis=0, tiled=True
    )
    values = arrived[:, :MODEL_WIDTH].astype(F32)
    routes = arrived[:, MODEL_WIDTH : MODEL_WIDTH + 2].astype(jnp.int32)
    gain_a = core_first(attn_gain.astype(F32))[0]
    gain_m = core_first(mlp_gain.astype(F32))[0]
    xn1 = (values * rms_scale(values) * gain_a).astype(BF)

    ranking = priority[0]
    pick_m = pick_of(mlp_routes)
    before = (ranking[None, :] < ranking[:, None]).astype(BF)
    earlier = jnp.dot(before, jnp.sum(pick_m, axis=1).astype(BF), preferred_element_type=F32)
    slots = jnp.sum(pick_m * earlier[:, None, :], axis=-1).astype(jnp.int32)
    kept = slots < capacity
    dest = jnp.where(kept, mlp_routes * room + slots, -1)
    lanes = jnp.arange(EXPERTS * room, dtype=jnp.int32)
    to_row = (dest.T[:, :, None] == lanes[None, None, :]).astype(BF)
    any_row = to_row[0] + to_row[1]
    both_rows = to_row.reshape(2 * count, EXPERTS * room)

    def to_experts(rows):
        columns = rows.shape[1]
        return exchange(rows.reshape(EXPERTS, room, columns), ("y", "core")).reshape(
            EXPERTS * room, columns
        )

    def with_other(j):
        others = jnp.concatenate([pick_m[:, 1 - j], jnp.ones((count, 1), F32)], axis=1)
        return jnp.concatenate([cotangent, widen(others.astype(BF))], axis=1)

    grad_sent = lax.dot_general(
        both_rows,
        jnp.concatenate([with_other(0), with_other(1)], axis=0),
        ROWS,
        preferred_element_type=F32,
    ).astype(BF)
    def places(half):
        blocks = 2 * jnp.arange(4, dtype=jnp.int32)[:, None] + half
        return (blocks * count + jnp.arange(count, dtype=jnp.int32)[None, :]).reshape(-1)

    inverse = 10000.0 ** (-(jnp.arange(HEAD_SIZE // 2).astype(F32) * 2.0 / HEAD_SIZE))
    angle = places(core).astype(F32)[:, None] * inverse[None, :]
    cosine = jnp.tile(jnp.cos(angle), (1, 2))
    sine = jnp.concatenate([-jnp.sin(angle), jnp.sin(angle)], axis=1)

    first = x * quarter
    cot_own = core_first(lax.dynamic_slice_in_dim(cotangent, first, quarter)).astype(F32)
    all_w, down_before, down_after, xn1, grad_sent, cosine, sine, cot_own = (
        lax.optimization_barrier(
            (all_w, down_before, down_after, xn1, grad_sent, cosine, sine, cot_own)
        )
    )
    in_w, out_w = all_w[:, :1408], all_w[:, 1408:]
    far_a = lax.ppermute(down_before[:, :256], "dp", UP)
    far_b = lax.ppermute(down_after[:, 256:], "dp", DOWN)
    down_pieces = (down_own, down_after, far_a, far_b, down_before)
    gate_up_own = gate_up_weight.reshape(4, 2, 64, 2816).transpose(1, 0, 2, 3).reshape(512, 2816)
    gate_up_w = lax.all_gather(after(gate_up_own, all_w), "dp", axis=0, tiled=True)
    router_m = in_w[:, 1288:1296]

    grad_landed = to_experts(grad_sent)

    of_sequence = lax.dynamic_slice_in_dim(segments, z * sequence, sequence).reshape(4, 2, count)

    def meta(half):
        documents = lax.dynamic_index_in_dim(of_sequence, half, 1, keepdims=False).reshape(-1)
        return jnp.stack([places(half), documents])

    key_meta = jnp.stack([meta(core), meta(1 - core)])
    row_meta = key_meta[0].T
    def swapped(rows):
        return jnp.concatenate([rows[:, 64:], rows[:, :64]], axis=1)

    half = 4 * count
    projected = jnp.dot(xn1, in_w, preferred_element_type=F32)
    key_raw = projected[:, 1024:1152]
    kv_own = jnp.concatenate(
        [key_raw * cosine + swapped(key_raw) * sine, projected[:, 1152:1280]], axis=1
    ).astype(BF)
    kv_other = lax.ppermute(kv_own, "core", SWAP)
    shared = (routes, cosine, sine, row_meta, key_meta)
    query, attended, totals, gate_a, mixed = in_vmem(
        forward_kernel,
        [
            jax.ShapeDtypeStruct((4, 2 * count, HEAD_SIZE), BF),
            jax.ShapeDtypeStruct((4, 2 * count, HEAD_SIZE), F32),
            jax.ShapeDtypeStruct((4, 2 * count, 1), F32),
            jax.ShapeDtypeStruct((half, 2), F32),
            jax.ShapeDtypeStruct((half, EXPERTS * HEAD_SIZE), BF),
        ],
        [],
        6 << 28,
        projected,
        kv_own,
        kv_other,
        *shared,
    )
    branch_part = lax.dot_general(mixed, out_w, LAST, preferred_element_type=F32).astype(BF)
    branch_part = after(branch_part, grad_landed)
    grad_received = grad_landed[:, :MODEL_WIDTH]
    branch = exchange(branch_part.reshape(16, quarter, MODEL_WIDTH), plane).astype(F32).sum(axis=0)

    own_values = lax.dynamic_slice_in_dim(values, y * count + first, quarter)
    own_factor = rms_scale(own_values)
    hidden = after(own_values, (far_a, far_b)) + branch
    factor_m = rms_scale(hidden)
    xn2_own = (hidden * factor_m * gain_m).astype(BF)
    xn2 = spread(xn2_own, "tensor", 4).reshape(count, MODEL_WIDTH)
    gate_m = pair_gates(jnp.dot(xn2, router_m, preferred_element_type=F32), pick_m)

    received = to_experts(
        lax.dot_general(any_row, xn2, ROWS, preferred_element_type=F32).astype(BF)
    )
    grad_act_raw = down_back(grad_received, down_pieces, z)
    received, grad_act_raw, hidden_last, gate_m = lax.optimization_barrier(
        (received, grad_act_raw, core_last(hidden), gate_m)
    )
    weight_m = gate_m * kept.astype(F32)
    activated, grad_pair, row_gate, grad_back = expert_middle(
        received,
        grad_landed[:, MODEL_WIDTH:],
        jnp.pad(router_m, ((0, 0), (0, 120))),
        gate_up_w,
        grad_act_raw,
        2 * y + core,
    )
    grad_back, late_pair, late_act = lax.optimization_barrier((grad_back, grad_pair, activated))
    grad_returned = to_experts(grad_back)
    grad_down_w = down_product(late_act, grad_received, row_gate)
    down_sum = lax.psum_scatter(grad_down_w, "dp", scatter_dimension=1, tiled=True)
    quarters = expert_quarters(late_act, down_pieces, z, x)
    grad_gate_up_w = gate_up_product(received, late_pair)
    gate_up_sum = lax.psum_scatter(grad_gate_up_w, "dp", scatter_dimension=0, tiled=True)
    late_any = after(any_row, (grad_down_w, quarters, grad_gate_up_w))
    expert_out = (
        quarters[0].astype(F32)
        + sum(from_ahead(quarters[4 - k], "tensor", k).astype(F32) for k in (1, 2, 3))
    ).astype(BF)

    grad_xn2_part = jnp.dot(
        late_any, grad_returned[:, :MODEL_WIDTH], preferred_element_type=F32
    ).astype(BF)
    row_gate_parts = grad_returned[:, MODEL_WIDTH : MODEL_WIDTH + 2]
    gate_m_part = jnp.sum(
        jnp.einsum("jtr,rd->tjd", to_row, row_gate_parts, preferred_element_type=F32), axis=2
    )
    shares = jnp.concatenate([grad_xn2_part, widen(in_two(gate_m_part))], axis=1)
    landed = (
        exchange(shares.reshape(4, quarter, MODEL_WIDTH + HEAD_SIZE), "tensor")
        .astype(F32)
        .sum(axis=0)
    )
    landed, expert_out = lax.optimization_barrier((landed, expert_out))
    returned = to_experts(expert_out)
    grad_gate_m = (
        landed[:, MODEL_WIDTH : MODEL_WIDTH + 2] + landed[:, MODEL_WIDTH + 2 : MODEL_WIDTH + 4]
    )

    def quarter_of(array, offset=0):
        return lax.dynamic_slice_in_dim(array, first + offset, quarter)

    grad_logit_m = gate_back(quarter_of(gate_m), grad_gate_m, quarter_of(pick_m))
    grad_xn2 = landed[:, :MODEL_WIDTH] + lax.dot_general(
        grad_logit_m, router_m.astype(F32), LAST, preferred_element_type=F32
    )
    grad_norm, gain_m_part = norm_back(grad_xn2, hidden, factor_m, gain_m)
    grad_hidden = cot_own + grad_norm
    grad_sent_back, returned = lax.optimization_barrier((grad_hidden.astype(BF), returned))
    grad_branch = spread(grad_sent_back, plane, 16).reshape(4 * count, MODEL_WIDTH)

    fetched = jnp.einsum("jtr,rd->jtd", to_row, returned, preferred_element_type=F32)
    moe_part = jnp.sum(weight_m.T[:, :, None] * fetched, axis=0).astype(BF)
    width = down_own.shape[0]
    grad_branch, moe_part = lax.optimization_barrier((grad_branch, moe_part))
    moe_pieces = exchange(moe_part.reshape(4, quarter, MODEL_WIDTH // 4), "tensor")

    grad_mixed = jnp.dot(grad_branch, out_w, preferred_element_type=F32)
    grad_q_all, grad_logit_a, grad_kv_own, grad_kv_give = in_vmem(
        backward_kernel,
        [
            jax.ShapeDtypeStruct((half, EXPERTS * HEAD_SIZE), BF),
            jax.ShapeDtypeStruct((half, HEAD_SIZE), BF),
            jax.ShapeDtypeStruct((half, 2 * HEAD_SIZE), F32),
            jax.ShapeDtypeStruct((half, 2 * HEAD_SIZE), BF),
        ],
        [pltpu.VMEM((2, half, 2 * HEAD_SIZE), F32)],
        40 << 28,
        grad_mixed,
        query,
        kv_own,
        kv_other,
        attended,
        totals,
        gate_a,
        *shared,
    )
    out_pairs = [(grad_branch, mixed)]
    out_give = lax.ppermute(give_terms(out_pairs, z, core), "core", SWAP)
    kv_back, moe_pieces = lax.optimization_barrier(
        (lax.ppermute(grad_kv_give, "core", SWAP), moe_pieces)
    )
    moe = moe_pieces.transpose(1, 0, 2).reshape(quarter, MODEL_WIDTH).astype(F32)
    output_own = (hidden_last + moe).astype(BF)
    own_grad_kv = grad_kv_own + kv_back.astype(F32)
    grad_key = own_grad_kv[:, :HEAD_SIZE]
    grad_kv = jnp.concatenate(
        [grad_key * cosine - swapped(grad_key) * sine, own_grad_kv[:, HEAD_SIZE:]], axis=1
    ).astype(BF)
    grad_in = jnp.concatenate([grad_q_all, grad_kv, grad_logit_a], axis=1)
    grad_xn1_part = lax.dot_general(grad_in, in_w, LAST, preferred_element_type=F32).astype(BF)
    gain_row = jnp.pad(gain_m_part[None].astype(BF), ((0, 7), (0, 0)))
    lane = jnp.arange(1408, dtype=jnp.int32)[None, :]
    router_cols = jnp.pad(grad_logit_m.astype(BF), ((0, 0), (1288, 112)))
    gain_cols = ((jnp.arange(8)[:, None] == 0) & (lane == 1296)).astype(BF)
    in_pairs = [
        (xn1, after(grad_in, grad_xn1_part)),
        (
            jnp.concatenate([xn2_own, gain_row], axis=0),
            jnp.concatenate([router_cols, gain_cols], axis=0),
        ),
    ]
    in_give = lax.ppermute(give_terms(in_pairs, z, core), "core", SWAP)
    out_own, *out_rest = keep_terms(out_pairs, after(out_give, grad_xn1_part), z, core)
    in_own_rows, *in_rest = keep_terms(in_pairs, in_give, z, core)
    out_rest[0], out_rest[3], _ = lax.optimization_barrier(
        (out_rest[0], out_rest[3], in_own_rows)
    )
    out_ahead, out_back = ring_first(*out_rest, "dp")
    in_ahead, in_back = ring_first(*in_rest, "dp")
    out_sum = ring_second(after(out_own, gate_up_sum), out_ahead, out_back, "dp").astype(BF)
    landed_raw = exchange(grad_xn1_part.reshape(16, quarter, MODEL_WIDTH), plane)
    landed_raw, down_sum, in_ahead, in_back = lax.optimization_barrier(
        (landed_raw, down_sum, in_ahead, in_back)
    )
    in_sum = ring_second(after(in_own_rows, out_sum), in_ahead, in_back, "dp").astype(BF)
    landed_a = landed_raw.astype(F32).sum(axis=0)
    grad_x_norm, _ = norm_back(landed_a, own_values, own_factor, gain_a)
    columns = jnp.arange(1408, dtype=jnp.int32)[None, :]
    gain_a_part = jnp.sum(
        jnp.where(columns < 1288, in_sum.astype(F32) * mine[:, :1408].astype(F32), 0.0),
        axis=1,
        keepdims=True,
    )
    small_part = jnp.where(columns[:, :128] == 17, gain_a_part, in_sum[:, 1280:].astype(F32))
    gain_rows = lax.dynamic_slice_in_dim(attn_gain.astype(F32), z * 512 + y * 128 + core * 64, 64)

    ends = jnp.concatenate(
        [output_own, core_last((grad_hidden + grad_x_norm).astype(BF))], axis=1
    )
    both_sums = jnp.concatenate(
        [in_sum[:, :1280], out_sum, small_part.astype(BF)], axis=1
    ).reshape(4, 64, 2432)
    y_parts = send_direct(both_sums, "y")
    gate_up_grad = (
        after(gate_up_sum, both_sums)
        .reshape(2, 4, 64, 2816)
        .transpose(1, 0, 2, 3)
        .reshape(1, 512, 2, width)
        .astype(F32)
    )
    _, _, *y_parts = lax.optimization_barrier((gate_up_grad, ends, *y_parts))
    both_ends = spread(ends, "tensor", 4)
    small_y = sum(p[:, 2304:].astype(F32) for p in y_parts).astype(BF)
    small_y = after(small_y, both_ends)
    small_sum = small_y.astype(F32) + sum(
        from_ahead(small_y, "tensor", k).astype(F32) for k in (1, 2, 3)
    )
    down_grad = down_sum.astype(F32)[None]
    both_ends = both_ends.reshape(count, 2 * MODEL_WIDTH)
    output, input_grad = both_ends[:, :MODEL_WIDTH], both_ends[:, MODEL_WIDTH:]
    query_grad, kv_grad, out_grad = heads_placed(y_parts, y)
    return (
        output,
        input_grad,
        small_sum[:, 17] / gain_rows,
        small_sum[:, 16],
        small_sum[:, :8],
        kv_grad,
        query_grad,
        out_grad,
        small_sum[:, 8:16],
        gate_up_grad,
        down_grad,
    )


def solution(mesh):
    split = Mesh(mesh.devices.reshape(4, 4, 2, 4), ("dp", "y", "core", "tensor"))
    rows = ("dp", "y", "core")
    expert = ("y", "core")
    placed = (
        P(rows, None),
        P(rows, None),
        P(),
        P(),
        P(rows, None),
        P(rows, None, "tensor"),
        P(rows, None, "tensor"),
        P(rows, None, "tensor"),
        P(rows, None),
        P(expert, "dp", None, "tensor"),
        P(expert, "tensor", "dp"),
        P(rows, None),
        P(rows, None),
        P(rows, None),
        P(),
    )
    return jax.shard_map(
        body,
        mesh=split,
        in_specs=placed,
        out_specs=(
            P(rows, None),
            P(rows, None),
            P(rows),
            P(rows),
            P(rows, None),
            P(rows, None, "tensor"),
            P(rows, None, "tensor"),
            P(rows, None, "tensor"),
            P(rows, None),
            P(expert, "dp", None, "tensor"),
            P(expert, "tensor", "dp"),
        ),
        check_vma=False,
    )
```

```python
import jax
import jax.numpy as jnp
from jax import lax
from jax.experimental import pallas as pl
from jax.experimental.pallas import tpu as pltpu
from jax.sharding import Mesh
from jax.sharding import PartitionSpec as P

MODEL_WIDTH = 2048
HEAD_SIZE = 128
EXPERTS = 8
WINDOW = 1024
NORM_EPS = 1e-06
BF = jnp.bfloat16
F32 = jnp.float32
ROWS = (((0,), (0,)), ((), ()))
LAST = (((1,), (1,)), ((), ()))
UP = [(0, 1), (1, 2), (2, 3), (3, 0)]
DOWN = [(0, 3), (1, 0), (2, 1), (3, 2)]
SWAP = [(0, 1), (1, 0)]


def exchange(blocks, axis):
    return lax.all_to_all(blocks, axis, split_axis=0, concat_axis=0, tiled=True)


def spread(block, axis, count):
    return exchange(jnp.broadcast_to(block, (count, *block.shape)), axis)


def from_ahead(block, axis, steps):
    return lax.ppermute(block, axis, [(i, (i - steps) % 4) for i in range(4)])


def in_order(pieces, first):
    both = jnp.stack(pieces + pieces[:3])
    return lax.dynamic_slice_in_dim(both, lax.rem(4 - first, 4), 4)


def pick_block(blocks, index):
    return lax.dynamic_index_in_dim(blocks, lax.rem(index, 4), 0, keepdims=False)


def send_direct(blocks, axis):
    me = lax.axis_index(axis)
    return [pick_block(blocks, me)] + [
        from_ahead(pick_block(blocks, me + 4 - k), axis, k) for k in (1, 2, 3)
    ]


def heads_first(shard):
    columns = shard.shape[1] * HEAD_SIZE
    return shard.reshape(64, -1, 4, HEAD_SIZE).transpose(2, 0, 1, 3).reshape(4, 64, columns)


def after(value, other):
    return lax.optimization_barrier((value, other))[0]


def core_first(rows):
    return rows.reshape(-1, 4, 4, 2, 64).transpose(0, 1, 3, 2, 4).reshape(-1, MODEL_WIDTH)


def core_last(rows):
    return rows.reshape(-1, 4, 2, 4, 64).transpose(0, 1, 3, 2, 4).reshape(-1, MODEL_WIDTH)


def ring_first(ahead, low, high, back, axis):
    low = lax.ppermute(low, axis, UP)
    high = lax.ppermute(high, axis, DOWN)
    half = low.shape[0]
    ahead = jnp.concatenate([(ahead[:half].astype(F32) + low.astype(F32)).astype(BF), ahead[half:]])
    back = jnp.concatenate([back[:half], (back[half:].astype(F32) + high.astype(F32)).astype(BF)])
    return ahead, back


def ring_second(own, ahead, back, axis):
    return (
        own.astype(F32)
        + lax.ppermute(ahead, axis, UP).astype(F32)
        + lax.ppermute(back, axis, DOWN).astype(F32)
    )


def rms_scale(values):
    return lax.rsqrt(jnp.mean(values * values, axis=-1, keepdims=True) + NORM_EPS)


def turn(heads, cosine, sine):
    first, second = heads[..., :64], heads[..., 64:]
    return jnp.concatenate([first * cosine - second * sine, second * cosine + first * sine], axis=-1)


EXTENTS = (256, 384, 512, 640)
SCALE = HEAD_SIZE**-0.5


def masked_scores(query, key, row_meta, key_meta):
    raw = lax.dot_general(query, key, LAST, preferred_element_type=F32) * SCALE
    gap = row_meta[:, 0:1] - key_meta[0:1]
    allowed = (gap >= 0) & (gap < WINDOW) & (row_meta[:, 1:2] == key_meta[1:2])
    return jnp.where(jnp.concatenate([allowed, allowed], axis=0), raw, -1e30)


def forward_kernel(proj, own, other, routes, cosine, sine, row_meta, key_meta, *outs):
    query_out, attended_out, total_out, gates_out, mixed_out = outs
    count = proj.shape[0] // 4
    for i in range(4):
        rows = pl.ds(count * i, count)
        extent = EXTENTS[i]
        logits = proj[rows, 1280:1288]
        lane = lax.broadcasted_iota(jnp.int32, (count, EXPERTS), 1)
        named = [routes[rows, 0:1], routes[rows, 1:2]]
        chosen = [jnp.sum(jnp.where(lane == n, logits, 0.0), axis=1, keepdims=True) for n in named]
        top = jnp.maximum(chosen[0], chosen[1])
        power = [jnp.exp(c - top) for c in chosen]
        gates = [p / (power[0] + power[1]) for p in power]
        gates_out[rows, 0:1] = gates[0]
        gates_out[rows, 1:2] = gates[1]
        cos, sin = cosine[rows, :], sine[rows, :]
        picked = []
        for n in named:
            q = jnp.zeros((count, HEAD_SIZE), F32)
            for e in range(EXPERTS):
                q = q + jnp.where(n == e, proj[rows, HEAD_SIZE * e : HEAD_SIZE * (e + 1)], 0.0)
            picked.append(q * cos + pltpu.roll(q, 64, 1) * sin)
        query = jnp.concatenate(picked, axis=0).astype(BF)
        query_out[i] = query
        halves = (own, other)
        scores = [
            masked_scores(
                query, h[:extent, :HEAD_SIZE], row_meta[rows, :], key_meta[k, :, :extent]
            )
            for k, h in enumerate(halves)
        ]
        row_max = jnp.maximum(
            jnp.max(scores[0], axis=1, keepdims=True), jnp.max(scores[1], axis=1, keepdims=True)
        )
        weights = [jnp.exp(s - row_max) for s in scores]
        total = jnp.sum(weights[0], axis=1, keepdims=True) + jnp.sum(weights[1], axis=1, keepdims=True)
        inverse = 1.0 / total
        attended = sum(
            jnp.dot((w * inverse).astype(BF), h[:extent, HEAD_SIZE:], preferred_element_type=F32)
            for w, h in zip(weights, halves)
        )
        attended_out[i] = attended
        total_out[i] = row_max + jnp.log(total)
        for e in range(EXPERTS):
            mixed_out[rows, HEAD_SIZE * e : HEAD_SIZE * (e + 1)] = (
                jnp.where(named[0] == e, gates[0], 0.0) * attended[:count]
                + jnp.where(named[1] == e, gates[1], 0.0) * attended[count:]
            ).astype(BF)


def backward_kernel(
    grad_mixed, query_in, own, other, attended_in, total_in, gates_in, routes, cosine, sine, row_meta, key_meta, *outs
):
    grad_query_out, grad_logit_out, grad_own_out, grad_other_out, sums = outs
    count = grad_mixed.shape[0] // 4
    sums[...] = jnp.zeros_like(sums)
    for i in range(4):
        rows = pl.ds(count * i, count)
        extent = EXTENTS[i]
        named = [routes[rows, 0:1], routes[rows, 1:2]]
        gates = [gates_in[rows, 0:1], gates_in[rows, 1:2]]
        cos, sin = cosine[rows, :], sine[rows, :]
        attended = attended_in[i]
        picked = []
        for n in named:
            g = jnp.zeros((count, HEAD_SIZE), F32)
            for e in range(EXPERTS):
                g = g + jnp.where(n == e, grad_mixed[rows, HEAD_SIZE * e : HEAD_SIZE * (e + 1)], 0.0)
            picked.append(g)
        gate_grads = [
            jnp.sum(p * attended[count * j : count * (j + 1)], axis=1, keepdims=True)
            for j, p in enumerate(picked)
        ]
        level = gates[0] * gate_grads[0] + gates[1] * gate_grads[1]
        lane = lax.broadcasted_iota(jnp.int32, (count, HEAD_SIZE), 1)
        grad_logit_out[rows, :] = sum(
            jnp.where(lane == n, g * (d - level), 0.0) for n, g, d in zip(named, gates, gate_grads)
        ).astype(BF)
        grad_attended = jnp.concatenate(
            [gates[0] * picked[0], gates[1] * picked[1]], axis=0
        ).astype(BF)
        query = query_in[i]
        total = total_in[i]
        probs, grad_probs = [], []
        delta = jnp.zeros((2 * count, 1), F32)
        for k, h in enumerate((own, other)):
            score = masked_scores(
                query, h[:extent, :HEAD_SIZE], row_meta[rows, :], key_meta[k, :, :extent]
            )
            prob = jnp.exp(score - total)
            grad_prob = lax.dot_general(
                grad_attended, h[:extent, HEAD_SIZE:], LAST, preferred_element_type=F32
            )
            delta = delta + jnp.sum(prob * grad_prob, axis=1, keepdims=True)
            probs.append(prob)
            grad_probs.append(grad_prob)
        grad_query = jnp.zeros((2 * count, HEAD_SIZE), F32)
        for k, h in enumerate((own, other)):
            grad_score = (probs[k] * (grad_probs[k] - delta)).astype(BF)
            grad_query = grad_query + jnp.dot(
                grad_score, h[:extent, :HEAD_SIZE], preferred_element_type=F32
            )
            sums[k, :extent, :HEAD_SIZE] += (
                lax.dot_general(grad_score, query, ROWS, preferred_element_type=F32) * SCALE
            )
            sums[k, :extent, HEAD_SIZE:] += lax.dot_general(
                probs[k].astype(BF), grad_attended, ROWS, preferred_element_type=F32
            )
        grad_query = grad_query * SCALE
        turned = [
            g * cos - pltpu.roll(g, 64, 1) * sin for g in (grad_query[:count], grad_query[count:])
        ]
        for e in range(EXPERTS):
            grad_query_out[rows, HEAD_SIZE * e : HEAD_SIZE * (e + 1)] = (
                jnp.where(named[0] == e, turned[0], 0.0) + jnp.where(named[1] == e, turned[1], 0.0)
            ).astype(BF)
    grad_own_out[...] = sums[0]
    grad_other_out[...] = sums[1].astype(BF)


def in_vmem(kernel, outs, scratch, flops, *args):
    spec = pl.BlockSpec(memory_space=pltpu.VMEM)
    moved = sum(a.size * a.dtype.itemsize for a in args)
    return pl.pallas_call(
        kernel,
        out_shape=outs,
        in_specs=[spec] * len(args),
        out_specs=[spec] * len(outs),
        scratch_shapes=scratch,
        compiler_params=pltpu.CompilerParams(vmem_limit_bytes=40 * 1024 * 1024),
        cost_estimate=pl.CostEstimate(flops=flops, bytes_accessed=moved, transcendentals=1 << 20),
    )(*args)


SOME = pl.CostEstimate(flops=1 << 35, bytes_accessed=1 << 27, transcendentals=0)


def on_grid(kernel, scalars, grid, in_specs, out_specs, outs, scratch, *args, cost=SOME):
    return pl.pallas_call(
        kernel,
        out_shape=outs,
        grid_spec=pltpu.PrefetchScalarGridSpec(
            num_scalar_prefetch=1,
            grid=grid,
            in_specs=in_specs,
            out_specs=out_specs,
            scratch_shapes=scratch,
        ),
        compiler_params=pltpu.CompilerParams(vmem_limit_bytes=48 * 1024 * 1024),
        cost_estimate=cost,
    )(jnp.stack(scalars).astype(jnp.int32), *args)


def give_terms(pairs, place, core):
    columns = pairs[0][1].shape[1]

    def kernel(at, *refs):
        out = refs[-1]
        total = sum(
            lax.dot_general(refs[j][...], refs[j + 1][...], ROWS, preferred_element_type=F32)
            for j in range(0, len(refs) - 1, 2)
        )
        out[0] = total.astype(BF)

    specs = []
    for tall, terms in pairs:
        specs.append(pl.BlockSpec((tall.shape[0], 256), lambda i, at: (0, 2 * i + 1 - at[1])))
        specs.append(pl.BlockSpec(terms.shape, lambda i, at: (0, 0)))
    return on_grid(
        kernel,
        (place, core),
        (4,),
        specs,
        pl.BlockSpec((1, 256, columns), lambda i, at: (i, 0, 0)),
        jax.ShapeDtypeStruct((4, 256, columns), BF),
        [],
        *[a for pair in pairs for a in pair],
    )


def keep_terms(pairs, landed, place, core):
    columns = pairs[0][1].shape[1]
    count = 2 * len(pairs)

    def kernel(at, *refs):
        more, own, ahead, low, high, back = refs[count:]
        total = sum(
            lax.dot_general(refs[j][...], refs[j + 1][...], ROWS, preferred_element_type=F32)
            for j in range(0, count, 2)
        )
        total = (total.astype(BF).astype(F32) + more[0].astype(F32)).astype(BF)
        step = pl.program_id(0)

        @pl.when(step == 0)
        def _():
            own[...] = total

        @pl.when(step == 1)
        def _():
            ahead[...] = total

        @pl.when(step == 2)
        def _():
            low[...] = total[:128]
            high[...] = total[128:]

        @pl.when(step == 3)
        def _():
            back[...] = total

    def whole(rows):
        return pl.BlockSpec((rows, columns), lambda i, at: (0, 0))

    specs = []
    for tall, terms in pairs:
        specs.append(
            pl.BlockSpec(
                (tall.shape[0], 256), lambda i, at: (0, 2 * lax.rem(at[0] + i, 4) + at[1])
            )
        )
        specs.append(pl.BlockSpec(terms.shape, lambda i, at: (0, 0)))
    specs.append(pl.BlockSpec((1, 256, columns), lambda i, at: (lax.rem(at[0] + i, 4), 0, 0)))
    return on_grid(
        kernel,
        (place, core),
        (4,),
        specs,
        [whole(256), whole(256), whole(128), whole(128), whole(256)],
        [jax.ShapeDtypeStruct((r, columns), BF) for r in (256, 256, 128, 128, 256)],
        [],
        *[a for pair in pairs for a in pair],
        landed,
    )


def gate_up_product(rows, pair):
    depth, width = pair.shape[1:]

    def kernel(at, left, right, out):
        for half in range(2):
            out[:, width * half : width * (half + 1)] = lax.dot_general(
                left[...], right[half], ROWS, preferred_element_type=F32
            ).astype(BF)

    return on_grid(
        kernel,
        (jnp.int32(0),),
        (8,),
        [
            pl.BlockSpec((depth, 256), lambda i, at: (0, i)),
            pl.BlockSpec((2, depth, width), lambda i, at: (0, 0, 0)),
        ],
        pl.BlockSpec((256, 2 * width), lambda i, at: (i, 0)),
        jax.ShapeDtypeStruct((MODEL_WIDTH, 2 * width), BF),
        [],
        rows,
        pair,
    )


def down_product(activated, grads, gate):
    def kernel(at, left, right, scale, out):
        scaled = (scale[...] * right[...].astype(F32)).astype(BF)
        out[...] = lax.dot_general(left[...], scaled, ROWS, preferred_element_type=F32).astype(BF)

    depth, width = activated.shape
    return on_grid(
        kernel,
        (jnp.int32(0),),
        (4,),
        [
            pl.BlockSpec((depth, width), lambda i, at: (0, 0)),
            pl.BlockSpec((depth, 512), lambda i, at: (0, i)),
            pl.BlockSpec((depth, 1), lambda i, at: (0, 0)),
        ],
        pl.BlockSpec((width, 512), lambda i, at: (0, i)),
        jax.ShapeDtypeStruct((width, MODEL_WIDTH), BF),
        [],
        activated,
        grads,
        gate,
    )


def down_back(grads, pieces, place):
    def kernel(at, left, own, ahead, far_a, far_b, back, out):
        total = None
        for shift, start, piece in (
            (0, 0, own), (1, 0, ahead), (2, 0, far_a), (2, 256, far_b), (3, 0, back)
        ):
            size = piece.shape[1]
            lanes = pl.ds(pl.multiple_of(lax.rem(at[0] + shift, 4) * 512 + start, 256), size)
            term = lax.dot_general(left[:, lanes], piece[...], LAST, preferred_element_type=F32)
            total = term if total is None else total + term
        out[...] = total

    depth, width = grads.shape[0], pieces[0].shape[0]
    return on_grid(
        kernel,
        (place,),
        (width // 128,),
        [pl.BlockSpec(grads.shape, lambda i, at: (0, 0))]
        + [pl.BlockSpec((128, p.shape[1]), lambda i, at: (i, 0)) for p in pieces],
        pl.BlockSpec((depth, 128), lambda i, at: (0, i)),
        jax.ShapeDtypeStruct((depth, width), F32),
        [],
        grads,
        *pieces,
    )


def expert_quarters(activated, pieces, place, x):
    def kernel(at, left, own, ahead, far_a, far_b, back, out):
        step = pl.program_id(0)
        for shift, refs in enumerate(((own,), (ahead,), (far_a, far_b), (back,))):

            @pl.when(step == shift)
            def _():
                terms = [jnp.dot(left[...], r[...], preferred_element_type=F32) for r in refs]
                out[0] = jnp.concatenate(terms, axis=1).astype(BF)

    depth = activated.shape[0]
    return on_grid(
        kernel,
        (place, x),
        (4,),
        [pl.BlockSpec(a.shape, lambda i, at: (0, 0)) for a in (activated, *pieces)],
        pl.BlockSpec((1, depth, 512), lambda i, at: (lax.rem(at[0] + i + 4 - at[1], 4), 0, 0)),
        jax.ShapeDtypeStruct((4, depth, 512), BF),
        [],
        activated,
        *pieces,
    )


def expert_middle(rows, marks, router, gate_up_w, grad_act, expert):
    depth, width = grad_act.shape
    blocks = width // 128

    def kernel(
        at, rows_ref, marks_ref, router_ref, gate_ref, up_ref, flat_ref, grad_ref,
        act_out, pair_out, gate_out, back_out, pair_all, row_gate, row_grad,
    ):
        step = pl.program_id(0)
        lane = lax.broadcasted_iota(jnp.int32, (depth, 128), 1)

        @pl.when(step == 0)
        def _():
            logits = jnp.dot(rows_ref[...], router_ref[...], preferred_element_type=F32)
            marks_f = marks_ref[...].astype(F32)
            own = jnp.sum(jnp.where(lane == at[0], logits, 0.0), axis=1, keepdims=True)
            other = jnp.sum(jnp.where(lane < 8, logits * marks_f, 0.0), axis=1, keepdims=True)
            valid = jnp.sum(jnp.where(lane == 8, marks_f, 0.0), axis=1, keepdims=True)
            top = jnp.maximum(own, other)
            power = jnp.exp(own - top)
            row_gate[...] = valid * power / (power + jnp.exp(other - top))
            gate_out[...] = row_gate[...]
            row_grad[...] = jnp.zeros_like(row_grad)

        @pl.when(step < blocks)
        def _():
            both = jnp.concatenate([gate_ref[...], up_ref[...]], axis=1)
            gate_up = jnp.dot(rows_ref[...], both, preferred_element_type=F32)
            gate, up = gate_up[:, :128], gate_up[:, 128:]
            sigmoid = 1.0 / (1.0 + jnp.exp(-gate))
            silu = gate * sigmoid
            act = (silu * up).astype(BF)
            raw = grad_ref[...]
            grad = row_gate[...] * raw
            grad_gate = (grad * up * sigmoid * (1.0 + gate * (1.0 - sigmoid))).astype(BF)
            grad_up = (grad * silu).astype(BF)
            act_out[...] = act
            pair_out[0] = grad_gate
            pair_out[1] = grad_up
            at_lane = pl.multiple_of(step * 128, 128)
            pair_all[:, pl.ds(at_lane, 128)] = grad_gate
            pair_all[:, pl.ds(at_lane + width, 128)] = grad_up
            row_grad[...] += jnp.sum(act.astype(F32) * raw, axis=1, keepdims=True)

        @pl.when(step >= blocks)
        def _():
            back_lane = pl.multiple_of((step - blocks) * 512, 512)
            back_out[:, pl.ds(back_lane, 512)] = lax.dot_general(
                pair_all[...], flat_ref[...], LAST, preferred_element_type=F32
            ).astype(BF)

        @pl.when(step == blocks + 3)
        def _():
            high = row_grad[...].astype(BF).astype(F32)
            low = row_grad[...] - high
            back_out[:, MODEL_WIDTH:] = jnp.where(
                lane == 0, high, jnp.where(lane == 1, low, 0.0)
            ).astype(BF)

    def first(i):
        return jnp.minimum(i, blocks - 1)

    def second(i):
        return jnp.clip(i - blocks, 0, 3)

    return on_grid(
        kernel,
        (expert,),
        (blocks + 4,),
        [
            pl.BlockSpec((depth, MODEL_WIDTH), lambda i, at: (0, 0)),
            pl.BlockSpec((depth, 128), lambda i, at: (0, 0)),
            pl.BlockSpec((MODEL_WIDTH, 128), lambda i, at: (0, 0)),
            pl.BlockSpec((MODEL_WIDTH, 128), lambda i, at: (0, first(i))),
            pl.BlockSpec((MODEL_WIDTH, 128), lambda i, at: (0, blocks + first(i))),
            pl.BlockSpec((512, 2 * width), lambda i, at: (second(i), 0)),
            pl.BlockSpec((depth, 128), lambda i, at: (0, first(i))),
        ],
        [
            pl.BlockSpec((depth, 128), lambda i, at: (0, first(i))),
            pl.BlockSpec((2, depth, 128), lambda i, at: (0, 0, first(i))),
            pl.BlockSpec((depth, 1), lambda i, at: (0, 0)),
            pl.BlockSpec((depth, MODEL_WIDTH + 128), lambda i, at: (0, 0)),
        ],
        [
            jax.ShapeDtypeStruct((depth, width), BF),
            jax.ShapeDtypeStruct((2, depth, width), BF),
            jax.ShapeDtypeStruct((depth, 1), F32),
            jax.ShapeDtypeStruct((depth, MODEL_WIDTH + 128), BF),
        ],
        [
            pltpu.VMEM((depth, 2 * width), BF),
            pltpu.VMEM((depth, 1), F32),
            pltpu.VMEM((depth, 1), F32),
        ],
        rows,
        marks,
        router,
        gate_up_w,
        gate_up_w,
        gate_up_w,
        grad_act,
        cost=pl.CostEstimate(
            flops=8 * depth * MODEL_WIDTH * width, bytes_accessed=1 << 24, transcendentals=1 << 20
        ),
    )


def heads_placed(pieces, y):
    def kernel(at, p0, p1, p2, p3, query, kv, out):
        for k, piece in enumerate((p0, p1, p2, p3)):
            lanes = pl.ds(pl.multiple_of(lax.rem(at[0] + k, 4) * 128, 128), 128)
            for e in range(18):
                block = piece[:, 128 * e : 128 * (e + 1)].astype(F32)
                if e < 8:
                    query[:, e, lanes] = block
                elif e < 10:
                    kv[:, e - 8, lanes] = block
                else:
                    out[:, e - 10, lanes] = block

    shapes = [(64, 8, 512), (64, 2, 512), (64, 8, 512)]
    return on_grid(
        kernel,
        (y,),
        (1,),
        [pl.BlockSpec((64, 2432), lambda i, at: (0, 0))] * 4,
        [pl.BlockSpec(s, lambda i, at: (0, 0, 0)) for s in shapes],
        [jax.ShapeDtypeStruct(s, F32) for s in shapes],
        [],
        *pieces,
        cost=pl.CostEstimate(flops=0, bytes_accessed=0, transcendentals=0),
    )


def pick_of(routes):
    return (routes[:, :, None] == jnp.arange(EXPERTS, dtype=jnp.int32)[None, None, :]).astype(F32)


def pair_gates(logits, pick):
    chosen = jnp.sum(logits[:, None, :] * pick, axis=-1)
    weights = jnp.exp(chosen - jnp.max(chosen, axis=1, keepdims=True))
    return weights / jnp.sum(weights, axis=1, keepdims=True)


def gate_back(gates, grad_gates, pick):
    inner = gates * (grad_gates - jnp.sum(gates * grad_gates, axis=1, keepdims=True))
    return jnp.sum(inner[:, :, None] * pick, axis=1)


def norm_back(grad_normed, values, factor, gain):
    gain_part = jnp.sum(grad_normed * values * factor, axis=0)
    inner = grad_normed * gain
    grad_values = factor * inner - values * factor * factor * factor * jnp.mean(
        inner * values, axis=-1, keepdims=True
    )
    return grad_values, gain_part


def in_two(values):
    high = values.astype(BF)
    low = (values - high.astype(F32)).astype(BF)
    return jnp.concatenate([high, low], axis=1)


def widen(columns):
    return jnp.pad(columns, ((0, 0), (0, HEAD_SIZE - columns.shape[1])))


def body(
    tokens,
    cotangent,
    attn_gain,
    mlp_gain,
    attn_router,
    key_value_weight,
    query_matrix,
    output_matrix,
    mlp_router,
    gate_up_weight,
    down_weight,
    attn_routes,
    mlp_routes,
    priority,
    segments,
):
    z, y = lax.axis_index("dp"), lax.axis_index("y")
    core, x = lax.axis_index("core"), lax.axis_index("tensor")
    count = tokens.shape[0]
    quarter = count // 4
    capacity = 50
    room = 56
    sequence = 8 * count
    plane = ("y", "tensor")

    routers_own = jnp.concatenate([attn_router, mlp_router], axis=1)
    down_own = down_weight[0]
    down_before = lax.ppermute(down_own, "dp", UP)
    down_after = lax.ppermute(down_own, "dp", DOWN)
    mine = exchange(
        jnp.concatenate(
            [
                heads_first(query_matrix),
                heads_first(key_value_weight),
                jnp.broadcast_to(widen(routers_own), (4, 64, HEAD_SIZE)),
                heads_first(output_matrix),
            ],
            axis=2,
        ),
        "y",
    ).reshape(256, 2432)
    sent = jnp.concatenate([core_first(tokens), widen(attn_routes.astype(BF))], axis=1)
    arrived = spread(after(sent, mine), "y", 4).reshape(4 * count, MODEL_WIDTH + HEAD_SIZE)
    all_w = lax.all_gather(
        after(mine, (down_before, down_after)), ("dp", "core"), axis=0, tiled=True
    )
    values = arrived[:, :MODEL_WIDTH].astype(F32)
    routes = arrived[:, MODEL_WIDTH : MODEL_WIDTH + 2].astype(jnp.int32)
    gain_a = core_first(attn_gain.astype(F32))[0]
    gain_m = core_first(mlp_gain.astype(F32))[0]
    xn1 = (values * rms_scale(values) * gain_a).astype(BF)

    ranking = priority[0]
    pick_m = pick_of(mlp_routes)
    before = (ranking[None, :] < ranking[:, None]).astype(BF)
    earlier = jnp.dot(before, jnp.sum(pick_m, axis=1).astype(BF), preferred_element_type=F32)
    slots = jnp.sum(pick_m * earlier[:, None, :], axis=-1).astype(jnp.int32)
    kept = slots < capacity
    dest = jnp.where(kept, mlp_routes * room + slots, -1)
    lanes = jnp.arange(EXPERTS * room, dtype=jnp.int32)
    to_row = (dest.T[:, :, None] == lanes[None, None, :]).astype(BF)
    any_row = to_row[0] + to_row[1]
    both_rows = to_row.reshape(2 * count, EXPERTS * room)

    def to_experts(rows):
        columns = rows.shape[1]
        return exchange(rows.reshape(EXPERTS, room, columns), ("y", "core")).reshape(
            EXPERTS * room, columns
        )

    def with_other(j):
        others = jnp.concatenate([pick_m[:, 1 - j], jnp.ones((count, 1), F32)], axis=1)
        return jnp.concatenate([cotangent, widen(others.astype(BF))], axis=1)

    grad_sent = lax.dot_general(
        both_rows,
        jnp.concatenate([with_other(0), with_other(1)], axis=0),
        ROWS,
        preferred_element_type=F32,
    ).astype(BF)
    def places(half):
        blocks = 2 * jnp.arange(4, dtype=jnp.int32)[:, None] + half
        return (blocks * count + jnp.arange(count, dtype=jnp.int32)[None, :]).reshape(-1)

    inverse = 10000.0 ** (-(jnp.arange(HEAD_SIZE // 2).astype(F32) * 2.0 / HEAD_SIZE))
    angle = places(core).astype(F32)[:, None] * inverse[None, :]
    cosine = jnp.tile(jnp.cos(angle), (1, 2))
    sine = jnp.concatenate([-jnp.sin(angle), jnp.sin(angle)], axis=1)

    first = x * quarter
    cot_own = core_first(lax.dynamic_slice_in_dim(cotangent, first, quarter)).astype(F32)
    all_w, down_before, down_after, xn1, grad_sent, cosine, sine, cot_own = (
        lax.optimization_barrier(
            (all_w, down_before, down_after, xn1, grad_sent, cosine, sine, cot_own)
        )
    )
    in_w, out_w = all_w[:, :1408], all_w[:, 1408:]
    far_a = lax.ppermute(down_before[:, :256], "dp", UP)
    far_b = lax.ppermute(down_after[:, 256:], "dp", DOWN)
    down_pieces = (down_own, down_after, far_a, far_b, down_before)
    gate_up_own = gate_up_weight.reshape(4, 2, 64, 2816).transpose(1, 0, 2, 3).reshape(512, 2816)
    gate_up_w = lax.all_gather(after(gate_up_own, all_w), "dp", axis=0, tiled=True)
    router_m = in_w[:, 1288:1296]

    grad_landed = to_experts(grad_sent)

    of_sequence = lax.dynamic_slice_in_dim(segments, z * sequence, sequence).reshape(4, 2, count)

    def meta(half):
        documents = lax.dynamic_index_in_dim(of_sequence, half, 1, keepdims=False).reshape(-1)
        return jnp.stack([places(half), documents])

    key_meta = jnp.stack([meta(core), meta(1 - core)])
    row_meta = key_meta[0].T
    def swapped(rows):
        return jnp.concatenate([rows[:, 64:], rows[:, :64]], axis=1)

    half = 4 * count
    projected = jnp.dot(xn1, in_w, preferred_element_type=F32)
    key_raw = projected[:, 1024:1152]
    kv_own = jnp.concatenate(
        [key_raw * cosine + swapped(key_raw) * sine, projected[:, 1152:1280]], axis=1
    ).astype(BF)
    kv_other = lax.ppermute(kv_own, "core", SWAP)
    shared = (routes, cosine, sine, row_meta, key_meta)
    query, attended, totals, gate_a, mixed = in_vmem(
        forward_kernel,
        [
            jax.ShapeDtypeStruct((4, 2 * count, HEAD_SIZE), BF),
            jax.ShapeDtypeStruct((4, 2 * count, HEAD_SIZE), F32),
            jax.ShapeDtypeStruct((4, 2 * count, 1), F32),
            jax.ShapeDtypeStruct((half, 2), F32),
            jax.ShapeDtypeStruct((half, EXPERTS * HEAD_SIZE), BF),
        ],
        [],
        6 << 28,
        projected,
        kv_own,
        kv_other,
        *shared,
    )
    branch_part = lax.dot_general(mixed, out_w, LAST, preferred_element_type=F32).astype(BF)
    branch_part = after(branch_part, grad_landed)
    grad_received = grad_landed[:, :MODEL_WIDTH]
    branch = exchange(branch_part.reshape(16, quarter, MODEL_WIDTH), plane).astype(F32).sum(axis=0)

    own_values = lax.dynamic_slice_in_dim(values, y * count + first, quarter)
    own_factor = rms_scale(own_values)
    hidden = after(own_values, (far_a, far_b)) + branch
    factor_m = rms_scale(hidden)
    xn2_own = (hidden * factor_m * gain_m).astype(BF)
    xn2 = spread(xn2_own, "tensor", 4).reshape(count, MODEL_WIDTH)
    gate_m = pair_gates(jnp.dot(xn2, router_m, preferred_element_type=F32), pick_m)

    received = to_experts(
        lax.dot_general(any_row, xn2, ROWS, preferred_element_type=F32).astype(BF)
    )
    grad_act_raw = down_back(grad_received, down_pieces, z)
    received, grad_act_raw, hidden_last, gate_m = lax.optimization_barrier(
        (received, grad_act_raw, core_last(hidden), gate_m)
    )
    weight_m = gate_m * kept.astype(F32)
    activated, grad_pair, row_gate, grad_back = expert_middle(
        received,
        grad_landed[:, MODEL_WIDTH:],
        jnp.pad(router_m, ((0, 0), (0, 120))),
        gate_up_w,
        grad_act_raw,
        2 * y + core,
    )
    grad_back, late_pair, late_act = lax.optimization_barrier((grad_back, grad_pair, activated))
    grad_returned = to_experts(grad_back)
    grad_down_w = down_product(late_act, grad_received, row_gate)
    down_sum = lax.psum_scatter(grad_down_w, "dp", scatter_dimension=1, tiled=True)
    quarters = expert_quarters(late_act, down_pieces, z, x)
    grad_gate_up_w = gate_up_product(received, late_pair)
    gate_up_sum = lax.psum_scatter(grad_gate_up_w, "dp", scatter_dimension=0, tiled=True)
    late_any = after(any_row, (grad_down_w, quarters, grad_gate_up_w))
    expert_out = (
        quarters[0].astype(F32)
        + sum(from_ahead(quarters[4 - k], "tensor", k).astype(F32) for k in (1, 2, 3))
    ).astype(BF)

    grad_xn2_part = jnp.dot(
        late_any, grad_returned[:, :MODEL_WIDTH], preferred_element_type=F32
    ).astype(BF)
    row_gate_parts = grad_returned[:, MODEL_WIDTH : MODEL_WIDTH + 2]
    gate_m_part = jnp.sum(
        jnp.einsum("jtr,rd->tjd", to_row, row_gate_parts, preferred_element_type=F32), axis=2
    )
    shares = jnp.concatenate([grad_xn2_part, widen(in_two(gate_m_part))], axis=1)
    landed = (
        exchange(shares.reshape(4, quarter, MODEL_WIDTH + HEAD_SIZE), "tensor")
        .astype(F32)
        .sum(axis=0)
    )
    landed, expert_out = lax.optimization_barrier((landed, expert_out))
    returned = to_experts(expert_out)
    grad_gate_m = (
        landed[:, MODEL_WIDTH : MODEL_WIDTH + 2] + landed[:, MODEL_WIDTH + 2 : MODEL_WIDTH + 4]
    )

    def quarter_of(array, offset=0):
        return lax.dynamic_slice_in_dim(array, first + offset, quarter)

    grad_logit_m = gate_back(quarter_of(gate_m), grad_gate_m, quarter_of(pick_m))
    grad_xn2 = landed[:, :MODEL_WIDTH] + lax.dot_general(
        grad_logit_m, router_m.astype(F32), LAST, preferred_element_type=F32
    )
    grad_norm, gain_m_part = norm_back(grad_xn2, hidden, factor_m, gain_m)
    grad_hidden = cot_own + grad_norm
    grad_sent_back, returned = lax.optimization_barrier((grad_hidden.astype(BF), returned))
    grad_branch = spread(grad_sent_back, plane, 16).reshape(4 * count, MODEL_WIDTH)

    fetched = jnp.einsum("jtr,rd->jtd", to_row, returned, preferred_element_type=F32)
    moe_part = jnp.sum(weight_m.T[:, :, None] * fetched, axis=0).astype(BF)
    width = down_own.shape[0]
    grad_branch, moe_part = lax.optimization_barrier((grad_branch, moe_part))
    moe_pieces = exchange(moe_part.reshape(4, quarter, MODEL_WIDTH // 4), "tensor")

    grad_mixed = jnp.dot(grad_branch, out_w, preferred_element_type=F32)
    grad_q_all, grad_logit_a, grad_kv_own, grad_kv_give = in_vmem(
        backward_kernel,
        [
            jax.ShapeDtypeStruct((half, EXPERTS * HEAD_SIZE), BF),
            jax.ShapeDtypeStruct((half, HEAD_SIZE), BF),
            jax.ShapeDtypeStruct((half, 2 * HEAD_SIZE), F32),
            jax.ShapeDtypeStruct((half, 2 * HEAD_SIZE), BF),
        ],
        [pltpu.VMEM((2, half, 2 * HEAD_SIZE), F32)],
        40 << 28,
        grad_mixed,
        query,
        kv_own,
        kv_other,
        attended,
        totals,
        gate_a,
        *shared,
    )
    out_pairs = [(grad_branch, mixed)]
    out_give = lax.ppermute(give_terms(out_pairs, z, core), "core", SWAP)
    kv_back, moe_pieces = lax.optimization_barrier(
        (lax.ppermute(grad_kv_give, "core", SWAP), moe_pieces)
    )
    moe = moe_pieces.transpose(1, 0, 2).reshape(quarter, MODEL_WIDTH).astype(F32)
    output_own = (hidden_last + moe).astype(BF)
    own_grad_kv = grad_kv_own + kv_back.astype(F32)
    grad_key = own_grad_kv[:, :HEAD_SIZE]
    grad_kv = jnp.concatenate(
        [grad_key * cosine - swapped(grad_key) * sine, own_grad_kv[:, HEAD_SIZE:]], axis=1
    ).astype(BF)
    grad_in = jnp.concatenate([grad_q_all, grad_kv, grad_logit_a], axis=1)
    grad_xn1_part = lax.dot_general(grad_in, in_w, LAST, preferred_element_type=F32).astype(BF)
    gain_row = jnp.pad(gain_m_part[None].astype(BF), ((0, 7), (0, 0)))
    lane = jnp.arange(1408, dtype=jnp.int32)[None, :]
    router_cols = jnp.pad(grad_logit_m.astype(BF), ((0, 0), (1288, 112)))
    gain_cols = ((jnp.arange(8)[:, None] == 0) & (lane == 1296)).astype(BF)
    in_pairs = [
        (xn1, after(grad_in, grad_xn1_part)),
        (
            jnp.concatenate([xn2_own, gain_row], axis=0),
            jnp.concatenate([router_cols, gain_cols], axis=0),
        ),
    ]
    in_give = lax.ppermute(give_terms(in_pairs, z, core), "core", SWAP)
    out_own, *out_rest = keep_terms(out_pairs, after(out_give, grad_xn1_part), z, core)
    in_own_rows, *in_rest = keep_terms(in_pairs, in_give, z, core)
    out_rest[0], out_rest[3], _ = lax.optimization_barrier(
        (out_rest[0], out_rest[3], in_own_rows)
    )
    out_ahead, out_back = ring_first(*out_rest, "dp")
    in_ahead, in_back = ring_first(*in_rest, "dp")
    out_sum = ring_second(after(out_own, gate_up_sum), out_ahead, out_back, "dp").astype(BF)
    landed_raw = exchange(grad_xn1_part.reshape(16, quarter, MODEL_WIDTH), plane)
    landed_raw, down_sum, *_ = lax.optimization_barrier((landed_raw, down_sum, in_ahead, in_back))
    in_sum = ring_second(after(in_own_rows, out_sum), in_ahead, in_back, "dp").astype(BF)
    landed_a = landed_raw.astype(F32).sum(axis=0)
    grad_x_norm, _ = norm_back(landed_a, own_values, own_factor, gain_a)
    columns = jnp.arange(1408, dtype=jnp.int32)[None, :]
    gain_rows = lax.dynamic_index_in_dim(
        lax.dynamic_index_in_dim(attn_gain.astype(F32).reshape(4, 4, 2, 64), z, 0, keepdims=False),
        core,
        1,
        keepdims=False,
    ).reshape(256, 1)
    gain_a_part = (
        jnp.sum(
            jnp.where(columns < 1288, in_sum.astype(F32) * mine[:, :1408].astype(F32), 0.0),
            axis=1,
            keepdims=True,
        )
        / gain_rows
    )
    small_part = jnp.where(columns[:, :128] == 17, gain_a_part, in_sum[:, 1280:].astype(F32))

    ends = jnp.concatenate(
        [output_own, core_last((grad_hidden + grad_x_norm).astype(BF))], axis=1
    )
    both_sums = jnp.concatenate(
        [in_sum[:, :1280], out_sum, small_part.astype(BF)], axis=1
    ).reshape(4, 64, 2432)
    y_parts = send_direct(both_sums, "y")
    gate_up_grad = (
        after(gate_up_sum, both_sums)
        .reshape(2, 4, 64, 2816)
        .transpose(1, 0, 2, 3)
        .reshape(1, 512, 2, width)
        .astype(F32)
    )
    _, _, *y_parts = lax.optimization_barrier((gate_up_grad, ends, *y_parts))
    both_ends = spread(ends, "tensor", 4)
    small_y = sum(p[:, 2304:].astype(F32) for p in y_parts).astype(BF)
    small_y = after(small_y, both_ends)
    small_sum = small_y.astype(F32) + sum(
        from_ahead(small_y, "tensor", k).astype(F32) for k in (1, 2, 3)
    )
    down_grad = down_sum.astype(F32)[None]
    both_ends = both_ends.reshape(count, 2 * MODEL_WIDTH)
    output, input_grad = both_ends[:, :MODEL_WIDTH], both_ends[:, MODEL_WIDTH:]
    query_grad, kv_grad, out_grad = heads_placed(y_parts, y)
    return (
        output,
        input_grad,
        small_sum[:, 17],
        small_sum[:, 16],
        small_sum[:, :8],
        kv_grad,
        query_grad,
        out_grad,
        small_sum[:, 8:16],
        gate_up_grad,
        down_grad,
    )


def solution(mesh):
    split = Mesh(mesh.devices.reshape(4, 4, 2, 4), ("dp", "y", "core", "tensor"))
    rows = ("dp", "y", "core")
    expert = ("y", "core")
    placed = (
        P(rows, None),
        P(rows, None),
        P(),
        P(),
        P(rows, None),
        P(rows, None, "tensor"),
        P(rows, None, "tensor"),
        P(rows, None, "tensor"),
        P(rows, None),
        P(expert, "dp", None, "tensor"),
        P(expert, "tensor", "dp"),
        P(rows, None),
        P(rows, None),
        P(rows, None),
        P(),
    )
    return jax.shard_map(
        body,
        mesh=split,
        in_specs=placed,
        out_specs=(
            P(rows, None),
            P(rows, None),
            P(rows),
            P(rows),
            P(rows, None),
            P(rows, None, "tensor"),
            P(rows, None, "tensor"),
            P(rows, None, "tensor"),
            P(rows, None),
            P(expert, "dp", None, "tensor"),
            P(expert, "tensor", "dp"),
        ),
        check_vma=False,
    )
```

```python
import jax
import jax.numpy as jnp
from jax import lax
from jax.experimental import pallas as pl
from jax.experimental.pallas import tpu as pltpu
from jax.sharding import Mesh
from jax.sharding import PartitionSpec as P

MODEL_WIDTH = 2048
HEAD_SIZE = 128
EXPERTS = 8
WINDOW = 1024
NORM_EPS = 1e-06
BF = jnp.bfloat16
F32 = jnp.float32
ROWS = (((0,), (0,)), ((), ()))
LAST = (((1,), (1,)), ((), ()))
UP = [(0, 1), (1, 2), (2, 3), (3, 0)]
DOWN = [(0, 3), (1, 0), (2, 1), (3, 2)]
SWAP = [(0, 1), (1, 0)]


def exchange(blocks, axis):
    return lax.all_to_all(blocks, axis, split_axis=0, concat_axis=0, tiled=True)


def spread(block, axis, count):
    return exchange(jnp.broadcast_to(block, (count, *block.shape)), axis)


def from_ahead(block, axis, steps):
    return lax.ppermute(block, axis, [(i, (i - steps) % 4) for i in range(4)])


def in_order(pieces, first):
    both = jnp.stack(pieces + pieces[:3])
    return lax.dynamic_slice_in_dim(both, lax.rem(4 - first, 4), 4)


def pick_block(blocks, index):
    return lax.dynamic_index_in_dim(blocks, lax.rem(index, 4), 0, keepdims=False)


def send_direct(blocks, axis):
    me = lax.axis_index(axis)
    return [pick_block(blocks, me)] + [
        from_ahead(pick_block(blocks, me + 4 - k), axis, k) for k in (1, 2, 3)
    ]


def heads_first(shard):
    columns = shard.shape[1] * HEAD_SIZE
    return shard.reshape(64, -1, 4, HEAD_SIZE).transpose(2, 0, 1, 3).reshape(4, 64, columns)


def after(value, other):
    return lax.optimization_barrier((value, other))[0]


def core_first(rows):
    return rows.reshape(-1, 4, 4, 2, 64).transpose(0, 1, 3, 2, 4).reshape(-1, MODEL_WIDTH)


def core_last(rows):
    return rows.reshape(-1, 4, 2, 4, 64).transpose(0, 1, 3, 2, 4).reshape(-1, MODEL_WIDTH)


def ring_first(ahead, low, high, back, axis):
    low = lax.ppermute(low, axis, UP)
    high = lax.ppermute(high, axis, DOWN)
    half = low.shape[0]
    ahead = jnp.concatenate([(ahead[:half].astype(F32) + low.astype(F32)).astype(BF), ahead[half:]])
    back = jnp.concatenate([back[:half], (back[half:].astype(F32) + high.astype(F32)).astype(BF)])
    return ahead, back


def ring_second(own, ahead, back, axis):
    return (
        own.astype(F32)
        + lax.ppermute(ahead, axis, UP).astype(F32)
        + lax.ppermute(back, axis, DOWN).astype(F32)
    )


def rms_scale(values):
    return lax.rsqrt(jnp.mean(values * values, axis=-1, keepdims=True) + NORM_EPS)


def turn(heads, cosine, sine):
    first, second = heads[..., :64], heads[..., 64:]
    return jnp.concatenate([first * cosine - second * sine, second * cosine + first * sine], axis=-1)


EXTENTS = (256, 384, 512, 640)
SCALE = HEAD_SIZE**-0.5


def masked_scores(query, key, row_meta, key_meta):
    raw = lax.dot_general(query, key, LAST, preferred_element_type=F32) * SCALE
    gap = row_meta[:, 0:1] - key_meta[0:1]
    allowed = (gap >= 0) & (gap < WINDOW) & (row_meta[:, 1:2] == key_meta[1:2])
    return jnp.where(jnp.concatenate([allowed, allowed], axis=0), raw, -1e30)


def forward_kernel(proj, own, other, routes, cosine, sine, row_meta, key_meta, *outs):
    query_out, attended_out, total_out, gates_out, mixed_out = outs
    count = proj.shape[0] // 4
    for i in range(4):
        rows = pl.ds(count * i, count)
        extent = EXTENTS[i]
        logits = proj[rows, 1280:1288]
        lane = lax.broadcasted_iota(jnp.int32, (count, EXPERTS), 1)
        named = [routes[rows, 0:1], routes[rows, 1:2]]
        chosen = [jnp.sum(jnp.where(lane == n, logits, 0.0), axis=1, keepdims=True) for n in named]
        top = jnp.maximum(chosen[0], chosen[1])
        power = [jnp.exp(c - top) for c in chosen]
        gates = [p / (power[0] + power[1]) for p in power]
        gates_out[rows, 0:1] = gates[0]
        gates_out[rows, 1:2] = gates[1]
        cos, sin = cosine[rows, :], sine[rows, :]
        picked = []
        for n in named:
            q = jnp.zeros((count, HEAD_SIZE), F32)
            for e in range(EXPERTS):
                q = q + jnp.where(n == e, proj[rows, HEAD_SIZE * e : HEAD_SIZE * (e + 1)], 0.0)
            picked.append(q * cos + pltpu.roll(q, 64, 1) * sin)
        query = jnp.concatenate(picked, axis=0).astype(BF)
        query_out[i] = query
        halves = (own, other)
        scores = [
            masked_scores(
                query, h[:extent, :HEAD_SIZE], row_meta[rows, :], key_meta[k, :, :extent]
            )
            for k, h in enumerate(halves)
        ]
        row_max = jnp.maximum(
            jnp.max(scores[0], axis=1, keepdims=True), jnp.max(scores[1], axis=1, keepdims=True)
        )
        weights = [jnp.exp(s - row_max) for s in scores]
        total = jnp.sum(weights[0], axis=1, keepdims=True) + jnp.sum(weights[1], axis=1, keepdims=True)
        inverse = 1.0 / total
        attended = sum(
            jnp.dot((w * inverse).astype(BF), h[:extent, HEAD_SIZE:], preferred_element_type=F32)
            for w, h in zip(weights, halves)
        )
        attended_out[i] = attended
        total_out[i] = row_max + jnp.log(total)
        for e in range(EXPERTS):
            mixed_out[rows, HEAD_SIZE * e : HEAD_SIZE * (e + 1)] = (
                jnp.where(named[0] == e, gates[0], 0.0) * attended[:count]
                + jnp.where(named[1] == e, gates[1], 0.0) * attended[count:]
            ).astype(BF)


def backward_kernel(
    grad_mixed, query_in, own, other, attended_in, total_in, gates_in, routes, cosine, sine, row_meta, key_meta, *outs
):
    grad_query_out, grad_logit_out, grad_own_out, grad_other_out, sums = outs
    count = grad_mixed.shape[0] // 4
    sums[...] = jnp.zeros_like(sums)
    for i in range(4):
        rows = pl.ds(count * i, count)
        extent = EXTENTS[i]
        named = [routes[rows, 0:1], routes[rows, 1:2]]
        gates = [gates_in[rows, 0:1], gates_in[rows, 1:2]]
        cos, sin = cosine[rows, :], sine[rows, :]
        attended = attended_in[i]
        picked = []
        for n in named:
            g = jnp.zeros((count, HEAD_SIZE), F32)
            for e in range(EXPERTS):
                g = g + jnp.where(n == e, grad_mixed[rows, HEAD_SIZE * e : HEAD_SIZE * (e + 1)], 0.0)
            picked.append(g)
        gate_grads = [
            jnp.sum(p * attended[count * j : count * (j + 1)], axis=1, keepdims=True)
            for j, p in enumerate(picked)
        ]
        level = gates[0] * gate_grads[0] + gates[1] * gate_grads[1]
        lane = lax.broadcasted_iota(jnp.int32, (count, HEAD_SIZE), 1)
        grad_logit_out[rows, :] = sum(
            jnp.where(lane == n, g * (d - level), 0.0) for n, g, d in zip(named, gates, gate_grads)
        ).astype(BF)
        grad_attended = jnp.concatenate(
            [gates[0] * picked[0], gates[1] * picked[1]], axis=0
        ).astype(BF)
        query = query_in[i]
        total = total_in[i]
        probs, grad_probs = [], []
        delta = jnp.zeros((2 * count, 1), F32)
        for k, h in enumerate((own, other)):
            score = masked_scores(
                query, h[:extent, :HEAD_SIZE], row_meta[rows, :], key_meta[k, :, :extent]
            )
            prob = jnp.exp(score - total)
            grad_prob = lax.dot_general(
                grad_attended, h[:extent, HEAD_SIZE:], LAST, preferred_element_type=F32
            )
            delta = delta + jnp.sum(prob * grad_prob, axis=1, keepdims=True)
            probs.append(prob)
            grad_probs.append(grad_prob)
        grad_query = jnp.zeros((2 * count, HEAD_SIZE), F32)
        for k, h in enumerate((own, other)):
            grad_score = (probs[k] * (grad_probs[k] - delta)).astype(BF)
            grad_query = grad_query + jnp.dot(
                grad_score, h[:extent, :HEAD_SIZE], preferred_element_type=F32
            )
            sums[k, :extent, :HEAD_SIZE] += (
                lax.dot_general(grad_score, query, ROWS, preferred_element_type=F32) * SCALE
            )
            sums[k, :extent, HEAD_SIZE:] += lax.dot_general(
                probs[k].astype(BF), grad_attended, ROWS, preferred_element_type=F32
            )
        grad_query = grad_query * SCALE
        turned = [
            g * cos - pltpu.roll(g, 64, 1) * sin for g in (grad_query[:count], grad_query[count:])
        ]
        for e in range(EXPERTS):
            grad_query_out[rows, HEAD_SIZE * e : HEAD_SIZE * (e + 1)] = (
                jnp.where(named[0] == e, turned[0], 0.0) + jnp.where(named[1] == e, turned[1], 0.0)
            ).astype(BF)
    grad_own_out[...] = sums[0]
    grad_other_out[...] = sums[1].astype(BF)


def in_vmem(kernel, outs, scratch, flops, *args):
    spec = pl.BlockSpec(memory_space=pltpu.VMEM)
    moved = sum(a.size * a.dtype.itemsize for a in args)
    return pl.pallas_call(
        kernel,
        out_shape=outs,
        in_specs=[spec] * len(args),
        out_specs=[spec] * len(outs),
        scratch_shapes=scratch,
        compiler_params=pltpu.CompilerParams(vmem_limit_bytes=40 * 1024 * 1024),
        cost_estimate=pl.CostEstimate(flops=flops, bytes_accessed=moved, transcendentals=1 << 20),
    )(*args)


SOME = pl.CostEstimate(flops=1 << 35, bytes_accessed=1 << 27, transcendentals=0)


def on_grid(kernel, scalars, grid, in_specs, out_specs, outs, scratch, *args, cost=SOME):
    return pl.pallas_call(
        kernel,
        out_shape=outs,
        grid_spec=pltpu.PrefetchScalarGridSpec(
            num_scalar_prefetch=1,
            grid=grid,
            in_specs=in_specs,
            out_specs=out_specs,
            scratch_shapes=scratch,
        ),
        compiler_params=pltpu.CompilerParams(vmem_limit_bytes=48 * 1024 * 1024),
        cost_estimate=cost,
    )(jnp.stack(scalars).astype(jnp.int32), *args)


def give_terms(pairs, place, core):
    columns = pairs[0][1].shape[1]

    def kernel(at, *refs):
        out = refs[-1]
        total = sum(
            lax.dot_general(refs[j][...], refs[j + 1][...], ROWS, preferred_element_type=F32)
            for j in range(0, len(refs) - 1, 2)
        )
        out[0] = total.astype(BF)

    specs = []
    for tall, terms in pairs:
        specs.append(pl.BlockSpec((tall.shape[0], 256), lambda i, at: (0, 2 * i + 1 - at[1])))
        specs.append(pl.BlockSpec(terms.shape, lambda i, at: (0, 0)))
    return on_grid(
        kernel,
        (place, core),
        (4,),
        specs,
        pl.BlockSpec((1, 256, columns), lambda i, at: (i, 0, 0)),
        jax.ShapeDtypeStruct((4, 256, columns), BF),
        [],
        *[a for pair in pairs for a in pair],
    )


def keep_terms(pairs, landed, place, core):
    columns = pairs[0][1].shape[1]
    count = 2 * len(pairs)

    def kernel(at, *refs):
        more, own, ahead, low, high, back = refs[count:]
        total = sum(
            lax.dot_general(refs[j][...], refs[j + 1][...], ROWS, preferred_element_type=F32)
            for j in range(0, count, 2)
        )
        total = (total.astype(BF).astype(F32) + more[0].astype(F32)).astype(BF)
        step = pl.program_id(0)

        @pl.when(step == 0)
        def _():
            own[...] = total

        @pl.when(step == 1)
        def _():
            ahead[...] = total

        @pl.when(step == 2)
        def _():
            low[...] = total[:128]
            high[...] = total[128:]

        @pl.when(step == 3)
        def _():
            back[...] = total

    def whole(rows):
        return pl.BlockSpec((rows, columns), lambda i, at: (0, 0))

    specs = []
    for tall, terms in pairs:
        specs.append(
            pl.BlockSpec(
                (tall.shape[0], 256), lambda i, at: (0, 2 * lax.rem(at[0] + i, 4) + at[1])
            )
        )
        specs.append(pl.BlockSpec(terms.shape, lambda i, at: (0, 0)))
    specs.append(pl.BlockSpec((1, 256, columns), lambda i, at: (lax.rem(at[0] + i, 4), 0, 0)))
    return on_grid(
        kernel,
        (place, core),
        (4,),
        specs,
        [whole(256), whole(256), whole(128), whole(128), whole(256)],
        [jax.ShapeDtypeStruct((r, columns), BF) for r in (256, 256, 128, 128, 256)],
        [],
        *[a for pair in pairs for a in pair],
        landed,
    )


def gate_up_product(rows, pair):
    depth, width = pair.shape[1:]

    def kernel(at, left, right, out):
        for half in range(2):
            out[:, width * half : width * (half + 1)] = lax.dot_general(
                left[...], right[half], ROWS, preferred_element_type=F32
            ).astype(BF)

    return on_grid(
        kernel,
        (jnp.int32(0),),
        (8,),
        [
            pl.BlockSpec((depth, 256), lambda i, at: (0, i)),
            pl.BlockSpec((2, depth, width), lambda i, at: (0, 0, 0)),
        ],
        pl.BlockSpec((256, 2 * width), lambda i, at: (i, 0)),
        jax.ShapeDtypeStruct((MODEL_WIDTH, 2 * width), BF),
        [],
        rows,
        pair,
    )


def down_product(activated, grads, gate):
    def kernel(at, left, right, scale, out):
        scaled = (scale[...] * right[...].astype(F32)).astype(BF)
        out[...] = lax.dot_general(left[...], scaled, ROWS, preferred_element_type=F32).astype(BF)

    depth, width = activated.shape
    return on_grid(
        kernel,
        (jnp.int32(0),),
        (4,),
        [
            pl.BlockSpec((depth, width), lambda i, at: (0, 0)),
            pl.BlockSpec((depth, 512), lambda i, at: (0, i)),
            pl.BlockSpec((depth, 1), lambda i, at: (0, 0)),
        ],
        pl.BlockSpec((width, 512), lambda i, at: (0, i)),
        jax.ShapeDtypeStruct((width, MODEL_WIDTH), BF),
        [],
        activated,
        grads,
        gate,
    )


def down_back(grads, pieces, place):
    def kernel(at, left, own, ahead, far_a, far_b, back, out):
        total = None
        for shift, start, piece in (
            (0, 0, own), (1, 0, ahead), (2, 0, far_a), (2, 256, far_b), (3, 0, back)
        ):
            size = piece.shape[1]
            lanes = pl.ds(pl.multiple_of(lax.rem(at[0] + shift, 4) * 512 + start, 256), size)
            term = lax.dot_general(left[:, lanes], piece[...], LAST, preferred_element_type=F32)
            total = term if total is None else total + term
        out[...] = total

    depth, width = grads.shape[0], pieces[0].shape[0]
    return on_grid(
        kernel,
        (place,),
        (width // 128,),
        [pl.BlockSpec(grads.shape, lambda i, at: (0, 0))]
        + [pl.BlockSpec((128, p.shape[1]), lambda i, at: (i, 0)) for p in pieces],
        pl.BlockSpec((depth, 128), lambda i, at: (0, i)),
        jax.ShapeDtypeStruct((depth, width), F32),
        [],
        grads,
        *pieces,
    )


def expert_quarters(activated, pieces, place, x):
    def kernel(at, left, own, ahead, far_a, far_b, back, out):
        step = pl.program_id(0)
        for shift, refs in enumerate(((own,), (ahead,), (far_a, far_b), (back,))):

            @pl.when(step == shift)
            def _():
                terms = [jnp.dot(left[...], r[...], preferred_element_type=F32) for r in refs]
                out[0] = jnp.concatenate(terms, axis=1).astype(BF)

    depth = activated.shape[0]
    return on_grid(
        kernel,
        (place, x),
        (4,),
        [pl.BlockSpec(a.shape, lambda i, at: (0, 0)) for a in (activated, *pieces)],
        pl.BlockSpec((1, depth, 512), lambda i, at: (lax.rem(at[0] + i + 4 - at[1], 4), 0, 0)),
        jax.ShapeDtypeStruct((4, depth, 512), BF),
        [],
        activated,
        *pieces,
    )


def expert_middle(rows, marks, router, gate_up_w, grad_act, expert):
    depth, width = grad_act.shape
    blocks = width // 128

    def kernel(
        at, rows_ref, marks_ref, router_ref, gate_ref, up_ref, flat_ref, grad_ref,
        act_out, pair_out, gate_out, back_out, pair_all, row_gate, row_grad,
    ):
        step = pl.program_id(0)
        lane = lax.broadcasted_iota(jnp.int32, (depth, 128), 1)

        @pl.when(step == 0)
        def _():
            logits = jnp.dot(rows_ref[...], router_ref[...], preferred_element_type=F32)
            marks_f = marks_ref[...].astype(F32)
            own = jnp.sum(jnp.where(lane == at[0], logits, 0.0), axis=1, keepdims=True)
            other = jnp.sum(jnp.where(lane < 8, logits * marks_f, 0.0), axis=1, keepdims=True)
            valid = jnp.sum(jnp.where(lane == 8, marks_f, 0.0), axis=1, keepdims=True)
            top = jnp.maximum(own, other)
            power = jnp.exp(own - top)
            row_gate[...] = valid * power / (power + jnp.exp(other - top))
            gate_out[...] = row_gate[...]
            row_grad[...] = jnp.zeros_like(row_grad)

        @pl.when(step < blocks)
        def _():
            both = jnp.concatenate([gate_ref[...], up_ref[...]], axis=1)
            gate_up = jnp.dot(rows_ref[...], both, preferred_element_type=F32)
            gate, up = gate_up[:, :128], gate_up[:, 128:]
            sigmoid = 1.0 / (1.0 + jnp.exp(-gate))
            silu = gate * sigmoid
            act = (silu * up).astype(BF)
            raw = grad_ref[...]
            grad = row_gate[...] * raw
            grad_gate = (grad * up * sigmoid * (1.0 + gate * (1.0 - sigmoid))).astype(BF)
            grad_up = (grad * silu).astype(BF)
            act_out[...] = act
            pair_out[0] = grad_gate
            pair_out[1] = grad_up
            at_lane = pl.multiple_of(step * 128, 128)
            pair_all[:, pl.ds(at_lane, 128)] = grad_gate
            pair_all[:, pl.ds(at_lane + width, 128)] = grad_up
            row_grad[...] += jnp.sum(act.astype(F32) * raw, axis=1, keepdims=True)

        @pl.when(step >= blocks)
        def _():
            back_lane = pl.multiple_of((step - blocks) * 512, 512)
            back_out[:, pl.ds(back_lane, 512)] = lax.dot_general(
                pair_all[...], flat_ref[...], LAST, preferred_element_type=F32
            ).astype(BF)

        @pl.when(step == blocks + 3)
        def _():
            high = row_grad[...].astype(BF).astype(F32)
            low = row_grad[...] - high
            back_out[:, MODEL_WIDTH:] = jnp.where(
                lane == 0, high, jnp.where(lane == 1, low, 0.0)
            ).astype(BF)

    def first(i):
        return jnp.minimum(i, blocks - 1)

    def second(i):
        return jnp.clip(i - blocks, 0, 3)

    return on_grid(
        kernel,
        (expert,),
        (blocks + 4,),
        [
            pl.BlockSpec((depth, MODEL_WIDTH), lambda i, at: (0, 0)),
            pl.BlockSpec((depth, 128), lambda i, at: (0, 0)),
            pl.BlockSpec((MODEL_WIDTH, 128), lambda i, at: (0, 0)),
            pl.BlockSpec((MODEL_WIDTH, 128), lambda i, at: (0, first(i))),
            pl.BlockSpec((MODEL_WIDTH, 128), lambda i, at: (0, blocks + first(i))),
            pl.BlockSpec((512, 2 * width), lambda i, at: (second(i), 0)),
            pl.BlockSpec((depth, 128), lambda i, at: (0, first(i))),
        ],
        [
            pl.BlockSpec((depth, 128), lambda i, at: (0, first(i))),
            pl.BlockSpec((2, depth, 128), lambda i, at: (0, 0, first(i))),
            pl.BlockSpec((depth, 1), lambda i, at: (0, 0)),
            pl.BlockSpec((depth, MODEL_WIDTH + 128), lambda i, at: (0, 0)),
        ],
        [
            jax.ShapeDtypeStruct((depth, width), BF),
            jax.ShapeDtypeStruct((2, depth, width), BF),
            jax.ShapeDtypeStruct((depth, 1), F32),
            jax.ShapeDtypeStruct((depth, MODEL_WIDTH + 128), BF),
        ],
        [
            pltpu.VMEM((depth, 2 * width), BF),
            pltpu.VMEM((depth, 1), F32),
            pltpu.VMEM((depth, 1), F32),
        ],
        rows,
        marks,
        router,
        gate_up_w,
        gate_up_w,
        gate_up_w,
        grad_act,
        cost=pl.CostEstimate(
            flops=8 * depth * MODEL_WIDTH * width, bytes_accessed=1 << 24, transcendentals=1 << 20
        ),
    )


def heads_placed(pieces, y):
    def kernel(at, p0, p1, p2, p3, query, kv, out):
        for k, piece in enumerate((p0, p1, p2, p3)):
            lanes = pl.ds(pl.multiple_of(lax.rem(at[0] + k, 4) * 128, 128), 128)
            for e in range(18):
                block = piece[:, 128 * e : 128 * (e + 1)].astype(F32)
                if e < 8:
                    query[:, e, lanes] = block
                elif e < 10:
                    kv[:, e - 8, lanes] = block
                else:
                    out[:, e - 10, lanes] = block

    shapes = [(64, 8, 512), (64, 2, 512), (64, 8, 512)]
    return on_grid(
        kernel,
        (y,),
        (1,),
        [pl.BlockSpec((64, 2432), lambda i, at: (0, 0))] * 4,
        [pl.BlockSpec(s, lambda i, at: (0, 0, 0)) for s in shapes],
        [jax.ShapeDtypeStruct(s, F32) for s in shapes],
        [],
        *pieces,
        cost=pl.CostEstimate(flops=0, bytes_accessed=0, transcendentals=0),
    )


def pick_of(routes):
    return (routes[:, :, None] == jnp.arange(EXPERTS, dtype=jnp.int32)[None, None, :]).astype(F32)


def pair_gates(logits, pick):
    chosen = jnp.sum(logits[:, None, :] * pick, axis=-1)
    weights = jnp.exp(chosen - jnp.max(chosen, axis=1, keepdims=True))
    return weights / jnp.sum(weights, axis=1, keepdims=True)


def gate_back(gates, grad_gates, pick):
    inner = gates * (grad_gates - jnp.sum(gates * grad_gates, axis=1, keepdims=True))
    return jnp.sum(inner[:, :, None] * pick, axis=1)


def norm_back(grad_normed, values, factor, gain):
    gain_part = jnp.sum(grad_normed * values * factor, axis=0)
    inner = grad_normed * gain
    grad_values = factor * inner - values * factor * factor * factor * jnp.mean(
        inner * values, axis=-1, keepdims=True
    )
    return grad_values, gain_part


def in_two(values):
    high = values.astype(BF)
    low = (values - high.astype(F32)).astype(BF)
    return jnp.concatenate([high, low], axis=1)


def widen(columns):
    return jnp.pad(columns, ((0, 0), (0, HEAD_SIZE - columns.shape[1])))


def body(
    tokens,
    cotangent,
    attn_gain,
    mlp_gain,
    attn_router,
    key_value_weight,
    query_matrix,
    output_matrix,
    mlp_router,
    gate_up_weight,
    down_weight,
    attn_routes,
    mlp_routes,
    priority,
    segments,
):
    z, y = lax.axis_index("dp"), lax.axis_index("y")
    core, x = lax.axis_index("core"), lax.axis_index("tensor")
    count = tokens.shape[0]
    quarter = count // 4
    capacity = 50
    room = 56
    sequence = 8 * count
    plane = ("y", "tensor")

    routers_own = jnp.concatenate([attn_router, mlp_router], axis=1)
    down_own = down_weight[0]
    down_before = lax.ppermute(down_own, "dp", UP)
    down_after = lax.ppermute(down_own, "dp", DOWN)
    mine = exchange(
        jnp.concatenate(
            [
                heads_first(query_matrix),
                heads_first(key_value_weight),
                jnp.broadcast_to(widen(routers_own), (4, 64, HEAD_SIZE)),
                heads_first(output_matrix),
            ],
            axis=2,
        ),
        "y",
    ).reshape(256, 2432)
    sent = jnp.concatenate([core_first(tokens), widen(attn_routes.astype(BF))], axis=1)
    arrived = spread(after(sent, mine), "y", 4).reshape(4 * count, MODEL_WIDTH + HEAD_SIZE)
    all_w = lax.all_gather(
        after(mine, (down_before, down_after)), ("dp", "core"), axis=0, tiled=True
    )
    values = arrived[:, :MODEL_WIDTH].astype(F32)
    routes = arrived[:, MODEL_WIDTH : MODEL_WIDTH + 2].astype(jnp.int32)
    gain_a = core_first(attn_gain.astype(F32))[0]
    gain_m = core_first(mlp_gain.astype(F32))[0]
    xn1 = (values * rms_scale(values) * gain_a).astype(BF)

    ranking = priority[0]
    pick_m = pick_of(mlp_routes)
    before = (ranking[None, :] < ranking[:, None]).astype(BF)
    earlier = jnp.dot(before, jnp.sum(pick_m, axis=1).astype(BF), preferred_element_type=F32)
    slots = jnp.sum(pick_m * earlier[:, None, :], axis=-1).astype(jnp.int32)
    kept = slots < capacity
    dest = jnp.where(kept, mlp_routes * room + slots, -1)
    lanes = jnp.arange(EXPERTS * room, dtype=jnp.int32)
    to_row = (dest.T[:, :, None] == lanes[None, None, :]).astype(BF)
    any_row = to_row[0] + to_row[1]
    both_rows = to_row.reshape(2 * count, EXPERTS * room)

    def to_experts(rows):
        columns = rows.shape[1]
        return exchange(rows.reshape(EXPERTS, room, columns), ("y", "core")).reshape(
            EXPERTS * room, columns
        )

    def with_other(j):
        others = jnp.concatenate([pick_m[:, 1 - j], jnp.ones((count, 1), F32)], axis=1)
        return jnp.concatenate([cotangent, widen(others.astype(BF))], axis=1)

    grad_sent = lax.dot_general(
        both_rows,
        jnp.concatenate([with_other(0), with_other(1)], axis=0),
        ROWS,
        preferred_element_type=F32,
    ).astype(BF)
    def places(half):
        blocks = 2 * jnp.arange(4, dtype=jnp.int32)[:, None] + half
        return (blocks * count + jnp.arange(count, dtype=jnp.int32)[None, :]).reshape(-1)

    inverse = 10000.0 ** (-(jnp.arange(HEAD_SIZE // 2).astype(F32) * 2.0 / HEAD_SIZE))
    angle = places(core).astype(F32)[:, None] * inverse[None, :]
    cosine = jnp.tile(jnp.cos(angle), (1, 2))
    sine = jnp.concatenate([-jnp.sin(angle), jnp.sin(angle)], axis=1)

    first = x * quarter
    cot_own = core_first(lax.dynamic_slice_in_dim(cotangent, first, quarter)).astype(F32)
    all_w, down_before, down_after, xn1, grad_sent, cosine, sine, cot_own = (
        lax.optimization_barrier(
            (all_w, down_before, down_after, xn1, grad_sent, cosine, sine, cot_own)
        )
    )
    in_w, out_w = all_w[:, :1408], all_w[:, 1408:]
    far_a = lax.ppermute(down_before[:, :256], "dp", UP)
    far_b = lax.ppermute(down_after[:, 256:], "dp", DOWN)
    down_pieces = (down_own, down_after, far_a, far_b, down_before)
    gate_up_own = gate_up_weight.reshape(4, 2, 64, 2816).transpose(1, 0, 2, 3).reshape(512, 2816)
    gate_up_w = lax.all_gather(after(gate_up_own, all_w), "dp", axis=0, tiled=True)
    router_m = in_w[:, 1288:1296]

    grad_landed = to_experts(grad_sent)

    of_sequence = lax.dynamic_slice_in_dim(segments, z * sequence, sequence).reshape(4, 2, count)

    def meta(half):
        documents = lax.dynamic_index_in_dim(of_sequence, half, 1, keepdims=False).reshape(-1)
        return jnp.stack([places(half), documents])

    key_meta = jnp.stack([meta(core), meta(1 - core)])
    row_meta = key_meta[0].T
    def swapped(rows):
        return jnp.concatenate([rows[:, 64:], rows[:, :64]], axis=1)

    half = 4 * count
    projected = jnp.dot(xn1, in_w, preferred_element_type=F32)
    key_raw = projected[:, 1024:1152]
    kv_own = jnp.concatenate(
        [key_raw * cosine + swapped(key_raw) * sine, projected[:, 1152:1280]], axis=1
    ).astype(BF)
    kv_other = lax.ppermute(kv_own, "core", SWAP)
    shared = (routes, cosine, sine, row_meta, key_meta)
    query, attended, totals, gate_a, mixed = in_vmem(
        forward_kernel,
        [
            jax.ShapeDtypeStruct((4, 2 * count, HEAD_SIZE), BF),
            jax.ShapeDtypeStruct((4, 2 * count, HEAD_SIZE), F32),
            jax.ShapeDtypeStruct((4, 2 * count, 1), F32),
            jax.ShapeDtypeStruct((half, 2), F32),
            jax.ShapeDtypeStruct((half, EXPERTS * HEAD_SIZE), BF),
        ],
        [],
        6 << 28,
        projected,
        kv_own,
        kv_other,
        *shared,
    )
    branch_part = lax.dot_general(mixed, out_w, LAST, preferred_element_type=F32).astype(BF)
    branch_part = after(branch_part, grad_landed)
    grad_received = grad_landed[:, :MODEL_WIDTH]
    branch = exchange(branch_part.reshape(16, quarter, MODEL_WIDTH), plane).astype(F32).sum(axis=0)

    own_values = lax.dynamic_slice_in_dim(values, y * count + first, quarter)
    own_factor = rms_scale(own_values)
    hidden = after(own_values, (far_a, far_b)) + branch
    factor_m = rms_scale(hidden)
    xn2_own = (hidden * factor_m * gain_m).astype(BF)
    xn2 = spread(xn2_own, "tensor", 4).reshape(count, MODEL_WIDTH)
    gate_m = pair_gates(jnp.dot(xn2, router_m, preferred_element_type=F32), pick_m)

    received = to_experts(
        lax.dot_general(any_row, xn2, ROWS, preferred_element_type=F32).astype(BF)
    )
    grad_act_raw = down_back(grad_received, down_pieces, z)
    received, grad_act_raw, hidden_last, gate_m = lax.optimization_barrier(
        (received, grad_act_raw, core_last(hidden), gate_m)
    )
    weight_m = gate_m * kept.astype(F32)
    activated, grad_pair, row_gate, grad_back = expert_middle(
        received,
        grad_landed[:, MODEL_WIDTH:],
        jnp.pad(router_m, ((0, 0), (0, 120))),
        gate_up_w,
        grad_act_raw,
        2 * y + core,
    )
    grad_back, late_pair, late_act = lax.optimization_barrier((grad_back, grad_pair, activated))
    grad_returned = to_experts(grad_back)
    grad_down_w = down_product(late_act, grad_received, row_gate)
    down_sum = lax.psum_scatter(grad_down_w, "dp", scatter_dimension=1, tiled=True)
    quarters = expert_quarters(late_act, down_pieces, z, x)
    grad_gate_up_w = gate_up_product(received, late_pair)
    gate_up_sum = lax.psum_scatter(grad_gate_up_w, "dp", scatter_dimension=0, tiled=True)
    late_any = after(any_row, (grad_down_w, quarters, grad_gate_up_w))
    expert_out = (
        quarters[0].astype(F32)
        + sum(from_ahead(quarters[4 - k], "tensor", k).astype(F32) for k in (1, 2, 3))
    ).astype(BF)

    grad_xn2_part = jnp.dot(
        late_any, grad_returned[:, :MODEL_WIDTH], preferred_element_type=F32
    ).astype(BF)
    row_gate_parts = grad_returned[:, MODEL_WIDTH : MODEL_WIDTH + 2]
    gate_m_part = jnp.sum(
        jnp.einsum("jtr,rd->tjd", to_row, row_gate_parts, preferred_element_type=F32), axis=2
    )
    shares = jnp.concatenate([grad_xn2_part, widen(in_two(gate_m_part))], axis=1)
    landed = (
        exchange(shares.reshape(4, quarter, MODEL_WIDTH + HEAD_SIZE), "tensor")
        .astype(F32)
        .sum(axis=0)
    )
    landed, expert_out = lax.optimization_barrier((landed, expert_out))
    returned = to_experts(expert_out)
    grad_gate_m = (
        landed[:, MODEL_WIDTH : MODEL_WIDTH + 2] + landed[:, MODEL_WIDTH + 2 : MODEL_WIDTH + 4]
    )

    def quarter_of(array, offset=0):
        return lax.dynamic_slice_in_dim(array, first + offset, quarter)

    grad_logit_m = gate_back(quarter_of(gate_m), grad_gate_m, quarter_of(pick_m))
    grad_xn2 = landed[:, :MODEL_WIDTH] + lax.dot_general(
        grad_logit_m, router_m.astype(F32), LAST, preferred_element_type=F32
    )
    grad_norm, gain_m_part = norm_back(grad_xn2, hidden, factor_m, gain_m)
    grad_hidden = cot_own + grad_norm
    grad_sent_back, returned = lax.optimization_barrier((grad_hidden.astype(BF), returned))
    grad_branch = spread(grad_sent_back, plane, 16).reshape(4 * count, MODEL_WIDTH)

    fetched = jnp.einsum("jtr,rd->jtd", to_row, returned, preferred_element_type=F32)
    moe_part = jnp.sum(weight_m.T[:, :, None] * fetched, axis=0).astype(BF)
    width = down_own.shape[0]
    grad_branch, moe_part = lax.optimization_barrier((grad_branch, moe_part))
    moe_pieces = exchange(moe_part.reshape(4, quarter, MODEL_WIDTH // 4), "tensor")

    grad_mixed = jnp.dot(grad_branch, out_w, preferred_element_type=F32)
    grad_q_all, grad_logit_a, grad_kv_own, grad_kv_give = in_vmem(
        backward_kernel,
        [
            jax.ShapeDtypeStruct((half, EXPERTS * HEAD_SIZE), BF),
            jax.ShapeDtypeStruct((half, HEAD_SIZE), BF),
            jax.ShapeDtypeStruct((half, 2 * HEAD_SIZE), F32),
            jax.ShapeDtypeStruct((half, 2 * HEAD_SIZE), BF),
        ],
        [pltpu.VMEM((2, half, 2 * HEAD_SIZE), F32)],
        40 << 28,
        grad_mixed,
        query,
        kv_own,
        kv_other,
        attended,
        totals,
        gate_a,
        *shared,
    )
    out_pairs = [(grad_branch, mixed)]
    out_terms = give_terms(out_pairs, z, core)
    kv_back, moe_pieces, out_terms = lax.optimization_barrier(
        (lax.ppermute(grad_kv_give, "core", SWAP), moe_pieces, out_terms)
    )
    out_give = lax.ppermute(out_terms, "core", SWAP)
    moe = moe_pieces.transpose(1, 0, 2).reshape(quarter, MODEL_WIDTH).astype(F32)
    output_own = (hidden_last + moe).astype(BF)
    own_grad_kv = grad_kv_own + kv_back.astype(F32)
    grad_key = own_grad_kv[:, :HEAD_SIZE]
    grad_kv = jnp.concatenate(
        [grad_key * cosine - swapped(grad_key) * sine, own_grad_kv[:, HEAD_SIZE:]], axis=1
    ).astype(BF)
    grad_in = jnp.concatenate([grad_q_all, grad_kv, grad_logit_a], axis=1)
    gain_row = jnp.pad(gain_m_part[None].astype(BF), ((0, 7), (0, 0)))
    lane = jnp.arange(1408, dtype=jnp.int32)[None, :]
    router_cols = jnp.pad(grad_logit_m.astype(BF), ((0, 0), (1288, 112)))
    gain_cols = ((jnp.arange(8)[:, None] == 0) & (lane == 1296)).astype(BF)
    in_pairs = [
        (xn1, grad_in),
        (
            jnp.concatenate([xn2_own, gain_row], axis=0),
            jnp.concatenate([router_cols, gain_cols], axis=0),
        ),
    ]
    in_terms = give_terms(in_pairs, z, core)
    in_give = lax.ppermute(in_terms, "core", SWAP)
    grad_xn1_part = lax.dot_general(
        after(grad_in, in_terms), in_w, LAST, preferred_element_type=F32
    ).astype(BF)
    in_own_rows, *in_rest = keep_terms(in_pairs, after(in_give, grad_xn1_part), z, core)
    out_own, *out_rest = keep_terms(out_pairs, after(out_give, in_own_rows), z, core)
    out_rest[0], out_rest[3], _ = lax.optimization_barrier(
        (out_rest[0], out_rest[3], in_own_rows)
    )
    out_ahead, out_back = ring_first(*out_rest, "dp")
    in_ahead, in_back = ring_first(*in_rest, "dp")
    out_sum = ring_second(after(out_own, gate_up_sum), out_ahead, out_back, "dp").astype(BF)
    landed_raw = exchange(grad_xn1_part.reshape(16, quarter, MODEL_WIDTH), plane)
    landed_raw, down_sum, *_ = lax.optimization_barrier((landed_raw, down_sum, in_ahead, in_back))
    in_sum = ring_second(after(in_own_rows, out_sum), in_ahead, in_back, "dp").astype(BF)
    landed_a = landed_raw.astype(F32).sum(axis=0)
    grad_x_norm, _ = norm_back(landed_a, own_values, own_factor, gain_a)
    columns = jnp.arange(1408, dtype=jnp.int32)[None, :]
    gain_rows = lax.dynamic_index_in_dim(
        lax.dynamic_index_in_dim(attn_gain.astype(F32).reshape(4, 4, 2, 64), z, 0, keepdims=False),
        core,
        1,
        keepdims=False,
    ).reshape(256, 1)
    gain_a_part = (
        jnp.sum(
            jnp.where(columns < 1288, in_sum.astype(F32) * mine[:, :1408].astype(F32), 0.0),
            axis=1,
            keepdims=True,
        )
        / gain_rows
    )
    small_part = jnp.where(columns[:, :128] == 17, gain_a_part, in_sum[:, 1280:].astype(F32))

    ends = jnp.concatenate(
        [output_own, core_last((grad_hidden + grad_x_norm).astype(BF))], axis=1
    )
    both_sums = jnp.concatenate(
        [in_sum[:, :1280], out_sum, small_part.astype(BF)], axis=1
    ).reshape(4, 64, 2432)
    y_parts = send_direct(both_sums, "y")
    gate_up_grad = (
        after(gate_up_sum, both_sums)
        .reshape(2, 4, 64, 2816)
        .transpose(1, 0, 2, 3)
        .reshape(1, 512, 2, width)
        .astype(F32)
    )
    _, _, *y_parts = lax.optimization_barrier((gate_up_grad, ends, *y_parts))
    both_ends = spread(ends, "tensor", 4)
    small_y = sum(p[:, 2304:].astype(F32) for p in y_parts).astype(BF)
    small_y = after(small_y, both_ends)
    small_sum = small_y.astype(F32) + sum(
        from_ahead(small_y, "tensor", k).astype(F32) for k in (1, 2, 3)
    )
    down_grad = down_sum.astype(F32)[None]
    both_ends = both_ends.reshape(count, 2 * MODEL_WIDTH)
    output, input_grad = both_ends[:, :MODEL_WIDTH], both_ends[:, MODEL_WIDTH:]
    query_grad, kv_grad, out_grad = heads_placed(y_parts, y)
    return (
        output,
        input_grad,
        small_sum[:, 17],
        small_sum[:, 16],
        small_sum[:, :8],
        kv_grad,
        query_grad,
        out_grad,
        small_sum[:, 8:16],
        gate_up_grad,
        down_grad,
    )


def solution(mesh):
    split = Mesh(mesh.devices.reshape(4, 4, 2, 4), ("dp", "y", "core", "tensor"))
    rows = ("dp", "y", "core")
    expert = ("y", "core")
    placed = (
        P(rows, None),
        P(rows, None),
        P(),
        P(),
        P(rows, None),
        P(rows, None, "tensor"),
        P(rows, None, "tensor"),
        P(rows, None, "tensor"),
        P(rows, None),
        P(expert, "dp", None, "tensor"),
        P(expert, "tensor", "dp"),
        P(rows, None),
        P(rows, None),
        P(rows, None),
        P(),
    )
    return jax.shard_map(
        body,
        mesh=split,
        in_specs=placed,
        out_specs=(
            P(rows, None),
            P(rows, None),
            P(rows),
            P(rows),
            P(rows, None),
            P(rows, None, "tensor"),
            P(rows, None, "tensor"),
            P(rows, None, "tensor"),
            P(rows, None),
            P(expert, "dp", None, "tensor"),
            P(expert, "tensor", "dp"),
        ),
        check_vma=False,
    )
```
